32 devices in a mesh: dp: 4 (over y, core), tok: 8 (over z, x).
Axes of the slice: x: 2, y: 2, z: 4, core: 2. Of those that a mesh axis runs over, the one named last changes fastest.
Arguments:
- query_in: bfloat16 [4, 2048, 640], P('dp', 'tok'), may hold values from -6 to 6
- key_in: bfloat16 [4, 2048, 640], P('dp', 'tok'), may hold values from -6 to 6
- value_in: bfloat16 [4, 2048, 640], P('dp', 'tok'), may hold values from -6 to 6
- out_grad: bfloat16 [4, 2048, 640], P('dp', 'tok'), may hold values from -6 to 6
- bias: bfloat16 [3, 640], replicated, may hold values from -3 to 3
- lengths: int32 [4, 4], P('dp'), may hold values from 0 to 4, as said below
- widths: int32 [4, 4], P('dp'), may hold values from 64 to 256, as said below
Outputs:
- attn_out: bfloat16 [4, 2048, 640], P('dp', 'tok')
- query_grad: bfloat16 [4, 2048, 640], P('dp', 'tok')
- key_grad: bfloat16 [4, 2048, 640], P('dp', 'tok')
- value_grad: bfloat16 [4, 2048, 640], P('dp', 'tok')
- bias_grad: float32 [3, 640], replicated
The draws below stay inside these ranges and needn't reach their ends.
Inputs may be any that keep to these rules, and one draw needn't show every extreme that they name: Each replica's lengths sum to 8; the nonzero ones come first and zeros follow; the first is 4; every nonzero length but the last nonzero one is at least 3. `widths`: each width is 256 divided by 1, 2 or 4; the first image of every replica has width 256.
All inputs are finite; a program needn't handle non-finite values.
Results may differ from the reference program's by a relative error of at most 0.025.
Values may be sent and summed in bfloat16 or wider, within the bound.
No kernel may reach another device: no remote copies, remote signals or barrier semaphores. Data moves between devices by JAX's collectives and lax.ppermute only.
A program may use at most 64 MiB of HBM per device.

```python
import jax
import jax.numpy as jnp
from jax import lax

HEADS = 8
HEAD_DIM = 80
D = 640
TOK_DEV = 256
SPAN = 4
IMAGES = 4
ROW_TOKENS = 2048
BATCH_ROWS = 4
N_DP = 4
N_TOK = 8


def draw_query_in(key, part):
    key = jax.random.fold_in(key, 1)
    values = jnp.clip(jax.random.normal(key, (BATCH_ROWS, ROW_TOKENS, D), jnp.float32), -6.0, 6.0)
    return values.astype(jnp.bfloat16)


def draw_key_in(key, part):
    key = jax.random.fold_in(key, 2)
    values = jnp.clip(jax.random.normal(key, (BATCH_ROWS, ROW_TOKENS, D), jnp.float32), -6.0, 6.0)
    return values.astype(jnp.bfloat16)


def draw_widths(key, part):
    key = jax.random.fold_in(key, 3)
    powers = jax.random.randint(key, (BATCH_ROWS, IMAGES), 0, 3)
    widths = TOK_DEV // 2 ** powers
    widths = widths.at[:, 0].set(TOK_DEV)
    return widths.astype(jnp.int32)


def draw_lengths(key, part):
    key = jax.random.fold_in(key, 4)
    drawn = SPAN - jax.random.randint(key, (BATCH_ROWS, IMAGES), 0, SPAN // 2)
    drawn = drawn.at[:, 0].set(SPAN)
    finish = jnp.cumsum(drawn, axis=1)
    begins = finish - drawn
    lengths = jnp.clip(N_TOK - begins, 0, drawn)
    return lengths.astype(jnp.int32)


def block_levels(key, shape, pieces, least, largest):
    def one(dim, parts):
        draws = jax.random.uniform(jax.random.fold_in(jax.random.fold_in(key, 6), dim), (parts,), jnp.float32, least / len(pieces), largest / len(pieces))
        return jnp.repeat(jnp.exp(draws), shape[dim] // parts).reshape((-1,) + (1,) * (len(shape) - dim - 1))

    factor_of = one(*pieces[0])
    for cut in pieces[1:]:
        factor_of = factor_of * one(*cut)
    return factor_of


def bell_draw(key, shape, scale, most, shards=(), kind=jnp.bfloat16):
    gain = block_levels(key, shape, shards, -0.22, 0.18) if shards else 1.0
    entries = jax.random.normal(key, shape, jnp.float32) * scale * gain
    return jnp.minimum(jnp.maximum(entries, -most), most).astype(kind)


def setup_inputs(seed: int = 0) -> dict:
    arg_keys = jax.random.split(jax.random.key(seed), 8)
    return {
        "query_in": draw_query_in(jax.random.fold_in(arg_keys[7], 71), 0),
        "key_in": draw_key_in(jax.random.fold_in(arg_keys[7], 71), 0),
        "value_in": bell_draw(arg_keys[2], (BATCH_ROWS, ROW_TOKENS, D), 1.0, 6.0, ((0, 4), (1, 8))),
        "out_grad": bell_draw(arg_keys[3], (BATCH_ROWS, ROW_TOKENS, D), 1.0, 6.0, ((0, 4), (1, 8))),
        "bias": bell_draw(arg_keys[4], (3, D), 0.5, 3.0),
        "lengths": draw_lengths(jax.random.fold_in(arg_keys[7], 71), 0),
        "widths": draw_widths(jax.random.fold_in(arg_keys[7], 71), 0),
    }


rope_base = 10000.0


def image_ids(spots, ends):
    return jnp.sum((spots[:, None] >= ends[None, :]).astype(jnp.int32), axis=1)


def rotary(spots, lengths_row, widths_row, tokd):
    ends = (jnp.cumsum(lengths_row) * tokd).astype(jnp.int32)
    ids = image_ids(spots, ends)
    starts = (ends - lengths_row * tokd).astype(jnp.int32)
    onehot = ids[:, None] == jnp.arange(lengths_row.shape[0], dtype=jnp.int32)[None, :]
    start = jnp.sum(jnp.where(onehot, starts[None, :], 0), axis=1).astype(jnp.int32)
    width = jnp.sum(jnp.where(onehot, widths_row[None, :], 1), axis=1).astype(jnp.int32)
    width = jnp.maximum(width - (lengths_row.shape[0] - 1), 1)
    local = spots - start
    rowpos = local // width
    colpos = local % width
    quarter = HEAD_DIM // 4
    inverse = rope_base ** (-jnp.arange(quarter, dtype=jnp.float32) / quarter)
    angles = jnp.concatenate([rowpos.astype(jnp.float32)[:, None] * inverse, colpos.astype(jnp.float32)[:, None] * inverse], axis=1)
    angles = jnp.concatenate([angles, angles], axis=1)
    return jnp.cos(angles), jnp.sin(angles), ids


def rotate(values, cosv, sinv):
    half = values.shape[-1] // 2
    turned = jnp.concatenate([-values[..., half:], values[..., :half]], axis=-1)
    return values * cosv + turned * sinv


def unrotate(values, cosv, sinv):
    half = values.shape[-1] // 2
    scaled = values * sinv
    return values * cosv + jnp.concatenate([scaled[..., half:], -scaled[..., :half]], axis=-1)


def attend(query_blk, key_win, value_win, grad_blk, mask):
    scale = HEAD_DIM ** -0.5
    scores = jnp.einsum('qhd,khd->hqk', query_blk.astype(jnp.float32), key_win.astype(jnp.float32)) * scale
    scores = jnp.where(mask[None], scores, -1e30)
    top = jnp.max(scores, axis=-1, keepdims=True)
    expo = jnp.exp(scores - top)
    probs = expo / jnp.sum(expo, axis=-1, keepdims=True)
    probs_b = probs.astype(jnp.bfloat16)
    out_b = jnp.einsum('hqk,khd->qhd', probs_b.astype(jnp.float32), value_win.astype(jnp.float32)).astype(jnp.bfloat16)
    delta = jnp.sum(grad_blk.astype(jnp.float32) * out_b.astype(jnp.float32), axis=-1).T
    dprobs = jnp.einsum('qhd,khd->hqk', grad_blk.astype(jnp.float32), value_win.astype(jnp.float32))
    dscore_b = (probs * (dprobs - delta[:, :, None]) * scale).astype(jnp.bfloat16)
    dquery = jnp.einsum('hqk,khd->qhd', dscore_b.astype(jnp.float32), key_win.astype(jnp.float32))
    dkey = jnp.einsum('hqk,qhd->khd', dscore_b.astype(jnp.float32), query_blk.astype(jnp.float32))
    dvalue = jnp.einsum('hqk,qhd->khd', probs_b.astype(jnp.float32), grad_blk.astype(jnp.float32))
    return out_b, dquery, dkey, dvalue


def one_row(query_in, key_in, value_in, out_grad, bias, lengths_row, widths_row):
    total = N_TOK * TOK_DEV
    spots = jnp.arange(total, dtype=jnp.int32)
    cosv, sinv, ids = rotary(spots, lengths_row, widths_row, TOK_DEV)
    cosv = cosv[:, None, :]
    sinv = sinv[:, None, :]
    bias_f = bias.astype(jnp.float32).reshape(3, HEADS, HEAD_DIM)
    query_rot = rotate(query_in.astype(jnp.float32).reshape(total, HEADS, HEAD_DIM) + bias_f[0], cosv, sinv).astype(jnp.bfloat16)
    key_rot = rotate(key_in.astype(jnp.float32).reshape(total, HEADS, HEAD_DIM) + bias_f[1], cosv, sinv).astype(jnp.bfloat16)
    value_b = (value_in.astype(jnp.float32).reshape(total, HEADS, HEAD_DIM) + bias_f[2]).astype(jnp.bfloat16)
    grads = out_grad.reshape(total, HEADS, HEAD_DIM)
    margin = (SPAN - 1) * TOK_DEV
    window = (2 * SPAN - 1) * TOK_DEV
    key_pad = jnp.pad(key_rot, ((margin, margin), (0, 0), (0, 0)))
    value_pad = jnp.pad(value_b, ((margin, margin), (0, 0), (0, 0)))
    ids_pad = jnp.pad(ids, (margin, margin), constant_values=-1)

    def shard(number):
        begin = (number * TOK_DEV).astype(jnp.int32)
        query_blk = lax.dynamic_slice_in_dim(query_rot, begin, TOK_DEV, 0)
        grad_blk = lax.dynamic_slice_in_dim(grads, begin, TOK_DEV, 0)
        own_ids = lax.dynamic_slice_in_dim(ids, begin, TOK_DEV, 0)
        key_win = lax.dynamic_slice_in_dim(key_pad, begin, window, 0)
        value_win = lax.dynamic_slice_in_dim(value_pad, begin, window, 0)
        win_ids = lax.dynamic_slice_in_dim(ids_pad, begin, window, 0)
        mask = own_ids[:, None] == win_ids[None, :]
        return attend(query_blk, key_win, value_win, grad_blk, mask)

    outs, dquery, dkey, dvalue = lax.map(shard, jnp.arange(N_TOK, dtype=jnp.int32))
    terms = jnp.stack([dkey, dvalue], axis=1)

    def add_window(carry, item):
        number, piece = item
        begin = (number * TOK_DEV).astype(jnp.int32)
        current = lax.dynamic_slice_in_dim(carry, begin, window, 1)
        return lax.dynamic_update_slice_in_dim(carry, current + piece, begin, 1), None

    start_acc = jnp.zeros((2, total + 2 * margin, HEADS, HEAD_DIM), jnp.float32)
    summed, _ = lax.scan(add_window, start_acc, (jnp.arange(N_TOK, dtype=jnp.int32), terms))
    summed = summed[:, margin:margin + total]
    dquery_rot = dquery.reshape(total, HEADS, HEAD_DIM)
    dquery_f = unrotate(dquery_rot, cosv, sinv).reshape(total, HEADS * HEAD_DIM)
    dkey_f = unrotate(summed[0], cosv, sinv).reshape(total, HEADS * HEAD_DIM)
    dvalue_f = summed[1].reshape(total, HEADS * HEAD_DIM)
    sums = jnp.stack([jnp.sum(dquery_f, axis=0), jnp.sum(dkey_f, axis=0), jnp.sum(dvalue_f, axis=0)])
    return (outs.reshape(total, HEADS * HEAD_DIM), dquery_f.astype(jnp.bfloat16), dkey_f.astype(jnp.bfloat16), dvalue_f.astype(jnp.bfloat16), sums)


def reference(query_in, key_in, value_in, out_grad, bias, lengths, widths):
    def per_row(items):
        return one_row(items[0], items[1], items[2], items[3], bias, items[4], items[5])

    attn_out, query_grad, key_grad, value_grad, sums = lax.map(per_row, (query_in, key_in, value_in, out_grad, lengths, widths))
    count = N_DP * N_TOK * TOK_DEV
    bias_grad = jnp.sum(sums, axis=0) * (1.0 / (count ** 0.5))
    return attn_out, query_grad, key_grad, value_grad, bias_grad
```

```python
import functools

import jax
import jax.numpy as jnp
import numpy as np
from jax import lax
from jax.experimental import pallas as pl
from jax.experimental.pallas import tpu as pltpu
from jax.sharding import PartitionSpec as P

HEADS = 8
HEAD_DIM = 80
SPAN = 4
OWN_HEADS = HEADS // SPAN
PART = OWN_HEADS * HEAD_DIM
SCALE = HEAD_DIM**-0.5
LOG2E = 1.4426950408889634
NEG = -1e30

rope_base = 10000.0


def trade_rounds(count):
    def pairs_of(shift):
        found = []
        for source in range(count):
            target = source + shift
            if 0 <= target < count and (source < SPAN) == (target < SPAN):
                found.append((source, target))
        return found

    rounds = []
    for shift in range(1, SPAN):
        ahead, back = pairs_of(shift), pairs_of(shift - SPAN)
        both = ahead + back
        if len({s for s, _ in both}) == len(both) and len({t for _, t in both}) == len(both):
            rounds.append((shift, both))
        else:
            rounds.append((shift, ahead))
            rounds.append((shift - SPAN, back))
    return rounds


def source_table(rounds, count):
    table = np.full((len(rounds), count), -1, np.int32)
    for number, (_, pairs) in enumerate(rounds):
        for source, target in pairs:
            table[number, target] = source
    return table


def target_table(rounds, count):
    table = np.full((len(rounds), count), -1, np.int32)
    for number, (_, pairs) in enumerate(rounds):
        for source, target in pairs:
            table[number, source] = target
    return table


def image_of(block, lengths, images):
    image = jnp.int32(0)
    start = jnp.int32(0)
    begin = jnp.int32(0)
    for number in range(images):
        size = lengths[0, number]
        inside = (block >= begin) & (block < begin + size)
        image = jnp.where(inside, number, image)
        start = jnp.where(inside, begin, start)
        begin = begin + size
    return image, start


def handler_of(start, residue, count):
    device = start + lax.rem(residue - lax.rem(start, SPAN) + SPAN, SPAN)
    return jnp.where(device >= count, device - SPAN, device)


def swap_halves(values):
    half = HEAD_DIM // 2
    return jnp.concatenate([values[:, half:], values[:, :half]], axis=1)


def pack_kernel(shifts, query, key, value, grad, *outs):
    me = lax.axis_index("tok")
    for residue in range(SPAN):
        lanes = slice(residue * PART, (residue + 1) * PART)
        piece = jnp.concatenate([ref[:, lanes] for ref in (query, key, value, grad)], axis=1)
        for shift, out in zip(shifts, outs):

            @pl.when(lax.rem(me + shift + SPAN, SPAN) == residue)
            def _(out=out, piece=piece):
                out[...] = piece


def angles_kernel(images, tokd, lengths, widths, table, inverse, cos_out, sin_out):
    me = lax.axis_index("tok")
    slots = table.shape[0] + 1
    lane = lax.broadcasted_iota(jnp.int32, (tokd, HEAD_DIM), 1)
    spot = lax.broadcasted_iota(jnp.int32, (tokd, HEAD_DIM), 0)
    quarter = HEAD_DIM // 4
    by_row = lax.rem(lane, 2 * quarter) < quarter
    sign = jnp.where(lane < 2 * quarter, -1.0, 1.0)

    def one(slot, carry):
        block = jnp.where(slot == 0, me, table[jnp.maximum(slot - 1, 0), me])
        image, start = image_of(block, lengths, images)
        width = widths[0, image]
        bits = jnp.where(width == tokd, 0, jnp.where(width * 2 == tokd, 1, 2))
        full = tokd.bit_length() - 1
        local = spot + (block - start) * tokd
        shift = full - bits
        rowpos = lax.shift_right_logical(local, jnp.broadcast_to(shift, local.shape))
        colpos = local & (width - 1)
        angle = jnp.where(by_row, rowpos, colpos).astype(jnp.float32) * inverse[0:1, :]
        rows = pl.ds(pl.multiple_of(slot * tokd, tokd), tokd)
        cos_out[rows, :] = jnp.cos(angle)
        sin_out[rows, :] = jnp.sin(angle) * sign
        return carry

    lax.fori_loop(0, slots, one, 0)


def attend_kernel(slots, count, images, tokd, lengths, table, cosv, sinv, bias, *refs):
    msgs, outs, sums = refs[:slots], refs[slots : 2 * slots], refs[2 * slots]
    q_all, k_all, v_all, dk_acc, dv_acc = refs[2 * slots + 1 :]
    me = lax.axis_index("tok")
    residue = lax.rem(me, SPAN)
    ids = []
    for slot in range(slots):
        block = me if slot == 0 else table[slot - 1, me]
        image, start = image_of(block, lengths, images)
        handled = (block >= 0) & (handler_of(start, residue, count) == me)
        ids.append(jnp.where(handled, image, -1 - slot))
    own_bias = jnp.zeros((3, PART), jnp.float32)
    for number in range(SPAN):
        piece = bias[:, number * PART : (number + 1) * PART].astype(jnp.float32)
        own_bias = jnp.where(residue == number, piece, own_bias)
    transposed = (((1,), (1,)), ((), ()))

    def cut(slot, tensor, head):
        begin = tensor * PART + head * HEAD_DIM
        return slice(begin, begin + HEAD_DIM)

    def block_rows(slot):
        return slice(slot * tokd, (slot + 1) * tokd)

    sums[...] = jnp.zeros_like(sums)
    for head in range(OWN_HEADS):
        lanes = slice(head * HEAD_DIM, (head + 1) * HEAD_DIM)
        for slot in range(slots):
            rows = block_rows(slot)
            cos_b, sin_b = cosv[rows, :], sinv[rows, :]
            for tensor, store in ((0, q_all), (1, k_all)):
                plain = msgs[slot][:, cut(slot, tensor, head)].astype(jnp.float32)
                plain = plain + own_bias[tensor : tensor + 1, lanes]
                turned = plain * cos_b + swap_halves(plain) * sin_b
                store[rows, :] = turned.astype(jnp.bfloat16)
            plain = msgs[slot][:, cut(slot, 2, head)].astype(jnp.float32)
            v_all[rows, :] = (plain + own_bias[2:3, lanes]).astype(jnp.bfloat16)
        dq_total = jnp.zeros((1, HEAD_DIM), jnp.float32)
        for slot in range(slots):
            rows = block_rows(slot)
            query_b = q_all[rows, :]
            grad_b = msgs[slot][:, cut(slot, 3, head)]
            scores = lax.dot_general(
                query_b, k_all[...], transposed, preferred_element_type=jnp.float32
            )
            offs = [jnp.where(ids[slot] == ids[other], 0.0, NEG) for other in range(slots)]
            tops = [
                jnp.max(scores[:, block_rows(other)], axis=1, keepdims=True) + offs[other]
                for other in range(slots)
            ]
            top = functools.reduce(jnp.maximum, tops)
            expo = jnp.concatenate(
                [
                    jnp.exp2(
                        (scores[:, block_rows(other)] - (top - offs[other])) * (SCALE * LOG2E)
                    )
                    for other in range(slots)
                ],
                axis=1,
            )
            probs = expo * (1.0 / jnp.sum(expo, axis=1, keepdims=True))
            probs_b = probs.astype(jnp.bfloat16)
            out_b = jnp.dot(probs_b, v_all[...], preferred_element_type=jnp.float32).astype(
                jnp.bfloat16
            )
            delta = jnp.sum(
                grad_b.astype(jnp.float32) * out_b.astype(jnp.float32), axis=1, keepdims=True
            )
            dprobs = lax.dot_general(
                grad_b, v_all[...], transposed, preferred_element_type=jnp.float32
            )
            dscore_b = (probs * (dprobs - delta)).astype(jnp.bfloat16)
            dquery = jnp.dot(dscore_b, k_all[...], preferred_element_type=jnp.float32) * SCALE
            part_k = jnp.dot(query_b.T, dscore_b, preferred_element_type=jnp.float32)
            part_v = jnp.dot(grad_b.T, probs_b, preferred_element_type=jnp.float32)
            if slot == 0:
                dk_acc[...] = part_k
                dv_acc[...] = part_v
            else:
                dk_acc[...] += part_k
                dv_acc[...] += part_v
            outs[slot][:, cut(slot, 0, head)] = out_b
            dquery = dquery * cosv[rows, :] - swap_halves(dquery) * sinv[rows, :]
            dq_total = dq_total + jnp.where(
                ids[slot] >= 0, jnp.sum(dquery, axis=0, keepdims=True), 0.0
            )
            outs[slot][:, cut(slot, 1, head)] = dquery.astype(jnp.bfloat16)
        dk_total = jnp.zeros((1, HEAD_DIM), jnp.float32)
        dv_total = jnp.zeros((1, HEAD_DIM), jnp.float32)
        for slot in range(slots):
            rows = block_rows(slot)
            dkey = dk_acc[:, rows].T * SCALE
            dkey = dkey * cosv[rows, :] - swap_halves(dkey) * sinv[rows, :]
            dvalue = dv_acc[:, rows].T
            outs[slot][:, cut(slot, 2, head)] = dkey.astype(jnp.bfloat16)
            outs[slot][:, cut(slot, 3, head)] = dvalue.astype(jnp.bfloat16)
            live = ids[slot] >= 0
            dk_total = dk_total + jnp.where(live, jnp.sum(dkey, axis=0, keepdims=True), 0.0)
            dv_total = dv_total + jnp.where(live, jnp.sum(dvalue, axis=0, keepdims=True), 0.0)
        for number, total in enumerate((dq_total, dk_total, dv_total)):
            at = number * OWN_HEADS + head
            sums[at : at + 1, :HEAD_DIM] = total


def unpack_kernel(slots, count, images, lengths, table, *refs):
    msgs, outs = refs[:slots], refs[slots:]
    me = lax.axis_index("tok")
    _, start = image_of(me, lengths, images)
    for residue in range(SPAN):
        lanes = slice(residue * PART, (residue + 1) * PART)
        handler = handler_of(start, residue, count)
        for slot in range(slots):
            source = me if slot == 0 else table[slot - 1, me]

            @pl.when(source == handler)
            def _(slot=slot, lanes=lanes):
                for number, out in enumerate(outs):
                    out[:, lanes] = msgs[slot][:, number * PART : (number + 1) * PART]


def on_device(query_in, key_in, value_in, out_grad, bias, lengths, widths):
    tokd = query_in.shape[1]
    model = query_in.shape[2]
    images = lengths.shape[1]
    count = lax.axis_size("tok")
    rounds = trade_rounds(count)
    shifts = [0] + [shift for shift, _ in rounds]
    slots = len(shifts)
    table = jnp.asarray(source_table(rounds, count))
    quarter = HEAD_DIM // 4
    inverse = rope_base ** (-np.arange(quarter, dtype=np.float64) / quarter)
    inverse = jnp.asarray(np.tile(inverse, 4)[None], jnp.float32)
    smem = pl.BlockSpec(memory_space=pltpu.SMEM)
    vmem = pl.BlockSpec(memory_space=pltpu.VMEM)
    message = jax.ShapeDtypeStruct((tokd, model), jnp.bfloat16)

    def params(mib):
        return pltpu.CompilerParams(vmem_limit_bytes=mib * 1024 * 1024)

    sends = pl.pallas_call(
        functools.partial(pack_kernel, shifts),
        out_shape=[message] * slots,
        in_specs=[vmem] * 4,
        out_specs=[vmem] * slots,
        compiler_params=params(16),
        name="pack_heads",
    )(query_in[0], key_in[0], value_in[0], out_grad[0])
    got = [sends[0]] + [
        lax.ppermute(send, "tok", pairs) for send, (_, pairs) in zip(sends[1:], rounds)
    ]
    table_shape = jax.ShapeDtypeStruct((slots * tokd, HEAD_DIM), jnp.float32)
    cosv, sinv = pl.pallas_call(
        functools.partial(angles_kernel, images, tokd),
        out_shape=[table_shape] * 2,
        in_specs=[smem, smem, smem, vmem],
        out_specs=[vmem] * 2,
        compiler_params=params(16),
        cost_estimate=pl.CostEstimate(
            flops=slots * tokd * HEAD_DIM * 200, bytes_accessed=0, transcendentals=0
        ),
        name="rotary_angles",
    )(lengths, widths, table, inverse)
    span = slots * tokd
    results = pl.pallas_call(
        functools.partial(attend_kernel, slots, count, images, tokd),
        out_shape=[message] * slots + [jax.ShapeDtypeStruct((8, 128), jnp.float32)],
        in_specs=[smem, smem] + [vmem] * (3 + slots),
        out_specs=[vmem] * (slots + 1),
        scratch_shapes=[pltpu.VMEM((span, HEAD_DIM), jnp.bfloat16)] * 3
        + [pltpu.VMEM((HEAD_DIM, span), jnp.float32)] * 2,
        compiler_params=params(40),
        cost_estimate=pl.CostEstimate(
            flops=12 * span * span * PART, bytes_accessed=0, transcendentals=0
        ),
        name="attend",
    )(lengths, table, cosv, sinv, bias, *got)
    sums = results[slots]
    back = [results[0]] + [
        lax.ppermute(result, "tok", [(target, source) for source, target in pairs])
        for result, (_, pairs) in zip(results[1:slots], rounds)
    ]
    every = lax.all_gather(sums, ("dp", "tok"))
    n_dp = lax.axis_size("dp")
    every = jnp.sum(every.reshape(n_dp * (count // SPAN), SPAN, 8, 128), axis=0)
    parts = every[:, : 3 * OWN_HEADS, :HEAD_DIM].reshape(SPAN, 3, PART)
    tokens_all = n_dp * count * tokd
    bias_grad = parts.transpose(1, 0, 2).reshape(3, model) * (1.0 / tokens_all**0.5)
    outs = pl.pallas_call(
        functools.partial(unpack_kernel, slots, count, images),
        out_shape=[message] * 4,
        in_specs=[smem, smem] + [vmem] * slots,
        out_specs=[vmem] * 4,
        compiler_params=params(16),
        name="unpack_heads",
    )(lengths, jnp.asarray(target_table(rounds, count)), *back)
    return tuple(out[None] for out in outs) + (bias_grad,)


def solution(mesh):
    in_specs = (
        P("dp", "tok", None),
        P("dp", "tok", None),
        P("dp", "tok", None),
        P("dp", "tok", None),
        P(),
        P("dp", None),
        P("dp", None),
    )
    out_specs = (
        P("dp", "tok", None),
        P("dp", "tok", None),
        P("dp", "tok", None),
        P("dp", "tok", None),
        P(),
    )
    return jax.shard_map(
        on_device, mesh=mesh, in_specs=in_specs, out_specs=out_specs, check_vma=False
    )
```

```python
import functools

import jax
import jax.numpy as jnp
import numpy as np
from jax import lax
from jax.experimental import pallas as pl
from jax.experimental.pallas import tpu as pltpu
from jax.sharding import PartitionSpec as P

HEADS = 8
HEAD_DIM = 80
SPAN = 4
OWN_HEADS = HEADS // SPAN
PART = OWN_HEADS * HEAD_DIM
SCALE = HEAD_DIM**-0.5
LOG2E = 1.4426950408889634
NEG = -1e30
LANES = 128

rope_base = 10000.0


def trade_rounds(count):
    def pairs_of(shift):
        found = []
        for source in range(count):
            target = source + shift
            if 0 <= target < count and (source < SPAN) == (target < SPAN):
                found.append((source, target))
        return found

    rounds = []
    for shift in range(1, SPAN):
        ahead, back = pairs_of(shift), pairs_of(shift - SPAN)
        both = ahead + back
        if len({s for s, _ in both}) == len(both) and len({t for _, t in both}) == len(both):
            rounds.append((shift, both))
        else:
            rounds.append((shift, ahead))
            rounds.append((shift - SPAN, back))
    return rounds


def source_table(rounds, count):
    table = np.full((len(rounds), count), -1, np.int32)
    for number, (_, pairs) in enumerate(rounds):
        for source, target in pairs:
            table[number, target] = source
    return table


def target_table(rounds, count):
    table = np.full((len(rounds), count), -1, np.int32)
    for number, (_, pairs) in enumerate(rounds):
        for source, target in pairs:
            table[number, source] = target
    return table


def image_of(block, lengths, images):
    image = jnp.int32(0)
    start = jnp.int32(0)
    begin = jnp.int32(0)
    for number in range(images):
        size = lengths[0, number]
        inside = (block >= begin) & (block < begin + size)
        image = jnp.where(inside, number, image)
        start = jnp.where(inside, begin, start)
        begin = begin + size
    return image, start


def handler_of(start, residue, count):
    device = start + lax.rem(residue - lax.rem(start, SPAN) + SPAN, SPAN)
    return jnp.where(device >= count, device - SPAN, device)


def swap_halves(values):
    half = HEAD_DIM // 2
    zeros = jnp.zeros((values.shape[0], LANES - HEAD_DIM), values.dtype)
    return jnp.concatenate([values[:, half:HEAD_DIM], values[:, :half], zeros], axis=1)


def padded(values):
    zeros = jnp.zeros((values.shape[0], LANES - values.shape[1]), values.dtype)
    return jnp.concatenate([values, zeros], axis=1)


def message_lanes(half, tensor):
    begin = (half * 4 + tensor) * HEAD_DIM
    return slice(begin, begin + HEAD_DIM)


def pack_kernel(shifts, *refs):
    inputs, outs, held, sems = refs[:4], refs[4:-5], refs[-5:-1], refs[-1]
    slots = len(shifts)
    me = lax.axis_index("tok")
    copies = [
        pltpu.make_async_copy(source, target, sems.at[number])
        for number, (source, target) in enumerate(zip(inputs, held))
    ]
    for copy in copies:
        copy.start()
    for copy in copies:
        copy.wait()
    rows = held[0].shape[0] // 2
    for head in range(OWN_HEADS):
        for residue in range(SPAN):
            begin = (residue * OWN_HEADS + head) * HEAD_DIM
            piece = jnp.concatenate(
                [
                    ref[half * rows : (half + 1) * rows, begin : begin + HEAD_DIM]
                    for half in range(2)
                    for ref in held
                ],
                axis=1,
            )
            for slot, shift in enumerate(shifts):

                @pl.when(lax.rem(me + shift + SPAN, SPAN) == residue)
                def _(out=outs[head * slots + slot], piece=piece):
                    out[...] = piece


def angles_kernel(images, tokd, lengths, widths, table, inverse, cos_out, sin_out):
    me = lax.axis_index("tok")
    slots = table.shape[0] + 1
    lane = lax.broadcasted_iota(jnp.int32, (tokd, LANES), 1)
    spot = lax.broadcasted_iota(jnp.int32, (tokd, LANES), 0)
    quarter = HEAD_DIM // 4
    by_row = lax.rem(lane, 2 * quarter) < quarter
    sign = jnp.where(lane < 2 * quarter, -1.0, 1.0)
    keep = jnp.where(lane < HEAD_DIM, 1.0, 0.0)

    def one(slot, carry):
        block = jnp.where(slot == 0, me, table[jnp.maximum(slot - 1, 0), me])
        image, start = image_of(block, lengths, images)
        width = widths[0, image]
        bits = jnp.where(width == tokd, 0, jnp.where(width * 2 == tokd, 1, 2))
        full = tokd.bit_length() - 1
        local = spot + (block - start) * tokd
        shift = full - bits
        rowpos = lax.shift_right_logical(local, jnp.broadcast_to(shift, local.shape))
        colpos = local & (width - 1)
        angle = jnp.where(by_row, rowpos, colpos).astype(jnp.float32) * inverse[0:1, :]
        rows = pl.ds(pl.multiple_of(slot * tokd, tokd), tokd)
        cos_out[rows, :] = jnp.cos(angle) * keep
        sin_out[rows, :] = jnp.sin(angle) * sign
        return carry

    lax.fori_loop(0, slots, one, 0)


def attend_kernel(slots, count, images, tokd, head, factor, lengths, table, cosv, sinv, bias, *refs):
    msgs, refs = refs[:slots], refs[slots:]
    if head > 0:
        before, refs = refs[0], refs[1:]
    outs, sums = refs[:slots], refs[slots]
    q_all, k_all, v_all, dk_acc, dv_acc = refs[slots + 1 :]
    me = lax.axis_index("tok")
    residue = lax.rem(me, SPAN)
    ids = []
    for slot in range(slots):
        block = me if slot == 0 else table[slot - 1, me]
        image, start = image_of(block, lengths, images)
        handled = (block >= 0) & (handler_of(start, residue, count) == me)
        ids.append(jnp.where(handled, image, -1 - slot))
    own_bias = jnp.zeros((3, HEAD_DIM), jnp.float32)
    for number in range(SPAN):
        begin = (number * OWN_HEADS + head) * HEAD_DIM
        piece = bias[:, begin : begin + HEAD_DIM].astype(jnp.float32)
        own_bias = jnp.where(residue == number, piece, own_bias)
    own_bias = padded(own_bias)
    transposed = (((1,), (1,)), ((), ()))
    part = tokd // 2
    lane = lax.broadcasted_iota(jnp.int32, (1, LANES), 1)
    ones = jnp.where((lane == HEAD_DIM) | (lane == HEAD_DIM + 1), 1.0, 0.0)

    def block_rows(slot):
        return slice(slot * tokd, (slot + 1) * tokd)

    for slot in range(slots):
        for half in range(2):
            begin = slot * tokd + half * part
            rows = slice(begin, begin + part)
            cos_b, sin_b = cosv[rows, :], sinv[rows, :]
            for tensor, store in ((0, q_all), (1, k_all)):
                plain = msgs[slot][:, message_lanes(half, tensor)].astype(jnp.float32)
                plain = padded(plain) + own_bias[tensor : tensor + 1, :]
                turned = plain * cos_b + swap_halves(plain) * sin_b
                store[rows, :] = turned.astype(jnp.bfloat16)
            plain = msgs[slot][:, message_lanes(half, 2)].astype(jnp.float32)
            plain = padded(plain) + own_bias[2:3, :] + ones
            v_all[rows, :] = plain.astype(jnp.bfloat16)
    dq_total = jnp.zeros((1, LANES), jnp.float32)
    for slot in range(slots):
        rows = block_rows(slot)
        query_b = q_all[rows, :]
        scores = lax.dot_general(
            query_b, k_all[...], transposed, preferred_element_type=jnp.float32
        )
        offs = [jnp.where(ids[slot] == ids[other], 0.0, NEG) for other in range(slots)]
        tops = [
            jnp.max(scores[:, block_rows(other)], axis=1, keepdims=True) + offs[other]
            for other in range(slots)
        ]
        top = functools.reduce(jnp.maximum, tops)
        expo_b = jnp.concatenate(
            [
                jnp.exp2(
                    (scores[:, block_rows(other)] - (top - offs[other])) * (SCALE * LOG2E)
                ).astype(jnp.bfloat16)
                for other in range(slots)
            ],
            axis=1,
        )
        mixed = jnp.dot(expo_b, v_all[...], preferred_element_type=jnp.float32)
        inv = 1.0 / mixed[:, HEAD_DIM : HEAD_DIM + 1]
        out_b = (mixed * inv).astype(jnp.bfloat16)
        grad = jnp.concatenate(
            [msgs[slot][:, message_lanes(half, 3)] for half in range(2)], axis=0
        ).astype(jnp.float32)
        grad = padded(grad)
        delta = jnp.sum(grad * out_b.astype(jnp.float32), axis=1, keepdims=True) * inv
        coarse = delta.astype(jnp.bfloat16).astype(jnp.float32)
        grad_b = jnp.where(
            lane == HEAD_DIM,
            -coarse,
            jnp.where(lane == HEAD_DIM + 1, coarse - delta, grad * inv),
        ).astype(jnp.bfloat16)
        dprobs = lax.dot_general(
            grad_b, v_all[...], transposed, preferred_element_type=jnp.float32
        )
        dscore_b = (expo_b.astype(jnp.float32) * dprobs).astype(jnp.bfloat16)
        dquery = jnp.dot(dscore_b, k_all[...], preferred_element_type=jnp.float32) * SCALE
        part_k = jnp.dot(query_b.T, dscore_b, preferred_element_type=jnp.float32)
        part_v = jnp.dot(grad_b.T, expo_b, preferred_element_type=jnp.float32)
        if slot == 0:
            dk_acc[...] = part_k
            dv_acc[...] = part_v
        else:
            dk_acc[...] += part_k
            dv_acc[...] += part_v
        dquery = dquery * cosv[rows, :] - swap_halves(dquery) * sinv[rows, :]
        dq_total = dq_total + jnp.where(
            ids[slot] >= 0, jnp.sum(dquery, axis=0, keepdims=True), 0.0
        )
        dquery_b = dquery.astype(jnp.bfloat16)
        for half in range(2):
            inner = slice(half * part, (half + 1) * part)
            outs[slot][:, message_lanes(half, 0)] = out_b[inner, :HEAD_DIM]
            outs[slot][:, message_lanes(half, 1)] = dquery_b[inner, :HEAD_DIM]
    dk_total = jnp.zeros((1, LANES), jnp.float32)
    dv_total = jnp.zeros((1, LANES), jnp.float32)
    for slot in range(slots):
        rows = block_rows(slot)
        dkey = dk_acc[:, rows].T * SCALE
        dkey = dkey * cosv[rows, :] - swap_halves(dkey) * sinv[rows, :]
        dvalue = dv_acc[:, rows].T
        dkey_b, dvalue_b = dkey.astype(jnp.bfloat16), dvalue.astype(jnp.bfloat16)
        for half in range(2):
            inner = slice(half * part, (half + 1) * part)
            outs[slot][:, message_lanes(half, 2)] = dkey_b[inner, :HEAD_DIM]
            outs[slot][:, message_lanes(half, 3)] = dvalue_b[inner, :HEAD_DIM]
        live = ids[slot] >= 0
        dk_total = dk_total + jnp.where(live, jnp.sum(dkey, axis=0, keepdims=True), 0.0)
        dv_total = dv_total + jnp.where(live, jnp.sum(dvalue, axis=0, keepdims=True), 0.0)
    sums[...] = jnp.zeros_like(sums) if head == 0 else before[...]
    for number in range(SPAN):
        begin = (number * OWN_HEADS + head) * HEAD_DIM

        @pl.when(residue == number)
        def _(begin=begin):
            for at, total in enumerate((dq_total, dk_total, dv_total)):
                sums[at : at + 1, begin : begin + HEAD_DIM] = total[:, :HEAD_DIM] * factor


def unpack_kernel(slots, count, images, lengths, table, *refs):
    msgs, outs = refs[: OWN_HEADS * slots], refs[OWN_HEADS * slots :]
    me = lax.axis_index("tok")
    _, start = image_of(me, lengths, images)
    part = outs[0].shape[0] // 2
    for residue in range(SPAN):
        handler = handler_of(start, residue, count)
        for slot in range(slots):
            source = me if slot == 0 else table[slot - 1, me]

            @pl.when(source == handler)
            def _(slot=slot, residue=residue):
                for number, out in enumerate(outs):
                    for half in range(2):
                        lanes = message_lanes(half, number)
                        piece = jnp.concatenate(
                            [msgs[head * slots + slot][:, lanes] for head in range(OWN_HEADS)],
                            axis=1,
                        )
                        out[half * part : (half + 1) * part, residue * PART : (residue + 1) * PART] = piece


def sum_over(value, axis):
    size = lax.axis_size(axis)
    if size & (size - 1):
        return lax.psum(value, axis)
    step = 1
    while step < size:
        value = value + lax.ppermute(value, axis, [(one, one ^ step) for one in range(size)])
        step *= 2
    return value


def on_device(query_in, key_in, value_in, out_grad, bias, lengths, widths):
    tokd = query_in.shape[1]
    model = query_in.shape[2]
    images = lengths.shape[1]
    count = lax.axis_size("tok")
    rounds = trade_rounds(count)
    shifts = [0] + [shift for shift, _ in rounds]
    slots = len(shifts)
    table = jnp.asarray(source_table(rounds, count))
    quarter = HEAD_DIM // 4
    inverse = rope_base ** (-np.arange(quarter, dtype=np.float64) / quarter)
    inverse = np.concatenate([np.tile(inverse, 4), np.zeros(LANES - HEAD_DIM)])
    inverse = jnp.asarray(inverse[None], jnp.float32)
    smem = pl.BlockSpec(memory_space=pltpu.SMEM)
    vmem = pl.BlockSpec(memory_space=pltpu.VMEM)
    hbm = pl.BlockSpec(memory_space=pltpu.HBM)
    whole = jax.ShapeDtypeStruct((tokd, model), jnp.bfloat16)
    message = jax.ShapeDtypeStruct((tokd // 2, model), jnp.bfloat16)
    sums_shape = jax.ShapeDtypeStruct((8, model), jnp.float32)
    tokens_all = lax.axis_size("dp") * count * tokd

    def params(mib):
        return pltpu.CompilerParams(vmem_limit_bytes=mib * 1024 * 1024)

    sends = pl.pallas_call(
        functools.partial(pack_kernel, shifts),
        out_shape=[message] * (OWN_HEADS * slots),
        in_specs=[hbm] * 4,
        out_specs=[vmem] * (OWN_HEADS * slots),
        scratch_shapes=[pltpu.VMEM((tokd, model), jnp.bfloat16)] * 4
        + [pltpu.SemaphoreType.DMA((4,))],
        compiler_params=params(16),
        name="pack_heads",
    )(query_in[0], key_in[0], value_in[0], out_grad[0])
    got = []
    for head in range(OWN_HEADS):
        mine = sends[head * slots : (head + 1) * slots]
        got.append(
            [mine[0]]
            + [lax.ppermute(send, "tok", pairs) for send, (_, pairs) in zip(mine[1:], rounds)]
        )
    span = slots * tokd
    table_shape = jax.ShapeDtypeStruct((span, LANES), jnp.float32)
    cosv, sinv = pl.pallas_call(
        functools.partial(angles_kernel, images, tokd),
        out_shape=[table_shape] * 2,
        in_specs=[smem, smem, smem, vmem],
        out_specs=[vmem] * 2,
        compiler_params=params(16),
        cost_estimate=pl.CostEstimate(
            flops=span * LANES * 200, bytes_accessed=0, transcendentals=0
        ),
        name="rotary_angles",
    )(lengths, widths, table, inverse)
    back = []
    sums = None
    for head in range(OWN_HEADS):
        operands = [lengths, table, cosv, sinv, bias] + got[head]
        if head > 0:
            operands.append(sums)
        results = pl.pallas_call(
            functools.partial(
                attend_kernel, slots, count, images, tokd, head, 1.0 / tokens_all**0.5
            ),
            out_shape=[message] * slots + [sums_shape],
            in_specs=[smem, smem] + [vmem] * (len(operands) - 2),
            out_specs=[vmem] * (slots + 1),
            scratch_shapes=[pltpu.VMEM((span, LANES), jnp.bfloat16)] * 3
            + [pltpu.VMEM((LANES, span), jnp.float32)] * 2,
            compiler_params=params(32),
            cost_estimate=pl.CostEstimate(
                flops=12 * span * span * 256, bytes_accessed=0, transcendentals=0
            ),
            name="attend_head",
        )(*operands)
        sums = results[slots]
        back.append(results[0])
        back += [
            lax.ppermute(result, "tok", [(target, source) for source, target in pairs])
            for result, (_, pairs) in zip(results[1:slots], rounds)
        ]
    sums = sum_over(sum_over(sums, "dp"), "tok")
    outs = pl.pallas_call(
        functools.partial(unpack_kernel, slots, count, images),
        out_shape=[whole] * 4,
        in_specs=[smem, smem] + [vmem] * (OWN_HEADS * slots),
        out_specs=[vmem] * 4,
        compiler_params=params(16),
        name="unpack_heads",
    )(lengths, jnp.asarray(target_table(rounds, count)), *back)
    return tuple(out[None] for out in outs) + (sums[:3],)


def solution(mesh):
    in_specs = (
        P("dp", "tok", None),
        P("dp", "tok", None),
        P("dp", "tok", None),
        P("dp", "tok", None),
        P(),
        P("dp", None),
        P("dp", None),
    )
    out_specs = (
        P("dp", "tok", None),
        P("dp", "tok", None),
        P("dp", "tok", None),
        P("dp", "tok", None),
        P(),
    )
    return jax.shard_map(
        on_device, mesh=mesh, in_specs=in_specs, out_specs=out_specs, check_vma=False
    )
```

```python
import functools

import jax
import jax.numpy as jnp
import numpy as np
from jax import lax
from jax.experimental import pallas as pl
from jax.experimental.pallas import tpu as pltpu
from jax.sharding import PartitionSpec as P

HEADS = 8
HEAD_DIM = 80
SPAN = 4
OWN_HEADS = HEADS // SPAN
PART = OWN_HEADS * HEAD_DIM
SCALE = HEAD_DIM**-0.5
LOG2E = 1.4426950408889634
NEG = -1e30
LANES = 128
HALF = HEAD_DIM // 2
PACK_MIB = 60

rope_base = 10000.0


def trade_rounds(count):
    def pairs_of(shift):
        found = []
        for source in range(count):
            target = source + shift
            if 0 <= target < count and (source < SPAN) == (target < SPAN):
                found.append((source, target))
        return found

    rounds = []
    for shift in range(1, SPAN):
        ahead, back = pairs_of(shift), pairs_of(shift - SPAN)
        both = ahead + back
        if len({s for s, _ in both}) == len(both) and len({t for _, t in both}) == len(both):
            rounds.append((shift, both))
        else:
            rounds.append((shift, ahead))
            rounds.append((shift - SPAN, back))
    return rounds


def source_table(rounds, count):
    table = np.full((len(rounds), count), -1, np.int32)
    for number, (_, pairs) in enumerate(rounds):
        for source, target in pairs:
            table[number, target] = source
    return table


def target_table(rounds, count):
    table = np.full((len(rounds), count), -1, np.int32)
    for number, (_, pairs) in enumerate(rounds):
        for source, target in pairs:
            table[number, source] = target
    return table


def image_of(block, lengths, images):
    image = jnp.int32(0)
    start = jnp.int32(0)
    begin = jnp.int32(0)
    for number in range(images):
        size = lengths[0, number]
        inside = (block >= begin) & (block < begin + size)
        image = jnp.where(inside, number, image)
        start = jnp.where(inside, begin, start)
        begin = begin + size
    return image, start


def handler_of(start, residue, count):
    device = start + lax.rem(residue - lax.rem(start, SPAN) + SPAN, SPAN)
    return jnp.where(device >= count, device - SPAN, device)


def message_rows(tensor):
    return slice(tensor * HEAD_DIM, (tensor + 1) * HEAD_DIM)


def head_rows(residue, head):
    begin = (residue * OWN_HEADS + head) * HEAD_DIM
    return pl.ds(pl.multiple_of(begin, 16), HEAD_DIM)


def rotate(values, cosv, sinv):
    first, second = values[:HALF], values[HALF:]
    return jnp.concatenate([first * cosv - second * sinv, second * cosv + first * sinv], axis=0)


def unrotate(values, cosv, sinv):
    first, second = values[:HALF], values[HALF:]
    return jnp.concatenate([first * cosv + second * sinv, second * cosv - first * sinv], axis=0)


def pack_kernel(shifts, *refs):
    inputs, outs, held, turned, sems = refs[:4], refs[4:-9], refs[-9:-5], refs[-5:-1], refs[-1]
    slots = len(shifts)
    me = lax.axis_index("tok")
    copies = [
        pltpu.make_async_copy(source, target, sems.at[number])
        for number, (source, target) in enumerate(zip(inputs, held))
    ]
    for copy in copies:
        copy.start()
    for copy, source, target in zip(copies, held, turned):
        copy.wait()
        target[...] = source[...].T
    for head in range(OWN_HEADS):
        for slot, shift in enumerate(shifts):
            residue = lax.rem(me + shift + SPAN, SPAN)
            for number, source in enumerate(turned):
                outs[head * slots + slot][message_rows(number), :] = source[
                    head_rows(residue, head), :
                ]


def tables_kernel(images, tokd, lengths, widths, table, inverse, bias, cos_out, sin_out, bias_out):
    me = lax.axis_index("tok")
    slots = table.shape[0] + 1
    spot = lax.broadcasted_iota(jnp.int32, (HALF, tokd), 1)
    by_row = lax.broadcasted_iota(jnp.int32, (HALF, tokd), 0) < HALF // 2
    for slot in range(slots):
        block = me if slot == 0 else table[slot - 1, me]
        image, start = image_of(block, lengths, images)
        width = widths[0, image]
        bits = jnp.where(width == tokd, 0, jnp.where(width * 2 == tokd, 1, 2))
        shift = tokd.bit_length() - 1 - bits
        local = spot + (block - start) * tokd
        rowpos = lax.shift_right_logical(local, jnp.broadcast_to(shift, local.shape))
        colpos = local & (width - 1)
        angle = jnp.where(by_row, rowpos, colpos).astype(jnp.float32) * inverse[:, 0:1]
        cos_out[:, slot * tokd : (slot + 1) * tokd] = jnp.cos(angle)
        sin_out[:, slot * tokd : (slot + 1) * tokd] = jnp.sin(angle)
    plain = bias[...].astype(jnp.float32)
    rest = jnp.zeros((LANES - plain.shape[0], plain.shape[1]), jnp.float32)
    bias_out[...] = jnp.concatenate([plain, rest], axis=0).T


def attend_kernel(slots, count, images, tokd, head, factor, lengths, table, cosv, sinv, bias, *refs):
    msgs, refs = refs[:slots], refs[slots:]
    if head > 0:
        before, refs = refs[0], refs[1:]
    outs, sums = refs[:slots], refs[slots]
    qt_all, kt_all, vt_all, q_all, k_all, v_all, g_all, s_buf, e_buf, d_buf = refs[slots + 1 :]
    me = lax.axis_index("tok")
    residue = lax.rem(me, SPAN)
    ids = []
    for slot in range(slots):
        block = me if slot == 0 else table[slot - 1, me]
        image, start = image_of(block, lengths, images)
        handled = (block >= 0) & (handler_of(start, residue, count) == me)
        ids.append(jnp.where(handled, image, -1 - slot))
    own_bias = bias[head_rows(residue, head), :]
    rest_row = lax.broadcasted_iota(jnp.int32, (LANES - HEAD_DIM, tokd), 0)
    zeros = jnp.zeros((LANES - HEAD_DIM, tokd), jnp.float32)
    ones = jnp.where(rest_row < 2, 1.0, 0.0)

    def block_of(slot):
        return slice(slot * tokd, (slot + 1) * tokd)

    def stage(slot):
        at = block_of(slot)
        cos_b, sin_b = cosv[:, at], sinv[:, at]
        query, key, value = (
            msgs[slot][message_rows(tensor), :].astype(jnp.float32)
            + own_bias[:, tensor : tensor + 1]
            for tensor in range(3)
        )
        query = rotate(query, cos_b, sin_b) * (SCALE * LOG2E)
        for values, rest, turned, plain in (
            (query, zeros, qt_all, q_all),
            (rotate(key, cos_b, sin_b), zeros, kt_all, k_all),
            (value, ones, vt_all, v_all),
        ):
            values = jnp.concatenate([values, rest], axis=0).astype(jnp.bfloat16)
            turned[:, at] = values
            plain[at, :] = values.T

    def scores(slot, other):
        part = jnp.dot(
            k_all[block_of(other), :], qt_all[:, block_of(slot)], preferred_element_type=jnp.float32
        )
        s_buf[block_of(other), :] = part
        return jnp.max(part, axis=0, keepdims=True)

    def exponentials(slot, other, top):
        part = jnp.exp2(s_buf[block_of(other), :] - top)
        e_buf[block_of(other), block_of(slot)] = part.astype(jnp.bfloat16)

    def output(slot):
        mixed = jnp.dot(
            vt_all[...], e_buf[:, block_of(slot)], preferred_element_type=jnp.float32
        )
        inv = 1.0 / mixed[HEAD_DIM : HEAD_DIM + 1]
        out_b = (mixed[:HEAD_DIM] * inv).astype(jnp.bfloat16)
        outs[slot][message_rows(0), :] = out_b
        grad = msgs[slot][message_rows(3), :].astype(jnp.float32)
        delta = jnp.sum(grad * out_b.astype(jnp.float32), axis=0, keepdims=True) * inv
        coarse = delta.astype(jnp.bfloat16).astype(jnp.float32)
        rest = jnp.where(rest_row == 0, -coarse, jnp.where(rest_row == 1, coarse - delta, 0.0))
        grad = jnp.concatenate([grad * inv, rest], axis=0).astype(jnp.bfloat16)
        g_all[block_of(slot), :] = grad.T
        return grad

    def dscores(slot, other, grad):
        part = jnp.dot(v_all[block_of(other), :], grad, preferred_element_type=jnp.float32)
        d_buf[block_of(other), block_of(slot)] = (
            e_buf[block_of(other), block_of(slot)] * part.astype(jnp.bfloat16)
        )

    def query_part(slot):
        at = block_of(slot)
        dquery = jnp.dot(kt_all[:HEAD_DIM, :], d_buf[:, at], preferred_element_type=jnp.float32)
        dquery = unrotate(dquery * SCALE, cosv[:, at], sinv[:, at])
        outs[slot][message_rows(1), :] = dquery.astype(jnp.bfloat16)
        return jnp.where(ids[slot] >= 0, dquery, 0.0)

    for slot in range(slots):
        stage(slot)
    dq_total = jnp.zeros((HEAD_DIM, tokd), jnp.float32)
    grad = None
    for slot in range(slots + 1):
        if slot < slots:
            offs = [jnp.where(ids[slot] == ids[other], 0.0, NEG) for other in range(slots)]
            tops = [scores(slot, other) + offs[other] for other in range(slots)]
            top = functools.reduce(jnp.maximum, tops)
        for other in range(slots):
            if slot > 0:
                dscores(slot - 1, other, grad)
            if slot < slots:
                exponentials(slot, other, top - offs[other])
        if slot > 0:
            dq_total = dq_total + query_part(slot - 1)
        if slot < slots:
            grad = output(slot)
    dk_total = jnp.zeros((HEAD_DIM, tokd), jnp.float32)
    dv_total = jnp.zeros((1, LANES), jnp.float32)
    for slot in range(slots):
        at = block_of(slot)
        live = ids[slot] >= 0
        dvalue = jnp.dot(e_buf[at, :], g_all[...], preferred_element_type=jnp.float32)
        dv_total = dv_total + jnp.where(live, jnp.sum(dvalue, axis=0, keepdims=True), 0.0)
        outs[slot][message_rows(3), :] = dvalue.astype(jnp.bfloat16).T[:HEAD_DIM]
        dkey = jnp.dot(d_buf[at, :], q_all[...], preferred_element_type=jnp.float32)
        dkey = unrotate(dkey.T[:HEAD_DIM] * (1.0 / LOG2E), cosv[:, at], sinv[:, at])
        outs[slot][message_rows(2), :] = dkey.astype(jnp.bfloat16)
        dk_total = dk_total + jnp.where(live, dkey, 0.0)
    lane = lax.broadcasted_iota(jnp.int32, (HEAD_DIM, LANES), 1)
    columns = jnp.where(
        lane == 0,
        jnp.sum(dq_total, axis=1, keepdims=True),
        jnp.where(lane == 1, jnp.sum(dk_total, axis=1, keepdims=True), 0.0),
    )
    columns = jnp.concatenate([columns, jnp.zeros((LANES - HEAD_DIM, LANES), jnp.float32)], axis=0)
    lines = columns.T
    sums[...] = jnp.zeros_like(sums) if head == 0 else before[...]
    for number, total in enumerate((lines[0:1], lines[1:2], dv_total)):
        at = number * OWN_HEADS + head
        sums[at : at + 1, :] = total * factor


def unpack_kernel(slots, count, images, lengths, table, *refs):
    msgs, tiles = refs[: OWN_HEADS * slots], refs[OWN_HEADS * slots]
    outs, bias_out = refs[OWN_HEADS * slots + 1 : -2], refs[-2]
    held = refs[-1]
    me = lax.axis_index("tok")
    _, start = image_of(me, lengths, images)
    for slot in range(slots):
        source = me if slot == 0 else table[slot - 1, me]
        residue = lax.rem(source + SPAN, SPAN)

        @pl.when((source >= 0) & (source == handler_of(start, residue, count)))
        def _(slot=slot, residue=residue):
            for head in range(OWN_HEADS):
                for number in range(4):
                    held[number, head_rows(residue, head), :] = msgs[head * slots + slot][
                        message_rows(number), :
                    ]

    for number, out in enumerate(outs):
        out[...] = held[number].T

    def add(group, totals):
        return tuple(
            total + tiles[group * SPAN + residue] for residue, total in enumerate(totals)
        )

    groups = tiles.shape[0] // SPAN
    zero = jnp.zeros(tiles.shape[1:], jnp.float32)
    totals = lax.fori_loop(0, groups, add, (zero,) * SPAN, unroll=groups <= 8)
    for residue, total in enumerate(totals):
        for head in range(OWN_HEADS):
            begin = (residue * OWN_HEADS + head) * HEAD_DIM
            for tensor in range(3):
                at = tensor * OWN_HEADS + head
                bias_out[tensor : tensor + 1, begin : begin + HEAD_DIM] = total[
                    at : at + 1, :HEAD_DIM
                ]


def on_device(query_in, key_in, value_in, out_grad, bias, lengths, widths):
    tokd = query_in.shape[1]
    model = query_in.shape[2]
    images = lengths.shape[1]
    count = lax.axis_size("tok")
    rounds = trade_rounds(count)
    shifts = [0] + [shift for shift, _ in rounds]
    slots = len(shifts)
    table = jnp.asarray(source_table(rounds, count))
    quarter = HEAD_DIM // 4
    inverse = rope_base ** (-np.arange(quarter, dtype=np.float64) / quarter)
    inverse = jnp.asarray(np.tile(np.tile(inverse, 2)[:, None], (1, LANES)), jnp.float32)
    smem = pl.BlockSpec(memory_space=pltpu.SMEM)
    vmem = pl.BlockSpec(memory_space=pltpu.VMEM)
    hbm = pl.BlockSpec(memory_space=pltpu.HBM)
    whole = jax.ShapeDtypeStruct((tokd, model), jnp.bfloat16)
    message = jax.ShapeDtypeStruct((4 * HEAD_DIM, tokd), jnp.bfloat16)
    sums_shape = jax.ShapeDtypeStruct((8, LANES), jnp.float32)
    devices = lax.axis_size("dp") * count
    tokens_all = devices * tokd

    def params(mib):
        return pltpu.CompilerParams(vmem_limit_bytes=mib * 1024 * 1024)

    sends = pl.pallas_call(
        functools.partial(pack_kernel, shifts),
        out_shape=[message] * (OWN_HEADS * slots),
        in_specs=[hbm] * 4,
        out_specs=[vmem] * (OWN_HEADS * slots),
        scratch_shapes=[pltpu.VMEM((tokd, model), jnp.bfloat16)] * 4
        + [pltpu.VMEM((model, tokd), jnp.bfloat16)] * 4
        + [pltpu.SemaphoreType.DMA((4,))],
        compiler_params=params(PACK_MIB),
        name="pack_heads",
    )(query_in[0], key_in[0], value_in[0], out_grad[0])
    got = []
    for head in range(OWN_HEADS):
        mine = sends[head * slots : (head + 1) * slots]
        got.append(
            [mine[0]]
            + [lax.ppermute(send, "tok", pairs) for send, (_, pairs) in zip(mine[1:], rounds)]
        )
    span = slots * tokd
    table_shape = jax.ShapeDtypeStruct((HALF, span), jnp.float32)
    cosv, sinv, bias_cols = pl.pallas_call(
        functools.partial(tables_kernel, images, tokd),
        out_shape=[table_shape] * 2 + [jax.ShapeDtypeStruct((model, LANES), jnp.float32)],
        in_specs=[smem, smem, smem, vmem, vmem],
        out_specs=[vmem] * 3,
        compiler_params=params(16),
        cost_estimate=pl.CostEstimate(
            flops=span * LANES * 200, bytes_accessed=0, transcendentals=0
        ),
        name="rotary_tables",
    )(lengths, widths, table, inverse, bias)
    back = []
    sums = None
    for head in range(OWN_HEADS):
        operands = [lengths, table, cosv, sinv, bias_cols] + got[head]
        if head > 0:
            operands.append(sums)
        results = pl.pallas_call(
            functools.partial(
                attend_kernel, slots, count, images, tokd, head, 1.0 / tokens_all**0.5
            ),
            out_shape=[message] * slots + [sums_shape],
            in_specs=[smem, smem] + [vmem] * (len(operands) - 2),
            out_specs=[vmem] * (slots + 1),
            scratch_shapes=[pltpu.VMEM((LANES, span), jnp.bfloat16)] * 3
            + [pltpu.VMEM((span, LANES), jnp.bfloat16)] * 4
            + [pltpu.VMEM((span, tokd), jnp.float32)]
            + [pltpu.VMEM((span, span), jnp.bfloat16)] * 2,
            compiler_params=params(32),
            cost_estimate=pl.CostEstimate(
                flops=12 * span * span * 256, bytes_accessed=0, transcendentals=0
            ),
            name="attend_head",
        )(*operands)
        sums = results[slots]
        if head + 1 < OWN_HEADS:
            results, got[head + 1] = lax.optimization_barrier((results, got[head + 1]))
            sums = results[slots]
        back.append(results[0])
        back += [
            lax.ppermute(result, "tok", [(target, source) for source, target in pairs])
            for result, (_, pairs) in zip(results[1:slots], rounds)
        ]
    early = back[: slots * (OWN_HEADS - 1)]
    sums, early = lax.optimization_barrier((sums, early))
    back[: slots * (OWN_HEADS - 1)] = early
    tiles = lax.all_to_all(
        jnp.broadcast_to(sums[None], (devices,) + sums.shape), ("dp", "tok"), 0, 0, tiled=True
    )
    *outs, bias_grad = pl.pallas_call(
        functools.partial(unpack_kernel, slots, count, images),
        out_shape=[whole] * 4 + [jax.ShapeDtypeStruct((3, model), jnp.float32)],
        in_specs=[smem, smem] + [vmem] * (OWN_HEADS * slots + 1),
        out_specs=[vmem] * 5,
        scratch_shapes=[pltpu.VMEM((4, model, tokd), jnp.bfloat16)],
        compiler_params=params(16),
        name="unpack_heads",
    )(lengths, jnp.asarray(target_table(rounds, count)), *back, tiles)
    return tuple(out[None] for out in outs) + (bias_grad,)


def solution(mesh):
    in_specs = (
        P("dp", "tok", None),
        P("dp", "tok", None),
        P("dp", "tok", None),
        P("dp", "tok", None),
        P(),
        P("dp", None),
        P("dp", None),
    )
    out_specs = (
        P("dp", "tok", None),
        P("dp", "tok", None),
        P("dp", "tok", None),
        P("dp", "tok", None),
        P(),
    )
    return jax.shard_map(
        on_device, mesh=mesh, in_specs=in_specs, out_specs=out_specs, check_vma=False
    )
```

```python
import functools

import jax
import jax.numpy as jnp
import numpy as np
from jax import lax
from jax.experimental import pallas as pl
from jax.experimental.pallas import tpu as pltpu
from jax.sharding import PartitionSpec as P

HEADS = 8
HEAD_DIM = 80
SPAN = 4
OWN_HEADS = HEADS // SPAN
PART = OWN_HEADS * HEAD_DIM
SCALE = HEAD_DIM**-0.5
LOG2E = 1.4426950408889634
NEG = -1e30
LANES = 128
HALF = HEAD_DIM // 2
PACK_MIB = 60

rope_base = 10000.0


def is_closed(count):
    return count in (SPAN, 2 * SPAN)


def trade_rounds(count):
    rounds = []
    for shift in [*range(1, SPAN), *range(-1, -SPAN, -1)]:
        pairs = [
            (source, source + shift)
            for source in range(max(0, -shift), min(count, count - shift))
            if (source < SPAN) == (source + shift < SPAN)
        ]
        rounds.append((shift, pairs))
    return rounds


def trade_tables(count):
    device = np.arange(count, dtype=np.int32)
    if is_closed(count):
        table = device // SPAN * SPAN + np.arange(SPAN, dtype=np.int32)[:, None]
        return table, table
    rounds = trade_rounds(count)
    sources = np.full((1 + len(rounds), count), -1, np.int32)
    targets = sources.copy()
    sources[0] = targets[0] = device
    for slot, (_, pairs) in enumerate(rounds, 1):
        for source, target in pairs:
            sources[slot, target] = source
            targets[slot, source] = target
    return sources, targets


def trade(slices, back=False):
    count = lax.axis_size("tok")
    if is_closed(count):
        groups = [list(range(begin, begin + SPAN)) for begin in range(0, count, SPAN)]
        return lax.all_to_all(slices, "tok", 0, 0, axis_index_groups=groups, tiled=True)
    moved = [slices[0]]
    for slot, (_, pairs) in enumerate(trade_rounds(count), 1):
        if back:
            pairs = [(target, source) for source, target in pairs]
        moved.append(lax.ppermute(slices[slot], "tok", pairs))
    return jnp.stack(moved)


def image_of(block, lengths, images):
    image = jnp.int32(0)
    start = jnp.int32(0)
    begin = jnp.int32(0)
    for number in range(images):
        size = lengths[0, number]
        inside = (block >= begin) & (block < begin + size)
        image = jnp.where(inside, number, image)
        start = jnp.where(inside, begin, start)
        begin = begin + size
    return image, start


def handler_of(start, residue, count):
    device = start + lax.rem(residue - lax.rem(start, SPAN) + SPAN, SPAN)
    return jnp.where(device >= count, device - SPAN, device)


def message_rows(tensor):
    return slice(tensor * HEAD_DIM, (tensor + 1) * HEAD_DIM)


def rotate(values, cosv, sinv):
    first, second = values[:HALF], values[HALF:]
    return jnp.concatenate([first * cosv - second * sinv, second * cosv + first * sinv], axis=0)


def unrotate(values, cosv, sinv):
    first, second = values[:HALF], values[HALF:]
    return jnp.concatenate([first * cosv + second * sinv, second * cosv - first * sinv], axis=0)


def phase_lanes(phase, model):
    size = SPAN * HEAD_DIM
    begin = phase * size // LANES * LANES
    end = -(-(phase + 1) * size // LANES) * LANES
    return begin, min(end, model)


def pack_kernel(phase, shifts, *refs):
    inputs, out, held, turned, sems = refs[:4], refs[4], refs[5], refs[6], refs[7]
    begin, end = phase_lanes(phase, inputs[0].shape[1])
    copies = [
        pltpu.make_async_copy(source.at[:, begin:end], held.at[number], sems.at[number])
        for number, source in enumerate(inputs)
    ]
    for copy in copies:
        copy.start()
    me = lax.axis_index("tok")
    inner = phase * SPAN * HEAD_DIM - begin
    for number, copy in enumerate(copies):
        copy.wait()
        turned[number] = held[number].T
        for slot in range(out.shape[0]):
            if shifts is None:
                rows = slice(inner + slot * HEAD_DIM, inner + (slot + 1) * HEAD_DIM)
            else:
                residue = lax.rem(me + shifts[slot] + SPAN, SPAN)
                rows = pl.ds(pl.multiple_of(inner + residue * HEAD_DIM, 16), HEAD_DIM)
            out[slot, message_rows(number), :] = turned[number, rows, :]


def tables_kernel(images, tokd, lengths, widths, table, inverse, bias, cos_out, sin_out, bias_out):
    me = lax.axis_index("tok")
    slots = table.shape[0]
    spot = lax.broadcasted_iota(jnp.int32, (HALF, tokd), 1)
    by_row = lax.broadcasted_iota(jnp.int32, (HALF, tokd), 0) < HALF // 2
    for slot in range(slots):
        block = table[slot, me]
        image, start = image_of(block, lengths, images)
        width = widths[0, image]
        bits = jnp.where(width == tokd, 0, jnp.where(width * 2 == tokd, 1, 2))
        shift = tokd.bit_length() - 1 - bits
        local = spot + (block - start) * tokd
        rowpos = lax.shift_right_logical(local, jnp.broadcast_to(shift, local.shape))
        colpos = local & (width - 1)
        angle = jnp.where(by_row, rowpos, colpos).astype(jnp.float32) * inverse[:, 0:1]
        cos_out[:, slot * tokd : (slot + 1) * tokd] = jnp.cos(angle)
        sin_out[:, slot * tokd : (slot + 1) * tokd] = jnp.sin(angle)
    plain = bias[...].astype(jnp.float32)
    rest = jnp.zeros((LANES - plain.shape[0], plain.shape[1]), jnp.float32)
    bias_out[...] = jnp.concatenate([plain, rest], axis=0).T


def attend_kernel(slots, count, images, tokd, head, factor, lengths, table, cosv, sinv, bias, *refs):
    if head > 0:
        before, refs = refs[0], refs[1:]
    msgs, outs, sums = refs[:3]
    qt_all, kt_all, vt_all, q_all, k_all, v_all, g_all, s_buf, e_buf, d_buf = refs[3:]
    me = lax.axis_index("tok")
    residue = lax.rem(me, SPAN)
    ids = []
    for slot in range(slots):
        block = table[slot, me]
        image, start = image_of(block, lengths, images)
        handled = (block >= 0) & (handler_of(start, residue, count) == me)
        ids.append(jnp.where(handled, image, -1 - slot))
    begin = pl.multiple_of((head * SPAN + residue) * HEAD_DIM, 16)
    own_bias = bias[pl.ds(begin, HEAD_DIM), :]
    rest_row = lax.broadcasted_iota(jnp.int32, (LANES - HEAD_DIM, tokd), 0)
    zeros = jnp.zeros((LANES - HEAD_DIM, tokd), jnp.float32)
    ones = jnp.where(rest_row < 2, 1.0, 0.0)

    def block_of(slot):
        return slice(slot * tokd, (slot + 1) * tokd)

    def stage(slot):
        at = block_of(slot)
        cos_b, sin_b = cosv[:, at], sinv[:, at]
        query, key, value = (
            msgs[slot, message_rows(tensor), :].astype(jnp.float32)
            + own_bias[:, tensor : tensor + 1]
            for tensor in range(3)
        )
        query = rotate(query, cos_b, sin_b) * (SCALE * LOG2E)
        for values, rest, turned, plain in (
            (query, zeros, qt_all, q_all),
            (rotate(key, cos_b, sin_b), zeros, kt_all, k_all),
            (value, ones, vt_all, v_all),
        ):
            values = jnp.concatenate([values, rest], axis=0).astype(jnp.bfloat16)
            turned[:, at] = values
            plain[at, :] = values.T

    def scores(slot, other):
        part = jnp.dot(
            k_all[block_of(other), :], qt_all[:, block_of(slot)], preferred_element_type=jnp.float32
        )
        s_buf[block_of(other), :] = part
        return jnp.max(part, axis=0, keepdims=True)

    def exponentials(slot, other, top):
        part = jnp.exp2(s_buf[block_of(other), :] - top)
        e_buf[block_of(other), block_of(slot)] = part.astype(jnp.bfloat16)

    def output(slot):
        mixed = jnp.dot(
            vt_all[...], e_buf[:, block_of(slot)], preferred_element_type=jnp.float32
        )
        inv = 1.0 / mixed[HEAD_DIM : HEAD_DIM + 1]
        out_b = (mixed[:HEAD_DIM] * inv).astype(jnp.bfloat16)
        outs[slot, message_rows(0), :] = out_b
        grad = msgs[slot, message_rows(3), :].astype(jnp.float32)
        delta = jnp.sum(grad * out_b.astype(jnp.float32), axis=0, keepdims=True) * inv
        coarse = delta.astype(jnp.bfloat16).astype(jnp.float32)
        rest = jnp.where(rest_row == 0, -coarse, jnp.where(rest_row == 1, coarse - delta, 0.0))
        grad = jnp.concatenate([grad * inv, rest], axis=0).astype(jnp.bfloat16)
        g_all[block_of(slot), :] = grad.T
        return grad

    def dscores(slot, other, grad):
        part = jnp.dot(v_all[block_of(other), :], grad, preferred_element_type=jnp.float32)
        d_buf[block_of(other), block_of(slot)] = (
            e_buf[block_of(other), block_of(slot)] * part.astype(jnp.bfloat16)
        )

    def query_part(slot):
        at = block_of(slot)
        dquery = jnp.dot(kt_all[:HEAD_DIM, :], d_buf[:, at], preferred_element_type=jnp.float32)
        dquery = unrotate(dquery * SCALE, cosv[:, at], sinv[:, at])
        outs[slot, message_rows(1), :] = dquery.astype(jnp.bfloat16)
        return jnp.where(ids[slot] >= 0, dquery, 0.0)

    for slot in range(slots):
        stage(slot)
    dq_total = jnp.zeros((HEAD_DIM, tokd), jnp.float32)
    grad = None
    for slot in range(slots + 1):
        if slot < slots:
            offs = [jnp.where(ids[slot] == ids[other], 0.0, NEG) for other in range(slots)]
            tops = [scores(slot, other) + offs[other] for other in range(slots)]
            top = functools.reduce(jnp.maximum, tops)
        for other in range(slots):
            if slot > 0:
                dscores(slot - 1, other, grad)
            if slot < slots:
                exponentials(slot, other, top - offs[other])
        if slot > 0:
            dq_total = dq_total + query_part(slot - 1)
        if slot < slots:
            grad = output(slot)
    dk_total = jnp.zeros((HEAD_DIM, tokd), jnp.float32)
    dv_total = jnp.zeros((1, LANES), jnp.float32)
    for slot in range(slots):
        at = block_of(slot)
        live = ids[slot] >= 0
        dvalue = jnp.dot(e_buf[at, :], g_all[...], preferred_element_type=jnp.float32)
        dv_total = dv_total + jnp.where(live, jnp.sum(dvalue, axis=0, keepdims=True), 0.0)
        outs[slot, message_rows(3), :] = dvalue.astype(jnp.bfloat16).T[:HEAD_DIM]
        dkey = jnp.dot(d_buf[at, :], q_all[...], preferred_element_type=jnp.float32)
        dkey = unrotate(dkey.T[:HEAD_DIM] * (1.0 / LOG2E), cosv[:, at], sinv[:, at])
        outs[slot, message_rows(2), :] = dkey.astype(jnp.bfloat16)
        dk_total = dk_total + jnp.where(live, dkey, 0.0)
    lane = lax.broadcasted_iota(jnp.int32, (HEAD_DIM, LANES), 1)
    columns = jnp.where(
        lane == 0,
        jnp.sum(dq_total, axis=1, keepdims=True),
        jnp.where(lane == 1, jnp.sum(dk_total, axis=1, keepdims=True), 0.0),
    )
    columns = jnp.concatenate([columns, jnp.zeros((LANES - HEAD_DIM, LANES), jnp.float32)], axis=0)
    lines = columns.T
    sums[...] = jnp.zeros_like(sums) if head == 0 else before[...]
    for number, total in enumerate((lines[0:1], lines[1:2], dv_total)):
        at = number * OWN_HEADS + head
        sums[at : at + 1, :] = total * factor


def unpack_kernel(closed, count, images, lengths, table, *refs):
    msgs, tiles = refs[:OWN_HEADS], refs[OWN_HEADS]
    outs, bias_out, held = refs[OWN_HEADS + 1 : -2], refs[-2], refs[-1]
    me = lax.axis_index("tok")
    if closed:
        for slot in range(SPAN):
            for phase in range(OWN_HEADS):
                begin = (phase * SPAN + slot) * HEAD_DIM
                for number in range(4):
                    held[number, begin : begin + HEAD_DIM, :] = msgs[phase][
                        slot, message_rows(number), :
                    ]
    else:
        _, start = image_of(me, lengths, images)
        for slot in range(table.shape[0]):
            source = table[slot, me]
            residue = lax.rem(source + SPAN, SPAN)

            @pl.when((source >= 0) & (source == handler_of(start, residue, count)))
            def _(slot=slot, residue=residue):
                for phase in range(OWN_HEADS):
                    begin = pl.multiple_of((phase * SPAN + residue) * HEAD_DIM, 16)
                    for number in range(4):
                        held[number, pl.ds(begin, HEAD_DIM), :] = msgs[phase][
                            slot, message_rows(number), :
                        ]

    for number, out in enumerate(outs):
        out[...] = held[number].T

    def add(group, totals):
        return tuple(
            total + tiles[group * SPAN + residue] for residue, total in enumerate(totals)
        )

    groups = tiles.shape[0] // SPAN
    zero = jnp.zeros(tiles.shape[1:], jnp.float32)
    totals = lax.fori_loop(0, groups, add, (zero,) * SPAN, unroll=groups <= 8)
    for residue, total in enumerate(totals):
        for phase in range(OWN_HEADS):
            begin = (phase * SPAN + residue) * HEAD_DIM
            for tensor in range(3):
                at = tensor * OWN_HEADS + phase
                bias_out[tensor : tensor + 1, begin : begin + HEAD_DIM] = total[
                    at : at + 1, :HEAD_DIM
                ]


def on_device(query_in, key_in, value_in, out_grad, bias, lengths, widths):
    tokd = query_in.shape[1]
    model = query_in.shape[2]
    images = lengths.shape[1]
    count = lax.axis_size("tok")
    dp_size = lax.axis_size("dp")
    closed = is_closed(count)
    sources, targets = trade_tables(count)
    slots = sources.shape[0]
    span = slots * tokd
    table = jnp.asarray(sources)
    shifts = None if closed else [0] + [shift for shift, _ in trade_rounds(count)]
    quarter = HEAD_DIM // 4
    inverse = rope_base ** (-np.arange(quarter, dtype=np.float64) / quarter)
    inverse = jnp.asarray(np.tile(np.tile(inverse, 2)[:, None], (1, LANES)), jnp.float32)
    smem = pl.BlockSpec(memory_space=pltpu.SMEM)
    vmem = pl.BlockSpec(memory_space=pltpu.VMEM)
    hbm = pl.BlockSpec(memory_space=pltpu.HBM)
    whole = jax.ShapeDtypeStruct((tokd, model), jnp.bfloat16)
    messages = jax.ShapeDtypeStruct((slots, 4 * HEAD_DIM, tokd), jnp.bfloat16)
    sums_shape = jax.ShapeDtypeStruct((8, LANES), jnp.float32)
    tokens_all = dp_size * count * tokd

    def params(mib):
        return pltpu.CompilerParams(vmem_limit_bytes=mib * 1024 * 1024)

    def pack(phase, inputs):
        begin, end = phase_lanes(phase, model)
        return pl.pallas_call(
            functools.partial(pack_kernel, phase, shifts),
            out_shape=messages,
            in_specs=[hbm] * 4,
            out_specs=vmem,
            scratch_shapes=[
                pltpu.VMEM((4, tokd, end - begin), jnp.bfloat16),
                pltpu.VMEM((4, end - begin, tokd), jnp.bfloat16),
                pltpu.SemaphoreType.DMA((4,)),
            ],
            compiler_params=params(PACK_MIB),
            name="pack_heads",
        )(*inputs)

    inputs = (query_in[0], key_in[0], value_in[0], out_grad[0])
    got = [trade(pack(0, inputs))]
    table_shape = jax.ShapeDtypeStruct((HALF, span), jnp.float32)
    tables = pl.pallas_call(
        functools.partial(tables_kernel, images, tokd),
        out_shape=[table_shape] * 2 + [jax.ShapeDtypeStruct((model, LANES), jnp.float32)],
        in_specs=[smem, smem, smem, vmem, vmem],
        out_specs=[vmem] * 3,
        compiler_params=params(16),
        cost_estimate=pl.CostEstimate(
            flops=span * LANES * 200, bytes_accessed=0, transcendentals=0
        ),
        name="rotary_tables",
    )(lengths, widths, table, inverse, bias)
    for phase in range(1, OWN_HEADS):
        tables, inputs = lax.optimization_barrier((tables, inputs))
        packed = pack(phase, inputs)
        got[0], packed = lax.optimization_barrier((got[0], packed))
        got.append(trade(packed))
    back = []
    sums = []
    for phase in range(OWN_HEADS):
        results, total = pl.pallas_call(
            functools.partial(
                attend_kernel, slots, count, images, tokd, phase, 1.0 / tokens_all**0.5
            ),
            out_shape=[messages, sums_shape],
            in_specs=[smem, smem] + [vmem] * (4 + len(sums)),
            out_specs=[vmem] * 2,
            scratch_shapes=[pltpu.VMEM((LANES, span), jnp.bfloat16)] * 3
            + [pltpu.VMEM((span, LANES), jnp.bfloat16)] * 4
            + [pltpu.VMEM((span, tokd), jnp.float32)]
            + [pltpu.VMEM((span, span), jnp.bfloat16)] * 2,
            compiler_params=params(32),
            cost_estimate=pl.CostEstimate(
                flops=12 * span * span * 256, bytes_accessed=0, transcendentals=0
            ),
            name="attend_head",
        )(lengths, table, *tables, *sums, got[phase])
        sums = [total]
        back.append(trade(results, back=True))
    total, early = lax.optimization_barrier((sums[0], back[:-1]))
    back[:-1] = early
    tiles = total[None]
    for axis, size in (("dp", dp_size), ("tok", count)):
        tiles = jnp.sum(tiles, axis=0)
        tiles = jnp.broadcast_to(tiles[None], (size,) + total.shape)
        tiles = lax.all_to_all(tiles, axis, 0, 0, tiled=True)
    *outs, bias_grad = pl.pallas_call(
        functools.partial(unpack_kernel, closed, count, images),
        out_shape=[whole] * 4 + [jax.ShapeDtypeStruct((3, model), jnp.float32)],
        in_specs=[smem, smem] + [vmem] * (OWN_HEADS + 1),
        out_specs=[vmem] * 5,
        scratch_shapes=[pltpu.VMEM((4, model, tokd), jnp.bfloat16)],
        compiler_params=params(16),
        name="unpack_heads",
    )(lengths, jnp.asarray(targets), *back, tiles)
    return tuple(out[None] for out in outs) + (bias_grad,)


def solution(mesh):
    in_specs = (
        P("dp", "tok", None),
        P("dp", "tok", None),
        P("dp", "tok", None),
        P("dp", "tok", None),
        P(),
        P("dp", None),
        P("dp", None),
    )
    out_specs = (
        P("dp", "tok", None),
        P("dp", "tok", None),
        P("dp", "tok", None),
        P("dp", "tok", None),
        P(),
    )
    return jax.shard_map(
        on_device, mesh=mesh, in_specs=in_specs, out_specs=out_specs, check_vma=False
    )
```

```python
import functools

import jax
import jax.numpy as jnp
import numpy as np
from jax import lax
from jax.experimental import pallas as pl
from jax.experimental.pallas import tpu as pltpu
from jax.sharding import PartitionSpec as P

HEADS = 8
HEAD_DIM = 80
SPAN = 4
OWN_HEADS = HEADS // SPAN
PART = OWN_HEADS * HEAD_DIM
SCALE = HEAD_DIM**-0.5
LOG2E = 1.4426950408889634
NEG = -1e30
LANES = 128
HALF = HEAD_DIM // 2
PACK_MIB = 60
UNPACK_FLOPS = 20_000_000_000

rope_base = 10000.0


def is_closed(count):
    return count in (SPAN, 2 * SPAN)


def trade_rounds(count):
    if is_closed(count):
        return [[(one, one ^ step) for one in range(count)] for step in range(SPAN - 1, 0, -1)]
    rounds = []
    for shift in [*range(1, SPAN), *range(-1, -SPAN, -1)]:
        rounds.append(
            [
                (source, source + shift)
                for source in range(max(0, -shift), min(count, count - shift))
                if (source < SPAN) == (source + shift < SPAN)
            ]
        )
    return rounds


def trade_tables(count):
    rounds = trade_rounds(count)
    sources = np.full((1 + len(rounds), count), -1, np.int32)
    targets = sources.copy()
    sources[0] = targets[0] = np.arange(count)
    for slot, pairs in enumerate(rounds, 1):
        for source, target in pairs:
            sources[slot, target] = source
            targets[slot, source] = target
    return sources, targets


def trade(slices, back=False):
    moved = [slices[0]]
    for slot, pairs in enumerate(trade_rounds(lax.axis_size("tok")), 1):
        if back:
            pairs = [(target, source) for source, target in pairs]
        moved.append(lax.ppermute(slices[slot], "tok", pairs))
    return moved


def image_of(block, lengths, images):
    image = jnp.int32(0)
    start = jnp.int32(0)
    begin = jnp.int32(0)
    for number in range(images):
        size = lengths[0, number]
        inside = (block >= begin) & (block < begin + size)
        image = jnp.where(inside, number, image)
        start = jnp.where(inside, begin, start)
        begin = begin + size
    return image, start


def handler_of(start, residue, count):
    device = start + lax.rem(residue - lax.rem(start, SPAN) + SPAN, SPAN)
    return jnp.where(device >= count, device - SPAN, device)


def message_rows(tensor):
    return slice(tensor * HEAD_DIM, (tensor + 1) * HEAD_DIM)


def rotate(values, cosv, sinv):
    first, second = values[:HALF], values[HALF:]
    return jnp.concatenate([first * cosv - second * sinv, second * cosv + first * sinv], axis=0)


def unrotate(values, cosv, sinv):
    first, second = values[:HALF], values[HALF:]
    return jnp.concatenate([first * cosv + second * sinv, second * cosv - first * sinv], axis=0)


def phase_lanes(phase, model):
    size = SPAN * HEAD_DIM
    begin = phase * size // LANES * LANES
    end = -(-(phase + 1) * size // LANES) * LANES
    return begin, min(end, model)


def pack_kernel(phase, closed, *refs):
    inputs, outs, held, turned, sems = refs[:4], refs[4:-3], refs[-3], refs[-2], refs[-1]
    begin, end = phase_lanes(phase, inputs[0].shape[1])
    copies = [
        pltpu.make_async_copy(source.at[:, begin:end], held.at[number], sems.at[number])
        for number, source in enumerate(inputs)
    ]
    for copy in copies:
        copy.start()
    me = lax.rem(lax.axis_index("tok"), SPAN)
    inner = phase * SPAN * HEAD_DIM - begin
    steps = [0] + (
        [*range(SPAN - 1, 0, -1)] if closed else [*range(1, SPAN), *range(SPAN - 1, 0, -1)]
    )
    for number, copy in enumerate(copies):
        copy.wait()
        turned[number] = held[number].T
        for out, step in zip(outs, steps):
            residue = me ^ step if closed else lax.rem(me + step, SPAN)
            rows = pl.ds(pl.multiple_of(inner + residue * HEAD_DIM, 16), HEAD_DIM)
            out[message_rows(number), :] = turned[number, rows, :]


def tables_kernel(images, tokd, lengths, widths, table, inverse, bias, cos_out, sin_out, bias_out):
    me = lax.axis_index("tok")
    slots = table.shape[0]
    spot = lax.broadcasted_iota(jnp.int32, (HALF, tokd), 1)
    by_row = lax.broadcasted_iota(jnp.int32, (HALF, tokd), 0) < HALF // 2
    for slot in range(slots):
        block = table[slot, me]
        image, start = image_of(block, lengths, images)
        width = widths[0, image]
        bits = jnp.where(width == tokd, 0, jnp.where(width * 2 == tokd, 1, 2))
        shift = tokd.bit_length() - 1 - bits
        local = spot + (block - start) * tokd
        rowpos = lax.shift_right_logical(local, jnp.broadcast_to(shift, local.shape))
        colpos = local & (width - 1)
        angle = jnp.where(by_row, rowpos, colpos).astype(jnp.float32) * inverse[:, 0:1]
        cos_out[:, slot * tokd : (slot + 1) * tokd] = jnp.cos(angle)
        sin_out[:, slot * tokd : (slot + 1) * tokd] = jnp.sin(angle)
    plain = bias[...].astype(jnp.float32)
    rest = jnp.zeros((LANES - plain.shape[0], plain.shape[1]), jnp.float32)
    bias_out[...] = jnp.concatenate([plain, rest], axis=0).T


def attend_kernel(slots, count, images, tokd, head, factor, lengths, table, cosv, sinv, bias, *refs):
    if head > 0:
        before, refs = refs[0], refs[1:]
    msgs, outs, sums = refs[:slots], refs[slots : 2 * slots], refs[2 * slots]
    qt_all, kt_all, vt_all, q_all, k_all, v_all, g_all, s_buf, e_buf, d_buf = refs[2 * slots + 1 :]
    me = lax.axis_index("tok")
    residue = lax.rem(me, SPAN)
    ids = []
    for slot in range(slots):
        block = table[slot, me]
        image, start = image_of(block, lengths, images)
        handled = (block >= 0) & (handler_of(start, residue, count) == me)
        ids.append(jnp.where(handled, image, -1 - slot))
    begin = pl.multiple_of((head * SPAN + residue) * HEAD_DIM, 16)
    own_bias = bias[pl.ds(begin, HEAD_DIM), :]
    rest_row = lax.broadcasted_iota(jnp.int32, (LANES - HEAD_DIM, tokd), 0)
    zeros = jnp.zeros((LANES - HEAD_DIM, tokd), jnp.float32)
    ones = jnp.where(rest_row < 2, 1.0, 0.0)

    def block_of(slot):
        return slice(slot * tokd, (slot + 1) * tokd)

    def stage(slot):
        at = block_of(slot)
        cos_b, sin_b = cosv[:, at], sinv[:, at]
        query, key, value = (
            msgs[slot][message_rows(tensor), :].astype(jnp.float32)
            + own_bias[:, tensor : tensor + 1]
            for tensor in range(3)
        )
        query = rotate(query, cos_b, sin_b) * (SCALE * LOG2E)
        for values, rest, turned, plain in (
            (query, zeros, qt_all, q_all),
            (rotate(key, cos_b, sin_b), zeros, kt_all, k_all),
            (value, ones, vt_all, v_all),
        ):
            values = jnp.concatenate([values, rest], axis=0).astype(jnp.bfloat16)
            turned[:, at] = values
            plain[at, :] = values.T

    def scores(slot, other):
        part = jnp.dot(
            k_all[block_of(other), :], qt_all[:, block_of(slot)], preferred_element_type=jnp.float32
        )
        s_buf[block_of(other), :] = part
        return jnp.max(part, axis=0, keepdims=True)

    def exponentials(slot, other, top):
        part = jnp.exp2(s_buf[block_of(other), :] - top)
        e_buf[block_of(other), block_of(slot)] = part.astype(jnp.bfloat16)

    def output(slot):
        mixed = jnp.dot(
            vt_all[...], e_buf[:, block_of(slot)], preferred_element_type=jnp.float32
        )
        inv = 1.0 / mixed[HEAD_DIM : HEAD_DIM + 1]
        out_b = (mixed[:HEAD_DIM] * inv).astype(jnp.bfloat16)
        outs[slot][message_rows(0), :] = out_b
        grad = msgs[slot][message_rows(3), :].astype(jnp.float32)
        delta = jnp.sum(grad * out_b.astype(jnp.float32), axis=0, keepdims=True) * inv
        coarse = delta.astype(jnp.bfloat16).astype(jnp.float32)
        rest = jnp.where(rest_row == 0, -coarse, jnp.where(rest_row == 1, coarse - delta, 0.0))
        grad = jnp.concatenate([grad * inv, rest], axis=0).astype(jnp.bfloat16)
        g_all[block_of(slot), :] = grad.T
        return grad

    def dscores(slot, other, grad):
        part = jnp.dot(v_all[block_of(other), :], grad, preferred_element_type=jnp.float32)
        d_buf[block_of(other), block_of(slot)] = (
            e_buf[block_of(other), block_of(slot)] * part.astype(jnp.bfloat16)
        )

    def query_part(slot):
        at = block_of(slot)
        dquery = jnp.dot(kt_all[:HEAD_DIM, :], d_buf[:, at], preferred_element_type=jnp.float32)
        dquery = unrotate(dquery * SCALE, cosv[:, at], sinv[:, at])
        outs[slot][message_rows(1), :] = dquery.astype(jnp.bfloat16)
        return jnp.where(ids[slot] >= 0, dquery, 0.0)

    for slot in range(slots):
        stage(slot)
    dq_total = jnp.zeros((HEAD_DIM, tokd), jnp.float32)
    grad = None
    for slot in range(slots + 1):
        if slot < slots:
            offs = [jnp.where(ids[slot] == ids[other], 0.0, NEG) for other in range(slots)]
            tops = [scores(slot, other) + offs[other] for other in range(slots)]
            top = functools.reduce(jnp.maximum, tops)
        for other in range(slots):
            if slot > 0:
                dscores(slot - 1, other, grad)
            if slot < slots:
                exponentials(slot, other, top - offs[other])
        if slot > 0:
            dq_total = dq_total + query_part(slot - 1)
        if slot < slots:
            grad = output(slot)
    dk_total = jnp.zeros((HEAD_DIM, tokd), jnp.float32)
    dv_total = jnp.zeros((1, LANES), jnp.float32)
    for slot in range(slots):
        at = block_of(slot)
        live = ids[slot] >= 0
        dvalue = jnp.dot(e_buf[at, :], g_all[...], preferred_element_type=jnp.float32)
        dv_total = dv_total + jnp.where(live, jnp.sum(dvalue, axis=0, keepdims=True), 0.0)
        outs[slot][message_rows(3), :] = dvalue.astype(jnp.bfloat16).T[:HEAD_DIM]
        dkey = jnp.dot(d_buf[at, :], q_all[...], preferred_element_type=jnp.float32)
        dkey = unrotate(dkey.T[:HEAD_DIM] * (1.0 / LOG2E), cosv[:, at], sinv[:, at])
        outs[slot][message_rows(2), :] = dkey.astype(jnp.bfloat16)
        dk_total = dk_total + jnp.where(live, dkey, 0.0)
    lane = lax.broadcasted_iota(jnp.int32, (HEAD_DIM, LANES), 1)
    columns = jnp.where(
        lane == 0,
        jnp.sum(dq_total, axis=1, keepdims=True),
        jnp.where(lane == 1, jnp.sum(dk_total, axis=1, keepdims=True), 0.0),
    )
    columns = jnp.concatenate([columns, jnp.zeros((LANES - HEAD_DIM, LANES), jnp.float32)], axis=0)
    lines = columns.T
    sums[...] = jnp.zeros_like(sums) if head == 0 else before[...]
    for number, total in enumerate((lines[0:1], lines[1:2], dv_total)):
        at = number * OWN_HEADS + head
        sums[at : at + 1, :] = total * factor


def unpack_kernel(slots, count, images, lengths, table, *refs):
    msgs, outs, held = refs[: OWN_HEADS * slots], refs[OWN_HEADS * slots : -1], refs[-1]
    me = lax.axis_index("tok")
    _, start = image_of(me, lengths, images)
    for slot in range(slots):
        source = table[slot, me]
        residue = lax.rem(source + SPAN, SPAN)

        def place(slot=slot, residue=residue):
            for phase in range(OWN_HEADS):
                begin = pl.multiple_of((phase * SPAN + residue) * HEAD_DIM, 16)
                for number in range(4):
                    held[number, pl.ds(begin, HEAD_DIM), :] = msgs[phase * slots + slot][
                        message_rows(number), :
                    ]

        if is_closed(count):
            place()
        else:
            pl.when((source >= 0) & (source == handler_of(start, residue, count)))(place)
    for number, out in enumerate(outs):
        out[...] = held[number].T


def bias_kernel(tiles, bias_out):
    def add(group, totals):
        return tuple(
            total + tiles[group * SPAN + residue] for residue, total in enumerate(totals)
        )

    groups = tiles.shape[0] // SPAN
    zero = jnp.zeros(tiles.shape[1:], jnp.float32)
    totals = lax.fori_loop(0, groups, add, (zero,) * SPAN, unroll=groups <= 8)
    for residue, total in enumerate(totals):
        for phase in range(OWN_HEADS):
            begin = (phase * SPAN + residue) * HEAD_DIM
            for tensor in range(3):
                at = tensor * OWN_HEADS + phase
                bias_out[tensor : tensor + 1, begin : begin + HEAD_DIM] = total[
                    at : at + 1, :HEAD_DIM
                ]


def on_device(query_in, key_in, value_in, out_grad, bias, lengths, widths):
    tokd = query_in.shape[1]
    model = query_in.shape[2]
    images = lengths.shape[1]
    count = lax.axis_size("tok")
    dp_size = lax.axis_size("dp")
    closed = is_closed(count)
    sources, targets = trade_tables(count)
    slots = sources.shape[0]
    span = slots * tokd
    table = jnp.asarray(sources)
    quarter = HEAD_DIM // 4
    inverse = rope_base ** (-np.arange(quarter, dtype=np.float64) / quarter)
    inverse = jnp.asarray(np.tile(np.tile(inverse, 2)[:, None], (1, LANES)), jnp.float32)
    smem = pl.BlockSpec(memory_space=pltpu.SMEM)
    vmem = pl.BlockSpec(memory_space=pltpu.VMEM)
    hbm = pl.BlockSpec(memory_space=pltpu.HBM)
    whole = jax.ShapeDtypeStruct((tokd, model), jnp.bfloat16)
    messages = [jax.ShapeDtypeStruct((4 * HEAD_DIM, tokd), jnp.bfloat16)] * slots
    sums_shape = jax.ShapeDtypeStruct((8, LANES), jnp.float32)
    tokens_all = dp_size * count * tokd

    def params(mib):
        return pltpu.CompilerParams(vmem_limit_bytes=mib * 1024 * 1024)

    def pack(phase, inputs):
        begin, end = phase_lanes(phase, model)
        return pl.pallas_call(
            functools.partial(pack_kernel, phase, closed),
            out_shape=messages,
            in_specs=[hbm] * 4,
            out_specs=[vmem] * slots,
            scratch_shapes=[
                pltpu.VMEM((4, tokd, end - begin), jnp.bfloat16),
                pltpu.VMEM((4, end - begin, tokd), jnp.bfloat16),
                pltpu.SemaphoreType.DMA((4,)),
            ],
            compiler_params=params(PACK_MIB),
            name="pack_heads",
        )(*inputs)

    inputs = (query_in[0], key_in[0], value_in[0], out_grad[0])
    got = [trade(pack(0, inputs))]
    table_shape = jax.ShapeDtypeStruct((HALF, span), jnp.float32)
    tables = pl.pallas_call(
        functools.partial(tables_kernel, images, tokd),
        out_shape=[table_shape] * 2 + [jax.ShapeDtypeStruct((model, LANES), jnp.float32)],
        in_specs=[smem, smem, smem, vmem, vmem],
        out_specs=[vmem] * 3,
        compiler_params=params(16),
        cost_estimate=pl.CostEstimate(
            flops=span * LANES * 200, bytes_accessed=0, transcendentals=0
        ),
        name="rotary_tables",
    )(lengths, widths, table, inverse, bias)
    for phase in range(1, OWN_HEADS):
        tables, inputs = lax.optimization_barrier((tables, inputs))
        packed = pack(phase, inputs)
        tables, packed = lax.optimization_barrier((tables, packed))
        got.append(trade(packed))
    back = []
    sums = []
    for phase in range(OWN_HEADS):
        *results, total = pl.pallas_call(
            functools.partial(
                attend_kernel, slots, count, images, tokd, phase, 1.0 / tokens_all**0.5
            ),
            out_shape=messages + [sums_shape],
            in_specs=[smem, smem] + [vmem] * (3 + len(sums) + slots),
            out_specs=[vmem] * (slots + 1),
            scratch_shapes=[pltpu.VMEM((LANES, span), jnp.bfloat16)] * 3
            + [pltpu.VMEM((span, LANES), jnp.bfloat16)] * 4
            + [pltpu.VMEM((span, tokd), jnp.float32)]
            + [pltpu.VMEM((span, span), jnp.bfloat16)] * 2,
            compiler_params=params(32),
            cost_estimate=pl.CostEstimate(
                flops=12 * span * span * 256, bytes_accessed=0, transcendentals=0
            ),
            name="attend_head",
        )(lengths, table, *tables, *sums, *got[phase])
        sums = [total]
        if phase + 1 < OWN_HEADS:
            results, got[phase + 1] = lax.optimization_barrier((results, got[phase + 1]))
        back.append(trade(results, back=True))
    total, early = lax.optimization_barrier((sums[0], back[:-1]))
    back[:-1] = early
    devices = dp_size * count
    tiles = jnp.broadcast_to(total[None], (devices,) + total.shape)
    tiles = lax.all_to_all(tiles, ("dp", "tok"), 0, 0, tiled=True)
    outs = pl.pallas_call(
        functools.partial(unpack_kernel, slots, count, images),
        out_shape=[whole] * 4,
        in_specs=[smem, smem] + [vmem] * (OWN_HEADS * slots),
        out_specs=[vmem] * 4,
        scratch_shapes=[pltpu.VMEM((4, model, tokd), jnp.bfloat16)],
        compiler_params=params(16),
        cost_estimate=pl.CostEstimate(flops=UNPACK_FLOPS, bytes_accessed=0, transcendentals=0),
        name="unpack_heads",
    )(lengths, jnp.asarray(targets), *(result for results in back for result in results))
    outs, tiles = lax.optimization_barrier((outs, tiles))
    bias_grad = pl.pallas_call(
        bias_kernel,
        out_shape=jax.ShapeDtypeStruct((3, model), jnp.float32),
        in_specs=[vmem],
        out_specs=vmem,
        compiler_params=params(16),
        name="bias_sums",
    )(tiles)
    return tuple(out[None] for out in outs) + (bias_grad,)


def solution(mesh):
    in_specs = (
        P("dp", "tok", None),
        P("dp", "tok", None),
        P("dp", "tok", None),
        P("dp", "tok", None),
        P(),
        P("dp", None),
        P("dp", None),
    )
    out_specs = (
        P("dp", "tok", None),
        P("dp", "tok", None),
        P("dp", "tok", None),
        P("dp", "tok", None),
        P(),
    )
    return jax.shard_map(
        on_device, mesh=mesh, in_specs=in_specs, out_specs=out_specs, check_vma=False
    )
```

```python
import functools

import jax
import jax.numpy as jnp
import numpy as np
from jax import lax
from jax.experimental import pallas as pl
from jax.experimental.pallas import tpu as pltpu
from jax.sharding import PartitionSpec as P

HEADS = 8
HEAD_DIM = 80
SPAN = 4
OWN_HEADS = HEADS // SPAN
PART = OWN_HEADS * HEAD_DIM
SCALE = HEAD_DIM**-0.5
LOG2E = 1.4426950408889634
NEG = -1e30
LANES = 128
HALF = HEAD_DIM // 2
PACK_MIB = 52
UNPACK_FLOPS = 20_000_000_000

rope_base = 10000.0


def is_closed(count):
    return count in (SPAN, 2 * SPAN)


def trade_rounds(count):
    if is_closed(count):
        return [[(one, one ^ step) for one in range(count)] for step in range(SPAN - 1, 0, -1)]
    rounds = []
    for shift in [*range(1, SPAN), *range(-1, -SPAN, -1)]:
        rounds.append(
            [
                (source, source + shift)
                for source in range(max(0, -shift), min(count, count - shift))
                if (source < SPAN) == (source + shift < SPAN)
            ]
        )
    return rounds


def trade_tables(count):
    rounds = trade_rounds(count)
    sources = np.full((1 + len(rounds), count), -1, np.int32)
    targets = sources.copy()
    sources[0] = targets[0] = np.arange(count)
    for slot, pairs in enumerate(rounds, 1):
        for source, target in pairs:
            sources[slot, target] = source
            targets[slot, source] = target
    return sources, targets


def trade(slices):
    moved = [slices[0]]
    for one, pairs in zip(slices[1:], trade_rounds(lax.axis_size("tok"))):
        moved.append(lax.ppermute(one, "tok", pairs))
    return moved


def send_back(result, slot):
    if slot == 0:
        return result
    pairs = trade_rounds(lax.axis_size("tok"))[slot - 1]
    return lax.ppermute(result, "tok", [(target, source) for source, target in pairs])


EARLY = 1


def image_of(block, lengths, images):
    image = jnp.int32(0)
    start = jnp.int32(0)
    begin = jnp.int32(0)
    for number in range(images):
        size = lengths[0, number]
        inside = (block >= begin) & (block < begin + size)
        image = jnp.where(inside, number, image)
        start = jnp.where(inside, begin, start)
        begin = begin + size
    return image, start


def handler_of(start, residue, count):
    device = start + lax.rem(residue - lax.rem(start, SPAN) + SPAN, SPAN)
    return jnp.where(device >= count, device - SPAN, device)


def message_rows(tensor):
    return slice(tensor * HEAD_DIM, (tensor + 1) * HEAD_DIM)


def rotate(values, cosv, sinv):
    first, second = values[:HALF], values[HALF:]
    return jnp.concatenate([first * cosv - second * sinv, second * cosv + first * sinv], axis=0)


def unrotate(values, cosv, sinv):
    first, second = values[:HALF], values[HALF:]
    return jnp.concatenate([first * cosv + second * sinv, second * cosv - first * sinv], axis=0)


def pack_kernel(closed, *refs):
    inputs, outs, held, turned, sems = refs[:4], refs[4:-3], refs[-3], refs[-2], refs[-1]
    copies = [
        pltpu.make_async_copy(source, held.at[number], sems.at[number])
        for number, source in enumerate(inputs)
    ]
    for copy in copies:
        copy.start()
    me = lax.rem(lax.axis_index("tok"), SPAN)
    steps = [0] + (
        [*range(SPAN - 1, 0, -1)] if closed else [*range(1, SPAN), *range(SPAN - 1, 0, -1)]
    )
    for number, copy in enumerate(copies):
        copy.wait()
        turned[number] = held[number].T
        for phase in range(OWN_HEADS):
            for slot, step in enumerate(steps):
                residue = me ^ step if closed else lax.rem(me + step, SPAN)
                begin = pl.multiple_of((phase * SPAN + residue) * HEAD_DIM, 16)
                outs[phase * len(steps) + slot][message_rows(number), :] = turned[
                    number, pl.ds(begin, HEAD_DIM), :
                ]


def tables_kernel(images, tokd, lengths, widths, table, inverse, bias, cos_out, sin_out, bias_out):
    me = lax.axis_index("tok")
    slots = table.shape[0]
    spot = lax.broadcasted_iota(jnp.int32, (HALF, tokd), 1)
    by_row = lax.broadcasted_iota(jnp.int32, (HALF, tokd), 0) < HALF // 2
    for slot in range(slots):
        block = table[slot, me]
        image, start = image_of(block, lengths, images)
        width = widths[0, image]
        bits = jnp.where(width == tokd, 0, jnp.where(width * 2 == tokd, 1, 2))
        shift = tokd.bit_length() - 1 - bits
        local = spot + (block - start) * tokd
        rowpos = lax.shift_right_logical(local, jnp.broadcast_to(shift, local.shape))
        colpos = local & (width - 1)
        angle = jnp.where(by_row, rowpos, colpos).astype(jnp.float32) * inverse[:, 0:1]
        cos_out[:, slot * tokd : (slot + 1) * tokd] = jnp.cos(angle)
        sin_out[:, slot * tokd : (slot + 1) * tokd] = jnp.sin(angle)
    plain = bias[...].astype(jnp.float32)
    rest = jnp.zeros((LANES - plain.shape[0], plain.shape[1]), jnp.float32)
    bias_out[...] = jnp.concatenate([plain, rest], axis=0).T


def attend_kernel(slots, count, images, tokd, head, factor, lengths, table, cosv, sinv, bias, *refs):
    msgs, refs = refs[:slots], refs[slots:]
    if head > 0:
        before, refs = refs[0], refs[slots:]
    outs, sums = refs[:slots], refs[slots]
    qt_all, kt_all, vt_all, q_all, k_all, v_all, g_all, s_buf, e_buf, d_buf = refs[slots + 1 :]
    me = lax.axis_index("tok")
    residue = lax.rem(me, SPAN)
    ids = []
    for slot in range(slots):
        block = table[slot, me]
        image, start = image_of(block, lengths, images)
        handled = (block >= 0) & (handler_of(start, residue, count) == me)
        ids.append(jnp.where(handled, image, -1 - slot))
    begin = pl.multiple_of((head * SPAN + residue) * HEAD_DIM, 16)
    own_bias = bias[pl.ds(begin, HEAD_DIM), :]
    rest_row = lax.broadcasted_iota(jnp.int32, (LANES - HEAD_DIM, tokd), 0)
    zeros = jnp.zeros((LANES - HEAD_DIM, tokd), jnp.float32)
    ones = jnp.where(rest_row < 2, 1.0, 0.0)

    def block_of(slot):
        return slice(slot * tokd, (slot + 1) * tokd)

    def put(slot, tensor, values):
        begin = ((0 if slot == EARLY else 4 * head) + tensor) * HEAD_DIM
        outs[slot][begin : begin + HEAD_DIM, :] = values

    def stage(slot):
        at = block_of(slot)
        cos_b, sin_b = cosv[:, at], sinv[:, at]
        query, key, value = (
            msgs[slot][message_rows(tensor), :].astype(jnp.float32)
            + own_bias[:, tensor : tensor + 1]
            for tensor in range(3)
        )
        query = rotate(query, cos_b, sin_b) * (SCALE * LOG2E)
        for values, rest, turned, plain in (
            (query, zeros, qt_all, q_all),
            (rotate(key, cos_b, sin_b), zeros, kt_all, k_all),
            (value, ones, vt_all, v_all),
        ):
            values = jnp.concatenate([values, rest], axis=0).astype(jnp.bfloat16)
            turned[:, at] = values
            plain[at, :] = values.T

    def scores(slot, other):
        part = jnp.dot(
            k_all[block_of(other), :], qt_all[:, block_of(slot)], preferred_element_type=jnp.float32
        )
        s_buf[block_of(other), :] = part
        return jnp.max(part, axis=0, keepdims=True)

    def exponentials(slot, other, top):
        part = jnp.exp2(s_buf[block_of(other), :] - top)
        e_buf[block_of(other), block_of(slot)] = part.astype(jnp.bfloat16)

    def output(slot):
        mixed = jnp.dot(
            vt_all[...], e_buf[:, block_of(slot)], preferred_element_type=jnp.float32
        )
        inv = 1.0 / mixed[HEAD_DIM : HEAD_DIM + 1]
        out_b = (mixed[:HEAD_DIM] * inv).astype(jnp.bfloat16)
        put(slot, 0, out_b)
        grad = msgs[slot][message_rows(3), :].astype(jnp.float32)
        delta = jnp.sum(grad * out_b.astype(jnp.float32), axis=0, keepdims=True) * inv
        coarse = delta.astype(jnp.bfloat16).astype(jnp.float32)
        rest = jnp.where(rest_row == 0, -coarse, jnp.where(rest_row == 1, coarse - delta, 0.0))
        grad = jnp.concatenate([grad * inv, rest], axis=0).astype(jnp.bfloat16)
        g_all[block_of(slot), :] = grad.T
        return grad

    def dscores(slot, other, grad):
        part = jnp.dot(v_all[block_of(other), :], grad, preferred_element_type=jnp.float32)
        d_buf[block_of(other), block_of(slot)] = (
            e_buf[block_of(other), block_of(slot)] * part.astype(jnp.bfloat16)
        )

    def query_part(slot):
        at = block_of(slot)
        dquery = jnp.dot(kt_all[:HEAD_DIM, :], d_buf[:, at], preferred_element_type=jnp.float32)
        dquery = unrotate(dquery * SCALE, cosv[:, at], sinv[:, at])
        put(slot, 1, dquery.astype(jnp.bfloat16))
        return jnp.where(ids[slot] >= 0, dquery, 0.0)

    for slot in range(slots):
        stage(slot)
    dq_total = jnp.zeros((HEAD_DIM, tokd), jnp.float32)
    grad = None
    for slot in range(slots + 1):
        if slot < slots:
            offs = [jnp.where(ids[slot] == ids[other], 0.0, NEG) for other in range(slots)]
            tops = [scores(slot, other) + offs[other] for other in range(slots)]
            top = functools.reduce(jnp.maximum, tops)
        for other in range(slots):
            if slot > 0:
                dscores(slot - 1, other, grad)
            if slot < slots:
                exponentials(slot, other, top - offs[other])
        if slot > 0:
            dq_total = dq_total + query_part(slot - 1)
        if slot < slots:
            grad = output(slot)
    dk_total = jnp.zeros((HEAD_DIM, tokd), jnp.float32)
    dv_total = jnp.zeros((1, LANES), jnp.float32)
    for slot in range(slots):
        at = block_of(slot)
        live = ids[slot] >= 0
        dvalue = jnp.dot(e_buf[at, :], g_all[...], preferred_element_type=jnp.float32)
        dv_total = dv_total + jnp.where(live, jnp.sum(dvalue, axis=0, keepdims=True), 0.0)
        put(slot, 3, dvalue.astype(jnp.bfloat16).T[:HEAD_DIM])
        dkey = jnp.dot(d_buf[at, :], q_all[...], preferred_element_type=jnp.float32)
        dkey = unrotate(dkey.T[:HEAD_DIM] * (1.0 / LOG2E), cosv[:, at], sinv[:, at])
        put(slot, 2, dkey.astype(jnp.bfloat16))
        dk_total = dk_total + jnp.where(live, dkey, 0.0)
    lane = lax.broadcasted_iota(jnp.int32, (HEAD_DIM, LANES), 1)
    columns = jnp.where(
        lane == 0,
        jnp.sum(dq_total, axis=1, keepdims=True),
        jnp.where(lane == 1, jnp.sum(dk_total, axis=1, keepdims=True), 0.0),
    )
    columns = jnp.concatenate([columns, jnp.zeros((LANES - HEAD_DIM, LANES), jnp.float32)], axis=0)
    lines = columns.T
    row = lax.broadcasted_iota(jnp.int32, (8, LANES), 0)
    tile = jnp.zeros((8, LANES), jnp.float32) if head == 0 else before[...]
    for number, total in enumerate((lines[0:1], lines[1:2], dv_total)):
        tile = jnp.where(row == number * OWN_HEADS + head, total * factor, tile)
    if head + 1 < OWN_HEADS:
        sums[...] = tile
    else:

        def spread(device, carry):
            sums[device] = tile
            return carry

        lax.fori_loop(0, sums.shape[0], spread, 0, unroll=min(32, sums.shape[0]))


def unpack_kernel(slots, count, images, lengths, table, *refs):
    msgs, outs, held = refs[: slots + OWN_HEADS - 1], refs[slots + OWN_HEADS - 1 : -1], refs[-1]
    early, late = msgs[:OWN_HEADS], list(msgs[OWN_HEADS:])
    late.insert(EARLY, None)
    me = lax.axis_index("tok")
    _, start = image_of(me, lengths, images)
    for slot in range(slots):
        source = table[slot, me]
        residue = lax.rem(source + SPAN, SPAN)

        def place(slot=slot, residue=residue):
            for phase in range(OWN_HEADS):
                begin = pl.multiple_of((phase * SPAN + residue) * HEAD_DIM, 16)
                for number in range(4):
                    if slot == EARLY:
                        piece = early[phase][message_rows(number), :]
                    else:
                        piece = late[slot][message_rows(4 * phase + number), :]
                    held[number, pl.ds(begin, HEAD_DIM), :] = piece

        if is_closed(count):
            place()
        else:
            pl.when((source >= 0) & (source == handler_of(start, residue, count)))(place)
    for number, out in enumerate(outs):
        out[...] = held[number].T


def bias_kernel(tiles, bias_out):
    def add(group, totals):
        return tuple(
            total + tiles[group * SPAN + residue] for residue, total in enumerate(totals)
        )

    groups = tiles.shape[0] // SPAN
    zero = jnp.zeros(tiles.shape[1:], jnp.float32)
    totals = lax.fori_loop(0, groups, add, (zero,) * SPAN, unroll=groups <= 8)
    for residue, total in enumerate(totals):
        for phase in range(OWN_HEADS):
            begin = (phase * SPAN + residue) * HEAD_DIM
            for tensor in range(3):
                at = tensor * OWN_HEADS + phase
                bias_out[tensor : tensor + 1, begin : begin + HEAD_DIM] = total[
                    at : at + 1, :HEAD_DIM
                ]


def on_device(query_in, key_in, value_in, out_grad, bias, lengths, widths):
    tokd = query_in.shape[1]
    model = query_in.shape[2]
    images = lengths.shape[1]
    count = lax.axis_size("tok")
    dp_size = lax.axis_size("dp")
    closed = is_closed(count)
    sources, targets = trade_tables(count)
    slots = sources.shape[0]
    span = slots * tokd
    table = jnp.asarray(sources)
    quarter = HEAD_DIM // 4
    inverse = rope_base ** (-np.arange(quarter, dtype=np.float64) / quarter)
    inverse = jnp.asarray(np.tile(np.tile(inverse, 2)[:, None], (1, LANES)), jnp.float32)
    smem = pl.BlockSpec(memory_space=pltpu.SMEM)
    vmem = pl.BlockSpec(memory_space=pltpu.VMEM)
    hbm = pl.BlockSpec(memory_space=pltpu.HBM)
    whole = jax.ShapeDtypeStruct((tokd, model), jnp.bfloat16)
    message = jax.ShapeDtypeStruct((4 * HEAD_DIM, tokd), jnp.bfloat16)
    joined = jax.ShapeDtypeStruct((OWN_HEADS * 4 * HEAD_DIM, tokd), jnp.bfloat16)
    devices = dp_size * count
    tokens_all = devices * tokd

    def params(mib):
        return pltpu.CompilerParams(vmem_limit_bytes=mib * 1024 * 1024)

    inputs = (query_in[0], key_in[0], value_in[0], out_grad[0])
    sends = pl.pallas_call(
        functools.partial(pack_kernel, closed),
        out_shape=[message] * (OWN_HEADS * slots),
        in_specs=[hbm] * 4,
        out_specs=[vmem] * (OWN_HEADS * slots),
        scratch_shapes=[
            pltpu.VMEM((4, tokd, model), jnp.bfloat16),
            pltpu.VMEM((4, model, tokd), jnp.bfloat16),
            pltpu.SemaphoreType.DMA((4,)),
        ],
        compiler_params=params(PACK_MIB),
        name="pack_heads",
    )(*inputs)
    got = [trade(sends[:slots])]
    table_shape = jax.ShapeDtypeStruct((HALF, span), jnp.float32)
    tables = pl.pallas_call(
        functools.partial(tables_kernel, images, tokd),
        out_shape=[table_shape] * 2 + [jax.ShapeDtypeStruct((model, LANES), jnp.float32)],
        in_specs=[smem, smem, smem, vmem, vmem],
        out_specs=[vmem] * 3,
        compiler_params=params(16),
        cost_estimate=pl.CostEstimate(
            flops=span * LANES * 200, bytes_accessed=0, transcendentals=0
        ),
        name="rotary_tables",
    )(lengths, widths, table, inverse, bias)
    tables, sends = lax.optimization_barrier((tables, sends[slots:]))
    for phase in range(1, OWN_HEADS):
        got.append(trade(sends[(phase - 1) * slots : phase * slots]))
    early = []
    carried = []
    for phase in range(OWN_HEADS):
        last = phase + 1 == OWN_HEADS
        kept = [slot for slot in range(slots) if slot != EARLY]
        sums_shape = jax.ShapeDtypeStruct(
            (devices, 8, LANES) if last else (8, LANES), jnp.float32
        )
        first_carried = 5 + slots + 1
        *results, total = pl.pallas_call(
            functools.partial(
                attend_kernel, slots, count, images, tokd, phase, 1.0 / tokens_all**0.5
            ),
            out_shape=[message if slot == EARLY else joined for slot in range(slots)]
            + [sums_shape],
            in_specs=[smem, smem] + [vmem] * (3 + slots + len(carried)),
            out_specs=[vmem] * (slots + 1),
            input_output_aliases={first_carried + at: slot for at, slot in enumerate(kept)}
            if carried
            else {},
            scratch_shapes=[pltpu.VMEM((LANES, span), jnp.bfloat16)] * 3
            + [pltpu.VMEM((span, LANES), jnp.bfloat16)] * 4
            + [pltpu.VMEM((span, tokd), jnp.float32)]
            + [pltpu.VMEM((span, span), jnp.bfloat16)] * 2,
            compiler_params=params(32),
            cost_estimate=pl.CostEstimate(
                flops=12 * span * span * 256, bytes_accessed=0, transcendentals=0
            ),
            name="attend_head",
        )(lengths, table, *tables, *got[phase], *carried)
        early.append(send_back(results[EARLY], EARLY))
        carried = [total] + [results[slot] for slot in kept]
    total, early[:-1] = lax.optimization_barrier((total, early[:-1]))
    tiles = lax.all_to_all(total, ("dp", "tok"), 0, 0, tiled=True)
    late = [send_back(results[slot], slot) for slot in kept]
    outs = pl.pallas_call(
        functools.partial(unpack_kernel, slots, count, images),
        out_shape=[whole] * 4,
        in_specs=[smem, smem] + [vmem] * (OWN_HEADS + len(late)),
        out_specs=[vmem] * 4,
        scratch_shapes=[pltpu.VMEM((4, model, tokd), jnp.bfloat16)],
        compiler_params=params(16),
        cost_estimate=pl.CostEstimate(flops=UNPACK_FLOPS, bytes_accessed=0, transcendentals=0),
        name="unpack_heads",
    )(lengths, jnp.asarray(targets), *early, *late)
    outs, tiles = lax.optimization_barrier((outs, tiles))
    bias_grad = pl.pallas_call(
        bias_kernel,
        out_shape=jax.ShapeDtypeStruct((3, model), jnp.float32),
        in_specs=[vmem],
        out_specs=vmem,
        compiler_params=params(16),
        name="bias_sums",
    )(tiles)
    return tuple(out[None] for out in outs) + (bias_grad,)


def solution(mesh):
    in_specs = (
        P("dp", "tok", None),
        P("dp", "tok", None),
        P("dp", "tok", None),
        P("dp", "tok", None),
        P(),
        P("dp", None),
        P("dp", None),
    )
    out_specs = (
        P("dp", "tok", None),
        P("dp", "tok", None),
        P("dp", "tok", None),
        P("dp", "tok", None),
        P(),
    )
    return jax.shard_map(
        on_device, mesh=mesh, in_specs=in_specs, out_specs=out_specs, check_vma=False
    )
```

```python
import functools

import jax
import jax.numpy as jnp
import numpy as np
from jax import lax
from jax.experimental import pallas as pl
from jax.experimental.pallas import tpu as pltpu
from jax.sharding import PartitionSpec as P

HEADS = 8
HEAD_DIM = 80
SPAN = 4
OWN_HEADS = HEADS // SPAN
PART = OWN_HEADS * HEAD_DIM
SCALE = HEAD_DIM**-0.5
LOG2E = 1.4426950408889634
NEG = -1e30
LANES = 128
HALF = HEAD_DIM // 2
PACK_KIB = 52 * 1024 + 600
UNPACK_FLOPS = 20_000_000_000

rope_base = 10000.0


def is_closed(count):
    return count in (SPAN, 2 * SPAN)


def trade_rounds(count):
    if is_closed(count):
        return [[(one, one ^ step) for one in range(count)] for step in range(SPAN - 1, 0, -1)]
    rounds = []
    for shift in [*range(1, SPAN), *range(-1, -SPAN, -1)]:
        rounds.append(
            [
                (source, source + shift)
                for source in range(max(0, -shift), min(count, count - shift))
                if (source < SPAN) == (source + shift < SPAN)
            ]
        )
    return rounds


def trade_tables(count):
    rounds = trade_rounds(count)
    sources = np.full((1 + len(rounds), count), -1, np.int32)
    targets = sources.copy()
    sources[0] = targets[0] = np.arange(count)
    for slot, pairs in enumerate(rounds, 1):
        for source, target in pairs:
            sources[slot, target] = source
            targets[slot, source] = target
    return sources, targets


def trade(slices):
    moved = [slices[0]]
    for one, pairs in zip(slices[1:], trade_rounds(lax.axis_size("tok"))):
        moved.append(lax.ppermute(one, "tok", pairs))
    return moved


def send_back(result, slot):
    if slot == 0:
        return result
    pairs = trade_rounds(lax.axis_size("tok"))[slot - 1]
    return lax.ppermute(result, "tok", [(target, source) for source, target in pairs])


EARLY = 1


def image_of(block, lengths, images):
    image = jnp.int32(0)
    start = jnp.int32(0)
    begin = jnp.int32(0)
    for number in range(images):
        size = lengths[0, number]
        inside = (block >= begin) & (block < begin + size)
        image = jnp.where(inside, number, image)
        start = jnp.where(inside, begin, start)
        begin = begin + size
    return image, start


def handler_of(start, residue, count):
    device = start + lax.rem(residue - lax.rem(start, SPAN) + SPAN, SPAN)
    return jnp.where(device >= count, device - SPAN, device)


def message_rows(tensor):
    return slice(tensor * HEAD_DIM, (tensor + 1) * HEAD_DIM)


def rotate(values, cosv, sinv):
    first, second = values[:HALF], values[HALF:]
    return jnp.concatenate([first * cosv - second * sinv, second * cosv + first * sinv], axis=0)


def unrotate(values, cosv, sinv):
    first, second = values[:HALF], values[HALF:]
    return jnp.concatenate([first * cosv + second * sinv, second * cosv - first * sinv], axis=0)


def pack_kernel(closed, *refs):
    inputs, outs, held, turned, sems = refs[:4], refs[4:-3], refs[-3], refs[-2], refs[-1]
    copies = [
        pltpu.make_async_copy(source, held.at[number], sems.at[number])
        for number, source in enumerate(inputs)
    ]
    for copy in copies:
        copy.start()
    me = lax.rem(lax.axis_index("tok"), SPAN)
    steps = [0] + (
        [*range(SPAN - 1, 0, -1)] if closed else [*range(1, SPAN), *range(SPAN - 1, 0, -1)]
    )
    for number, copy in enumerate(copies):
        copy.wait()
        turned[number] = held[number].T
        for phase in range(OWN_HEADS):
            for slot, step in enumerate(steps):
                residue = me ^ step if closed else lax.rem(me + step, SPAN)
                begin = pl.multiple_of((phase * SPAN + residue) * HEAD_DIM, 16)
                outs[phase * len(steps) + slot][message_rows(number), :] = turned[
                    number, pl.ds(begin, HEAD_DIM), :
                ]


def tables_kernel(images, tokd, lengths, widths, table, inverse, bias, cos_out, sin_out, bias_out):
    me = lax.axis_index("tok")
    slots = table.shape[0]
    spot = lax.broadcasted_iota(jnp.int32, (HALF, tokd), 1)
    by_row = lax.broadcasted_iota(jnp.int32, (HALF, tokd), 0) < HALF // 2
    for slot in range(slots):
        block = table[slot, me]
        image, start = image_of(block, lengths, images)
        width = widths[0, image]
        bits = jnp.where(width == tokd, 0, jnp.where(width * 2 == tokd, 1, 2))
        shift = tokd.bit_length() - 1 - bits
        local = spot + (block - start) * tokd
        rowpos = lax.shift_right_logical(local, jnp.broadcast_to(shift, local.shape))
        colpos = local & (width - 1)
        angle = jnp.where(by_row, rowpos, colpos).astype(jnp.float32) * inverse[:, 0:1]
        cos_out[:, slot * tokd : (slot + 1) * tokd] = jnp.cos(angle)
        sin_out[:, slot * tokd : (slot + 1) * tokd] = jnp.sin(angle)
    plain = bias[...].astype(jnp.float32)
    rest = jnp.zeros((LANES - plain.shape[0], plain.shape[1]), jnp.float32)
    bias_out[...] = jnp.concatenate([plain, rest], axis=0).T


def attend_kernel(slots, count, images, tokd, head, factor, lengths, table, cosv, sinv, bias, *refs):
    msgs, refs = refs[:slots], refs[slots:]
    if head > 0:
        before, refs = refs[0], refs[slots:]
    outs, sums = refs[:slots], refs[slots]
    qt_all, kt_all, vt_all, gt_all, k_all, v_all, s_buf, e_buf, d_buf = refs[slots + 1 :]
    me = lax.axis_index("tok")
    residue = lax.rem(me, SPAN)
    ids = []
    for slot in range(slots):
        block = table[slot, me]
        image, start = image_of(block, lengths, images)
        handled = (block >= 0) & (handler_of(start, residue, count) == me)
        ids.append(jnp.where(handled, image, -1 - slot))
    begin = pl.multiple_of((head * SPAN + residue) * HEAD_DIM, 16)
    own_bias = bias[pl.ds(begin, HEAD_DIM), :]
    rest_row = lax.broadcasted_iota(jnp.int32, (LANES - HEAD_DIM, tokd), 0)
    zeros = jnp.zeros((LANES - HEAD_DIM, tokd), jnp.float32)
    ones = jnp.where(rest_row < 2, 1.0, 0.0)

    by_lanes = (((1,), (1,)), ((), ()))

    def block_of(slot):
        return slice(slot * tokd, (slot + 1) * tokd)

    def put(slot, tensor, values):
        begin = ((0 if slot == EARLY else 4 * head) + tensor) * HEAD_DIM
        outs[slot][begin : begin + HEAD_DIM, :] = values

    def stage(slot):
        at = block_of(slot)
        cos_b, sin_b = cosv[:, at], sinv[:, at]
        query, key, value = (
            msgs[slot][message_rows(tensor), :].astype(jnp.float32)
            + own_bias[:, tensor : tensor + 1]
            for tensor in range(3)
        )
        query = rotate(query, cos_b, sin_b) * (SCALE * LOG2E)
        for values, rest, turned, plain in (
            (query, zeros, qt_all, None),
            (rotate(key, cos_b, sin_b), zeros, kt_all, k_all),
            (value, ones, vt_all, v_all),
        ):
            values = jnp.concatenate([values, rest], axis=0).astype(jnp.bfloat16)
            turned[:, at] = values
            if plain is not None:
                plain[at, :] = values.T

    def scores(slot, other):
        part = jnp.dot(
            k_all[block_of(other), :], qt_all[:, block_of(slot)], preferred_element_type=jnp.float32
        )
        s_buf[block_of(other), :] = part
        return jnp.max(part, axis=0, keepdims=True)

    def exponentials(slot, other, top):
        part = jnp.exp2(s_buf[block_of(other), :] - top)
        e_buf[block_of(other), block_of(slot)] = part.astype(jnp.bfloat16)

    def output(slot):
        mixed = jnp.dot(
            vt_all[...], e_buf[:, block_of(slot)], preferred_element_type=jnp.float32
        )
        inv = 1.0 / mixed[HEAD_DIM : HEAD_DIM + 1]
        out_b = (mixed[:HEAD_DIM] * inv).astype(jnp.bfloat16)
        put(slot, 0, out_b)
        grad = msgs[slot][message_rows(3), :].astype(jnp.float32)
        delta = jnp.sum(grad * out_b.astype(jnp.float32), axis=0, keepdims=True) * inv
        coarse = delta.astype(jnp.bfloat16).astype(jnp.float32)
        rest = jnp.where(rest_row == 0, -coarse, jnp.where(rest_row == 1, coarse - delta, 0.0))
        grad = jnp.concatenate([grad * inv, rest], axis=0).astype(jnp.bfloat16)
        gt_all[:, block_of(slot)] = grad
        return grad

    def dscores(slot, other, grad):
        part = jnp.dot(v_all[block_of(other), :], grad, preferred_element_type=jnp.float32)
        d_buf[block_of(other), block_of(slot)] = (
            e_buf[block_of(other), block_of(slot)] * part.astype(jnp.bfloat16)
        )

    def query_part(slot):
        at = block_of(slot)
        dquery = jnp.dot(kt_all[:HEAD_DIM, :], d_buf[:, at], preferred_element_type=jnp.float32)
        dquery = unrotate(dquery * SCALE, cosv[:, at], sinv[:, at])
        put(slot, 1, dquery.astype(jnp.bfloat16))
        return jnp.where(ids[slot] >= 0, dquery, 0.0)

    def value_part(slot):
        dvalue = lax.dot_general(
            gt_all[:HEAD_DIM, :],
            e_buf[block_of(slot), :],
            by_lanes,
            preferred_element_type=jnp.float32,
        )
        put(slot, 3, dvalue.astype(jnp.bfloat16))
        return jnp.where(ids[slot] >= 0, dvalue, 0.0)

    for slot in range(slots):
        stage(slot)
    dq_total = jnp.zeros((HEAD_DIM, tokd), jnp.float32)
    dv_total = jnp.zeros((HEAD_DIM, tokd), jnp.float32)
    grad = None
    for slot in range(slots + 1):
        if slot < slots:
            offs = [jnp.where(ids[slot] == ids[other], 0.0, NEG) for other in range(slots)]
            tops = [scores(slot, other) + offs[other] for other in range(slots)]
            top = functools.reduce(jnp.maximum, tops)
        for other in range(slots):
            if slot > 0:
                dscores(slot - 1, other, grad)
            if slot < slots:
                exponentials(slot, other, top - offs[other])
            else:
                dv_total = dv_total + value_part(other)
        if slot > 0:
            dq_total = dq_total + query_part(slot - 1)
        if slot < slots:
            grad = output(slot)
    dk_total = jnp.zeros((HEAD_DIM, tokd), jnp.float32)
    for slot in range(slots):
        at = block_of(slot)
        dkey = lax.dot_general(
            qt_all[:HEAD_DIM, :], d_buf[at, :], by_lanes, preferred_element_type=jnp.float32
        )
        dkey = unrotate(dkey * (1.0 / LOG2E), cosv[:, at], sinv[:, at])
        put(slot, 2, dkey.astype(jnp.bfloat16))
        dk_total = dk_total + jnp.where(ids[slot] >= 0, dkey, 0.0)
    lane = lax.broadcasted_iota(jnp.int32, (HEAD_DIM, LANES), 1)
    columns = jnp.zeros((HEAD_DIM, LANES), jnp.float32)
    for number, total in enumerate((dq_total, dk_total, dv_total)):
        total = jnp.sum(total, axis=1, keepdims=True) * factor
        columns = jnp.where(lane == number, total, columns)
    columns = jnp.concatenate([columns, jnp.zeros((LANES - HEAD_DIM, LANES), jnp.float32)], axis=0)
    lines = columns.T
    if head + 1 < OWN_HEADS:
        sums[...] = lines[:8]
    else:
        tile = join_sums(before[...], lines)

        def spread(device, carry):
            sums[device] = tile
            return carry

        lax.fori_loop(0, sums.shape[0], spread, 0, unroll=min(32, sums.shape[0]))


FIT = LANES - HEAD_DIM
LEFT = HEAD_DIM - FIT


def join_sums(first, second):
    lane = lax.broadcasted_iota(jnp.int32, (1, LANES), 1)
    rows = []
    last = jnp.zeros((1, LANES), jnp.float32)
    for number in range(3):
        moved = pltpu.roll(second[number : number + 1], HEAD_DIM, 1)
        rows.append(jnp.where(lane < HEAD_DIM, first[number : number + 1], moved))
        rest = jnp.where(lane < LEFT, moved, 0.0)
        last = last + (pltpu.roll(rest, number * LEFT, 1) if number else rest)
    return jnp.concatenate(rows + [last], axis=0)


def unpack_kernel(slots, count, images, lengths, table, *refs):
    msgs, outs, held = refs[: slots + OWN_HEADS - 1], refs[slots + OWN_HEADS - 1 : -1], refs[-1]
    early, late = msgs[:OWN_HEADS], list(msgs[OWN_HEADS:])
    late.insert(EARLY, None)
    me = lax.axis_index("tok")
    _, start = image_of(me, lengths, images)
    for slot in range(slots):
        source = table[slot, me]
        residue = lax.rem(source + SPAN, SPAN)

        def place(slot=slot, residue=residue):
            for phase in range(OWN_HEADS):
                begin = pl.multiple_of((phase * SPAN + residue) * HEAD_DIM, 16)
                for number in range(4):
                    if slot == EARLY:
                        piece = early[phase][message_rows(number), :]
                    else:
                        piece = late[slot][message_rows(4 * phase + number), :]
                    held[number, pl.ds(begin, HEAD_DIM), :] = piece

        if is_closed(count):
            place()
        else:
            pl.when((source >= 0) & (source == handler_of(start, residue, count)))(place)
    for number, out in enumerate(outs):
        out[...] = held[number].T


def bias_kernel(tiles, bias_out):
    def add(group, totals):
        return tuple(
            total + tiles[group * SPAN + residue] for residue, total in enumerate(totals)
        )

    groups = tiles.shape[0] // SPAN
    zero = jnp.zeros(tiles.shape[1:], jnp.float32)
    totals = lax.fori_loop(0, groups, add, (zero,) * SPAN, unroll=groups <= 8)
    for residue, total in enumerate(totals):
        first = residue * HEAD_DIM
        second = (SPAN + residue) * HEAD_DIM
        for number in range(3):
            row = slice(number, number + 1)
            bias_out[row, first : first + HEAD_DIM] = total[row, :HEAD_DIM]
            bias_out[row, second : second + FIT] = total[row, HEAD_DIM:]
            bias_out[row, second + FIT : second + HEAD_DIM] = total[
                3:4, number * LEFT : (number + 1) * LEFT
            ]


def on_device(query_in, key_in, value_in, out_grad, bias, lengths, widths):
    tokd = query_in.shape[1]
    model = query_in.shape[2]
    images = lengths.shape[1]
    count = lax.axis_size("tok")
    dp_size = lax.axis_size("dp")
    closed = is_closed(count)
    sources, targets = trade_tables(count)
    slots = sources.shape[0]
    span = slots * tokd
    table = jnp.asarray(sources)
    quarter = HEAD_DIM // 4
    inverse = rope_base ** (-np.arange(quarter, dtype=np.float64) / quarter)
    inverse = jnp.asarray(np.tile(np.tile(inverse, 2)[:, None], (1, LANES)), jnp.float32)
    smem = pl.BlockSpec(memory_space=pltpu.SMEM)
    vmem = pl.BlockSpec(memory_space=pltpu.VMEM)
    hbm = pl.BlockSpec(memory_space=pltpu.HBM)
    whole = jax.ShapeDtypeStruct((tokd, model), jnp.bfloat16)
    message = jax.ShapeDtypeStruct((4 * HEAD_DIM, tokd), jnp.bfloat16)
    joined = jax.ShapeDtypeStruct((OWN_HEADS * 4 * HEAD_DIM, tokd), jnp.bfloat16)
    devices = dp_size * count
    tokens_all = devices * tokd

    def params(mib):
        return pltpu.CompilerParams(vmem_limit_bytes=int(mib * 1024 * 1024))

    inputs = (query_in[0], key_in[0], value_in[0], out_grad[0])
    sends = pl.pallas_call(
        functools.partial(pack_kernel, closed),
        out_shape=[message] * (OWN_HEADS * slots),
        in_specs=[hbm] * 4,
        out_specs=[vmem] * (OWN_HEADS * slots),
        scratch_shapes=[
            pltpu.VMEM((4, tokd, model), jnp.bfloat16),
            pltpu.VMEM((4, model, tokd), jnp.bfloat16),
            pltpu.SemaphoreType.DMA((4,)),
        ],
        compiler_params=params(PACK_KIB / 1024),
        name="pack_heads",
    )(*inputs)
    got = [trade(sends[:slots])]
    table_shape = jax.ShapeDtypeStruct((HALF, span), jnp.float32)
    tables = pl.pallas_call(
        functools.partial(tables_kernel, images, tokd),
        out_shape=[table_shape] * 2 + [jax.ShapeDtypeStruct((model, LANES), jnp.float32)],
        in_specs=[smem, smem, smem, vmem, vmem],
        out_specs=[vmem] * 3,
        compiler_params=params(16),
        cost_estimate=pl.CostEstimate(
            flops=span * LANES * 200, bytes_accessed=0, transcendentals=0
        ),
        name="rotary_tables",
    )(lengths, widths, table, inverse, bias)
    tables, sends = lax.optimization_barrier((tables, sends[slots:]))
    for phase in range(1, OWN_HEADS):
        got.append(trade(sends[(phase - 1) * slots : phase * slots]))
    early = []
    carried = []
    for phase in range(OWN_HEADS):
        last = phase + 1 == OWN_HEADS
        kept = [slot for slot in range(slots) if slot != EARLY]
        sums_shape = jax.ShapeDtypeStruct(
            (devices, 4, LANES) if last else (8, LANES), jnp.float32
        )
        first_carried = 5 + slots + 1
        *results, total = pl.pallas_call(
            functools.partial(
                attend_kernel, slots, count, images, tokd, phase, 1.0 / tokens_all**0.5
            ),
            out_shape=[message if slot == EARLY else joined for slot in range(slots)]
            + [sums_shape],
            in_specs=[smem, smem] + [vmem] * (3 + slots + len(carried)),
            out_specs=[vmem] * (slots + 1),
            input_output_aliases={first_carried + at: slot for at, slot in enumerate(kept)}
            if carried
            else {},
            scratch_shapes=[pltpu.VMEM((LANES, span), jnp.bfloat16)] * 4
            + [pltpu.VMEM((span, LANES), jnp.bfloat16)] * 2
            + [pltpu.VMEM((span, tokd), jnp.float32)]
            + [pltpu.VMEM((span, span), jnp.bfloat16)] * 2,
            compiler_params=params(32),
            cost_estimate=pl.CostEstimate(
                flops=12 * span * span * 256, bytes_accessed=0, transcendentals=0
            ),
            name="attend_head",
        )(lengths, table, *tables, *got[phase], *carried)
        results, total, early = lax.optimization_barrier((results, total, early))
        early.append(send_back(results[EARLY], EARLY))
        carried = [total] + [results[slot] for slot in kept]
    tiles = lax.all_to_all(total, ("dp", "tok"), 0, 0, tiled=True)
    late = [send_back(results[slot], slot) for slot in kept]
    outs = pl.pallas_call(
        functools.partial(unpack_kernel, slots, count, images),
        out_shape=[whole] * 4,
        in_specs=[smem, smem] + [vmem] * (OWN_HEADS + len(late)),
        out_specs=[vmem] * 4,
        scratch_shapes=[pltpu.VMEM((4, model, tokd), jnp.bfloat16)],
        compiler_params=params(16),
        cost_estimate=pl.CostEstimate(flops=UNPACK_FLOPS, bytes_accessed=0, transcendentals=0),
        name="unpack_heads",
    )(lengths, jnp.asarray(targets), *early, *late)
    outs, tiles = lax.optimization_barrier((outs, tiles))
    bias_grad = pl.pallas_call(
        bias_kernel,
        out_shape=jax.ShapeDtypeStruct((3, model), jnp.float32),
        in_specs=[vmem],
        out_specs=vmem,
        compiler_params=params(16),
        name="bias_sums",
    )(tiles)
    return tuple(out[None] for out in outs) + (bias_grad,)


def solution(mesh):
    in_specs = (
        P("dp", "tok", None),
        P("dp", "tok", None),
        P("dp", "tok", None),
        P("dp", "tok", None),
        P(),
        P("dp", None),
        P("dp", None),
    )
    out_specs = (
        P("dp", "tok", None),
        P("dp", "tok", None),
        P("dp", "tok", None),
        P("dp", "tok", None),
        P(),
    )
    return jax.shard_map(
        on_device, mesh=mesh, in_specs=in_specs, out_specs=out_specs, check_vma=False
    )
```

```python
import functools

import jax
import jax.numpy as jnp
import numpy as np
from jax import lax
from jax.experimental import pallas as pl
from jax.experimental.pallas import tpu as pltpu
from jax.sharding import PartitionSpec as P

HEADS = 8
HEAD_DIM = 80
SPAN = 4
OWN_HEADS = HEADS // SPAN
PART = OWN_HEADS * HEAD_DIM
SCALE = HEAD_DIM**-0.5
LOG2E = 1.4426950408889634
NEG = -1e30
LANES = 128
HALF = HEAD_DIM // 2
PACK_KIB = 52 * 1024 + 600
UNPACK_FLOPS = 20_000_000_000

rope_base = 10000.0


def is_closed(count):
    return count in (SPAN, 2 * SPAN)


def trade_rounds(count):
    if is_closed(count):
        return [[(one, one ^ step) for one in range(count)] for step in range(SPAN - 1, 0, -1)]
    rounds = []
    for shift in [*range(1, SPAN), *range(-1, -SPAN, -1)]:
        rounds.append(
            [
                (source, source + shift)
                for source in range(max(0, -shift), min(count, count - shift))
                if (source < SPAN) == (source + shift < SPAN)
            ]
        )
    return rounds


def trade_tables(count):
    rounds = trade_rounds(count)
    sources = np.full((1 + len(rounds), count), -1, np.int32)
    targets = sources.copy()
    sources[0] = targets[0] = np.arange(count)
    for slot, pairs in enumerate(rounds, 1):
        for source, target in pairs:
            sources[slot, target] = source
            targets[slot, source] = target
    return sources, targets


def trade(slices):
    moved = [slices[0]]
    for one, pairs in zip(slices[1:], trade_rounds(lax.axis_size("tok"))):
        moved.append(lax.ppermute(one, "tok", pairs))
    return moved


def send_back(result, slot):
    if slot == 0:
        return result
    pairs = trade_rounds(lax.axis_size("tok"))[slot - 1]
    return lax.ppermute(result, "tok", [(target, source) for source, target in pairs])


EARLY = 1


def image_of(block, lengths, images):
    image = jnp.int32(0)
    start = jnp.int32(0)
    begin = jnp.int32(0)
    for number in range(images):
        size = lengths[0, number]
        inside = (block >= begin) & (block < begin + size)
        image = jnp.where(inside, number, image)
        start = jnp.where(inside, begin, start)
        begin = begin + size
    return image, start


def handler_of(start, residue, count):
    device = start + lax.rem(residue - lax.rem(start, SPAN) + SPAN, SPAN)
    return jnp.where(device >= count, device - SPAN, device)


def message_rows(tensor):
    return slice(tensor * HEAD_DIM, (tensor + 1) * HEAD_DIM)


def rotate(values, cosv, sinv):
    first, second = values[:HALF], values[HALF:]
    return jnp.concatenate([first * cosv - second * sinv, second * cosv + first * sinv], axis=0)


def unrotate(values, cosv, sinv):
    first, second = values[:HALF], values[HALF:]
    return jnp.concatenate([first * cosv + second * sinv, second * cosv - first * sinv], axis=0)


def pack_kernel(closed, *refs):
    inputs, outs, held, turned, sems = refs[:4], refs[4:-3], refs[-3], refs[-2], refs[-1]
    copies = [
        pltpu.make_async_copy(source, held.at[number], sems.at[number])
        for number, source in enumerate(inputs)
    ]
    for copy in copies:
        copy.start()
    me = lax.rem(lax.axis_index("tok"), SPAN)
    steps = [0] + (
        [*range(SPAN - 1, 0, -1)] if closed else [*range(1, SPAN), *range(SPAN - 1, 0, -1)]
    )
    for number, copy in enumerate(copies):
        copy.wait()
        turned[number] = held[number].T
        for phase in range(OWN_HEADS):
            for slot, step in enumerate(steps):
                residue = me ^ step if closed else lax.rem(me + step, SPAN)
                begin = pl.multiple_of((phase * SPAN + residue) * HEAD_DIM, 16)
                outs[phase * len(steps) + slot][message_rows(number), :] = turned[
                    number, pl.ds(begin, HEAD_DIM), :
                ]


def tables_kernel(images, tokd, lengths, widths, table, inverse, bias, cos_out, sin_out, bias_out):
    me = lax.axis_index("tok")
    slots = table.shape[0]
    spot = lax.broadcasted_iota(jnp.int32, (HALF, tokd), 1)
    by_row = lax.broadcasted_iota(jnp.int32, (HALF, tokd), 0) < HALF // 2
    for slot in range(slots):
        block = table[slot, me]
        image, start = image_of(block, lengths, images)
        width = widths[0, image]
        bits = jnp.where(width == tokd, 0, jnp.where(width * 2 == tokd, 1, 2))
        shift = tokd.bit_length() - 1 - bits
        local = spot + (block - start) * tokd
        rowpos = lax.shift_right_logical(local, jnp.broadcast_to(shift, local.shape))
        colpos = local & (width - 1)
        angle = jnp.where(by_row, rowpos, colpos).astype(jnp.float32) * inverse[:, 0:1]
        cos_out[:, slot * tokd : (slot + 1) * tokd] = jnp.cos(angle)
        sin_out[:, slot * tokd : (slot + 1) * tokd] = jnp.sin(angle)
    plain = bias[...].astype(jnp.float32)
    rest = jnp.zeros((LANES - plain.shape[0], plain.shape[1]), jnp.float32)
    bias_out[...] = jnp.concatenate([plain, rest], axis=0).T


def attend_kernel(slots, count, images, tokd, head, factor, lengths, table, cosv, sinv, bias, *refs):
    msgs, refs = refs[:slots], refs[slots:]
    if head > 0:
        before, refs = refs[0], refs[slots:]
    outs, sums = refs[:slots], refs[slots]
    qt_all, kt_all, vt_all, gt_all, k_all, v_all, s_buf, e_buf, d_buf = refs[slots + 1 : slots + 10]
    me = lax.axis_index("tok")
    residue = lax.rem(me, SPAN)
    ids = []
    for slot in range(slots):
        block = table[slot, me]
        image, start = image_of(block, lengths, images)
        handled = (block >= 0) & (handler_of(start, residue, count) == me)
        ids.append(jnp.where(handled, image, -1 - slot))
    begin = pl.multiple_of((head * SPAN + residue) * HEAD_DIM, 16)
    own_bias = bias[pl.ds(begin, HEAD_DIM), :]
    rest_row = lax.broadcasted_iota(jnp.int32, (LANES - HEAD_DIM, tokd), 0)
    zeros = jnp.zeros((LANES - HEAD_DIM, tokd), jnp.float32)
    ones = jnp.where(rest_row < 2, 1.0, 0.0)

    by_lanes = (((1,), (1,)), ((), ()))

    def block_of(slot):
        return slice(slot * tokd, (slot + 1) * tokd)

    def put(slot, tensor, values):
        begin = ((0 if slot == EARLY else 4 * head) + tensor) * HEAD_DIM
        outs[slot][begin : begin + HEAD_DIM, :] = values

    def stage(slot):
        at = block_of(slot)
        cos_b, sin_b = cosv[:, at], sinv[:, at]
        query, key, value = (
            msgs[slot][message_rows(tensor), :].astype(jnp.float32)
            + own_bias[:, tensor : tensor + 1]
            for tensor in range(3)
        )
        query = rotate(query, cos_b, sin_b) * (SCALE * LOG2E)
        for values, rest, turned, plain in (
            (query, zeros, qt_all, None),
            (rotate(key, cos_b, sin_b), zeros, kt_all, k_all),
            (value, ones, vt_all, v_all),
        ):
            values = jnp.concatenate([values, rest], axis=0).astype(jnp.bfloat16)
            turned[:, at] = values
            if plain is not None:
                plain[at, :] = values.T

    def scores(slot, other):
        part = jnp.dot(
            k_all[block_of(other), :], qt_all[:, block_of(slot)], preferred_element_type=jnp.float32
        )
        s_buf[slot % 2, block_of(other), :] = part
        return jnp.max(part, axis=0, keepdims=True)

    def exponentials(slot, other, top):
        part = jnp.exp2(s_buf[slot % 2, block_of(other), :] - top)
        e_buf[block_of(other), block_of(slot)] = part.astype(jnp.bfloat16)

    def output(slot):
        mixed = jnp.dot(
            vt_all[...], e_buf[:, block_of(slot)], preferred_element_type=jnp.float32
        )
        inv = 1.0 / mixed[HEAD_DIM : HEAD_DIM + 1]
        out_b = (mixed[:HEAD_DIM] * inv).astype(jnp.bfloat16)
        put(slot, 0, out_b)
        grad = msgs[slot][message_rows(3), :].astype(jnp.float32)
        delta = jnp.sum(grad * out_b.astype(jnp.float32), axis=0, keepdims=True) * inv
        coarse = delta.astype(jnp.bfloat16).astype(jnp.float32)
        rest = jnp.where(rest_row == 0, -coarse, jnp.where(rest_row == 1, coarse - delta, 0.0))
        grad = jnp.concatenate([grad * inv, rest], axis=0).astype(jnp.bfloat16)
        gt_all[:, block_of(slot)] = grad
        spread = grad[:HEAD_DIM].astype(jnp.float32) * mixed[HEAD_DIM : HEAD_DIM + 1]
        return grad, jnp.where(ids[slot] >= 0, spread, 0.0)

    def dscores(slot, other, grad):
        part = jnp.dot(v_all[block_of(other), :], grad, preferred_element_type=jnp.float32)
        d_buf[block_of(other), block_of(slot)] = (
            e_buf[block_of(other), block_of(slot)] * part.astype(jnp.bfloat16)
        )

    def query_part(slot):
        at = block_of(slot)
        dquery = jnp.dot(kt_all[:HEAD_DIM, :], d_buf[:, at], preferred_element_type=jnp.float32)
        dquery = unrotate(dquery * SCALE, cosv[:, at], sinv[:, at])
        put(slot, 1, dquery.astype(jnp.bfloat16))
        return jnp.where(ids[slot] >= 0, dquery, 0.0)

    def value_part(slot):
        dvalue = lax.dot_general(
            gt_all[:HEAD_DIM, :],
            e_buf[block_of(slot), :],
            by_lanes,
            preferred_element_type=jnp.float32,
        )
        put(slot, 3, dvalue.astype(jnp.bfloat16))

    for slot in range(slots):
        stage(slot)
    dq_total = jnp.zeros((HEAD_DIM, tokd), jnp.float32)
    dv_total = jnp.zeros((HEAD_DIM, tokd), jnp.float32)
    grad = None
    offs = tops = None
    for step in range(slots + 2):
        ahead, slot, behind = step, step - 1, step - 2
        if 0 <= slot < slots:
            offs = [jnp.where(ids[slot] == ids[other], 0.0, NEG) for other in range(slots)]
            top = functools.reduce(jnp.maximum, [one + off for one, off in zip(tops, offs)])
        tops = []
        for other in range(slots):
            if ahead < slots:
                tops.append(scores(ahead, other))
            if 0 <= behind:
                dscores(behind, other, grad)
            if 0 <= slot < slots:
                exponentials(slot, other, top - offs[other])
        if 0 <= behind:
            dq_total = dq_total + query_part(behind)
        if 0 <= slot < slots:
            grad, spread = output(slot)
            dv_total = dv_total + spread
    dk_total = jnp.zeros((HEAD_DIM, tokd), jnp.float32)
    for slot in range(slots):
        at = block_of(slot)
        dkey = lax.dot_general(
            qt_all[:HEAD_DIM, :], d_buf[at, :], by_lanes, preferred_element_type=jnp.float32
        )
        dkey = unrotate(dkey * (1.0 / LOG2E), cosv[:, at], sinv[:, at])
        put(slot, 2, dkey.astype(jnp.bfloat16))
        dk_total = dk_total + jnp.where(ids[slot] >= 0, dkey, 0.0)
    lane = lax.broadcasted_iota(jnp.int32, (HEAD_DIM, LANES), 1)
    columns = jnp.zeros((HEAD_DIM, LANES), jnp.float32)
    for number, total in enumerate((dq_total, dk_total, dv_total)):
        total = jnp.sum(total, axis=1, keepdims=True) * factor
        columns = jnp.where(lane == number, total, columns)
    columns = jnp.concatenate([columns, jnp.zeros((LANES - HEAD_DIM, LANES), jnp.float32)], axis=0)
    lines = columns.T
    copy = None
    if head + 1 < OWN_HEADS:
        sums[...] = lines[:8]
    else:
        tiles, sem = refs[slots + 10 :]
        tile = join_sums(before[...], lines)

        def repeat(device, carry):
            tiles[device] = tile
            return carry

        lax.fori_loop(0, tiles.shape[0], repeat, 0, unroll=min(32, tiles.shape[0]))
        copy = pltpu.make_async_copy(tiles, sums, sem)
        copy.start()
    for slot in range(slots):
        value_part(slot)
    if copy is not None:
        copy.wait()


FIT = LANES - HEAD_DIM
LEFT = HEAD_DIM - FIT


def join_sums(first, second):
    lane = lax.broadcasted_iota(jnp.int32, (1, LANES), 1)
    rows = []
    last = jnp.zeros((1, LANES), jnp.float32)
    for number in range(3):
        moved = pltpu.roll(second[number : number + 1], HEAD_DIM, 1)
        rows.append(jnp.where(lane < HEAD_DIM, first[number : number + 1], moved))
        rest = jnp.where(lane < LEFT, moved, 0.0)
        last = last + (pltpu.roll(rest, number * LEFT, 1) if number else rest)
    return jnp.concatenate(rows + [last], axis=0)


def unpack_kernel(slots, count, images, lengths, table, *refs):
    msgs, outs, held = refs[: slots + OWN_HEADS - 1], refs[slots + OWN_HEADS - 1 : -1], refs[-1]
    early, late = msgs[:OWN_HEADS], list(msgs[OWN_HEADS:])
    late.insert(EARLY, None)
    me = lax.axis_index("tok")
    _, start = image_of(me, lengths, images)
    for slot in range(slots):
        source = table[slot, me]
        residue = lax.rem(source + SPAN, SPAN)

        def place(slot=slot, residue=residue):
            for phase in range(OWN_HEADS):
                begin = pl.multiple_of((phase * SPAN + residue) * HEAD_DIM, 16)
                for number in range(4):
                    if slot == EARLY:
                        piece = early[phase][message_rows(number), :]
                    else:
                        piece = late[slot][message_rows(4 * phase + number), :]
                    held[number, pl.ds(begin, HEAD_DIM), :] = piece

        if is_closed(count):
            place()
        else:
            pl.when((source >= 0) & (source == handler_of(start, residue, count)))(place)
    for number, out in enumerate(outs):
        out[...] = held[number].T


def bias_kernel(tiles, bias_out):
    def add(group, totals):
        return tuple(
            total + tiles[group * SPAN + residue] for residue, total in enumerate(totals)
        )

    groups = tiles.shape[0] // SPAN
    zero = jnp.zeros(tiles.shape[1:], jnp.float32)
    totals = lax.fori_loop(0, groups, add, (zero,) * SPAN, unroll=groups <= 8)
    for residue, total in enumerate(totals):
        first = residue * HEAD_DIM
        second = (SPAN + residue) * HEAD_DIM
        for number in range(3):
            row = slice(number, number + 1)
            bias_out[row, first : first + HEAD_DIM] = total[row, :HEAD_DIM]
            bias_out[row, second : second + FIT] = total[row, HEAD_DIM:]
            bias_out[row, second + FIT : second + HEAD_DIM] = total[
                3:4, number * LEFT : (number + 1) * LEFT
            ]


def on_device(query_in, key_in, value_in, out_grad, bias, lengths, widths):
    tokd = query_in.shape[1]
    model = query_in.shape[2]
    images = lengths.shape[1]
    count = lax.axis_size("tok")
    dp_size = lax.axis_size("dp")
    closed = is_closed(count)
    sources, targets = trade_tables(count)
    slots = sources.shape[0]
    span = slots * tokd
    table = jnp.asarray(sources)
    quarter = HEAD_DIM // 4
    inverse = rope_base ** (-np.arange(quarter, dtype=np.float64) / quarter)
    inverse = jnp.asarray(np.tile(np.tile(inverse, 2)[:, None], (1, LANES)), jnp.float32)
    smem = pl.BlockSpec(memory_space=pltpu.SMEM)
    vmem = pl.BlockSpec(memory_space=pltpu.VMEM)
    hbm = pl.BlockSpec(memory_space=pltpu.HBM)
    whole = jax.ShapeDtypeStruct((tokd, model), jnp.bfloat16)
    message = jax.ShapeDtypeStruct((4 * HEAD_DIM, tokd), jnp.bfloat16)
    joined = jax.ShapeDtypeStruct((OWN_HEADS * 4 * HEAD_DIM, tokd), jnp.bfloat16)
    devices = dp_size * count
    tokens_all = devices * tokd

    def params(mib):
        return pltpu.CompilerParams(vmem_limit_bytes=int(mib * 1024 * 1024))

    inputs = (query_in[0], key_in[0], value_in[0], out_grad[0])
    sends = pl.pallas_call(
        functools.partial(pack_kernel, closed),
        out_shape=[message] * (OWN_HEADS * slots),
        in_specs=[hbm] * 4,
        out_specs=[vmem] * (OWN_HEADS * slots),
        scratch_shapes=[
            pltpu.VMEM((4, tokd, model), jnp.bfloat16),
            pltpu.VMEM((4, model, tokd), jnp.bfloat16),
            pltpu.SemaphoreType.DMA((4,)),
        ],
        compiler_params=params(PACK_KIB / 1024),
        name="pack_heads",
    )(*inputs)
    got = [trade(sends[:slots])]
    table_shape = jax.ShapeDtypeStruct((HALF, span), jnp.float32)
    tables = pl.pallas_call(
        functools.partial(tables_kernel, images, tokd),
        out_shape=[table_shape] * 2 + [jax.ShapeDtypeStruct((model, LANES), jnp.float32)],
        in_specs=[smem, smem, smem, vmem, vmem],
        out_specs=[vmem] * 3,
        compiler_params=params(16),
        cost_estimate=pl.CostEstimate(
            flops=span * LANES * 200, bytes_accessed=0, transcendentals=0
        ),
        name="rotary_tables",
    )(lengths, widths, table, inverse, bias)
    tables, sends = lax.optimization_barrier((tables, sends[slots:]))
    for phase in range(1, OWN_HEADS):
        got.append(trade(sends[(phase - 1) * slots : phase * slots]))
    early = []
    carried = []
    for phase in range(OWN_HEADS):
        last = phase + 1 == OWN_HEADS
        kept = [slot for slot in range(slots) if slot != EARLY]
        sums_shape = jax.ShapeDtypeStruct(
            (devices, 4, LANES) if last else (8, LANES), jnp.float32
        )
        first_carried = 5 + slots + 1
        *results, total = pl.pallas_call(
            functools.partial(
                attend_kernel, slots, count, images, tokd, phase, 1.0 / tokens_all**0.5
            ),
            out_shape=[message if slot == EARLY else joined for slot in range(slots)]
            + [sums_shape],
            in_specs=[smem, smem] + [vmem] * (3 + slots + len(carried)),
            out_specs=[vmem] * slots + [hbm if last else vmem],
            input_output_aliases={first_carried + at: slot for at, slot in enumerate(kept)}
            if carried
            else {},
            scratch_shapes=[pltpu.VMEM((LANES, span), jnp.bfloat16)] * 4
            + [pltpu.VMEM((span, LANES), jnp.bfloat16)] * 2
            + [pltpu.VMEM((2, span, tokd), jnp.float32)]
            + [pltpu.VMEM((span, span), jnp.bfloat16)] * 2
            + (
                [pltpu.VMEM(sums_shape.shape, jnp.float32), pltpu.SemaphoreType.DMA(())]
                if last
                else []
            ),
            compiler_params=params(32),
            cost_estimate=pl.CostEstimate(
                flops=12 * span * span * 256, bytes_accessed=0, transcendentals=0
            ),
            name="attend_head",
        )(lengths, table, *tables, *got[phase], *carried)
        results, total, early = lax.optimization_barrier((results, total, early))
        early.append(send_back(results[EARLY], EARLY))
        carried = [total] + [results[slot] for slot in kept]
    tiles = lax.all_to_all(total, ("dp", "tok"), 0, 0, tiled=True)
    late = [send_back(results[slot], slot) for slot in kept]
    outs = pl.pallas_call(
        functools.partial(unpack_kernel, slots, count, images),
        out_shape=[whole] * 4,
        in_specs=[smem, smem] + [vmem] * (OWN_HEADS + len(late)),
        out_specs=[vmem] * 4,
        scratch_shapes=[pltpu.VMEM((4, model, tokd), jnp.bfloat16)],
        compiler_params=params(16),
        cost_estimate=pl.CostEstimate(flops=UNPACK_FLOPS, bytes_accessed=0, transcendentals=0),
        name="unpack_heads",
    )(lengths, jnp.asarray(targets), *early, *late)
    outs, tiles = lax.optimization_barrier((outs, tiles))
    bias_grad = pl.pallas_call(
        bias_kernel,
        out_shape=jax.ShapeDtypeStruct((3, model), jnp.float32),
        in_specs=[vmem],
        out_specs=vmem,
        compiler_params=params(16),
        name="bias_sums",
    )(tiles)
    return tuple(out[None] for out in outs) + (bias_grad,)


def solution(mesh):
    in_specs = (
        P("dp", "tok", None),
        P("dp", "tok", None),
        P("dp", "tok", None),
        P("dp", "tok", None),
        P(),
        P("dp", None),
        P("dp", None),
    )
    out_specs = (
        P("dp", "tok", None),
        P("dp", "tok", None),
        P("dp", "tok", None),
        P("dp", "tok", None),
        P(),
    )
    return jax.shard_map(
        on_device, mesh=mesh, in_specs=in_specs, out_specs=out_specs, check_vma=False
    )
```

```python
import functools

import jax
import jax.numpy as jnp
import numpy as np
from jax import lax
from jax.experimental import pallas as pl
from jax.experimental.pallas import tpu as pltpu
from jax.sharding import PartitionSpec as P

HEADS = 8
HEAD_DIM = 80
SPAN = 4
OWN_HEADS = HEADS // SPAN
PART = OWN_HEADS * HEAD_DIM
SCALE = HEAD_DIM**-0.5
LOG2E = 1.4426950408889634
NEG = -1e30
LANES = 128
HALF = HEAD_DIM // 2
PACK_KIB = 52 * 1024 + 600
UNPACK_FLOPS = 20_000_000_000

rope_base = 10000.0


def is_closed(count):
    return count in (SPAN, 2 * SPAN)


def closed_step(slot):
    return (SPAN - slot) % SPAN


def trade_rounds(count):
    if is_closed(count):
        return [
            [(one, one ^ closed_step(slot)) for one in range(count)] for slot in range(1, SPAN)
        ]
    rounds = []
    for shift in [*range(1, SPAN), *range(-1, -SPAN, -1)]:
        rounds.append(
            [
                (source, source + shift)
                for source in range(max(0, -shift), min(count, count - shift))
                if (source < SPAN) == (source + shift < SPAN)
            ]
        )
    return rounds


def trade_tables(count):
    rounds = trade_rounds(count)
    sources = np.full((1 + len(rounds), count), -1, np.int32)
    targets = sources.copy()
    sources[0] = targets[0] = np.arange(count)
    for slot, pairs in enumerate(rounds, 1):
        for source, target in pairs:
            sources[slot, target] = source
            targets[slot, source] = target
    return sources, targets


def trade(slices):
    moved = [slices[0]]
    for one, pairs in zip(slices[1:], trade_rounds(lax.axis_size("tok"))):
        moved.append(lax.ppermute(one, "tok", pairs))
    return moved


def send_back(result, slot):
    if slot == 0:
        return result
    pairs = trade_rounds(lax.axis_size("tok"))[slot - 1]
    return lax.ppermute(result, "tok", [(target, source) for source, target in pairs])


EARLY = 1


def image_of(block, lengths, images):
    image = jnp.int32(0)
    start = jnp.int32(0)
    begin = jnp.int32(0)
    for number in range(images):
        size = lengths[0, number]
        inside = (block >= begin) & (block < begin + size)
        image = jnp.where(inside, number, image)
        start = jnp.where(inside, begin, start)
        begin = begin + size
    return image, start


def handler_of(start, residue, count):
    device = start + lax.rem(residue - lax.rem(start, SPAN) + SPAN, SPAN)
    return jnp.where(device >= count, device - SPAN, device)


def message_rows(tensor):
    return slice(tensor * HEAD_DIM, (tensor + 1) * HEAD_DIM)


def rotate(values, cosv, sinv):
    first, second = values[:HALF], values[HALF:]
    return jnp.concatenate([first * cosv - second * sinv, second * cosv + first * sinv], axis=0)


def unrotate(values, cosv, sinv):
    first, second = values[:HALF], values[HALF:]
    return jnp.concatenate([first * cosv + second * sinv, second * cosv - first * sinv], axis=0)


def pack_kernel(closed, *refs):
    inputs, outs, held, turned, sems = refs[:4], refs[4:-3], refs[-3], refs[-2], refs[-1]
    copies = [
        pltpu.make_async_copy(source, held.at[number], sems.at[number])
        for number, source in enumerate(inputs)
    ]
    for copy in copies:
        copy.start()
    me = lax.rem(lax.axis_index("tok"), SPAN)
    steps = (
        [closed_step(slot) for slot in range(SPAN)]
        if closed
        else [0, *range(1, SPAN), *range(SPAN - 1, 0, -1)]
    )
    for number, copy in enumerate(copies):
        copy.wait()
        turned[number] = held[number].T
        for phase in range(OWN_HEADS):
            for slot, step in enumerate(steps):
                residue = me ^ step if closed else lax.rem(me + step, SPAN)
                begin = pl.multiple_of((phase * SPAN + residue) * HEAD_DIM, 16)
                outs[phase * len(steps) + slot][message_rows(number), :] = turned[
                    number, pl.ds(begin, HEAD_DIM), :
                ]


def tables_kernel(images, count, tokd, lengths, widths, table, inverse, bias, *refs):
    cos_out, sin_out, mask_out, bias_out, turned = refs
    me = lax.axis_index("tok")
    residue = lax.rem(me, SPAN)
    slots = table.shape[0]
    spot = lax.broadcasted_iota(jnp.int32, (HALF, tokd), 1)
    by_row = lax.broadcasted_iota(jnp.int32, (HALF, tokd), 0) < HALF // 2
    ids = []
    for slot in range(slots):
        block = table[slot, me]
        image, start = image_of(block, lengths, images)
        handled = (block >= 0) & (handler_of(start, residue, count) == me)
        ids.append(jnp.where(handled, image, -1 - slot))
        width = widths[0, image]
        bits = jnp.where(width == tokd, 0, jnp.where(width * 2 == tokd, 1, 2))
        shift = tokd.bit_length() - 1 - bits
        local = spot + (block - start) * tokd
        rowpos = lax.shift_right_logical(local, jnp.broadcast_to(shift, local.shape))
        colpos = local & (width - 1)
        angle = jnp.where(by_row, rowpos, colpos).astype(jnp.float32) * inverse[:, 0:1]
        cos_out[:, slot * tokd : (slot + 1) * tokd] = jnp.cos(angle)
        sin_out[:, slot * tokd : (slot + 1) * tokd] = jnp.sin(angle)
    for slot in range(slots):
        for other in range(slots):
            off = jnp.where(ids[slot] == ids[other], 0.0, NEG)
            row = slot * slots + other
            mask_out[row : row + 1, :] = jnp.full((1, tokd), off, jnp.float32)
        row = slots * slots + slot
        live = jnp.where(ids[slot] >= 0, 1.0, 0.0)
        mask_out[row : row + 1, :] = jnp.full((1, tokd), live, jnp.float32)
    plain = bias[...].astype(jnp.float32)
    rest = jnp.zeros((LANES - plain.shape[0], plain.shape[1]), jnp.float32)
    turned[...] = jnp.concatenate([plain, rest], axis=0).T
    for phase in range(OWN_HEADS):
        begin = pl.multiple_of((phase * SPAN + residue) * HEAD_DIM, 16)
        bias_out[phase * HEAD_DIM : (phase + 1) * HEAD_DIM, :] = turned[pl.ds(begin, HEAD_DIM), :]


def attend_kernel(slots, closed, tokd, head, factor, cosv, sinv, masks, bias, *refs):
    msgs, refs = refs[:slots], refs[slots:]
    if head > 0:
        before, refs = refs[0], refs[slots:]
    outs, sums = refs[:slots], refs[slots]
    qt_all, kt_all, vt_all, gt_all, k_all, v_all, s_buf, e_buf, d_buf = refs[slots + 1 : slots + 10]
    own_bias = bias[head * HEAD_DIM : (head + 1) * HEAD_DIM, :]
    rest_row = lax.broadcasted_iota(jnp.int32, (LANES - HEAD_DIM, tokd), 0)
    zeros = jnp.zeros((LANES - HEAD_DIM, tokd), jnp.float32)
    ones = jnp.where(rest_row < 2, 1.0, 0.0)

    by_lanes = (((1,), (1,)), ((), ()))

    def off_row(slot, other):
        row = slot * slots + other
        return masks[row : row + 1, :]

    def live(slot, values):
        if closed:
            return values
        row = slots * slots + slot
        return values * masks[row : row + 1, :]

    def block_of(slot):
        return slice(slot * tokd, (slot + 1) * tokd)

    def put(slot, tensor, values):
        begin = ((0 if slot == EARLY else 4 * head) + tensor) * HEAD_DIM
        outs[slot][begin : begin + HEAD_DIM, :] = values

    def stage(slot):
        at = block_of(slot)
        cos_b, sin_b = cosv[:, at], sinv[:, at]
        query, key, value = (
            msgs[slot][message_rows(tensor), :].astype(jnp.float32)
            + own_bias[:, tensor : tensor + 1]
            for tensor in range(3)
        )
        query = rotate(query, cos_b, sin_b) * (SCALE * LOG2E)
        for values, rest, turned, plain in (
            (query, zeros, qt_all, None),
            (rotate(key, cos_b, sin_b), zeros, kt_all, k_all),
            (value, ones, vt_all, v_all),
        ):
            values = jnp.concatenate([values, rest], axis=0).astype(jnp.bfloat16)
            turned[:, at] = values
            if plain is not None:
                plain[at, :] = values.T

    def scores(slot, other):
        part = jnp.dot(
            k_all[block_of(other), :], qt_all[:, block_of(slot)], preferred_element_type=jnp.float32
        )
        s_buf[slot % 2, block_of(other), :] = part
        return jnp.max(part, axis=0, keepdims=True)

    def exponentials(slot, other, top):
        part = jnp.exp2(s_buf[slot % 2, block_of(other), :] - top)
        e_buf[block_of(other), block_of(slot)] = part.astype(jnp.bfloat16)

    def output(slot):
        mixed = jnp.dot(
            vt_all[...], e_buf[:, block_of(slot)], preferred_element_type=jnp.float32
        )
        inv = 1.0 / mixed[HEAD_DIM : HEAD_DIM + 1]
        out_b = (mixed[:HEAD_DIM] * inv).astype(jnp.bfloat16)
        put(slot, 0, out_b)
        grad = msgs[slot][message_rows(3), :].astype(jnp.float32)
        delta = jnp.sum(grad * out_b.astype(jnp.float32), axis=0, keepdims=True) * inv
        coarse = delta.astype(jnp.bfloat16).astype(jnp.float32)
        rest = jnp.where(rest_row == 0, -coarse, jnp.where(rest_row == 1, coarse - delta, 0.0))
        grad = jnp.concatenate([grad * inv, rest], axis=0).astype(jnp.bfloat16)
        gt_all[:, block_of(slot)] = grad
        spread = grad[:HEAD_DIM].astype(jnp.float32) * mixed[HEAD_DIM : HEAD_DIM + 1]
        return grad, live(slot, spread)

    def dscores(slot, other, grad):
        part = jnp.dot(v_all[block_of(other), :], grad, preferred_element_type=jnp.float32)
        d_buf[block_of(other), block_of(slot)] = (
            e_buf[block_of(other), block_of(slot)] * part.astype(jnp.bfloat16)
        )

    def query_part(slot):
        at = block_of(slot)
        dquery = jnp.dot(kt_all[:HEAD_DIM, :], d_buf[:, at], preferred_element_type=jnp.float32)
        dquery = unrotate(dquery * SCALE, cosv[:, at], sinv[:, at])
        put(slot, 1, dquery.astype(jnp.bfloat16))
        return live(slot, dquery)

    def value_part(slot):
        dvalue = lax.dot_general(
            gt_all[:HEAD_DIM, :],
            e_buf[block_of(slot), :],
            by_lanes,
            preferred_element_type=jnp.float32,
        )
        put(slot, 3, dvalue.astype(jnp.bfloat16))

    for slot in range(slots):
        stage(slot)
    dq_total = jnp.zeros((HEAD_DIM, tokd), jnp.float32)
    dv_total = jnp.zeros((HEAD_DIM, tokd), jnp.float32)
    grad = None
    offs = tops = None
    for step in range(slots + 2):
        ahead, slot, behind = step, step - 1, step - 2
        if 0 <= slot < slots:
            offs = [off_row(slot, other) for other in range(slots)]
            top = functools.reduce(jnp.maximum, [one + off for one, off in zip(tops, offs)])
        tops = []
        for other in range(slots):
            if ahead < slots:
                tops.append(scores(ahead, other))
            if 0 <= behind:
                dscores(behind, other, grad)
            if 0 <= slot < slots:
                exponentials(slot, other, top - offs[other])
        if 0 <= behind:
            dq_total = dq_total + query_part(behind)
        if 0 <= slot < slots:
            grad, spread = output(slot)
            dv_total = dv_total + spread
    dk_total = jnp.zeros((HEAD_DIM, tokd), jnp.float32)
    for slot in range(slots):
        at = block_of(slot)
        dkey = lax.dot_general(
            qt_all[:HEAD_DIM, :], d_buf[at, :], by_lanes, preferred_element_type=jnp.float32
        )
        dkey = unrotate(dkey * (1.0 / LOG2E), cosv[:, at], sinv[:, at])
        put(slot, 2, dkey.astype(jnp.bfloat16))
        dk_total = dk_total + live(slot, dkey)
    lane = lax.broadcasted_iota(jnp.int32, (HEAD_DIM, LANES), 1)
    columns = jnp.zeros((HEAD_DIM, LANES), jnp.float32)
    for number, total in enumerate((dq_total, dk_total, dv_total)):
        total = jnp.sum(total, axis=1, keepdims=True) * factor
        columns = jnp.where(lane == number, total, columns)
    columns = jnp.concatenate([columns, jnp.zeros((LANES - HEAD_DIM, LANES), jnp.float32)], axis=0)
    lines = columns.T
    copy = None
    if head + 1 < OWN_HEADS:
        sums[...] = lines[:8]
    else:
        tiles, sem = refs[slots + 10 :]
        tile = join_sums(before[...], lines)

        def repeat(device, carry):
            tiles[device] = tile
            return carry

        lax.fori_loop(0, tiles.shape[0], repeat, 0, unroll=min(32, tiles.shape[0]))
        copy = pltpu.make_async_copy(tiles, sums, sem)
        copy.start()
    for slot in range(slots):
        value_part(slot)
    if copy is not None:
        copy.wait()


FIT = LANES - HEAD_DIM
LEFT = HEAD_DIM - FIT


def join_sums(first, second):
    lane = lax.broadcasted_iota(jnp.int32, (1, LANES), 1)
    rows = []
    last = jnp.zeros((1, LANES), jnp.float32)
    for number in range(3):
        moved = pltpu.roll(second[number : number + 1], HEAD_DIM, 1)
        rows.append(jnp.where(lane < HEAD_DIM, first[number : number + 1], moved))
        rest = jnp.where(lane < LEFT, moved, 0.0)
        last = last + (pltpu.roll(rest, number * LEFT, 1) if number else rest)
    return jnp.concatenate(rows + [last], axis=0)


def unpack_kernel(slots, count, images, *refs):
    closed = is_closed(count)
    if not closed:
        lengths, table, *refs = refs
    msgs, refs = refs[: slots + OWN_HEADS - 1], refs[slots + OWN_HEADS - 1 :]
    outs, held, ready, sems = refs[:4], refs[4], refs[5], refs[6]
    early, late = msgs[:OWN_HEADS], list(msgs[OWN_HEADS:])
    late.insert(EARLY, None)
    me = lax.axis_index("tok")

    def place(slot, residue):
        for phase in range(OWN_HEADS):
            begin = pl.multiple_of((phase * SPAN + residue) * HEAD_DIM, 16)
            for number in range(4):
                if slot == EARLY:
                    piece = early[phase][message_rows(number), :]
                else:
                    piece = late[slot][message_rows(4 * phase + number), :]
                held[number, pl.ds(begin, HEAD_DIM), :] = piece

    for slot in range(slots):
        if closed:
            place(slot, lax.rem(me, SPAN) ^ closed_step(slot))
        else:
            _, start = image_of(me, lengths, images)
            source = table[slot, me]
            residue = lax.rem(source + SPAN, SPAN)
            chosen = (source >= 0) & (source == handler_of(start, residue, count))
            pl.when(chosen)(functools.partial(place, slot, residue))
    copies = []
    for number, out in enumerate(outs):
        ready[number] = held[number].T
        copies.append(pltpu.make_async_copy(ready.at[number], out, sems.at[number]))
        copies[-1].start()
    for copy in copies:
        copy.wait()


def bias_kernel(tiles, bias_out):
    def add(group, totals):
        return tuple(
            total + tiles[group * SPAN + residue] for residue, total in enumerate(totals)
        )

    groups = tiles.shape[0] // SPAN
    zero = jnp.zeros(tiles.shape[1:], jnp.float32)
    totals = lax.fori_loop(0, groups, add, (zero,) * SPAN, unroll=groups <= 8)
    for residue, total in enumerate(totals):
        first = residue * HEAD_DIM
        second = (SPAN + residue) * HEAD_DIM
        for number in range(3):
            row = slice(number, number + 1)
            bias_out[row, first : first + HEAD_DIM] = total[row, :HEAD_DIM]
            bias_out[row, second : second + FIT] = total[row, HEAD_DIM:]
            bias_out[row, second + FIT : second + HEAD_DIM] = total[
                3:4, number * LEFT : (number + 1) * LEFT
            ]


def on_device(query_in, key_in, value_in, out_grad, bias, lengths, widths):
    tokd = query_in.shape[1]
    model = query_in.shape[2]
    images = lengths.shape[1]
    count = lax.axis_size("tok")
    dp_size = lax.axis_size("dp")
    closed = is_closed(count)
    sources, targets = trade_tables(count)
    slots = sources.shape[0]
    span = slots * tokd
    table = jnp.asarray(sources)
    quarter = HEAD_DIM // 4
    inverse = rope_base ** (-np.arange(quarter, dtype=np.float64) / quarter)
    inverse = jnp.asarray(np.tile(np.tile(inverse, 2)[:, None], (1, LANES)), jnp.float32)
    smem = pl.BlockSpec(memory_space=pltpu.SMEM)
    vmem = pl.BlockSpec(memory_space=pltpu.VMEM)
    hbm = pl.BlockSpec(memory_space=pltpu.HBM)
    whole = jax.ShapeDtypeStruct((tokd, model), jnp.bfloat16)
    message = jax.ShapeDtypeStruct((4 * HEAD_DIM, tokd), jnp.bfloat16)
    joined = jax.ShapeDtypeStruct((OWN_HEADS * 4 * HEAD_DIM, tokd), jnp.bfloat16)
    devices = dp_size * count
    tokens_all = devices * tokd

    def params(mib):
        return pltpu.CompilerParams(vmem_limit_bytes=int(mib * 1024 * 1024))

    inputs = (query_in[0], key_in[0], value_in[0], out_grad[0])
    sends = pl.pallas_call(
        functools.partial(pack_kernel, closed),
        out_shape=[message] * (OWN_HEADS * slots),
        in_specs=[hbm] * 4,
        out_specs=[vmem] * (OWN_HEADS * slots),
        scratch_shapes=[
            pltpu.VMEM((4, tokd, model), jnp.bfloat16),
            pltpu.VMEM((4, model, tokd), jnp.bfloat16),
            pltpu.SemaphoreType.DMA((4,)),
        ],
        compiler_params=params(PACK_KIB / 1024),
        name="pack_heads",
    )(*inputs)
    got = [trade(sends[:slots])]
    table_shape = jax.ShapeDtypeStruct((HALF, span), jnp.float32)
    mask_rows = -(-slots * (slots + 1) // 8) * 8
    tables = pl.pallas_call(
        functools.partial(tables_kernel, images, count, tokd),
        out_shape=[table_shape] * 2
        + [
            jax.ShapeDtypeStruct((mask_rows, tokd), jnp.float32),
            jax.ShapeDtypeStruct((OWN_HEADS * HEAD_DIM, LANES), jnp.float32),
        ],
        in_specs=[smem, smem, smem, vmem, vmem],
        out_specs=[vmem] * 4,
        scratch_shapes=[pltpu.VMEM((model, LANES), jnp.float32)],
        compiler_params=params(16),
        cost_estimate=pl.CostEstimate(
            flops=span * LANES * 200, bytes_accessed=0, transcendentals=0
        ),
        name="rotary_tables",
    )(lengths, widths, table, inverse, bias)
    tables, sends = lax.optimization_barrier((tables, sends[slots:]))
    for phase in range(1, OWN_HEADS):
        got.append(trade(sends[(phase - 1) * slots : phase * slots]))
    early = []
    carried = []
    for phase in range(OWN_HEADS):
        last = phase + 1 == OWN_HEADS
        kept = [slot for slot in range(slots) if slot != EARLY]
        sums_shape = jax.ShapeDtypeStruct(
            (devices, 4, LANES) if last else (8, LANES), jnp.float32
        )
        first_carried = 4 + slots + 1
        *results, total = pl.pallas_call(
            functools.partial(
                attend_kernel, slots, closed, tokd, phase, 1.0 / tokens_all**0.5
            ),
            out_shape=[message if slot == EARLY else joined for slot in range(slots)]
            + [sums_shape],
            in_specs=[vmem] * (4 + slots + len(carried)),
            out_specs=[vmem] * slots + [hbm if last else vmem],
            input_output_aliases={first_carried + at: slot for at, slot in enumerate(kept)}
            if carried
            else {},
            scratch_shapes=[pltpu.VMEM((LANES, span), jnp.bfloat16)] * 4
            + [pltpu.VMEM((span, LANES), jnp.bfloat16)] * 2
            + [pltpu.VMEM((2, span, tokd), jnp.float32)]
            + [pltpu.VMEM((span, span), jnp.bfloat16)] * 2
            + (
                [pltpu.VMEM(sums_shape.shape, jnp.float32), pltpu.SemaphoreType.DMA(())]
                if last
                else []
            ),
            compiler_params=params(32),
            cost_estimate=pl.CostEstimate(
                flops=12 * span * span * 256, bytes_accessed=0, transcendentals=0
            ),
            name="attend_head",
        )(*tables, *got[phase], *carried)
        results, total, early = lax.optimization_barrier((results, total, early))
        early.append(send_back(results[EARLY], EARLY))
        carried = [total] + [results[slot] for slot in kept]
    tiles = lax.all_to_all(total, ("dp", "tok"), 0, 0, tiled=True)
    late = [send_back(results[slot], slot) for slot in kept]
    places = [] if closed else [lengths, jnp.asarray(targets)]
    outs = pl.pallas_call(
        functools.partial(unpack_kernel, slots, count, images),
        out_shape=[whole] * 4,
        in_specs=[smem] * len(places) + [vmem] * (OWN_HEADS + len(late)),
        out_specs=[hbm] * 4,
        scratch_shapes=[
            pltpu.VMEM((4, model, tokd), jnp.bfloat16),
            pltpu.VMEM((4, tokd, model), jnp.bfloat16),
            pltpu.SemaphoreType.DMA((4,)),
        ],
        compiler_params=params(16),
        cost_estimate=pl.CostEstimate(flops=UNPACK_FLOPS, bytes_accessed=0, transcendentals=0),
        name="unpack_heads",
    )(*places, *early, *late)
    outs, tiles = lax.optimization_barrier((outs, tiles))
    bias_grad = pl.pallas_call(
        bias_kernel,
        out_shape=jax.ShapeDtypeStruct((3, model), jnp.float32),
        in_specs=[vmem],
        out_specs=vmem,
        compiler_params=params(16),
        name="bias_sums",
    )(tiles)
    return tuple(out[None] for out in outs) + (bias_grad,)


def solution(mesh):
    in_specs = (
        P("dp", "tok", None),
        P("dp", "tok", None),
        P("dp", "tok", None),
        P("dp", "tok", None),
        P(),
        P("dp", None),
        P("dp", None),
    )
    out_specs = (
        P("dp", "tok", None),
        P("dp", "tok", None),
        P("dp", "tok", None),
        P("dp", "tok", None),
        P(),
    )
    return jax.shard_map(
        on_device, mesh=mesh, in_specs=in_specs, out_specs=out_specs, check_vma=False
    )
```

```python
import functools

import jax
import jax.numpy as jnp
import numpy as np
from jax import lax
from jax.experimental import pallas as pl
from jax.experimental.pallas import tpu as pltpu
from jax.sharding import PartitionSpec as P

HEADS = 8
HEAD_DIM = 80
SPAN = 4
OWN_HEADS = HEADS // SPAN
PART = OWN_HEADS * HEAD_DIM
SCALE = HEAD_DIM**-0.5
LOG2E = 1.4426950408889634
NEG = -1e30
LANES = 128
USED = HEAD_DIM + 16
HALF = HEAD_DIM // 2
PACK_KIB = 52 * 1024 + 600

rope_base = 10000.0


def is_closed(count):
    return count in (SPAN, 2 * SPAN)


def closed_step(slot):
    return (SPAN - slot) % SPAN


def trade_rounds(count):
    if is_closed(count):
        return [
            [(one, one ^ closed_step(slot)) for one in range(count)] for slot in range(1, SPAN)
        ]
    rounds = []
    for shift in [*range(1, SPAN), *range(-1, -SPAN, -1)]:
        rounds.append(
            [
                (source, source + shift)
                for source in range(max(0, -shift), min(count, count - shift))
                if (source < SPAN) == (source + shift < SPAN)
            ]
        )
    return rounds


def trade_tables(count):
    rounds = trade_rounds(count)
    sources = np.full((1 + len(rounds), count), -1, np.int32)
    targets = sources.copy()
    sources[0] = targets[0] = np.arange(count)
    for slot, pairs in enumerate(rounds, 1):
        for source, target in pairs:
            sources[slot, target] = source
            targets[slot, source] = target
    return sources, targets


def trade(slices):
    moved = [slices[0]]
    for one, pairs in zip(slices[1:], trade_rounds(lax.axis_size("tok"))):
        moved.append(lax.ppermute(one, "tok", pairs))
    return moved


def send_back(result, slot):
    if slot == 0:
        return result
    pairs = trade_rounds(lax.axis_size("tok"))[slot - 1]
    return lax.ppermute(result, "tok", [(target, source) for source, target in pairs])


EARLY = 1


def image_of(block, lengths, images):
    image = jnp.int32(0)
    start = jnp.int32(0)
    begin = jnp.int32(0)
    for number in range(images):
        size = lengths[0, number]
        inside = (block >= begin) & (block < begin + size)
        image = jnp.where(inside, number, image)
        start = jnp.where(inside, begin, start)
        begin = begin + size
    return image, start


def handler_of(start, residue, count):
    device = start + lax.rem(residue - lax.rem(start, SPAN) + SPAN, SPAN)
    return jnp.where(device >= count, device - SPAN, device)


def message_rows(tensor):
    return slice(tensor * HEAD_DIM, (tensor + 1) * HEAD_DIM)


def rotate(values, cosv, sinv):
    first, second = values[:HALF], values[HALF:]
    return jnp.concatenate([first * cosv - second * sinv, second * cosv + first * sinv], axis=0)


def unrotate(values, cosv, sinv):
    first, second = values[:HALF], values[HALF:]
    return jnp.concatenate([first * cosv + second * sinv, second * cosv - first * sinv], axis=0)


def pack_kernel(closed, *refs):
    inputs, outs, held, turned, sems = refs[:4], refs[4:-3], refs[-3], refs[-2], refs[-1]
    copies = [
        pltpu.make_async_copy(source, held.at[number], sems.at[number])
        for number, source in enumerate(inputs)
    ]
    for copy in copies:
        copy.start()
    me = lax.rem(lax.axis_index("tok"), SPAN)
    steps = (
        [closed_step(slot) for slot in range(SPAN)]
        if closed
        else [0, *range(1, SPAN), *range(SPAN - 1, 0, -1)]
    )
    for number, copy in enumerate(copies):
        copy.wait()
        turned[number] = held[number].T
        for phase in range(OWN_HEADS):
            for slot, step in enumerate(steps):
                residue = me ^ step if closed else lax.rem(me + step, SPAN)
                begin = pl.multiple_of((phase * SPAN + residue) * HEAD_DIM, 16)
                outs[phase * len(steps) + slot][message_rows(number), :] = turned[
                    number, pl.ds(begin, HEAD_DIM), :
                ]


def tables_kernel(images, count, tokd, lengths, widths, table, inverse, bias, *refs):
    cos_out, sin_out, mask_out, bias_out, turned = refs
    me = lax.axis_index("tok")
    residue = lax.rem(me, SPAN)
    slots = table.shape[0]
    spot = lax.broadcasted_iota(jnp.int32, (HALF, tokd), 1)
    by_row = lax.broadcasted_iota(jnp.int32, (HALF, tokd), 0) < HALF // 2
    ids = []
    for slot in range(slots):
        block = table[slot, me]
        image, start = image_of(block, lengths, images)
        handled = (block >= 0) & (handler_of(start, residue, count) == me)
        ids.append(jnp.where(handled, image, -1 - slot))
        width = widths[0, image]
        bits = jnp.where(width == tokd, 0, jnp.where(width * 2 == tokd, 1, 2))
        shift = tokd.bit_length() - 1 - bits
        local = spot + (block - start) * tokd
        rowpos = lax.shift_right_logical(local, jnp.broadcast_to(shift, local.shape))
        colpos = local & (width - 1)
        angle = jnp.where(by_row, rowpos, colpos).astype(jnp.float32) * inverse[:, 0:1]
        cos_out[:, slot * tokd : (slot + 1) * tokd] = jnp.cos(angle)
        sin_out[:, slot * tokd : (slot + 1) * tokd] = jnp.sin(angle)
    for slot in range(slots):
        for other in range(slots):
            off = jnp.where(ids[slot] == ids[other], 0.0, NEG)
            row = slot * slots + other
            mask_out[row : row + 1, :] = jnp.full((1, tokd), off, jnp.float32)
        row = slots * slots + slot
        live = jnp.where(ids[slot] >= 0, 1.0, 0.0)
        mask_out[row : row + 1, :] = jnp.full((1, tokd), live, jnp.float32)
    plain = bias[...].astype(jnp.float32)
    rest = jnp.zeros((LANES - plain.shape[0], plain.shape[1]), jnp.float32)
    turned[...] = jnp.concatenate([plain, rest], axis=0).T
    for phase in range(OWN_HEADS):
        begin = pl.multiple_of((phase * SPAN + residue) * HEAD_DIM, 16)
        bias_out[phase * HEAD_DIM : (phase + 1) * HEAD_DIM, :] = turned[pl.ds(begin, HEAD_DIM), :]


def attend_kernel(slots, closed, tokd, head, factor, cosv, sinv, masks, bias, *refs):
    msgs, refs = refs[:slots], refs[slots:]
    earlier = ()
    if head > 0:
        before, earlier, refs = refs[0], refs[1:slots], refs[slots:]
    outs, sums = refs[:slots], refs[slots]
    for result, out in zip(earlier, [out for slot, out in enumerate(outs) if slot != EARLY]):
        done = head * 4 * HEAD_DIM
        out[:done, :] = result[:done, :]
    qt_all, kt_all, vt_all, gt_all, k_all, v_all, s_buf, e_buf, d_buf = refs[slots + 1 : slots + 10]
    own_bias = bias[head * HEAD_DIM : (head + 1) * HEAD_DIM, :]
    rest_row = lax.broadcasted_iota(jnp.int32, (LANES - HEAD_DIM, tokd), 0)
    zeros = jnp.zeros((LANES - HEAD_DIM, tokd), jnp.float32)
    ones = jnp.where(rest_row < 2, 1.0, 0.0)

    by_lanes = (((1,), (1,)), ((), ()))

    def off_row(slot, other):
        row = slot * slots + other
        return masks[row : row + 1, :]

    def live(slot, values):
        if closed:
            return values
        row = slots * slots + slot
        return values * masks[row : row + 1, :]

    def block_of(slot):
        return slice(slot * tokd, (slot + 1) * tokd)

    def put(slot, tensor, values):
        begin = ((0 if slot == EARLY else 4 * head) + tensor) * HEAD_DIM
        outs[slot][begin : begin + HEAD_DIM, :] = values

    def stage(slot):
        at = block_of(slot)
        cos_b, sin_b = cosv[:, at], sinv[:, at]
        query, key, value = (
            msgs[slot][message_rows(tensor), :].astype(jnp.float32)
            + own_bias[:, tensor : tensor + 1]
            for tensor in range(3)
        )
        query = rotate(query, cos_b, sin_b) * (SCALE * LOG2E)
        for values, rest, turned, plain in (
            (query, zeros, qt_all, None),
            (rotate(key, cos_b, sin_b), zeros, kt_all, k_all),
            (value, ones, vt_all, v_all),
        ):
            values = jnp.concatenate([values, rest], axis=0).astype(jnp.bfloat16)
            turned[:, at] = values
            if plain is not None:
                plain[at, :] = values.T

    def scores(slot, other):
        part = jnp.dot(
            k_all[block_of(other), :], qt_all[:, block_of(slot)], preferred_element_type=jnp.float32
        )
        s_buf[slot % 2, block_of(other), :] = part
        return jnp.max(part, axis=0, keepdims=True)

    def exponentials(slot, other, top):
        part = jnp.exp2(s_buf[slot % 2, block_of(other), :] - top)
        e_buf[block_of(other), block_of(slot)] = part.astype(jnp.bfloat16)

    def output(slot):
        mixed = jnp.dot(
            vt_all[:USED, :], e_buf[:, block_of(slot)], preferred_element_type=jnp.float32
        )
        inv = 1.0 / mixed[HEAD_DIM : HEAD_DIM + 1]
        out_b = (mixed[:HEAD_DIM] * inv).astype(jnp.bfloat16)
        put(slot, 0, out_b)
        grad = msgs[slot][message_rows(3), :].astype(jnp.float32)
        delta = jnp.sum(grad * out_b.astype(jnp.float32), axis=0, keepdims=True) * inv
        coarse = delta.astype(jnp.bfloat16).astype(jnp.float32)
        rest = jnp.where(rest_row == 0, -coarse, jnp.where(rest_row == 1, coarse - delta, 0.0))
        grad = jnp.concatenate([grad * inv, rest], axis=0).astype(jnp.bfloat16)
        gt_all[:, block_of(slot)] = grad
        spread = grad[:HEAD_DIM].astype(jnp.float32) * mixed[HEAD_DIM : HEAD_DIM + 1]
        return grad, live(slot, spread)

    def dscores(slot, other, grad):
        part = jnp.dot(v_all[block_of(other), :], grad, preferred_element_type=jnp.float32)
        d_buf[block_of(other), block_of(slot)] = (
            e_buf[block_of(other), block_of(slot)] * part.astype(jnp.bfloat16)
        )

    def query_part(slot):
        at = block_of(slot)
        dquery = jnp.dot(kt_all[:HEAD_DIM, :], d_buf[:, at], preferred_element_type=jnp.float32)
        dquery = unrotate(dquery * SCALE, cosv[:, at], sinv[:, at])
        put(slot, 1, dquery.astype(jnp.bfloat16))
        return live(slot, dquery)

    def value_part(slot):
        dvalue = lax.dot_general(
            gt_all[:HEAD_DIM, :],
            e_buf[block_of(slot), :],
            by_lanes,
            preferred_element_type=jnp.float32,
        )
        put(slot, 3, dvalue.astype(jnp.bfloat16))

    for slot in range(slots):
        stage(slot)
    dq_total = jnp.zeros((HEAD_DIM, tokd), jnp.float32)
    dv_total = jnp.zeros((HEAD_DIM, tokd), jnp.float32)
    grad = None
    offs = tops = None
    for step in range(slots + 2):
        ahead, slot, behind = step, step - 1, step - 2
        if 0 <= slot < slots:
            offs = [off_row(slot, other) for other in range(slots)]
            top = functools.reduce(jnp.maximum, [one + off for one, off in zip(tops, offs)])
        tops = []
        for other in range(slots):
            if ahead < slots:
                tops.append(scores(ahead, other))
            if 0 <= behind:
                dscores(behind, other, grad)
            if 0 <= slot < slots:
                exponentials(slot, other, top - offs[other])
        if 0 <= behind:
            dq_total = dq_total + query_part(behind)
        if 0 <= slot < slots:
            grad, spread = output(slot)
            dv_total = dv_total + spread
    dk_total = jnp.zeros((HEAD_DIM, tokd), jnp.float32)
    for slot in range(slots):
        at = block_of(slot)
        dkey = lax.dot_general(
            qt_all[:HEAD_DIM, :], d_buf[at, :], by_lanes, preferred_element_type=jnp.float32
        )
        dkey = unrotate(dkey * (1.0 / LOG2E), cosv[:, at], sinv[:, at])
        put(slot, 2, dkey.astype(jnp.bfloat16))
        dk_total = dk_total + live(slot, dkey)
    lane = lax.broadcasted_iota(jnp.int32, (HEAD_DIM, LANES), 1)
    columns = jnp.zeros((HEAD_DIM, LANES), jnp.float32)
    for number, total in enumerate((dq_total, dk_total, dv_total)):
        total = jnp.sum(total, axis=1, keepdims=True) * factor
        columns = jnp.where(lane == number, total, columns)
    columns = jnp.concatenate([columns, jnp.zeros((LANES - HEAD_DIM, LANES), jnp.float32)], axis=0)
    lines = columns.T
    copy = None
    if head + 1 < OWN_HEADS:
        sums[...] = lines[:8]
    else:
        tiles, sem = refs[slots + 10 :]
        tile = join_sums(before[...], lines)

        def repeat(device, carry):
            tiles[device] = tile
            return carry

        lax.fori_loop(0, tiles.shape[0], repeat, 0, unroll=min(32, tiles.shape[0]))
        copy = pltpu.make_async_copy(tiles, sums, sem)
        copy.start()
    for slot in range(slots):
        value_part(slot)
    if copy is not None:
        copy.wait()


FIT = LANES - HEAD_DIM
LEFT = HEAD_DIM - FIT


def join_sums(first, second):
    lane = lax.broadcasted_iota(jnp.int32, (1, LANES), 1)
    rows = []
    last = jnp.zeros((1, LANES), jnp.float32)
    for number in range(3):
        moved = pltpu.roll(second[number : number + 1], HEAD_DIM, 1)
        rows.append(jnp.where(lane < HEAD_DIM, first[number : number + 1], moved))
        rest = jnp.where(lane < LEFT, moved, 0.0)
        last = last + (pltpu.roll(rest, number * LEFT, 1) if number else rest)
    return jnp.concatenate(rows + [last], axis=0)


def unpack_kernel(slots, count, images, *refs):
    closed = is_closed(count)
    if not closed:
        lengths, table, *refs = refs
    msgs, refs = refs[: slots + OWN_HEADS - 1], refs[slots + OWN_HEADS - 1 :]
    tiles, *outs, bias_out, held, ready, sems = refs
    early, late = msgs[:OWN_HEADS], list(msgs[OWN_HEADS:])
    late.insert(EARLY, None)
    me = lax.axis_index("tok")

    def place(slot, residue):
        for phase in range(OWN_HEADS):
            begin = pl.multiple_of((phase * SPAN + residue) * HEAD_DIM, 16)
            for number in range(4):
                if slot == EARLY:
                    piece = early[phase][message_rows(number), :]
                else:
                    piece = late[slot][message_rows(4 * phase + number), :]
                held[number, pl.ds(begin, HEAD_DIM), :] = piece

    for slot in range(slots):
        if closed:
            place(slot, lax.rem(me, SPAN) ^ closed_step(slot))
        else:
            _, start = image_of(me, lengths, images)
            source = table[slot, me]
            residue = lax.rem(source + SPAN, SPAN)
            chosen = (source >= 0) & (source == handler_of(start, residue, count))
            pl.when(chosen)(functools.partial(place, slot, residue))
    copies = []
    for number, out in enumerate(outs):
        ready[number] = held[number].T
        copies.append(pltpu.make_async_copy(ready.at[number], out, sems.at[number]))
        copies[-1].start()
    sum_tiles(tiles, bias_out)
    for copy in copies:
        copy.wait()


def sum_tiles(tiles, bias_out):
    def add(group, totals):
        return tuple(
            total + tiles[group * SPAN + residue] for residue, total in enumerate(totals)
        )

    groups = tiles.shape[0] // SPAN
    zero = jnp.zeros(tiles.shape[1:], jnp.float32)
    totals = lax.fori_loop(0, groups, add, (zero,) * SPAN, unroll=groups <= 8)
    for residue, total in enumerate(totals):
        first = residue * HEAD_DIM
        second = (SPAN + residue) * HEAD_DIM
        for number in range(3):
            row = slice(number, number + 1)
            bias_out[row, first : first + HEAD_DIM] = total[row, :HEAD_DIM]
            bias_out[row, second : second + FIT] = total[row, HEAD_DIM:]
            bias_out[row, second + FIT : second + HEAD_DIM] = total[
                3:4, number * LEFT : (number + 1) * LEFT
            ]


def on_device(query_in, key_in, value_in, out_grad, bias, lengths, widths):
    tokd = query_in.shape[1]
    model = query_in.shape[2]
    images = lengths.shape[1]
    count = lax.axis_size("tok")
    dp_size = lax.axis_size("dp")
    closed = is_closed(count)
    sources, targets = trade_tables(count)
    slots = sources.shape[0]
    span = slots * tokd
    table = jnp.asarray(sources)
    quarter = HEAD_DIM // 4
    inverse = rope_base ** (-np.arange(quarter, dtype=np.float64) / quarter)
    inverse = jnp.asarray(np.tile(np.tile(inverse, 2)[:, None], (1, LANES)), jnp.float32)
    smem = pl.BlockSpec(memory_space=pltpu.SMEM)
    vmem = pl.BlockSpec(memory_space=pltpu.VMEM)
    hbm = pl.BlockSpec(memory_space=pltpu.HBM)
    whole = jax.ShapeDtypeStruct((tokd, model), jnp.bfloat16)
    message = jax.ShapeDtypeStruct((4 * HEAD_DIM, tokd), jnp.bfloat16)
    joined = jax.ShapeDtypeStruct((OWN_HEADS * 4 * HEAD_DIM, tokd), jnp.bfloat16)
    devices = dp_size * count
    tokens_all = devices * tokd

    def params(mib):
        return pltpu.CompilerParams(vmem_limit_bytes=int(mib * 1024 * 1024))

    inputs = (query_in[0], key_in[0], value_in[0], out_grad[0])
    sends = pl.pallas_call(
        functools.partial(pack_kernel, closed),
        out_shape=[message] * (OWN_HEADS * slots),
        in_specs=[hbm] * 4,
        out_specs=[vmem] * (OWN_HEADS * slots),
        scratch_shapes=[
            pltpu.VMEM((4, tokd, model), jnp.bfloat16),
            pltpu.VMEM((4, model, tokd), jnp.bfloat16),
            pltpu.SemaphoreType.DMA((4,)),
        ],
        compiler_params=params(PACK_KIB / 1024),
        name="pack_heads",
    )(*inputs)
    got = [trade(sends[:slots])]
    table_shape = jax.ShapeDtypeStruct((HALF, span), jnp.float32)
    mask_rows = -(-slots * (slots + 1) // 8) * 8
    tables = pl.pallas_call(
        functools.partial(tables_kernel, images, count, tokd),
        out_shape=[table_shape] * 2
        + [
            jax.ShapeDtypeStruct((mask_rows, tokd), jnp.float32),
            jax.ShapeDtypeStruct((OWN_HEADS * HEAD_DIM, LANES), jnp.float32),
        ],
        in_specs=[smem, smem, smem, vmem, vmem],
        out_specs=[vmem] * 4,
        scratch_shapes=[pltpu.VMEM((model, LANES), jnp.float32)],
        compiler_params=params(16),
        cost_estimate=pl.CostEstimate(
            flops=span * LANES * 200, bytes_accessed=0, transcendentals=0
        ),
        name="rotary_tables",
    )(lengths, widths, table, inverse, bias)
    tables, sends = lax.optimization_barrier((tables, sends[slots:]))
    for phase in range(1, OWN_HEADS):
        got.append(trade(sends[(phase - 1) * slots : phase * slots]))
    early = []
    carried = []
    for phase in range(OWN_HEADS):
        last = phase + 1 == OWN_HEADS
        kept = [slot for slot in range(slots) if slot != EARLY]
        sums_shape = jax.ShapeDtypeStruct(
            (devices, 4, LANES) if last else (8, LANES), jnp.float32
        )
        *results, total = pl.pallas_call(
            functools.partial(
                attend_kernel, slots, closed, tokd, phase, 1.0 / tokens_all**0.5
            ),
            out_shape=[message if slot == EARLY else joined for slot in range(slots)]
            + [sums_shape],
            in_specs=[vmem] * (4 + slots + len(carried)),
            out_specs=[vmem] * slots + [hbm if last else vmem],
            scratch_shapes=[pltpu.VMEM((LANES, span), jnp.bfloat16)] * 4
            + [pltpu.VMEM((span, LANES), jnp.bfloat16)] * 2
            + [pltpu.VMEM((2, span, tokd), jnp.float32)]
            + [pltpu.VMEM((span, span), jnp.bfloat16)] * 2
            + (
                [pltpu.VMEM(sums_shape.shape, jnp.float32), pltpu.SemaphoreType.DMA(())]
                if last
                else []
            ),
            compiler_params=params(32),
            cost_estimate=pl.CostEstimate(
                flops=12 * span * span * 256, bytes_accessed=0, transcendentals=0
            ),
            name="attend_head",
        )(*tables, *got[phase], *carried)
        results, total, early = lax.optimization_barrier((results, total, early))
        early.append(send_back(results[EARLY], EARLY))
        carried = [total] + [results[slot] for slot in kept]
    tiles = lax.all_to_all(total, ("dp", "tok"), 0, 0, tiled=True)
    late = [send_back(results[slot], slot) for slot in kept]
    places = [] if closed else [lengths, jnp.asarray(targets)]
    *outs, bias_grad = pl.pallas_call(
        functools.partial(unpack_kernel, slots, count, images),
        out_shape=[whole] * 4 + [jax.ShapeDtypeStruct((3, model), jnp.float32)],
        in_specs=[smem] * len(places) + [vmem] * (OWN_HEADS + len(late) + 1),
        out_specs=[hbm] * 4 + [vmem],
        scratch_shapes=[
            pltpu.VMEM((4, model, tokd), jnp.bfloat16),
            pltpu.VMEM((4, tokd, model), jnp.bfloat16),
            pltpu.SemaphoreType.DMA((4,)),
        ],
        compiler_params=params(16),
        name="unpack_heads",
    )(*places, *early, *late, tiles)
    return tuple(out[None] for out in outs) + (bias_grad,)


def solution(mesh):
    in_specs = (
        P("dp", "tok", None),
        P("dp", "tok", None),
        P("dp", "tok", None),
        P("dp", "tok", None),
        P(),
        P("dp", None),
        P("dp", None),
    )
    out_specs = (
        P("dp", "tok", None),
        P("dp", "tok", None),
        P("dp", "tok", None),
        P("dp", "tok", None),
        P(),
    )
    return jax.shard_map(
        on_device, mesh=mesh, in_specs=in_specs, out_specs=out_specs, check_vma=False
    )
```

```python
import functools

import jax
import jax.numpy as jnp
import numpy as np
from jax import lax
from jax.experimental import pallas as pl
from jax.experimental.pallas import tpu as pltpu
from jax.sharding import PartitionSpec as P

HEADS = 8
HEAD_DIM = 80
SPAN = 4
OWN_HEADS = HEADS // SPAN
PART = OWN_HEADS * HEAD_DIM
SCALE = HEAD_DIM**-0.5
LOG2E = 1.4426950408889634
NEG = -1e30
LANES = 128
USED = HEAD_DIM + 16
HALF = HEAD_DIM // 2
PACK_KIB = 52 * 1024 + 600

rope_base = 10000.0


def is_closed(count):
    return count in (SPAN, 2 * SPAN)


def closed_step(slot):
    return (SPAN - slot) % SPAN


def trade_rounds(count):
    if is_closed(count):
        return [
            [(one, one ^ closed_step(slot)) for one in range(count)] for slot in range(1, SPAN)
        ]
    rounds = []
    for shift in [*range(1, SPAN), *range(-1, -SPAN, -1)]:
        rounds.append(
            [
                (source, source + shift)
                for source in range(max(0, -shift), min(count, count - shift))
                if (source < SPAN) == (source + shift < SPAN)
            ]
        )
    return rounds


def trade_tables(count):
    rounds = trade_rounds(count)
    sources = np.full((1 + len(rounds), count), -1, np.int32)
    targets = sources.copy()
    sources[0] = targets[0] = np.arange(count)
    for slot, pairs in enumerate(rounds, 1):
        for source, target in pairs:
            sources[slot, target] = source
            targets[slot, source] = target
    return sources, targets


def send_back(result, slot):
    if slot == 0:
        return result
    pairs = trade_rounds(lax.axis_size("tok"))[slot - 1]
    return lax.ppermute(result, "tok", [(target, source) for source, target in pairs])


EARLY = 1


def image_of(block, lengths, images):
    image = jnp.int32(0)
    start = jnp.int32(0)
    begin = jnp.int32(0)
    for number in range(images):
        size = lengths[0, number]
        inside = (block >= begin) & (block < begin + size)
        image = jnp.where(inside, number, image)
        start = jnp.where(inside, begin, start)
        begin = begin + size
    return image, start


def handler_of(start, residue, count):
    device = start + lax.rem(residue - lax.rem(start, SPAN) + SPAN, SPAN)
    return jnp.where(device >= count, device - SPAN, device)


def message_rows(tensor):
    return slice(tensor * HEAD_DIM, (tensor + 1) * HEAD_DIM)


def rotate(values, cosv, sinv):
    first, second = values[:HALF], values[HALF:]
    return jnp.concatenate([first * cosv - second * sinv, second * cosv + first * sinv], axis=0)


def unrotate(values, cosv, sinv):
    first, second = values[:HALF], values[HALF:]
    return jnp.concatenate([first * cosv + second * sinv, second * cosv - first * sinv], axis=0)


def pack_kernel(closed, *refs):
    inputs, outs, held, turned, sems = refs[:4], refs[4:-3], refs[-3], refs[-2], refs[-1]
    copies = [
        pltpu.make_async_copy(source, held.at[number], sems.at[number])
        for number, source in enumerate(inputs)
    ]
    for copy in copies:
        copy.start()
    me = lax.rem(lax.axis_index("tok"), SPAN)
    steps = (
        [closed_step(slot) for slot in range(SPAN)]
        if closed
        else [0, *range(1, SPAN), *range(SPAN - 1, 0, -1)]
    )
    for number, copy in enumerate(copies):
        copy.wait()
        turned[number] = held[number].T
        for phase in range(OWN_HEADS):
            for slot, step in enumerate(steps):
                residue = me ^ step if closed else lax.rem(me + step, SPAN)
                begin = pl.multiple_of((phase * SPAN + residue) * HEAD_DIM, 16)
                outs[phase * len(steps) + slot][message_rows(number), :] = turned[
                    number, pl.ds(begin, HEAD_DIM), :
                ]


def tables_kernel(images, count, tokd, lengths, widths, table, inverse, bias, *refs):
    cos_out, sin_out, mask_out, bias_out, turned = refs
    me = lax.axis_index("tok")
    residue = lax.rem(me, SPAN)
    slots = table.shape[0]
    spot = lax.broadcasted_iota(jnp.int32, (HALF, tokd), 1)
    by_row = lax.broadcasted_iota(jnp.int32, (HALF, tokd), 0) < HALF // 2
    ids = []
    for slot in range(slots):
        block = table[slot, me]
        image, start = image_of(block, lengths, images)
        handled = (block >= 0) & (handler_of(start, residue, count) == me)
        ids.append(jnp.where(handled, image, -1 - slot))
        width = widths[0, image]
        bits = jnp.where(width == tokd, 0, jnp.where(width * 2 == tokd, 1, 2))
        shift = tokd.bit_length() - 1 - bits
        local = spot + (block - start) * tokd
        rowpos = lax.shift_right_logical(local, jnp.broadcast_to(shift, local.shape))
        colpos = local & (width - 1)
        angle = jnp.where(by_row, rowpos, colpos).astype(jnp.float32) * inverse[:, 0:1]
        cos_out[:, slot * tokd : (slot + 1) * tokd] = jnp.cos(angle)
        sin_out[:, slot * tokd : (slot + 1) * tokd] = jnp.sin(angle)
    for slot in range(slots):
        for other in range(slots):
            off = jnp.where(ids[slot] == ids[other], 0.0, NEG)
            row = slot * slots + other
            mask_out[row : row + 1, :] = jnp.full((1, tokd), off, jnp.float32)
        row = slots * slots + slot
        live = jnp.where(ids[slot] >= 0, 1.0, 0.0)
        mask_out[row : row + 1, :] = jnp.full((1, tokd), live, jnp.float32)
    plain = bias[...].astype(jnp.float32)
    rest = jnp.zeros((LANES - plain.shape[0], plain.shape[1]), jnp.float32)
    turned[...] = jnp.concatenate([plain, rest], axis=0).T
    for phase in range(OWN_HEADS):
        begin = pl.multiple_of((phase * SPAN + residue) * HEAD_DIM, 16)
        bias_out[phase * HEAD_DIM : (phase + 1) * HEAD_DIM, :] = turned[pl.ds(begin, HEAD_DIM), :]


def stage(slot, tokd, message, cosv, sinv, bias):
    at = slice(slot * tokd, (slot + 1) * tokd)
    cos_b, sin_b = cosv[:, at], sinv[:, at]
    query, key, value = (
        message[message_rows(tensor), :].astype(jnp.float32) + bias[:, tensor : tensor + 1]
        for tensor in range(3)
    )
    rest_row = lax.broadcasted_iota(jnp.int32, (LANES - HEAD_DIM, tokd), 0)
    zeros = jnp.zeros((LANES - HEAD_DIM, tokd), jnp.float32)
    ones = jnp.where(rest_row < 2, 1.0, 0.0)
    return [
        jnp.concatenate(pair, axis=0).astype(jnp.bfloat16)
        for pair in (
            (rotate(query, cos_b, sin_b) * (SCALE * LOG2E), zeros),
            (rotate(key, cos_b, sin_b), zeros),
            (value, ones),
        )
    ]


def stage_kernel(slot, phases, tokd, cosv, sinv, bias, *refs):
    count = len(phases)
    msgs, turned, plain = refs[:count], refs[count : 2 * count], refs[2 * count :]
    for number, phase in enumerate(phases):
        own_bias = bias[phase * HEAD_DIM : (phase + 1) * HEAD_DIM, :]
        values = stage(slot, tokd, msgs[number], cosv, sinv, own_bias)
        for tensor, value in enumerate(values):
            turned[number][tensor] = value
            if tensor > 0:
                plain[number][tensor - 1] = value.T


def attend_kernel(slots, staged, closed, tokd, head, factor, cosv, sinv, masks, bias, *refs):
    msgs, refs = refs[:slots], refs[slots:]
    ready = {slot: refs[2 * at : 2 * at + 2] for at, slot in enumerate(staged)}
    refs = refs[2 * len(staged) :]
    earlier = ()
    if head > 0:
        before, earlier, refs = refs[0], refs[1:slots], refs[slots:]
    outs, sums = refs[:slots], refs[slots]
    for result, out in zip(earlier, [out for slot, out in enumerate(outs) if slot != EARLY]):
        done = head * 4 * HEAD_DIM
        out[:done, :] = result[:done, :]
    qt_all, kt_all, vt_all, gt_all, k_all, v_all, s_buf, e_buf, d_buf = refs[slots + 1 : slots + 10]
    own_bias = bias[head * HEAD_DIM : (head + 1) * HEAD_DIM, :]
    rest_row = lax.broadcasted_iota(jnp.int32, (LANES - HEAD_DIM, tokd), 0)

    by_lanes = (((1,), (1,)), ((), ()))

    def off_row(slot, other):
        row = slot * slots + other
        return masks[row : row + 1, :]

    def live(slot, values):
        if closed:
            return values
        row = slots * slots + slot
        return values * masks[row : row + 1, :]

    def block_of(slot):
        return slice(slot * tokd, (slot + 1) * tokd)

    def put(slot, tensor, values):
        begin = ((0 if slot == EARLY else 4 * head) + tensor) * HEAD_DIM
        outs[slot][begin : begin + HEAD_DIM, :] = values

    def scores(slot, other):
        part = jnp.dot(
            k_all[block_of(other), :], qt_all[:, block_of(slot)], preferred_element_type=jnp.float32
        )
        s_buf[slot % 2, block_of(other), :] = part
        return jnp.max(part, axis=0, keepdims=True)

    def exponentials(slot, other, top):
        part = jnp.exp2(s_buf[slot % 2, block_of(other), :] - top)
        e_buf[block_of(other), block_of(slot)] = part.astype(jnp.bfloat16)

    def output(slot):
        mixed = jnp.dot(
            vt_all[:USED, :], e_buf[:, block_of(slot)], preferred_element_type=jnp.float32
        )
        inv = 1.0 / mixed[HEAD_DIM : HEAD_DIM + 1]
        out_b = (mixed[:HEAD_DIM] * inv).astype(jnp.bfloat16)
        put(slot, 0, out_b)
        grad = msgs[slot][message_rows(3), :].astype(jnp.float32)
        delta = jnp.sum(grad * out_b.astype(jnp.float32), axis=0, keepdims=True) * inv
        coarse = delta.astype(jnp.bfloat16).astype(jnp.float32)
        rest = jnp.where(rest_row == 0, -coarse, jnp.where(rest_row == 1, coarse - delta, 0.0))
        grad = jnp.concatenate([grad * inv, rest], axis=0).astype(jnp.bfloat16)
        gt_all[:, block_of(slot)] = grad
        spread = grad[:HEAD_DIM].astype(jnp.float32) * mixed[HEAD_DIM : HEAD_DIM + 1]
        return grad, live(slot, spread)

    def dscores(slot, other, grad):
        part = jnp.dot(v_all[block_of(other), :], grad, preferred_element_type=jnp.float32)
        d_buf[block_of(other), block_of(slot)] = (
            e_buf[block_of(other), block_of(slot)] * part.astype(jnp.bfloat16)
        )

    def query_part(slot):
        at = block_of(slot)
        dquery = jnp.dot(kt_all[:HEAD_DIM, :], d_buf[:, at], preferred_element_type=jnp.float32)
        dquery = unrotate(dquery * SCALE, cosv[:, at], sinv[:, at])
        put(slot, 1, dquery.astype(jnp.bfloat16))
        return live(slot, dquery)

    def value_part(slot):
        dvalue = lax.dot_general(
            gt_all[:HEAD_DIM, :],
            e_buf[block_of(slot), :],
            by_lanes,
            preferred_element_type=jnp.float32,
        )
        put(slot, 3, dvalue.astype(jnp.bfloat16))

    for slot in range(slots):
        at = block_of(slot)
        if slot in ready:
            turned, plain = ready[slot]
            values, natural = [turned[number] for number in range(3)], [plain[0], plain[1]]
        else:
            values = stage(slot, tokd, msgs[slot], cosv, sinv, own_bias)
            natural = [value.T for value in values[1:]]
        qt_all[:, at], kt_all[:, at], vt_all[:, at] = values
        k_all[at, :], v_all[at, :] = natural
    dq_total = jnp.zeros((HEAD_DIM, tokd), jnp.float32)
    dv_total = jnp.zeros((HEAD_DIM, tokd), jnp.float32)
    grad = None
    offs = tops = None
    for step in range(slots + 2):
        ahead, slot, behind = step, step - 1, step - 2
        if 0 <= slot < slots:
            offs = [off_row(slot, other) for other in range(slots)]
            top = functools.reduce(jnp.maximum, [one + off for one, off in zip(tops, offs)])
        tops = []
        for other in range(slots):
            if ahead < slots:
                tops.append(scores(ahead, other))
            if 0 <= behind:
                dscores(behind, other, grad)
            if 0 <= slot < slots:
                exponentials(slot, other, top - offs[other])
        if 0 <= behind:
            dq_total = dq_total + query_part(behind)
        if 0 <= slot < slots:
            grad, spread = output(slot)
            dv_total = dv_total + spread
    dk_total = jnp.zeros((HEAD_DIM, tokd), jnp.float32)
    for slot in range(slots):
        at = block_of(slot)
        dkey = lax.dot_general(
            qt_all[:HEAD_DIM, :], d_buf[at, :], by_lanes, preferred_element_type=jnp.float32
        )
        dkey = unrotate(dkey * (1.0 / LOG2E), cosv[:, at], sinv[:, at])
        put(slot, 2, dkey.astype(jnp.bfloat16))
        dk_total = dk_total + live(slot, dkey)
    lane = lax.broadcasted_iota(jnp.int32, (HEAD_DIM, LANES), 1)
    columns = jnp.zeros((HEAD_DIM, LANES), jnp.float32)
    for number, total in enumerate((dq_total, dk_total, dv_total)):
        total = jnp.sum(total, axis=1, keepdims=True) * factor
        columns = jnp.where(lane == number, total, columns)
    columns = jnp.concatenate([columns, jnp.zeros((LANES - HEAD_DIM, LANES), jnp.float32)], axis=0)
    lines = columns.T
    copy = None
    if head + 1 < OWN_HEADS:
        sums[...] = lines[:8]
    else:
        tiles, sem = refs[slots + 10 :]
        tile = join_sums(before[...], lines)

        def repeat(device, carry):
            tiles[device] = tile
            return carry

        lax.fori_loop(0, tiles.shape[0], repeat, 0, unroll=min(32, tiles.shape[0]))
        copy = pltpu.make_async_copy(tiles, sums, sem)
        copy.start()
    for slot in range(slots):
        value_part(slot)
    if copy is not None:
        copy.wait()


FIT = LANES - HEAD_DIM
LEFT = HEAD_DIM - FIT


def join_sums(first, second):
    lane = lax.broadcasted_iota(jnp.int32, (1, LANES), 1)
    rows = []
    last = jnp.zeros((1, LANES), jnp.float32)
    for number in range(3):
        moved = pltpu.roll(second[number : number + 1], HEAD_DIM, 1)
        rows.append(jnp.where(lane < HEAD_DIM, first[number : number + 1], moved))
        rest = jnp.where(lane < LEFT, moved, 0.0)
        last = last + (pltpu.roll(rest, number * LEFT, 1) if number else rest)
    return jnp.concatenate(rows + [last, jnp.zeros((4, LANES), jnp.float32)], axis=0)


def unpack_kernel(slots, count, images, *refs):
    closed = is_closed(count)
    if not closed:
        lengths, table, *refs = refs
    msgs, refs = refs[: slots + OWN_HEADS - 1], refs[slots + OWN_HEADS - 1 :]
    *outs, held, ready, sems = refs
    early, late = msgs[:OWN_HEADS], list(msgs[OWN_HEADS:])
    late.insert(EARLY, None)
    me = lax.axis_index("tok")

    def place(slot, residue):
        for phase in range(OWN_HEADS):
            begin = pl.multiple_of((phase * SPAN + residue) * HEAD_DIM, 16)
            for number in range(4):
                if slot == EARLY:
                    piece = early[phase][message_rows(number), :]
                else:
                    piece = late[slot][message_rows(4 * phase + number), :]
                held[number, pl.ds(begin, HEAD_DIM), :] = piece

    for slot in range(slots):
        if closed:
            place(slot, lax.rem(me, SPAN) ^ closed_step(slot))
        else:
            _, start = image_of(me, lengths, images)
            source = table[slot, me]
            residue = lax.rem(source + SPAN, SPAN)
            chosen = (source >= 0) & (source == handler_of(start, residue, count))
            pl.when(chosen)(functools.partial(place, slot, residue))
    copies = []
    for number, out in enumerate(outs):
        ready[number] = held[number].T
        copies.append(pltpu.make_async_copy(ready.at[number], out, sems.at[number]))
        copies[-1].start()
    for copy in copies:
        copy.wait()


def bias_kernel(tiles, bias_out):
    def add(group, totals):
        return tuple(
            total + tiles[group * SPAN + residue] for residue, total in enumerate(totals)
        )

    groups = tiles.shape[0] // SPAN
    zero = jnp.zeros(tiles.shape[1:], jnp.float32)
    totals = lax.fori_loop(0, groups, add, (zero,) * SPAN, unroll=groups <= 8)
    for residue, total in enumerate(totals):
        first = residue * HEAD_DIM
        second = (SPAN + residue) * HEAD_DIM
        for number in range(3):
            row = slice(number, number + 1)
            bias_out[row, first : first + HEAD_DIM] = total[row, :HEAD_DIM]
            bias_out[row, second : second + FIT] = total[row, HEAD_DIM:]
            bias_out[row, second + FIT : second + HEAD_DIM] = total[
                3:4, number * LEFT : (number + 1) * LEFT
            ]


def on_device(query_in, key_in, value_in, out_grad, bias, lengths, widths):
    tokd = query_in.shape[1]
    model = query_in.shape[2]
    images = lengths.shape[1]
    count = lax.axis_size("tok")
    dp_size = lax.axis_size("dp")
    closed = is_closed(count)
    sources, targets = trade_tables(count)
    slots = sources.shape[0]
    span = slots * tokd
    table = jnp.asarray(sources)
    quarter = HEAD_DIM // 4
    inverse = rope_base ** (-np.arange(quarter, dtype=np.float64) / quarter)
    inverse = jnp.asarray(np.tile(np.tile(inverse, 2)[:, None], (1, LANES)), jnp.float32)
    smem = pl.BlockSpec(memory_space=pltpu.SMEM)
    vmem = pl.BlockSpec(memory_space=pltpu.VMEM)
    hbm = pl.BlockSpec(memory_space=pltpu.HBM)
    whole = jax.ShapeDtypeStruct((tokd, model), jnp.bfloat16)
    message = jax.ShapeDtypeStruct((4 * HEAD_DIM, tokd), jnp.bfloat16)
    joined = jax.ShapeDtypeStruct((OWN_HEADS * 4 * HEAD_DIM, tokd), jnp.bfloat16)
    devices = dp_size * count
    tokens_all = devices * tokd

    def params(mib):
        return pltpu.CompilerParams(vmem_limit_bytes=int(mib * 1024 * 1024))

    inputs = (query_in[0], key_in[0], value_in[0], out_grad[0])
    sends = pl.pallas_call(
        functools.partial(pack_kernel, closed),
        out_shape=[message] * (OWN_HEADS * slots),
        in_specs=[hbm] * 4,
        out_specs=[vmem] * (OWN_HEADS * slots),
        scratch_shapes=[
            pltpu.VMEM((4, tokd, model), jnp.bfloat16),
            pltpu.VMEM((4, model, tokd), jnp.bfloat16),
            pltpu.SemaphoreType.DMA((4,)),
        ],
        compiler_params=params(PACK_KIB / 1024),
        name="pack_heads",
    )(*inputs)
    rounds = trade_rounds(count)
    first = [sends[0]] + [
        lax.ppermute(send, "tok", pairs) for send, pairs in zip(sends[1:slots], rounds)
    ]
    table_shape = jax.ShapeDtypeStruct((HALF, span), jnp.float32)
    mask_rows = -(-slots * (slots + 1) // 8) * 8
    tables = pl.pallas_call(
        functools.partial(tables_kernel, images, count, tokd),
        out_shape=[table_shape] * 2
        + [
            jax.ShapeDtypeStruct((mask_rows, tokd), jnp.float32),
            jax.ShapeDtypeStruct((OWN_HEADS * HEAD_DIM, LANES), jnp.float32),
        ],
        in_specs=[smem, smem, smem, vmem, vmem],
        out_specs=[vmem] * 4,
        scratch_shapes=[pltpu.VMEM((model, LANES), jnp.float32)],
        compiler_params=params(16),
        cost_estimate=pl.CostEstimate(
            flops=span * LANES * 200, bytes_accessed=0, transcendentals=0
        ),
        name="rotary_tables",
    )(lengths, widths, table, inverse, bias)

    def stage_ahead(slot, phases, messages):
        number = len(phases)
        results = pl.pallas_call(
            functools.partial(stage_kernel, slot, phases, tokd),
            out_shape=[jax.ShapeDtypeStruct((3, LANES, tokd), jnp.bfloat16)] * number
            + [jax.ShapeDtypeStruct((2, tokd, LANES), jnp.bfloat16)] * number,
            in_specs=[vmem] * (3 + number),
            out_specs=[vmem] * (2 * number),
            compiler_params=params(16),
            cost_estimate=pl.CostEstimate(
                flops=1_000_000 * number, bytes_accessed=0, transcendentals=0
            ),
            name="stage_slot",
        )(tables[0], tables[1], tables[3], *messages)
        return [list(pair) for pair in zip(results[:number], results[number:])]

    phases = tuple(range(OWN_HEADS))
    own = stage_ahead(0, phases, [sends[phase * slots] for phase in phases])
    staged = [{0: pair} for pair in own]
    got = [first] + [[sends[phase * slots]] for phase in phases[1:]]
    latest = own
    for slot in range(1, slots):
        for phase in phases[1:]:
            send, latest = lax.optimization_barrier((sends[phase * slots + slot], latest))
            got[phase].append(lax.ppermute(send, "tok", rounds[slot - 1]))
        if slot == 1:
            staged[0][0], staged[1][0] = latest
        else:
            staged[0][slot - 1] = latest[0]
        if slot + 1 < slots:
            latest = stage_ahead(slot, (0,), [first[slot]])
    early = []
    carried = []
    for phase in range(OWN_HEADS):
        last = phase + 1 == OWN_HEADS
        kept = [slot for slot in range(slots) if slot != EARLY]
        sums_shape = jax.ShapeDtypeStruct(
            (devices, 8, LANES) if last else (8, LANES), jnp.float32
        )
        *results, total = pl.pallas_call(
            functools.partial(
                attend_kernel,
                slots,
                tuple(staged[phase]),
                closed,
                tokd,
                phase,
                1.0 / tokens_all**0.5,
            ),
            out_shape=[message if slot == EARLY else joined for slot in range(slots)]
            + [sums_shape],
            in_specs=[vmem] * (4 + slots + 2 * len(staged[phase]) + len(carried)),
            out_specs=[vmem] * slots + [hbm if last else vmem],
            scratch_shapes=[pltpu.VMEM((LANES, span), jnp.bfloat16)] * 4
            + [pltpu.VMEM((span, LANES), jnp.bfloat16)] * 2
            + [pltpu.VMEM((2, span, tokd), jnp.float32)]
            + [pltpu.VMEM((span, span), jnp.bfloat16)] * 2
            + (
                [pltpu.VMEM(sums_shape.shape, jnp.float32), pltpu.SemaphoreType.DMA(())]
                if last
                else []
            ),
            compiler_params=params(32),
            cost_estimate=pl.CostEstimate(
                flops=12 * span * span * 256, bytes_accessed=0, transcendentals=0
            ),
            name="attend_head",
        )(*tables, *got[phase], *(one for pair in staged[phase].values() for one in pair), *carried)
        results, total, early = lax.optimization_barrier((results, total, early))
        early.append(send_back(results[EARLY], EARLY))
        carried = [total] + [results[slot] for slot in kept]
    tiles = lax.all_to_all(total, ("dp", "tok"), 0, 0, tiled=True)
    late = [send_back(results[slot], slot) for slot in kept]
    places = [] if closed else [lengths, jnp.asarray(targets)]
    outs = pl.pallas_call(
        functools.partial(unpack_kernel, slots, count, images),
        out_shape=[whole] * 4,
        in_specs=[smem] * len(places) + [vmem] * (OWN_HEADS + len(late)),
        out_specs=[hbm] * 4,
        scratch_shapes=[
            pltpu.VMEM((4, model, tokd), jnp.bfloat16),
            pltpu.VMEM((4, tokd, model), jnp.bfloat16),
            pltpu.SemaphoreType.DMA((4,)),
        ],
        compiler_params=params(16),
        name="unpack_heads",
    )(*places, *early, *late)
    outs, tiles = lax.optimization_barrier((outs, tiles))
    bias_grad = pl.pallas_call(
        bias_kernel,
        out_shape=jax.ShapeDtypeStruct((3, model), jnp.float32),
        in_specs=[vmem],
        out_specs=vmem,
        compiler_params=params(16),
        name="bias_sums",
    )(tiles)
    return tuple(out[None] for out in outs) + (bias_grad,)


def solution(mesh):
    in_specs = (
        P("dp", "tok", None),
        P("dp", "tok", None),
        P("dp", "tok", None),
        P("dp", "tok", None),
        P(),
        P("dp", None),
        P("dp", None),
    )
    out_specs = (
        P("dp", "tok", None),
        P("dp", "tok", None),
        P("dp", "tok", None),
        P("dp", "tok", None),
        P(),
    )
    return jax.shard_map(
        on_device, mesh=mesh, in_specs=in_specs, out_specs=out_specs, check_vma=False
    )
```

```python
import functools

import jax
import jax.numpy as jnp
import numpy as np
from jax import lax
from jax.experimental import pallas as pl
from jax.experimental.pallas import tpu as pltpu
from jax.sharding import PartitionSpec as P

HEADS = 8
HEAD_DIM = 80
SPAN = 4
OWN_HEADS = HEADS // SPAN
PART = OWN_HEADS * HEAD_DIM
SCALE = HEAD_DIM**-0.5
LOG2E = 1.4426950408889634
NEG = -1e30
LANES = 128
USED = HEAD_DIM + 16
HALF = HEAD_DIM // 2
PACK_KIB = 52 * 1024 + 600
UNPACK_FLOPS = 20_000_000_000

rope_base = 10000.0


def is_closed(count):
    return count in (SPAN, 2 * SPAN)


def closed_step(slot):
    return (SPAN - slot) % SPAN


def trade_rounds(count):
    if is_closed(count):
        return [
            [(one, one ^ closed_step(slot)) for one in range(count)] for slot in range(1, SPAN)
        ]
    rounds = []
    for shift in [*range(1, SPAN), *range(-1, -SPAN, -1)]:
        rounds.append(
            [
                (source, source + shift)
                for source in range(max(0, -shift), min(count, count - shift))
                if (source < SPAN) == (source + shift < SPAN)
            ]
        )
    return rounds


def trade_tables(count):
    rounds = trade_rounds(count)
    sources = np.full((1 + len(rounds), count), -1, np.int32)
    targets = sources.copy()
    sources[0] = targets[0] = np.arange(count)
    for slot, pairs in enumerate(rounds, 1):
        for source, target in pairs:
            sources[slot, target] = source
            targets[slot, source] = target
    return sources, targets


def send_back(result, slot):
    if slot == 0:
        return result
    pairs = trade_rounds(lax.axis_size("tok"))[slot - 1]
    return lax.ppermute(result, "tok", [(target, source) for source, target in pairs])


EARLY = 1


def image_of(block, lengths, images):
    image = jnp.int32(0)
    start = jnp.int32(0)
    begin = jnp.int32(0)
    for number in range(images):
        size = lengths[0, number]
        inside = (block >= begin) & (block < begin + size)
        image = jnp.where(inside, number, image)
        start = jnp.where(inside, begin, start)
        begin = begin + size
    return image, start


def handler_of(start, residue, count):
    device = start + lax.rem(residue - lax.rem(start, SPAN) + SPAN, SPAN)
    return jnp.where(device >= count, device - SPAN, device)


def message_rows(tensor):
    return slice(tensor * HEAD_DIM, (tensor + 1) * HEAD_DIM)


def rotate(values, cosv, sinv):
    first, second = values[:HALF], values[HALF:]
    return jnp.concatenate([first * cosv - second * sinv, second * cosv + first * sinv], axis=0)


def unrotate(values, cosv, sinv):
    first, second = values[:HALF], values[HALF:]
    return jnp.concatenate([first * cosv + second * sinv, second * cosv - first * sinv], axis=0)


def pack_kernel(closed, *refs):
    inputs, outs, held, turned, sems = refs[:4], refs[4:-3], refs[-3], refs[-2], refs[-1]
    copies = [
        pltpu.make_async_copy(source, held.at[number], sems.at[number])
        for number, source in enumerate(inputs)
    ]
    for copy in copies:
        copy.start()
    me = lax.rem(lax.axis_index("tok"), SPAN)
    steps = (
        [closed_step(slot) for slot in range(SPAN)]
        if closed
        else [0, *range(1, SPAN), *range(SPAN - 1, 0, -1)]
    )
    for number, copy in enumerate(copies):
        copy.wait()
        turned[number] = held[number].T
        for phase in range(OWN_HEADS):
            for slot, step in enumerate(steps):
                residue = me ^ step if closed else lax.rem(me + step, SPAN)
                begin = pl.multiple_of((phase * SPAN + residue) * HEAD_DIM, 16)
                outs[phase * len(steps) + slot][message_rows(number), :] = turned[
                    number, pl.ds(begin, HEAD_DIM), :
                ]


def tables_kernel(images, count, tokd, lengths, widths, table, inverse, bias, *refs):
    cos_out, sin_out, mask_out, bias_out, turned = refs
    me = lax.axis_index("tok")
    residue = lax.rem(me, SPAN)
    slots = table.shape[0]
    spot = lax.broadcasted_iota(jnp.int32, (HALF, tokd), 1)
    by_row = lax.broadcasted_iota(jnp.int32, (HALF, tokd), 0) < HALF // 2
    ids = []
    for slot in range(slots):
        block = table[slot, me]
        image, start = image_of(block, lengths, images)
        handled = (block >= 0) & (handler_of(start, residue, count) == me)
        ids.append(jnp.where(handled, image, -1 - slot))
        width = widths[0, image]
        bits = jnp.where(width == tokd, 0, jnp.where(width * 2 == tokd, 1, 2))
        shift = tokd.bit_length() - 1 - bits
        local = spot + (block - start) * tokd
        rowpos = lax.shift_right_logical(local, jnp.broadcast_to(shift, local.shape))
        colpos = local & (width - 1)
        angle = jnp.where(by_row, rowpos, colpos).astype(jnp.float32) * inverse[:, 0:1]
        cos_out[:, slot * tokd : (slot + 1) * tokd] = jnp.cos(angle)
        sin_out[:, slot * tokd : (slot + 1) * tokd] = jnp.sin(angle)
    for slot in range(slots):
        for other in range(slots):
            off = jnp.where(ids[slot] == ids[other], 0.0, NEG)
            row = slot * slots + other
            mask_out[row : row + 1, :] = jnp.full((1, tokd), off, jnp.float32)
        row = slots * slots + slot
        live = jnp.where(ids[slot] >= 0, 1.0, 0.0)
        mask_out[row : row + 1, :] = jnp.full((1, tokd), live, jnp.float32)
    plain = bias[...].astype(jnp.float32)
    rest = jnp.zeros((LANES - plain.shape[0], plain.shape[1]), jnp.float32)
    turned[...] = jnp.concatenate([plain, rest], axis=0).T
    for phase in range(OWN_HEADS):
        begin = pl.multiple_of((phase * SPAN + residue) * HEAD_DIM, 16)
        bias_out[phase * HEAD_DIM : (phase + 1) * HEAD_DIM, :] = turned[pl.ds(begin, HEAD_DIM), :]


def stage(slot, tokd, message, cosv, sinv, bias):
    at = slice(slot * tokd, (slot + 1) * tokd)
    cos_b, sin_b = cosv[:, at], sinv[:, at]
    query, key, value = (
        message[message_rows(tensor), :].astype(jnp.float32) + bias[:, tensor : tensor + 1]
        for tensor in range(3)
    )
    rest_row = lax.broadcasted_iota(jnp.int32, (LANES - HEAD_DIM, tokd), 0)
    zeros = jnp.zeros((LANES - HEAD_DIM, tokd), jnp.float32)
    ones = jnp.where(rest_row < 2, 1.0, 0.0)
    return [
        jnp.concatenate(pair, axis=0).astype(jnp.bfloat16)
        for pair in (
            (rotate(query, cos_b, sin_b) * (SCALE * LOG2E), zeros),
            (rotate(key, cos_b, sin_b), zeros),
            (value, ones),
        )
    ]


def stage_kernel(slot, phases, tokd, cosv, sinv, bias, *refs):
    count = len(phases)
    msgs, turned, plain = refs[:count], refs[count : 2 * count], refs[2 * count :]
    for number, phase in enumerate(phases):
        own_bias = bias[phase * HEAD_DIM : (phase + 1) * HEAD_DIM, :]
        values = stage(slot, tokd, msgs[number], cosv, sinv, own_bias)
        for tensor, value in enumerate(values):
            turned[number][tensor] = value
            if tensor > 0:
                plain[number][tensor - 1] = value.T


def attend_kernel(slots, staged, closed, tokd, head, factor, cosv, sinv, masks, bias, *refs):
    msgs, refs = refs[:slots], refs[slots:]
    ready = {slot: refs[2 * at : 2 * at + 2] for at, slot in enumerate(staged)}
    refs = refs[2 * len(staged) :]
    earlier = ()
    if head > 0:
        before, earlier, refs = refs[0], refs[1:slots], refs[slots:]
    outs, sums = refs[:slots], refs[slots]
    for result, out in zip(earlier, [out for slot, out in enumerate(outs) if slot != EARLY]):
        done = head * 4 * HEAD_DIM
        out[:done, :] = result[:done, :]
    qt_all, kt_all, vt_all, gt_all, k_all, v_all, s_buf, e_buf, d_buf = refs[slots + 1 : slots + 10]
    own_bias = bias[head * HEAD_DIM : (head + 1) * HEAD_DIM, :]
    rest_row = lax.broadcasted_iota(jnp.int32, (LANES - HEAD_DIM, tokd), 0)

    by_lanes = (((1,), (1,)), ((), ()))

    def off_row(slot, other):
        row = slot * slots + other
        return masks[row : row + 1, :]

    def live(slot, values):
        if closed:
            return values
        row = slots * slots + slot
        return values * masks[row : row + 1, :]

    def block_of(slot):
        return slice(slot * tokd, (slot + 1) * tokd)

    def put(slot, tensor, values):
        begin = ((0 if slot == EARLY else 4 * head) + tensor) * HEAD_DIM
        outs[slot][begin : begin + HEAD_DIM, :] = values

    def scores(slot, other):
        part = jnp.dot(
            k_all[block_of(other), :], qt_all[:, block_of(slot)], preferred_element_type=jnp.float32
        )
        s_buf[slot % 2, block_of(other), :] = part
        return jnp.max(part, axis=0, keepdims=True)

    def exponentials(slot, other, top):
        part = jnp.exp2(s_buf[slot % 2, block_of(other), :] - top)
        e_buf[block_of(other), block_of(slot)] = part.astype(jnp.bfloat16)

    def output(slot):
        mixed = jnp.dot(
            vt_all[:USED, :], e_buf[:, block_of(slot)], preferred_element_type=jnp.float32
        )
        inv = 1.0 / mixed[HEAD_DIM : HEAD_DIM + 1]
        out_b = (mixed[:HEAD_DIM] * inv).astype(jnp.bfloat16)
        put(slot, 0, out_b)
        grad = msgs[slot][message_rows(3), :].astype(jnp.float32)
        delta = jnp.sum(grad * out_b.astype(jnp.float32), axis=0, keepdims=True) * inv
        coarse = delta.astype(jnp.bfloat16).astype(jnp.float32)
        rest = jnp.where(rest_row == 0, -coarse, jnp.where(rest_row == 1, coarse - delta, 0.0))
        grad = jnp.concatenate([grad * inv, rest], axis=0).astype(jnp.bfloat16)
        gt_all[:, block_of(slot)] = grad
        spread = grad[:HEAD_DIM].astype(jnp.float32) * mixed[HEAD_DIM : HEAD_DIM + 1]
        return grad, live(slot, spread)

    def dscores(slot, other, grad):
        part = jnp.dot(v_all[block_of(other), :], grad, preferred_element_type=jnp.float32)
        d_buf[block_of(other), block_of(slot)] = (
            e_buf[block_of(other), block_of(slot)] * part.astype(jnp.bfloat16)
        )

    def query_part(slot):
        at = block_of(slot)
        dquery = jnp.dot(kt_all[:HEAD_DIM, :], d_buf[:, at], preferred_element_type=jnp.float32)
        dquery = unrotate(dquery * SCALE, cosv[:, at], sinv[:, at])
        put(slot, 1, dquery.astype(jnp.bfloat16))
        return live(slot, dquery)

    def value_part(slot):
        dvalue = lax.dot_general(
            gt_all[:HEAD_DIM, :],
            e_buf[block_of(slot), :],
            by_lanes,
            preferred_element_type=jnp.float32,
        )
        put(slot, 3, dvalue.astype(jnp.bfloat16))

    for slot in range(slots):
        at = block_of(slot)
        if slot in ready:
            turned, plain = ready[slot]
            values, natural = [turned[number] for number in range(3)], [plain[0], plain[1]]
        else:
            values = stage(slot, tokd, msgs[slot], cosv, sinv, own_bias)
            natural = [value.T for value in values[1:]]
        qt_all[:, at], kt_all[:, at], vt_all[:, at] = values
        k_all[at, :], v_all[at, :] = natural
    dq_total = jnp.zeros((HEAD_DIM, tokd), jnp.float32)
    dv_total = jnp.zeros((HEAD_DIM, tokd), jnp.float32)
    grad = None
    offs = tops = None
    for step in range(slots + 2):
        ahead, slot, behind = step, step - 1, step - 2
        if 0 <= slot < slots:
            offs = [off_row(slot, other) for other in range(slots)]
            top = functools.reduce(jnp.maximum, [one + off for one, off in zip(tops, offs)])
        tops = []
        for other in range(slots):
            if ahead < slots:
                tops.append(scores(ahead, other))
            if 0 <= behind:
                dscores(behind, other, grad)
            if 0 <= slot < slots:
                exponentials(slot, other, top - offs[other])
        if 0 <= behind:
            dq_total = dq_total + query_part(behind)
        if 0 <= slot < slots:
            grad, spread = output(slot)
            dv_total = dv_total + spread
    dk_total = jnp.zeros((HEAD_DIM, tokd), jnp.float32)
    for slot in range(slots):
        at = block_of(slot)
        dkey = lax.dot_general(
            qt_all[:HEAD_DIM, :], d_buf[at, :], by_lanes, preferred_element_type=jnp.float32
        )
        dkey = unrotate(dkey * (1.0 / LOG2E), cosv[:, at], sinv[:, at])
        put(slot, 2, dkey.astype(jnp.bfloat16))
        dk_total = dk_total + live(slot, dkey)
    lane = lax.broadcasted_iota(jnp.int32, (HEAD_DIM, LANES), 1)
    columns = jnp.zeros((HEAD_DIM, LANES), jnp.float32)
    for number, total in enumerate((dq_total, dk_total, dv_total)):
        total = jnp.sum(total, axis=1, keepdims=True) * factor
        columns = jnp.where(lane == number, total, columns)
    columns = jnp.concatenate([columns, jnp.zeros((LANES - HEAD_DIM, LANES), jnp.float32)], axis=0)
    lines = columns.T
    copy = None
    if head + 1 < OWN_HEADS:
        sums[...] = lines[:8]
    else:
        tiles, sem = refs[slots + 10 :]
        tile = join_sums(before[...], lines)

        def repeat(device, carry):
            tiles[device] = tile
            return carry

        lax.fori_loop(0, tiles.shape[0], repeat, 0, unroll=min(32, tiles.shape[0]))
        copy = pltpu.make_async_copy(tiles, sums, sem)
        copy.start()
    for slot in range(slots):
        value_part(slot)
    if copy is not None:
        copy.wait()


FIT = LANES - HEAD_DIM
LEFT = HEAD_DIM - FIT


def join_sums(first, second):
    lane = lax.broadcasted_iota(jnp.int32, (1, LANES), 1)
    rows = []
    last = jnp.zeros((1, LANES), jnp.float32)
    for number in range(3):
        moved = pltpu.roll(second[number : number + 1], HEAD_DIM, 1)
        rows.append(jnp.where(lane < HEAD_DIM, first[number : number + 1], moved))
        rest = jnp.where(lane < LEFT, moved, 0.0)
        last = last + (pltpu.roll(rest, number * LEFT, 1) if number else rest)
    return jnp.concatenate(rows + [last], axis=0)


def unpack_kernel(slots, count, images, *refs):
    closed = is_closed(count)
    if not closed:
        lengths, table, *refs = refs
    msgs, refs = refs[: slots + OWN_HEADS - 1], refs[slots + OWN_HEADS - 1 :]
    *outs, held, ready, sems = refs
    early, late = msgs[:OWN_HEADS], list(msgs[OWN_HEADS:])
    late.insert(EARLY, None)
    me = lax.axis_index("tok")

    def place(slot, residue):
        for phase in range(OWN_HEADS):
            begin = pl.multiple_of((phase * SPAN + residue) * HEAD_DIM, 16)
            for number in range(4):
                if slot == EARLY:
                    piece = early[phase][message_rows(number), :]
                else:
                    piece = late[slot][message_rows(4 * phase + number), :]
                held[number, pl.ds(begin, HEAD_DIM), :] = piece

    for slot in range(slots):
        if closed:
            place(slot, lax.rem(me, SPAN) ^ closed_step(slot))
        else:
            _, start = image_of(me, lengths, images)
            source = table[slot, me]
            residue = lax.rem(source + SPAN, SPAN)
            chosen = (source >= 0) & (source == handler_of(start, residue, count))
            pl.when(chosen)(functools.partial(place, slot, residue))
    copies = []
    for number, out in enumerate(outs):
        ready[number] = held[number].T
        copies.append(pltpu.make_async_copy(ready.at[number], out, sems.at[number]))
        copies[-1].start()
    for copy in copies:
        copy.wait()


def bias_kernel(tiles, bias_out):
    def add(group, totals):
        return tuple(
            total + tiles[group * SPAN + residue] for residue, total in enumerate(totals)
        )

    groups = tiles.shape[0] // SPAN
    zero = jnp.zeros(tiles.shape[1:], jnp.float32)
    totals = lax.fori_loop(0, groups, add, (zero,) * SPAN, unroll=groups <= 8)
    for residue, total in enumerate(totals):
        first = residue * HEAD_DIM
        second = (SPAN + residue) * HEAD_DIM
        for number in range(3):
            row = slice(number, number + 1)
            bias_out[row, first : first + HEAD_DIM] = total[row, :HEAD_DIM]
            bias_out[row, second : second + FIT] = total[row, HEAD_DIM:]
            bias_out[row, second + FIT : second + HEAD_DIM] = total[
                3:4, number * LEFT : (number + 1) * LEFT
            ]


def on_device(query_in, key_in, value_in, out_grad, bias, lengths, widths):
    tokd = query_in.shape[1]
    model = query_in.shape[2]
    images = lengths.shape[1]
    count = lax.axis_size("tok")
    dp_size = lax.axis_size("dp")
    closed = is_closed(count)
    sources, targets = trade_tables(count)
    slots = sources.shape[0]
    span = slots * tokd
    table = jnp.asarray(sources)
    quarter = HEAD_DIM // 4
    inverse = rope_base ** (-np.arange(quarter, dtype=np.float64) / quarter)
    inverse = jnp.asarray(np.tile(np.tile(inverse, 2)[:, None], (1, LANES)), jnp.float32)
    smem = pl.BlockSpec(memory_space=pltpu.SMEM)
    vmem = pl.BlockSpec(memory_space=pltpu.VMEM)
    hbm = pl.BlockSpec(memory_space=pltpu.HBM)
    whole = jax.ShapeDtypeStruct((tokd, model), jnp.bfloat16)
    message = jax.ShapeDtypeStruct((4 * HEAD_DIM, tokd), jnp.bfloat16)
    joined = jax.ShapeDtypeStruct((OWN_HEADS * 4 * HEAD_DIM, tokd), jnp.bfloat16)
    devices = dp_size * count
    tokens_all = devices * tokd

    def params(mib):
        return pltpu.CompilerParams(vmem_limit_bytes=int(mib * 1024 * 1024))

    inputs = (query_in[0], key_in[0], value_in[0], out_grad[0])
    sends = pl.pallas_call(
        functools.partial(pack_kernel, closed),
        out_shape=[message] * (OWN_HEADS * slots),
        in_specs=[hbm] * 4,
        out_specs=[vmem] * (OWN_HEADS * slots),
        scratch_shapes=[
            pltpu.VMEM((4, tokd, model), jnp.bfloat16),
            pltpu.VMEM((4, model, tokd), jnp.bfloat16),
            pltpu.SemaphoreType.DMA((4,)),
        ],
        compiler_params=params(PACK_KIB / 1024),
        name="pack_heads",
    )(*inputs)
    rounds = trade_rounds(count)
    first = [sends[0]] + [
        lax.ppermute(send, "tok", pairs) for send, pairs in zip(sends[1:slots], rounds)
    ]
    table_shape = jax.ShapeDtypeStruct((HALF, span), jnp.float32)
    mask_rows = -(-slots * (slots + 1) // 8) * 8
    tables = pl.pallas_call(
        functools.partial(tables_kernel, images, count, tokd),
        out_shape=[table_shape] * 2
        + [
            jax.ShapeDtypeStruct((mask_rows, tokd), jnp.float32),
            jax.ShapeDtypeStruct((OWN_HEADS * HEAD_DIM, LANES), jnp.float32),
        ],
        in_specs=[smem, smem, smem, vmem, vmem],
        out_specs=[vmem] * 4,
        scratch_shapes=[pltpu.VMEM((model, LANES), jnp.float32)],
        compiler_params=params(16),
        cost_estimate=pl.CostEstimate(
            flops=span * LANES * 200, bytes_accessed=0, transcendentals=0
        ),
        name="rotary_tables",
    )(lengths, widths, table, inverse, bias)

    def stage_ahead(slot, phases, messages):
        number = len(phases)
        results = pl.pallas_call(
            functools.partial(stage_kernel, slot, phases, tokd),
            out_shape=[jax.ShapeDtypeStruct((3, LANES, tokd), jnp.bfloat16)] * number
            + [jax.ShapeDtypeStruct((2, tokd, LANES), jnp.bfloat16)] * number,
            in_specs=[vmem] * (3 + number),
            out_specs=[vmem] * (2 * number),
            compiler_params=params(16),
            cost_estimate=pl.CostEstimate(
                flops=1_000_000 * number, bytes_accessed=0, transcendentals=0
            ),
            name="stage_slot",
        )(tables[0], tables[1], tables[3], *messages)
        return [list(pair) for pair in zip(results[:number], results[number:])]

    phases = tuple(range(OWN_HEADS))
    own = stage_ahead(0, phases, [sends[phase * slots] for phase in phases])
    staged = [{0: pair} for pair in own]
    got = [first] + [[sends[phase * slots]] for phase in phases[1:]]
    latest = own
    for slot in range(1, slots):
        for phase in phases[1:]:
            send, latest = lax.optimization_barrier((sends[phase * slots + slot], latest))
            got[phase].append(lax.ppermute(send, "tok", rounds[slot - 1]))
        if slot == 1:
            staged[0][0], staged[1][0] = latest
        else:
            staged[0][slot - 1] = latest[0]
        if slot + 1 < slots:
            latest = stage_ahead(slot, (0,), [first[slot]])
    early = []
    carried = []
    for phase in range(OWN_HEADS):
        last = phase + 1 == OWN_HEADS
        kept = [slot for slot in range(slots) if slot != EARLY]
        sums_shape = jax.ShapeDtypeStruct(
            (devices, 4, LANES) if last else (8, LANES), jnp.float32
        )
        *results, total = pl.pallas_call(
            functools.partial(
                attend_kernel,
                slots,
                tuple(staged[phase]),
                closed,
                tokd,
                phase,
                1.0 / tokens_all**0.5,
            ),
            out_shape=[message if slot == EARLY else joined for slot in range(slots)]
            + [sums_shape],
            in_specs=[vmem] * (4 + slots + 2 * len(staged[phase]) + len(carried)),
            out_specs=[vmem] * slots + [hbm if last else vmem],
            scratch_shapes=[pltpu.VMEM((LANES, span), jnp.bfloat16)] * 4
            + [pltpu.VMEM((span, LANES), jnp.bfloat16)] * 2
            + [pltpu.VMEM((2, span, tokd), jnp.float32)]
            + [pltpu.VMEM((span, span), jnp.bfloat16)] * 2
            + (
                [pltpu.VMEM(sums_shape.shape, jnp.float32), pltpu.SemaphoreType.DMA(())]
                if last
                else []
            ),
            compiler_params=params(32),
            cost_estimate=pl.CostEstimate(
                flops=12 * span * span * 256, bytes_accessed=0, transcendentals=0
            ),
            name="attend_head",
        )(*tables, *got[phase], *(one for pair in staged[phase].values() for one in pair), *carried)
        results, total, early = lax.optimization_barrier((results, total, early))
        early.append(send_back(results[EARLY], EARLY))
        carried = [total] + [results[slot] for slot in kept]
    tiles = lax.all_to_all(total, ("dp", "tok"), 0, 0, tiled=True)
    late = [send_back(results[slot], slot) for slot in kept]
    places = [] if closed else [lengths, jnp.asarray(targets)]
    outs = pl.pallas_call(
        functools.partial(unpack_kernel, slots, count, images),
        out_shape=[whole] * 4,
        in_specs=[smem] * len(places) + [vmem] * (OWN_HEADS + len(late)),
        out_specs=[hbm] * 4,
        scratch_shapes=[
            pltpu.VMEM((4, model, tokd), jnp.bfloat16),
            pltpu.VMEM((4, tokd, model), jnp.bfloat16),
            pltpu.SemaphoreType.DMA((4,)),
        ],
        compiler_params=params(16),
        cost_estimate=pl.CostEstimate(flops=UNPACK_FLOPS, bytes_accessed=0, transcendentals=0),
        name="unpack_heads",
    )(*places, *early, *late)
    outs, tiles = lax.optimization_barrier((outs, tiles))
    bias_grad = pl.pallas_call(
        bias_kernel,
        out_shape=jax.ShapeDtypeStruct((3, model), jnp.float32),
        in_specs=[vmem],
        out_specs=vmem,
        compiler_params=params(16),
        name="bias_sums",
    )(tiles)
    return tuple(out[None] for out in outs) + (bias_grad,)


def solution(mesh):
    in_specs = (
        P("dp", "tok", None),
        P("dp", "tok", None),
        P("dp", "tok", None),
        P("dp", "tok", None),
        P(),
        P("dp", None),
        P("dp", None),
    )
    out_specs = (
        P("dp", "tok", None),
        P("dp", "tok", None),
        P("dp", "tok", None),
        P("dp", "tok", None),
        P(),
    )
    return jax.shard_map(
        on_device, mesh=mesh, in_specs=in_specs, out_specs=out_specs, check_vma=False
    )
```

```python
import functools

import jax
import jax.numpy as jnp
import numpy as np
from jax import lax
from jax.experimental import pallas as pl
from jax.experimental.pallas import tpu as pltpu
from jax.sharding import PartitionSpec as P

HEADS = 8
HEAD_DIM = 80
SPAN = 4
OWN_HEADS = HEADS // SPAN
PART = OWN_HEADS * HEAD_DIM
SCALE = HEAD_DIM**-0.5
LOG2E = 1.4426950408889634
NEG = -1e30
LANES = 128
USED = HEAD_DIM + 16
HALF = HEAD_DIM // 2
PACK_KIB = 52 * 1024 + 600
UNPACK_FLOPS = 20_000_000_000

rope_base = 10000.0


def is_closed(count):
    return count in (SPAN, 2 * SPAN)


def closed_step(slot):
    return (SPAN - slot) % SPAN


def trade_rounds(count):
    if is_closed(count):
        return [
            [(one, one ^ closed_step(slot)) for one in range(count)] for slot in range(1, SPAN)
        ]
    rounds = []
    for shift in [*range(1, SPAN), *range(-1, -SPAN, -1)]:
        rounds.append(
            [
                (source, source + shift)
                for source in range(max(0, -shift), min(count, count - shift))
                if (source < SPAN) == (source + shift < SPAN)
            ]
        )
    return rounds


def trade_tables(count):
    rounds = trade_rounds(count)
    sources = np.full((1 + len(rounds), count), -1, np.int32)
    targets = sources.copy()
    sources[0] = targets[0] = np.arange(count)
    for slot, pairs in enumerate(rounds, 1):
        for source, target in pairs:
            sources[slot, target] = source
            targets[slot, source] = target
    return sources, targets


def send_back(result, slot):
    if slot == 0:
        return result
    pairs = trade_rounds(lax.axis_size("tok"))[slot - 1]
    return lax.ppermute(result, "tok", [(target, source) for source, target in pairs])


EARLY = 1


def image_of(block, lengths, images):
    image = jnp.int32(0)
    start = jnp.int32(0)
    begin = jnp.int32(0)
    for number in range(images):
        size = lengths[0, number]
        inside = (block >= begin) & (block < begin + size)
        image = jnp.where(inside, number, image)
        start = jnp.where(inside, begin, start)
        begin = begin + size
    return image, start


def handler_of(start, residue, count):
    device = start + lax.rem(residue - lax.rem(start, SPAN) + SPAN, SPAN)
    return jnp.where(device >= count, device - SPAN, device)


def message_rows(tensor):
    return slice(tensor * HEAD_DIM, (tensor + 1) * HEAD_DIM)


def rotate(values, cosv, sinv):
    first, second = values[:HALF], values[HALF:]
    return jnp.concatenate([first * cosv - second * sinv, second * cosv + first * sinv], axis=0)


def unrotate(values, cosv, sinv):
    first, second = values[:HALF], values[HALF:]
    return jnp.concatenate([first * cosv + second * sinv, second * cosv - first * sinv], axis=0)


def pack_kernel(closed, *refs):
    inputs, outs, held, turned, sems = refs[:4], refs[4:-3], refs[-3], refs[-2], refs[-1]
    copies = [
        pltpu.make_async_copy(source, held.at[number], sems.at[number])
        for number, source in enumerate(inputs)
    ]
    for copy in copies:
        copy.start()
    me = lax.rem(lax.axis_index("tok"), SPAN)
    steps = (
        [closed_step(slot) for slot in range(SPAN)]
        if closed
        else [0, *range(1, SPAN), *range(SPAN - 1, 0, -1)]
    )
    for number, copy in enumerate(copies):
        copy.wait()
        turned[number] = held[number].T
        for phase in range(OWN_HEADS):
            for slot, step in enumerate(steps):
                residue = me ^ step if closed else lax.rem(me + step, SPAN)
                begin = pl.multiple_of((phase * SPAN + residue) * HEAD_DIM, 16)
                outs[phase * len(steps) + slot][message_rows(number), :] = turned[
                    number, pl.ds(begin, HEAD_DIM), :
                ]


def tables_kernel(images, count, tokd, lengths, widths, table, inverse, bias, *refs):
    cos_out, sin_out, mask_out, bias_out, turned = refs
    me = lax.axis_index("tok")
    residue = lax.rem(me, SPAN)
    slots = table.shape[0]
    spot = lax.broadcasted_iota(jnp.int32, (HALF, tokd), 1)
    by_row = lax.broadcasted_iota(jnp.int32, (HALF, tokd), 0) < HALF // 2
    ids = []
    for slot in range(slots):
        block = table[slot, me]
        image, start = image_of(block, lengths, images)
        handled = (block >= 0) & (handler_of(start, residue, count) == me)
        ids.append(jnp.where(handled, image, -1 - slot))
        width = widths[0, image]
        bits = jnp.where(width == tokd, 0, jnp.where(width * 2 == tokd, 1, 2))
        shift = tokd.bit_length() - 1 - bits
        local = spot + (block - start) * tokd
        rowpos = lax.shift_right_logical(local, jnp.broadcast_to(shift, local.shape))
        colpos = local & (width - 1)
        angle = jnp.where(by_row, rowpos, colpos).astype(jnp.float32) * inverse[:, 0:1]
        cos_out[:, slot * tokd : (slot + 1) * tokd] = jnp.cos(angle)
        sin_out[:, slot * tokd : (slot + 1) * tokd] = jnp.sin(angle)
    for slot in range(slots):
        for other in range(slots):
            off = jnp.where(ids[slot] == ids[other], 0.0, NEG)
            row = slot * slots + other
            mask_out[row : row + 1, :] = jnp.full((1, tokd), off, jnp.float32)
        row = slots * slots + slot
        live = jnp.where(ids[slot] >= 0, 1.0, 0.0)
        mask_out[row : row + 1, :] = jnp.full((1, tokd), live, jnp.float32)
    plain = bias[...].astype(jnp.float32)
    rest = jnp.zeros((LANES - plain.shape[0], plain.shape[1]), jnp.float32)
    turned[...] = jnp.concatenate([plain, rest], axis=0).T
    for phase in range(OWN_HEADS):
        begin = pl.multiple_of((phase * SPAN + residue) * HEAD_DIM, 16)
        bias_out[phase * HEAD_DIM : (phase + 1) * HEAD_DIM, :] = turned[pl.ds(begin, HEAD_DIM), :]


def stage(slot, tokd, message, cosv, sinv, bias):
    at = slice(slot * tokd, (slot + 1) * tokd)
    cos_b, sin_b = cosv[:, at], sinv[:, at]
    query, key, value = (
        message[message_rows(tensor), :].astype(jnp.float32) + bias[:, tensor : tensor + 1]
        for tensor in range(3)
    )
    rest_row = lax.broadcasted_iota(jnp.int32, (LANES - HEAD_DIM, tokd), 0)
    zeros = jnp.zeros((LANES - HEAD_DIM, tokd), jnp.float32)
    ones = jnp.where(rest_row < 2, 1.0, 0.0)
    return [
        jnp.concatenate(pair, axis=0).astype(jnp.bfloat16)
        for pair in (
            (rotate(query, cos_b, sin_b) * (SCALE * LOG2E), zeros),
            (rotate(key, cos_b, sin_b), zeros),
            (value, ones),
        )
    ]


def stage_kernel(slot, phases, tokd, cosv, sinv, bias, *refs):
    count = len(phases)
    msgs, turned, plain = refs[:count], refs[count : 2 * count], refs[2 * count :]
    for number, phase in enumerate(phases):
        own_bias = bias[phase * HEAD_DIM : (phase + 1) * HEAD_DIM, :]
        values = stage(slot, tokd, msgs[number], cosv, sinv, own_bias)
        for tensor, value in enumerate(values):
            turned[number][tensor] = value
            if tensor > 0:
                plain[number][tensor - 1] = value.T


def attend_kernel(slots, staged, closed, tokd, head, factor, cosv, sinv, masks, bias, *refs):
    msgs, refs = refs[:slots], refs[slots:]
    ready = {slot: refs[2 * at : 2 * at + 2] for at, slot in enumerate(staged)}
    refs = refs[2 * len(staged) :]
    earlier = ()
    if head > 0:
        before, earlier, refs = refs[0], refs[1:slots], refs[slots:]
    outs, sums = refs[:slots], refs[slots]
    for result, out in zip(earlier, [out for slot, out in enumerate(outs) if slot != EARLY]):
        done = head * 4 * HEAD_DIM
        out[:done, :] = result[:done, :]
    qt_all, kt_all, vt_all, gt_all, k_all, v_all, s_buf, e_buf, d_buf = refs[slots + 1 : slots + 10]
    own_bias = bias[head * HEAD_DIM : (head + 1) * HEAD_DIM, :]
    rest_row = lax.broadcasted_iota(jnp.int32, (LANES - HEAD_DIM, tokd), 0)

    by_lanes = (((1,), (1,)), ((), ()))

    def off_row(slot, other):
        row = slot * slots + other
        return masks[row : row + 1, :]

    def live(slot, values):
        if closed:
            return values
        row = slots * slots + slot
        return values * masks[row : row + 1, :]

    def block_of(slot):
        return slice(slot * tokd, (slot + 1) * tokd)

    def put(slot, tensor, values):
        begin = ((0 if slot == EARLY else 4 * head) + tensor) * HEAD_DIM
        outs[slot][begin : begin + HEAD_DIM, :] = values

    def scores(slot):
        part = jnp.dot(
            k_all[...], qt_all[:, block_of(slot)], preferred_element_type=jnp.float32
        )
        s_buf[slot % 2] = part
        return [jnp.max(part[block_of(other)], axis=0, keepdims=True) for other in range(slots)]

    def exponentials(slot, other, top):
        part = jnp.exp2(s_buf[slot % 2, block_of(other), :] - top)
        e_buf[block_of(other), block_of(slot)] = part.astype(jnp.bfloat16)

    def output(slot):
        mixed = jnp.dot(
            vt_all[:USED, :], e_buf[:, block_of(slot)], preferred_element_type=jnp.float32
        )
        inv = 1.0 / mixed[HEAD_DIM : HEAD_DIM + 1]
        out_b = (mixed[:HEAD_DIM] * inv).astype(jnp.bfloat16)
        put(slot, 0, out_b)
        grad = msgs[slot][message_rows(3), :].astype(jnp.float32)
        delta = jnp.sum(grad * out_b.astype(jnp.float32), axis=0, keepdims=True) * inv
        coarse = delta.astype(jnp.bfloat16).astype(jnp.float32)
        rest = jnp.where(rest_row == 0, -coarse, jnp.where(rest_row == 1, coarse - delta, 0.0))
        grad = jnp.concatenate([grad * inv, rest], axis=0).astype(jnp.bfloat16)
        gt_all[:, block_of(slot)] = grad
        spread = grad[:HEAD_DIM].astype(jnp.float32) * mixed[HEAD_DIM : HEAD_DIM + 1]
        return grad, live(slot, spread)

    def dscores(slot, grad):
        part = jnp.dot(v_all[...], grad, preferred_element_type=jnp.float32)
        d_buf[:, block_of(slot)] = e_buf[:, block_of(slot)] * part.astype(jnp.bfloat16)

    def query_part(slot):
        at = block_of(slot)
        dquery = jnp.dot(kt_all[:HEAD_DIM, :], d_buf[:, at], preferred_element_type=jnp.float32)
        dquery = unrotate(dquery * SCALE, cosv[:, at], sinv[:, at])
        put(slot, 1, dquery.astype(jnp.bfloat16))
        return live(slot, dquery)

    def value_part(slot):
        dvalue = lax.dot_general(
            gt_all[:HEAD_DIM, :],
            e_buf[block_of(slot), :],
            by_lanes,
            preferred_element_type=jnp.float32,
        )
        put(slot, 3, dvalue.astype(jnp.bfloat16))

    for slot in range(slots):
        at = block_of(slot)
        if slot in ready:
            turned, plain = ready[slot]
            values, natural = [turned[number] for number in range(3)], [plain[0], plain[1]]
        else:
            values = stage(slot, tokd, msgs[slot], cosv, sinv, own_bias)
            natural = [value.T for value in values[1:]]
        qt_all[:, at], kt_all[:, at], vt_all[:, at] = values
        k_all[at, :], v_all[at, :] = natural
    dq_total = jnp.zeros((HEAD_DIM, tokd), jnp.float32)
    dv_total = jnp.zeros((HEAD_DIM, tokd), jnp.float32)
    grad = None
    offs = tops = None
    for step in range(slots + 2):
        ahead, slot, behind = step, step - 1, step - 2
        if 0 <= slot < slots:
            offs = [off_row(slot, other) for other in range(slots)]
            top = functools.reduce(jnp.maximum, [one + off for one, off in zip(tops, offs)])
        if ahead < slots:
            tops = scores(ahead)
        if 0 <= behind:
            dscores(behind, grad)
        if 0 <= slot < slots:
            for other in range(slots):
                exponentials(slot, other, top - offs[other])
        if 0 <= behind:
            dq_total = dq_total + query_part(behind)
        if 0 <= slot < slots:
            grad, spread = output(slot)
            dv_total = dv_total + spread
    dk_total = jnp.zeros((HEAD_DIM, tokd), jnp.float32)
    for slot in range(slots // 2):
        value_part(slot)
    for slot in range(slots):
        at = block_of(slot)
        dkey = lax.dot_general(
            qt_all[:HEAD_DIM, :], d_buf[at, :], by_lanes, preferred_element_type=jnp.float32
        )
        dkey = unrotate(dkey * (1.0 / LOG2E), cosv[:, at], sinv[:, at])
        put(slot, 2, dkey.astype(jnp.bfloat16))
        dk_total = dk_total + live(slot, dkey)
    lane = lax.broadcasted_iota(jnp.int32, (HEAD_DIM, LANES), 1)
    columns = jnp.zeros((HEAD_DIM, LANES), jnp.float32)
    for number, total in enumerate((dq_total, dk_total, dv_total)):
        total = jnp.sum(total, axis=1, keepdims=True) * factor
        columns = jnp.where(lane == number, total, columns)
    columns = jnp.concatenate([columns, jnp.zeros((LANES - HEAD_DIM, LANES), jnp.float32)], axis=0)
    lines = columns.T
    copy = None
    if head + 1 < OWN_HEADS:
        sums[...] = lines[:8]
    else:
        tiles, sem = refs[slots + 10 :]
        tile = join_sums(before[...], lines)

        def repeat(device, carry):
            tiles[device] = tile
            return carry

        lax.fori_loop(0, tiles.shape[0], repeat, 0, unroll=min(32, tiles.shape[0]))
        copy = pltpu.make_async_copy(tiles, sums, sem)
        copy.start()
    for slot in range(slots // 2, slots):
        value_part(slot)
    if copy is not None:
        copy.wait()


FIT = LANES - HEAD_DIM
LEFT = HEAD_DIM - FIT


def join_sums(first, second):
    lane = lax.broadcasted_iota(jnp.int32, (1, LANES), 1)
    rows = []
    last = jnp.zeros((1, LANES), jnp.float32)
    for number in range(3):
        moved = pltpu.roll(second[number : number + 1], HEAD_DIM, 1)
        rows.append(jnp.where(lane < HEAD_DIM, first[number : number + 1], moved))
        rest = jnp.where(lane < LEFT, moved, 0.0)
        last = last + (pltpu.roll(rest, number * LEFT, 1) if number else rest)
    return jnp.concatenate(rows + [last], axis=0)


def unpack_kernel(slots, count, images, *refs):
    closed = is_closed(count)
    if not closed:
        lengths, table, *refs = refs
    msgs, refs = refs[: slots + OWN_HEADS - 1], refs[slots + OWN_HEADS - 1 :]
    *outs, held, ready, sems = refs
    early, late = msgs[:OWN_HEADS], list(msgs[OWN_HEADS:])
    late.insert(EARLY, None)
    me = lax.axis_index("tok")

    def place(slot, residue):
        for phase in range(OWN_HEADS):
            begin = pl.multiple_of((phase * SPAN + residue) * HEAD_DIM, 16)
            for number in range(4):
                if slot == EARLY:
                    piece = early[phase][message_rows(number), :]
                else:
                    piece = late[slot][message_rows(4 * phase + number), :]
                held[number, pl.ds(begin, HEAD_DIM), :] = piece

    for slot in range(slots):
        if closed:
            place(slot, lax.rem(me, SPAN) ^ closed_step(slot))
        else:
            _, start = image_of(me, lengths, images)
            source = table[slot, me]
            residue = lax.rem(source + SPAN, SPAN)
            chosen = (source >= 0) & (source == handler_of(start, residue, count))
            pl.when(chosen)(functools.partial(place, slot, residue))
    copies = []
    for number, out in enumerate(outs):
        ready[number] = held[number].T
        copies.append(pltpu.make_async_copy(ready.at[number], out, sems.at[number]))
        copies[-1].start()
    for copy in copies:
        copy.wait()


def bias_kernel(tiles, bias_out):
    def add(group, totals):
        return tuple(
            total + tiles[group * SPAN + residue] for residue, total in enumerate(totals)
        )

    groups = tiles.shape[0] // SPAN
    zero = jnp.zeros(tiles.shape[1:], jnp.float32)
    totals = lax.fori_loop(0, groups, add, (zero,) * SPAN, unroll=groups <= 8)
    for residue, total in enumerate(totals):
        first = residue * HEAD_DIM
        second = (SPAN + residue) * HEAD_DIM
        for number in range(3):
            row = slice(number, number + 1)
            bias_out[row, first : first + HEAD_DIM] = total[row, :HEAD_DIM]
            bias_out[row, second : second + FIT] = total[row, HEAD_DIM:]
            bias_out[row, second + FIT : second + HEAD_DIM] = total[
                3:4, number * LEFT : (number + 1) * LEFT
            ]


def on_device(query_in, key_in, value_in, out_grad, bias, lengths, widths):
    tokd = query_in.shape[1]
    model = query_in.shape[2]
    images = lengths.shape[1]
    count = lax.axis_size("tok")
    dp_size = lax.axis_size("dp")
    closed = is_closed(count)
    sources, targets = trade_tables(count)
    slots = sources.shape[0]
    span = slots * tokd
    table = jnp.asarray(sources)
    quarter = HEAD_DIM // 4
    inverse = rope_base ** (-np.arange(quarter, dtype=np.float64) / quarter)
    inverse = jnp.asarray(np.tile(np.tile(inverse, 2)[:, None], (1, LANES)), jnp.float32)
    smem = pl.BlockSpec(memory_space=pltpu.SMEM)
    vmem = pl.BlockSpec(memory_space=pltpu.VMEM)
    hbm = pl.BlockSpec(memory_space=pltpu.HBM)
    whole = jax.ShapeDtypeStruct((tokd, model), jnp.bfloat16)
    message = jax.ShapeDtypeStruct((4 * HEAD_DIM, tokd), jnp.bfloat16)
    joined = jax.ShapeDtypeStruct((OWN_HEADS * 4 * HEAD_DIM, tokd), jnp.bfloat16)
    devices = dp_size * count
    tokens_all = devices * tokd

    def params(mib):
        return pltpu.CompilerParams(vmem_limit_bytes=int(mib * 1024 * 1024))

    inputs = (query_in[0], key_in[0], value_in[0], out_grad[0])
    sends = pl.pallas_call(
        functools.partial(pack_kernel, closed),
        out_shape=[message] * (OWN_HEADS * slots),
        in_specs=[hbm] * 4,
        out_specs=[vmem] * (OWN_HEADS * slots),
        scratch_shapes=[
            pltpu.VMEM((4, tokd, model), jnp.bfloat16),
            pltpu.VMEM((4, model, tokd), jnp.bfloat16),
            pltpu.SemaphoreType.DMA((4,)),
        ],
        compiler_params=params(PACK_KIB / 1024),
        name="pack_heads",
    )(*inputs)
    rounds = trade_rounds(count)
    first = [sends[0]] + [
        lax.ppermute(send, "tok", pairs) for send, pairs in zip(sends[1:slots], rounds)
    ]
    table_shape = jax.ShapeDtypeStruct((HALF, span), jnp.float32)
    mask_rows = -(-slots * (slots + 1) // 8) * 8
    tables = pl.pallas_call(
        functools.partial(tables_kernel, images, count, tokd),
        out_shape=[table_shape] * 2
        + [
            jax.ShapeDtypeStruct((mask_rows, tokd), jnp.float32),
            jax.ShapeDtypeStruct((OWN_HEADS * HEAD_DIM, LANES), jnp.float32),
        ],
        in_specs=[smem, smem, smem, vmem, vmem],
        out_specs=[vmem] * 4,
        scratch_shapes=[pltpu.VMEM((model, LANES), jnp.float32)],
        compiler_params=params(16),
        cost_estimate=pl.CostEstimate(
            flops=span * LANES * 200, bytes_accessed=0, transcendentals=0
        ),
        name="rotary_tables",
    )(lengths, widths, table, inverse, bias)

    def stage_ahead(slot, phases, messages):
        number = len(phases)
        results = pl.pallas_call(
            functools.partial(stage_kernel, slot, phases, tokd),
            out_shape=[jax.ShapeDtypeStruct((3, LANES, tokd), jnp.bfloat16)] * number
            + [jax.ShapeDtypeStruct((2, tokd, LANES), jnp.bfloat16)] * number,
            in_specs=[vmem] * (3 + number),
            out_specs=[vmem] * (2 * number),
            compiler_params=params(16),
            cost_estimate=pl.CostEstimate(
                flops=1_000_000 * number, bytes_accessed=0, transcendentals=0
            ),
            name="stage_slot",
        )(tables[0], tables[1], tables[3], *messages)
        return [list(pair) for pair in zip(results[:number], results[number:])]

    phases = tuple(range(OWN_HEADS))
    own = stage_ahead(0, phases, [sends[phase * slots] for phase in phases])
    staged = [{0: pair} for pair in own]
    got = [first] + [[sends[phase * slots]] for phase in phases[1:]]
    latest = own
    for slot in range(1, slots):
        for phase in phases[1:]:
            send, latest = lax.optimization_barrier((sends[phase * slots + slot], latest))
            got[phase].append(lax.ppermute(send, "tok", rounds[slot - 1]))
        if slot == 1:
            staged[0][0], staged[1][0] = latest
        else:
            staged[0][slot - 1] = latest[0]
        if slot + 1 < slots:
            latest = stage_ahead(slot, (0,), [first[slot]])
    early = []
    carried = []
    for phase in range(OWN_HEADS):
        last = phase + 1 == OWN_HEADS
        kept = [slot for slot in range(slots) if slot != EARLY]
        sums_shape = jax.ShapeDtypeStruct(
            (devices, 4, LANES) if last else (8, LANES), jnp.float32
        )
        *results, total = pl.pallas_call(
            functools.partial(
                attend_kernel,
                slots,
                tuple(staged[phase]),
                closed,
                tokd,
                phase,
                1.0 / tokens_all**0.5,
            ),
            out_shape=[message if slot == EARLY else joined for slot in range(slots)]
            + [sums_shape],
            in_specs=[vmem] * (4 + slots + 2 * len(staged[phase]) + len(carried)),
            out_specs=[vmem] * slots + [hbm if last else vmem],
            scratch_shapes=[pltpu.VMEM((LANES, span), jnp.bfloat16)] * 4
            + [pltpu.VMEM((span, LANES), jnp.bfloat16)] * 2
            + [pltpu.VMEM((2, span, tokd), jnp.float32)]
            + [pltpu.VMEM((span, span), jnp.bfloat16)] * 2
            + (
                [pltpu.VMEM(sums_shape.shape, jnp.float32), pltpu.SemaphoreType.DMA(())]
                if last
                else []
            ),
            compiler_params=params(32),
            cost_estimate=pl.CostEstimate(
                flops=12 * span * span * 256, bytes_accessed=0, transcendentals=0
            ),
            name="attend_head",
        )(*tables, *got[phase], *(one for pair in staged[phase].values() for one in pair), *carried)
        results, total, early = lax.optimization_barrier((results, total, early))
        early.append(send_back(results[EARLY], EARLY))
        carried = [total] + [results[slot] for slot in kept]
    tiles = lax.all_to_all(total, ("dp", "tok"), 0, 0, tiled=True)
    late = [send_back(results[slot], slot) for slot in kept]
    places = [] if closed else [lengths, jnp.asarray(targets)]
    outs = pl.pallas_call(
        functools.partial(unpack_kernel, slots, count, images),
        out_shape=[whole] * 4,
        in_specs=[smem] * len(places) + [vmem] * (OWN_HEADS + len(late)),
        out_specs=[hbm] * 4,
        scratch_shapes=[
            pltpu.VMEM((4, model, tokd), jnp.bfloat16),
            pltpu.VMEM((4, tokd, model), jnp.bfloat16),
            pltpu.SemaphoreType.DMA((4,)),
        ],
        compiler_params=params(16),
        cost_estimate=pl.CostEstimate(flops=UNPACK_FLOPS, bytes_accessed=0, transcendentals=0),
        name="unpack_heads",
    )(*places, *early, *late)
    outs, tiles = lax.optimization_barrier((outs, tiles))
    bias_grad = pl.pallas_call(
        bias_kernel,
        out_shape=jax.ShapeDtypeStruct((3, model), jnp.float32),
        in_specs=[vmem],
        out_specs=vmem,
        compiler_params=params(16),
        name="bias_sums",
    )(tiles)
    return tuple(out[None] for out in outs) + (bias_grad,)


def solution(mesh):
    in_specs = (
        P("dp", "tok", None),
        P("dp", "tok", None),
        P("dp", "tok", None),
        P("dp", "tok", None),
        P(),
        P("dp", None),
        P("dp", None),
    )
    out_specs = (
        P("dp", "tok", None),
        P("dp", "tok", None),
        P("dp", "tok", None),
        P("dp", "tok", None),
        P(),
    )
    return jax.shard_map(
        on_device, mesh=mesh, in_specs=in_specs, out_specs=out_specs, check_vma=False
    )
```

```python
import functools

import jax
import jax.numpy as jnp
import numpy as np
from jax import lax
from jax.experimental import pallas as pl
from jax.experimental.pallas import tpu as pltpu
from jax.sharding import PartitionSpec as P

HEADS = 8
HEAD_DIM = 80
SPAN = 4
OWN_HEADS = HEADS // SPAN
PART = OWN_HEADS * HEAD_DIM
SCALE = HEAD_DIM**-0.5
LOG2E = 1.4426950408889634
NEG = -1e30
LANES = 128
USED = HEAD_DIM + 16
HALF = HEAD_DIM // 2
PIECES = 2
PACK_KIB = 52 * 1024 + 600
UNPACK_FLOPS = 20_000_000_000

rope_base = 10000.0


def is_closed(count):
    return count in (SPAN, 2 * SPAN)


def closed_step(slot):
    return (SPAN - slot) % SPAN


def trade_rounds(count):
    if is_closed(count):
        return [
            [(one, one ^ closed_step(slot)) for one in range(count)] for slot in range(1, SPAN)
        ]
    rounds = []
    for shift in [*range(1, SPAN), *range(-1, -SPAN, -1)]:
        rounds.append(
            [
                (source, source + shift)
                for source in range(max(0, -shift), min(count, count - shift))
                if (source < SPAN) == (source + shift < SPAN)
            ]
        )
    return rounds


def trade_tables(count):
    rounds = trade_rounds(count)
    sources = np.full((1 + len(rounds), count), -1, np.int32)
    targets = sources.copy()
    sources[0] = targets[0] = np.arange(count)
    for slot, pairs in enumerate(rounds, 1):
        for source, target in pairs:
            sources[slot, target] = source
            targets[slot, source] = target
    return sources, targets


def send_back(result, slot):
    if slot == 0:
        return result
    pairs = trade_rounds(lax.axis_size("tok"))[slot - 1]
    return lax.ppermute(result, "tok", [(target, source) for source, target in pairs])


EARLY = 1


def image_of(block, lengths, images):
    image = jnp.int32(0)
    start = jnp.int32(0)
    begin = jnp.int32(0)
    for number in range(images):
        size = lengths[0, number]
        inside = (block >= begin) & (block < begin + size)
        image = jnp.where(inside, number, image)
        start = jnp.where(inside, begin, start)
        begin = begin + size
    return image, start


def handler_of(start, residue, count):
    device = start + lax.rem(residue - lax.rem(start, SPAN) + SPAN, SPAN)
    return jnp.where(device >= count, device - SPAN, device)


def message_rows(tensor):
    return slice(tensor * HEAD_DIM, (tensor + 1) * HEAD_DIM)


def rotate(values, cosv, sinv):
    first, second = values[:HALF], values[HALF:]
    return jnp.concatenate([first * cosv - second * sinv, second * cosv + first * sinv], axis=0)


def unrotate(values, cosv, sinv):
    first, second = values[:HALF], values[HALF:]
    return jnp.concatenate([first * cosv + second * sinv, second * cosv - first * sinv], axis=0)


def pack_kernel(closed, *refs):
    inputs, outs, held, turned, sems = refs[:4], refs[4:-3], refs[-3], refs[-2], refs[-1]
    copies = [
        pltpu.make_async_copy(source, held.at[number], sems.at[number])
        for number, source in enumerate(inputs)
    ]
    for copy in copies:
        copy.start()
    me = lax.rem(lax.axis_index("tok"), SPAN)
    steps = (
        [closed_step(slot) for slot in range(SPAN)]
        if closed
        else [0, *range(1, SPAN), *range(SPAN - 1, 0, -1)]
    )
    for number, copy in enumerate(copies):
        copy.wait()
        turned[number] = held[number].T
        for phase in range(OWN_HEADS):
            for slot, step in enumerate(steps):
                residue = me ^ step if closed else lax.rem(me + step, SPAN)
                begin = pl.multiple_of((phase * SPAN + residue) * HEAD_DIM, 16)
                outs[phase * len(steps) + slot][message_rows(number), :] = turned[
                    number, pl.ds(begin, HEAD_DIM), :
                ]


def tables_kernel(images, count, tokd, lengths, widths, table, inverse, bias, *refs):
    cos_out, sin_out, mask_out, bias_out, turned = refs
    me = lax.axis_index("tok")
    residue = lax.rem(me, SPAN)
    slots = table.shape[0]
    spot = lax.broadcasted_iota(jnp.int32, (HALF, tokd), 1)
    by_row = lax.broadcasted_iota(jnp.int32, (HALF, tokd), 0) < HALF // 2
    ids = []
    for slot in range(slots):
        block = table[slot, me]
        image, start = image_of(block, lengths, images)
        handled = (block >= 0) & (handler_of(start, residue, count) == me)
        ids.append(jnp.where(handled, image, -1 - slot))
        width = widths[0, image]
        bits = jnp.where(width == tokd, 0, jnp.where(width * 2 == tokd, 1, 2))
        shift = tokd.bit_length() - 1 - bits
        local = spot + (block - start) * tokd
        rowpos = lax.shift_right_logical(local, jnp.broadcast_to(shift, local.shape))
        colpos = local & (width - 1)
        angle = jnp.where(by_row, rowpos, colpos).astype(jnp.float32) * inverse[:, 0:1]
        cos_out[:, slot * tokd : (slot + 1) * tokd] = jnp.cos(angle)
        sin_out[:, slot * tokd : (slot + 1) * tokd] = jnp.sin(angle)
    for slot in range(slots):
        for other in range(slots):
            off = jnp.where(ids[slot] == ids[other], 0.0, NEG)
            row = slot * slots + other
            mask_out[row : row + 1, :] = jnp.full((1, tokd), off, jnp.float32)
        row = slots * slots + slot
        live = jnp.where(ids[slot] >= 0, 1.0, 0.0)
        mask_out[row : row + 1, :] = jnp.full((1, tokd), live, jnp.float32)
    plain = bias[...].astype(jnp.float32)
    rest = jnp.zeros((LANES - plain.shape[0], plain.shape[1]), jnp.float32)
    turned[...] = jnp.concatenate([plain, rest], axis=0).T
    for phase in range(OWN_HEADS):
        begin = pl.multiple_of((phase * SPAN + residue) * HEAD_DIM, 16)
        bias_out[phase * HEAD_DIM : (phase + 1) * HEAD_DIM, :] = turned[pl.ds(begin, HEAD_DIM), :]


def stage(slot, tokd, message, cosv, sinv, bias):
    at = slice(slot * tokd, (slot + 1) * tokd)
    cos_b, sin_b = cosv[:, at], sinv[:, at]
    query, key, value = (
        message[message_rows(tensor), :].astype(jnp.float32) + bias[:, tensor : tensor + 1]
        for tensor in range(3)
    )
    rest_row = lax.broadcasted_iota(jnp.int32, (LANES - HEAD_DIM, tokd), 0)
    zeros = jnp.zeros((LANES - HEAD_DIM, tokd), jnp.float32)
    ones = jnp.where(rest_row < 2, 1.0, 0.0)
    return [
        jnp.concatenate(pair, axis=0).astype(jnp.bfloat16)
        for pair in (
            (rotate(query, cos_b, sin_b) * (SCALE * LOG2E), zeros),
            (rotate(key, cos_b, sin_b), zeros),
            (value, ones),
        )
    ]


def stage_kernel(slot, phases, tokd, cosv, sinv, bias, *refs):
    count = len(phases)
    msgs, turned, plain = refs[:count], refs[count : 2 * count], refs[2 * count :]
    for number, phase in enumerate(phases):
        own_bias = bias[phase * HEAD_DIM : (phase + 1) * HEAD_DIM, :]
        values = stage(slot, tokd, msgs[number], cosv, sinv, own_bias)
        for tensor, value in enumerate(values):
            turned[number][tensor] = value
            if tensor > 0:
                plain[number][tensor - 1] = value.T


def attend_kernel(slots, staged, closed, tokd, head, factor, cosv, sinv, masks, bias, *refs):
    msgs, refs = refs[:slots], refs[slots:]
    ready = {slot: refs[2 * at : 2 * at + 2] for at, slot in enumerate(staged)}
    refs = refs[2 * len(staged) :]
    earlier = ()
    if head > 0:
        before, earlier, refs = refs[0], refs[1:slots], refs[slots:]
    outs, sums = refs[:slots], refs[slots]
    for result, out in zip(earlier, [out for slot, out in enumerate(outs) if slot != EARLY]):
        done = head * 4 * HEAD_DIM
        out[:done, :] = result[:done, :]
    qt_all, kt_all, vt_all, gt_all, k_all, v_all, s_buf, e_buf, d_buf = refs[slots + 1 : slots + 10]
    own_bias = bias[head * HEAD_DIM : (head + 1) * HEAD_DIM, :]
    rest_row = lax.broadcasted_iota(jnp.int32, (LANES - HEAD_DIM, tokd), 0)

    by_lanes = (((1,), (1,)), ((), ()))

    def off_row(slot, other):
        row = slot * slots + other
        return masks[row : row + 1, :]

    def live(slot, values):
        if closed:
            return values
        row = slots * slots + slot
        return values * masks[row : row + 1, :]

    def block_of(slot):
        return slice(slot * tokd, (slot + 1) * tokd)

    def put(slot, tensor, values):
        begin = ((0 if slot == EARLY else 4 * head) + tensor) * HEAD_DIM
        outs[slot][begin : begin + HEAD_DIM, :] = values

    def pieces_of(other):
        step = tokd // PIECES
        return [
            slice(other * tokd + number * step, other * tokd + (number + 1) * step)
            for number in range(PIECES)
        ]

    def scores(slot, keys):
        part = jnp.dot(
            k_all[keys, :], qt_all[:, block_of(slot)], preferred_element_type=jnp.float32
        )
        s_buf[slot % 2, keys, :] = part
        return jnp.max(part, axis=0, keepdims=True)

    def exponentials(slot, keys, top):
        part = jnp.exp2(s_buf[slot % 2, keys, :] - top)
        e_buf[keys, block_of(slot)] = part.astype(jnp.bfloat16)

    def output(slot):
        mixed = jnp.dot(
            vt_all[:USED, :], e_buf[:, block_of(slot)], preferred_element_type=jnp.float32
        )
        inv = 1.0 / mixed[HEAD_DIM : HEAD_DIM + 1]
        out_b = (mixed[:HEAD_DIM] * inv).astype(jnp.bfloat16)
        put(slot, 0, out_b)
        grad = msgs[slot][message_rows(3), :].astype(jnp.float32)
        delta = jnp.sum(grad * out_b.astype(jnp.float32), axis=0, keepdims=True) * inv
        coarse = delta.astype(jnp.bfloat16).astype(jnp.float32)
        rest = jnp.where(rest_row == 0, -coarse, jnp.where(rest_row == 1, coarse - delta, 0.0))
        grad = jnp.concatenate([grad * inv, rest], axis=0).astype(jnp.bfloat16)
        gt_all[:, block_of(slot)] = grad
        spread = grad[:HEAD_DIM].astype(jnp.float32) * mixed[HEAD_DIM : HEAD_DIM + 1]
        return grad, live(slot, spread)

    def dscores(slot, keys, grad):
        part = jnp.dot(v_all[keys, :], grad, preferred_element_type=jnp.float32)
        d_buf[keys, block_of(slot)] = e_buf[keys, block_of(slot)] * part.astype(jnp.bfloat16)

    def query_part(slot):
        at = block_of(slot)
        dquery = jnp.dot(kt_all[:HEAD_DIM, :], d_buf[:, at], preferred_element_type=jnp.float32)
        dquery = unrotate(dquery * SCALE, cosv[:, at], sinv[:, at])
        put(slot, 1, dquery.astype(jnp.bfloat16))
        return live(slot, dquery)

    def value_part(slot):
        dvalue = lax.dot_general(
            gt_all[:HEAD_DIM, :],
            e_buf[block_of(slot), :],
            by_lanes,
            preferred_element_type=jnp.float32,
        )
        put(slot, 3, dvalue.astype(jnp.bfloat16))

    for slot in range(slots):
        at = block_of(slot)
        if slot in ready:
            turned, plain = ready[slot]
            values, natural = [turned[number] for number in range(3)], [plain[0], plain[1]]
        else:
            values = stage(slot, tokd, msgs[slot], cosv, sinv, own_bias)
            natural = [value.T for value in values[1:]]
        qt_all[:, at], kt_all[:, at], vt_all[:, at] = values
        k_all[at, :], v_all[at, :] = natural
    dq_total = jnp.zeros((HEAD_DIM, tokd), jnp.float32)
    dv_total = jnp.zeros((HEAD_DIM, tokd), jnp.float32)
    grad = None
    offs = tops = None
    for step in range(slots + 2):
        ahead, slot, behind = step, step - 1, step - 2
        if 0 <= slot < slots:
            offs = [off_row(slot, other) for other in range(slots)]
            top = functools.reduce(jnp.maximum, [one + off for one, off in zip(tops, offs)])
        tops = []
        for other in range(slots):
            found = []
            for keys in pieces_of(other):
                if ahead < slots:
                    found.append(scores(ahead, keys))
                if 0 <= behind:
                    dscores(behind, keys, grad)
                if 0 <= slot < slots:
                    exponentials(slot, keys, top - offs[other])
            if found:
                tops.append(functools.reduce(jnp.maximum, found))
        if 0 <= behind:
            dq_total = dq_total + query_part(behind)
        if 0 <= slot < slots:
            grad, spread = output(slot)
            dv_total = dv_total + spread
    dk_total = jnp.zeros((HEAD_DIM, tokd), jnp.float32)
    for slot in range(slots):
        at = block_of(slot)
        dkey = lax.dot_general(
            qt_all[:HEAD_DIM, :], d_buf[at, :], by_lanes, preferred_element_type=jnp.float32
        )
        dkey = unrotate(dkey * (1.0 / LOG2E), cosv[:, at], sinv[:, at])
        put(slot, 2, dkey.astype(jnp.bfloat16))
        dk_total = dk_total + live(slot, dkey)
    lane = lax.broadcasted_iota(jnp.int32, (HEAD_DIM, LANES), 1)
    columns = jnp.zeros((HEAD_DIM, LANES), jnp.float32)
    for number, total in enumerate((dq_total, dk_total, dv_total)):
        total = jnp.sum(total, axis=1, keepdims=True) * factor
        columns = jnp.where(lane == number, total, columns)
    columns = jnp.concatenate([columns, jnp.zeros((LANES - HEAD_DIM, LANES), jnp.float32)], axis=0)
    lines = columns.T
    copy = None
    if head + 1 < OWN_HEADS:
        sums[...] = lines[:8]
    else:
        tiles, sem = refs[slots + 10 :]
        tile = join_sums(before[...], lines)

        def repeat(device, carry):
            tiles[device] = tile
            return carry

        lax.fori_loop(0, tiles.shape[0], repeat, 0, unroll=min(32, tiles.shape[0]))
        copy = pltpu.make_async_copy(tiles, sums, sem)
        copy.start()
    for slot in range(slots):
        value_part(slot)
    if copy is not None:
        copy.wait()


FIT = LANES - HEAD_DIM
LEFT = HEAD_DIM - FIT


def join_sums(first, second):
    lane = lax.broadcasted_iota(jnp.int32, (1, LANES), 1)
    rows = []
    last = jnp.zeros((1, LANES), jnp.float32)
    for number in range(3):
        moved = pltpu.roll(second[number : number + 1], HEAD_DIM, 1)
        rows.append(jnp.where(lane < HEAD_DIM, first[number : number + 1], moved))
        rest = jnp.where(lane < LEFT, moved, 0.0)
        last = last + (pltpu.roll(rest, number * LEFT, 1) if number else rest)
    return jnp.concatenate(rows + [last], axis=0)


def unpack_kernel(slots, count, images, *refs):
    closed = is_closed(count)
    if not closed:
        lengths, table, *refs = refs
    msgs, refs = refs[: slots + OWN_HEADS - 1], refs[slots + OWN_HEADS - 1 :]
    *outs, held, ready, sems = refs
    early, late = msgs[:OWN_HEADS], list(msgs[OWN_HEADS:])
    late.insert(EARLY, None)
    me = lax.axis_index("tok")

    def place(slot, residue):
        for phase in range(OWN_HEADS):
            begin = pl.multiple_of((phase * SPAN + residue) * HEAD_DIM, 16)
            for number in range(4):
                if slot == EARLY:
                    piece = early[phase][message_rows(number), :]
                else:
                    piece = late[slot][message_rows(4 * phase + number), :]
                held[number, pl.ds(begin, HEAD_DIM), :] = piece

    for slot in range(slots):
        if closed:
            place(slot, lax.rem(me, SPAN) ^ closed_step(slot))
        else:
            _, start = image_of(me, lengths, images)
            source = table[slot, me]
            residue = lax.rem(source + SPAN, SPAN)
            chosen = (source >= 0) & (source == handler_of(start, residue, count))
            pl.when(chosen)(functools.partial(place, slot, residue))
    copies = []
    for number, out in enumerate(outs):
        ready[number] = held[number].T
        copies.append(pltpu.make_async_copy(ready.at[number], out, sems.at[number]))
        copies[-1].start()
    for copy in copies:
        copy.wait()


def bias_kernel(tiles, bias_out):
    def add(group, totals):
        return tuple(
            total + tiles[group * SPAN + residue] for residue, total in enumerate(totals)
        )

    groups = tiles.shape[0] // SPAN
    zero = jnp.zeros(tiles.shape[1:], jnp.float32)
    totals = lax.fori_loop(0, groups, add, (zero,) * SPAN, unroll=groups <= 8)
    for residue, total in enumerate(totals):
        first = residue * HEAD_DIM
        second = (SPAN + residue) * HEAD_DIM
        for number in range(3):
            row = slice(number, number + 1)
            bias_out[row, first : first + HEAD_DIM] = total[row, :HEAD_DIM]
            bias_out[row, second : second + FIT] = total[row, HEAD_DIM:]
            bias_out[row, second + FIT : second + HEAD_DIM] = total[
                3:4, number * LEFT : (number + 1) * LEFT
            ]


def on_device(query_in, key_in, value_in, out_grad, bias, lengths, widths):
    tokd = query_in.shape[1]
    model = query_in.shape[2]
    images = lengths.shape[1]
    count = lax.axis_size("tok")
    dp_size = lax.axis_size("dp")
    closed = is_closed(count)
    sources, targets = trade_tables(count)
    slots = sources.shape[0]
    span = slots * tokd
    table = jnp.asarray(sources)
    quarter = HEAD_DIM // 4
    inverse = rope_base ** (-np.arange(quarter, dtype=np.float64) / quarter)
    inverse = jnp.asarray(np.tile(np.tile(inverse, 2)[:, None], (1, LANES)), jnp.float32)
    smem = pl.BlockSpec(memory_space=pltpu.SMEM)
    vmem = pl.BlockSpec(memory_space=pltpu.VMEM)
    hbm = pl.BlockSpec(memory_space=pltpu.HBM)
    whole = jax.ShapeDtypeStruct((tokd, model), jnp.bfloat16)
    message = jax.ShapeDtypeStruct((4 * HEAD_DIM, tokd), jnp.bfloat16)
    joined = jax.ShapeDtypeStruct((OWN_HEADS * 4 * HEAD_DIM, tokd), jnp.bfloat16)
    devices = dp_size * count
    tokens_all = devices * tokd

    def params(mib):
        return pltpu.CompilerParams(vmem_limit_bytes=int(mib * 1024 * 1024))

    inputs = (query_in[0], key_in[0], value_in[0], out_grad[0])
    sends = pl.pallas_call(
        functools.partial(pack_kernel, closed),
        out_shape=[message] * (OWN_HEADS * slots),
        in_specs=[hbm] * 4,
        out_specs=[vmem] * (OWN_HEADS * slots),
        scratch_shapes=[
            pltpu.VMEM((4, tokd, model), jnp.bfloat16),
            pltpu.VMEM((4, model, tokd), jnp.bfloat16),
            pltpu.SemaphoreType.DMA((4,)),
        ],
        compiler_params=params(PACK_KIB / 1024),
        name="pack_heads",
    )(*inputs)
    rounds = trade_rounds(count)
    first = [sends[0]] + [
        lax.ppermute(send, "tok", pairs) for send, pairs in zip(sends[1:slots], rounds)
    ]
    table_shape = jax.ShapeDtypeStruct((HALF, span), jnp.float32)
    mask_rows = -(-slots * (slots + 1) // 8) * 8
    tables = pl.pallas_call(
        functools.partial(tables_kernel, images, count, tokd),
        out_shape=[table_shape] * 2
        + [
            jax.ShapeDtypeStruct((mask_rows, tokd), jnp.float32),
            jax.ShapeDtypeStruct((OWN_HEADS * HEAD_DIM, LANES), jnp.float32),
        ],
        in_specs=[smem, smem, smem, vmem, vmem],
        out_specs=[vmem] * 4,
        scratch_shapes=[pltpu.VMEM((model, LANES), jnp.float32)],
        compiler_params=params(16),
        cost_estimate=pl.CostEstimate(
            flops=span * LANES * 200, bytes_accessed=0, transcendentals=0
        ),
        name="rotary_tables",
    )(lengths, widths, table, inverse, bias)

    def stage_ahead(slot, phases, messages):
        number = len(phases)
        results = pl.pallas_call(
            functools.partial(stage_kernel, slot, phases, tokd),
            out_shape=[jax.ShapeDtypeStruct((3, LANES, tokd), jnp.bfloat16)] * number
            + [jax.ShapeDtypeStruct((2, tokd, LANES), jnp.bfloat16)] * number,
            in_specs=[vmem] * (3 + number),
            out_specs=[vmem] * (2 * number),
            compiler_params=params(16),
            cost_estimate=pl.CostEstimate(
                flops=1_000_000 * number, bytes_accessed=0, transcendentals=0
            ),
            name="stage_slot",
        )(tables[0], tables[1], tables[3], *messages)
        return [list(pair) for pair in zip(results[:number], results[number:])]

    phases = tuple(range(OWN_HEADS))
    own = stage_ahead(0, phases, [sends[phase * slots] for phase in phases])
    staged = [{0: pair} for pair in own]
    got = [first] + [[sends[phase * slots]] for phase in phases[1:]]
    latest = own
    for slot in range(1, slots):
        for phase in phases[1:]:
            send, latest = lax.optimization_barrier((sends[phase * slots + slot], latest))
            got[phase].append(lax.ppermute(send, "tok", rounds[slot - 1]))
        if slot == 1:
            staged[0][0], staged[1][0] = latest
        else:
            staged[0][slot - 1] = latest[0]
        if slot + 1 < slots:
            latest = stage_ahead(slot, (0,), [first[slot]])
    early = []
    carried = []
    for phase in range(OWN_HEADS):
        last = phase + 1 == OWN_HEADS
        kept = [slot for slot in range(slots) if slot != EARLY]
        sums_shape = jax.ShapeDtypeStruct(
            (devices, 4, LANES) if last else (8, LANES), jnp.float32
        )
        *results, total = pl.pallas_call(
            functools.partial(
                attend_kernel,
                slots,
                tuple(staged[phase]),
                closed,
                tokd,
                phase,
                1.0 / tokens_all**0.5,
            ),
            out_shape=[message if slot == EARLY else joined for slot in range(slots)]
            + [sums_shape],
            in_specs=[vmem] * (4 + slots + 2 * len(staged[phase]) + len(carried)),
            out_specs=[vmem] * slots + [hbm if last else vmem],
            scratch_shapes=[pltpu.VMEM((LANES, span), jnp.bfloat16)] * 4
            + [pltpu.VMEM((span, LANES), jnp.bfloat16)] * 2
            + [pltpu.VMEM((2, span, tokd), jnp.float32)]
            + [pltpu.VMEM((span, span), jnp.bfloat16)] * 2
            + (
                [pltpu.VMEM(sums_shape.shape, jnp.float32), pltpu.SemaphoreType.DMA(())]
                if last
                else []
            ),
            compiler_params=params(32),
            cost_estimate=pl.CostEstimate(
                flops=12 * span * span * 256, bytes_accessed=0, transcendentals=0
            ),
            name="attend_head",
        )(*tables, *got[phase], *(one for pair in staged[phase].values() for one in pair), *carried)
        results, total, early = lax.optimization_barrier((results, total, early))
        early.append(send_back(results[EARLY], EARLY))
        carried = [total] + [results[slot] for slot in kept]
    tiles = lax.all_to_all(total, ("dp", "tok"), 0, 0, tiled=True)
    late = [send_back(results[slot], slot) for slot in kept]
    places = [] if closed else [lengths, jnp.asarray(targets)]
    outs = pl.pallas_call(
        functools.partial(unpack_kernel, slots, count, images),
        out_shape=[whole] * 4,
        in_specs=[smem] * len(places) + [vmem] * (OWN_HEADS + len(late)),
        out_specs=[hbm] * 4,
        scratch_shapes=[
            pltpu.VMEM((4, model, tokd), jnp.bfloat16),
            pltpu.VMEM((4, tokd, model), jnp.bfloat16),
            pltpu.SemaphoreType.DMA((4,)),
        ],
        compiler_params=params(16),
        cost_estimate=pl.CostEstimate(flops=UNPACK_FLOPS, bytes_accessed=0, transcendentals=0),
        name="unpack_heads",
    )(*places, *early, *late)
    outs, tiles = lax.optimization_barrier((outs, tiles))
    bias_grad = pl.pallas_call(
        bias_kernel,
        out_shape=jax.ShapeDtypeStruct((3, model), jnp.float32),
        in_specs=[vmem],
        out_specs=vmem,
        compiler_params=params(16),
        name="bias_sums",
    )(tiles)
    return tuple(out[None] for out in outs) + (bias_grad,)


def solution(mesh):
    in_specs = (
        P("dp", "tok", None),
        P("dp", "tok", None),
        P("dp", "tok", None),
        P("dp", "tok", None),
        P(),
        P("dp", None),
        P("dp", None),
    )
    out_specs = (
        P("dp", "tok", None),
        P("dp", "tok", None),
        P("dp", "tok", None),
        P("dp", "tok", None),
        P(),
    )
    return jax.shard_map(
        on_device, mesh=mesh, in_specs=in_specs, out_specs=out_specs, check_vma=False
    )
```

```python
import functools

import jax
import jax.numpy as jnp
import numpy as np
from jax import lax
from jax.experimental import pallas as pl
from jax.experimental.pallas import tpu as pltpu
from jax.sharding import PartitionSpec as P

HEADS = 8
HEAD_DIM = 80
SPAN = 4
OWN_HEADS = HEADS // SPAN
PART = OWN_HEADS * HEAD_DIM
SCALE = HEAD_DIM**-0.5
LOG2E = 1.4426950408889634
NEG = -1e30
LANES = 128
USED = HEAD_DIM + 16
HALF = HEAD_DIM // 2
PIECES = 2
PACK_KIB = 52 * 1024 + 600
UNPACK_FLOPS = 20_000_000_000

rope_base = 10000.0


def is_closed(count):
    return count in (SPAN, 2 * SPAN)


def closed_step(slot):
    return (SPAN - slot) % SPAN


def trade_rounds(count):
    if is_closed(count):
        return [
            [(one, one ^ closed_step(slot)) for one in range(count)] for slot in range(1, SPAN)
        ]
    rounds = []
    for shift in [*range(1, SPAN), *range(-1, -SPAN, -1)]:
        rounds.append(
            [
                (source, source + shift)
                for source in range(max(0, -shift), min(count, count - shift))
                if (source < SPAN) == (source + shift < SPAN)
            ]
        )
    return rounds


def trade_tables(count):
    rounds = trade_rounds(count)
    sources = np.full((1 + len(rounds), count), -1, np.int32)
    targets = sources.copy()
    sources[0] = targets[0] = np.arange(count)
    for slot, pairs in enumerate(rounds, 1):
        for source, target in pairs:
            sources[slot, target] = source
            targets[slot, source] = target
    return sources, targets


def send_back(result, slot):
    if slot == 0:
        return result
    pairs = trade_rounds(lax.axis_size("tok"))[slot - 1]
    return lax.ppermute(result, "tok", [(target, source) for source, target in pairs])


EARLY = 1


def image_of(block, lengths, images):
    image = jnp.int32(0)
    start = jnp.int32(0)
    begin = jnp.int32(0)
    for number in range(images):
        size = lengths[0, number]
        inside = (block >= begin) & (block < begin + size)
        image = jnp.where(inside, number, image)
        start = jnp.where(inside, begin, start)
        begin = begin + size
    return image, start


def handler_of(start, residue, count):
    device = start + lax.rem(residue - lax.rem(start, SPAN) + SPAN, SPAN)
    return jnp.where(device >= count, device - SPAN, device)


def message_rows(tensor):
    return slice(tensor * HEAD_DIM, (tensor + 1) * HEAD_DIM)


def rotate(values, cosv, sinv):
    first, second = values[:HALF], values[HALF:]
    return jnp.concatenate([first * cosv - second * sinv, second * cosv + first * sinv], axis=0)


def unrotate(values, cosv, sinv):
    first, second = values[:HALF], values[HALF:]
    return jnp.concatenate([first * cosv + second * sinv, second * cosv - first * sinv], axis=0)


def pack_kernel(closed, *refs):
    inputs, outs, held, turned, sems = refs[:4], refs[4:-3], refs[-3], refs[-2], refs[-1]
    copies = [
        pltpu.make_async_copy(source, held.at[number], sems.at[number])
        for number, source in enumerate(inputs)
    ]
    for copy in copies:
        copy.start()
    me = lax.rem(lax.axis_index("tok"), SPAN)
    steps = (
        [closed_step(slot) for slot in range(SPAN)]
        if closed
        else [0, *range(1, SPAN), *range(SPAN - 1, 0, -1)]
    )
    for number, copy in enumerate(copies):
        copy.wait()
        turned[number] = held[number].T
        for phase in range(OWN_HEADS):
            for slot, step in enumerate(steps):
                residue = me ^ step if closed else lax.rem(me + step, SPAN)
                begin = pl.multiple_of((phase * SPAN + residue) * HEAD_DIM, 16)
                outs[phase * len(steps) + slot][message_rows(number), :] = turned[
                    number, pl.ds(begin, HEAD_DIM), :
                ]


def tables_kernel(images, count, tokd, lengths, widths, table, inverse, bias, *refs):
    cos_out, sin_out, mask_out, bias_out, turned = refs
    me = lax.axis_index("tok")
    residue = lax.rem(me, SPAN)
    slots = table.shape[0]
    spot = lax.broadcasted_iota(jnp.int32, (HALF, tokd), 1)
    by_row = lax.broadcasted_iota(jnp.int32, (HALF, tokd), 0) < HALF // 2
    ids = []
    for slot in range(slots):
        block = table[slot, me]
        image, start = image_of(block, lengths, images)
        handled = (block >= 0) & (handler_of(start, residue, count) == me)
        ids.append(jnp.where(handled, image, -1 - slot))
        width = widths[0, image]
        bits = jnp.where(width == tokd, 0, jnp.where(width * 2 == tokd, 1, 2))
        shift = tokd.bit_length() - 1 - bits
        local = spot + (block - start) * tokd
        rowpos = lax.shift_right_logical(local, jnp.broadcast_to(shift, local.shape))
        colpos = local & (width - 1)
        angle = jnp.where(by_row, rowpos, colpos).astype(jnp.float32) * inverse[:, 0:1]
        cos_out[:, slot * tokd : (slot + 1) * tokd] = jnp.cos(angle)
        sin_out[:, slot * tokd : (slot + 1) * tokd] = jnp.sin(angle)
    for slot in range(slots):
        for other in range(slots):
            off = jnp.where(ids[slot] == ids[other], 0.0, NEG)
            row = slot * slots + other
            mask_out[row : row + 1, :] = jnp.full((1, tokd), off, jnp.float32)
        row = slots * slots + slot
        live = jnp.where(ids[slot] >= 0, 1.0, 0.0)
        mask_out[row : row + 1, :] = jnp.full((1, tokd), live, jnp.float32)
    plain = bias[...].astype(jnp.float32)
    rest = jnp.zeros((LANES - plain.shape[0], plain.shape[1]), jnp.float32)
    turned[...] = jnp.concatenate([plain, rest], axis=0).T
    for phase in range(OWN_HEADS):
        begin = pl.multiple_of((phase * SPAN + residue) * HEAD_DIM, 16)
        bias_out[phase * HEAD_DIM : (phase + 1) * HEAD_DIM, :] = turned[pl.ds(begin, HEAD_DIM), :]


def stage(slot, tokd, message, cosv, sinv, bias):
    at = slice(slot * tokd, (slot + 1) * tokd)
    cos_b, sin_b = cosv[:, at], sinv[:, at]
    query, key, value = (
        message[message_rows(tensor), :].astype(jnp.float32) + bias[:, tensor : tensor + 1]
        for tensor in range(3)
    )
    rest_row = lax.broadcasted_iota(jnp.int32, (LANES - HEAD_DIM, tokd), 0)
    zeros = jnp.zeros((LANES - HEAD_DIM, tokd), jnp.float32)
    ones = jnp.where(rest_row < 2, 1.0, 0.0)
    return [
        jnp.concatenate(pair, axis=0).astype(jnp.bfloat16)
        for pair in (
            (rotate(query, cos_b, sin_b) * (SCALE * LOG2E), zeros),
            (rotate(key, cos_b, sin_b), zeros),
            (value, ones),
        )
    ]


def stage_kernel(slot, phases, tokd, cosv, sinv, bias, *refs):
    count = len(phases)
    msgs, turned, plain = refs[:count], refs[count : 2 * count], refs[2 * count :]
    for number, phase in enumerate(phases):
        own_bias = bias[phase * HEAD_DIM : (phase + 1) * HEAD_DIM, :]
        values = stage(slot, tokd, msgs[number], cosv, sinv, own_bias)
        for tensor, value in enumerate(values):
            turned[number][tensor] = value
            if tensor > 0:
                plain[number][tensor - 1] = value.T


def attend_kernel(slots, staged, closed, tokd, head, factor, cosv, sinv, masks, bias, *refs):
    msgs, refs = refs[:slots], refs[slots:]
    ready = {slot: refs[2 * at : 2 * at + 2] for at, slot in enumerate(staged)}
    refs = refs[2 * len(staged) :]
    earlier = ()
    if head > 0:
        before, earlier, refs = refs[0], refs[1:slots], refs[slots:]
    outs, sums = refs[:slots], refs[slots]
    for result, out in zip(earlier, [out for slot, out in enumerate(outs) if slot != EARLY]):
        done = head * 4 * HEAD_DIM
        out[:done, :] = result[:done, :]
    qt_all, kt_all, vt_all, g_all, k_all, v_all, s_buf, e_buf, d_buf = refs[slots + 1 : slots + 10]
    own_bias = bias[head * HEAD_DIM : (head + 1) * HEAD_DIM, :]
    rest_row = lax.broadcasted_iota(jnp.int32, (LANES - HEAD_DIM, tokd), 0)

    by_lanes = (((1,), (1,)), ((), ()))

    def off_row(slot, other):
        row = slot * slots + other
        return masks[row : row + 1, :]

    def live(slot, values):
        if closed:
            return values
        row = slots * slots + slot
        return values * masks[row : row + 1, :]

    def block_of(slot):
        return slice(slot * tokd, (slot + 1) * tokd)

    def put(slot, tensor, values):
        begin = ((0 if slot == EARLY else 4 * head) + tensor) * HEAD_DIM
        outs[slot][begin : begin + HEAD_DIM, :] = values

    def pieces_of(other):
        step = tokd // PIECES
        return [
            slice(other * tokd + number * step, other * tokd + (number + 1) * step)
            for number in range(PIECES)
        ]

    def scores(slot, keys):
        part = jnp.dot(
            k_all[keys, :], qt_all[:, block_of(slot)], preferred_element_type=jnp.float32
        )
        s_buf[slot % 2, keys, :] = part
        return jnp.max(part, axis=0, keepdims=True)

    def exponentials(slot, keys, top):
        part = jnp.exp2(s_buf[slot % 2, keys, :] - top)
        e_buf[keys, block_of(slot)] = part.astype(jnp.bfloat16)

    def output(slot):
        mixed = jnp.dot(
            vt_all[:USED, :], e_buf[:, block_of(slot)], preferred_element_type=jnp.float32
        )
        inv = 1.0 / mixed[HEAD_DIM : HEAD_DIM + 1]
        out_b = (mixed[:HEAD_DIM] * inv).astype(jnp.bfloat16)
        put(slot, 0, out_b)
        grad = msgs[slot][message_rows(3), :].astype(jnp.float32)
        delta = jnp.sum(grad * out_b.astype(jnp.float32), axis=0, keepdims=True) * inv
        coarse = delta.astype(jnp.bfloat16).astype(jnp.float32)
        rest = jnp.where(rest_row == 0, -coarse, jnp.where(rest_row == 1, coarse - delta, 0.0))
        grad = jnp.concatenate([grad * inv, rest], axis=0).astype(jnp.bfloat16)
        g_all[block_of(slot), :] = grad.T
        spread = grad[:HEAD_DIM].astype(jnp.float32) * mixed[HEAD_DIM : HEAD_DIM + 1]
        return grad, live(slot, spread)

    def dscores(slot, keys, grad):
        part = jnp.dot(v_all[keys, :], grad, preferred_element_type=jnp.float32)
        d_buf[keys, block_of(slot)] = e_buf[keys, block_of(slot)] * part.astype(jnp.bfloat16)

    def query_part(slot):
        at = block_of(slot)
        dquery = jnp.dot(kt_all[:HEAD_DIM, :], d_buf[:, at], preferred_element_type=jnp.float32)
        dquery = unrotate(dquery * SCALE, cosv[:, at], sinv[:, at])
        put(slot, 1, dquery.astype(jnp.bfloat16))
        return live(slot, dquery)

    def value_part(slot):
        dvalue = jnp.dot(
            e_buf[block_of(slot), :], g_all[...], preferred_element_type=jnp.float32
        )
        put(slot, 3, dvalue.astype(jnp.bfloat16).T[:HEAD_DIM])

    for slot in range(slots):
        at = block_of(slot)
        if slot in ready:
            turned, plain = ready[slot]
            values, natural = [turned[number] for number in range(3)], [plain[0], plain[1]]
        else:
            values = stage(slot, tokd, msgs[slot], cosv, sinv, own_bias)
            natural = [value.T for value in values[1:]]
        qt_all[:, at], kt_all[:, at], vt_all[:, at] = values
        k_all[at, :], v_all[at, :] = natural
    dq_total = jnp.zeros((HEAD_DIM, tokd), jnp.float32)
    dv_total = jnp.zeros((HEAD_DIM, tokd), jnp.float32)
    grad = None
    offs = tops = None
    for step in range(slots + 2):
        ahead, slot, behind = step, step - 1, step - 2
        if 0 <= slot < slots:
            offs = [off_row(slot, other) for other in range(slots)]
            top = functools.reduce(jnp.maximum, [one + off for one, off in zip(tops, offs)])
        tops = []
        for other in range(slots):
            found = []
            for keys in pieces_of(other):
                if ahead < slots:
                    found.append(scores(ahead, keys))
                if 0 <= behind:
                    dscores(behind, keys, grad)
                if 0 <= slot < slots:
                    exponentials(slot, keys, top - offs[other])
            if found:
                tops.append(functools.reduce(jnp.maximum, found))
        if 0 <= behind:
            dq_total = dq_total + query_part(behind)
        if 0 <= slot < slots:
            grad, spread = output(slot)
            dv_total = dv_total + spread
    dk_total = jnp.zeros((HEAD_DIM, tokd), jnp.float32)
    for slot in range(slots):
        at = block_of(slot)
        dkey = lax.dot_general(
            qt_all[:HEAD_DIM, :], d_buf[at, :], by_lanes, preferred_element_type=jnp.float32
        )
        dkey = unrotate(dkey * (1.0 / LOG2E), cosv[:, at], sinv[:, at])
        put(slot, 2, dkey.astype(jnp.bfloat16))
        dk_total = dk_total + live(slot, dkey)
    lane = lax.broadcasted_iota(jnp.int32, (HEAD_DIM, LANES), 1)
    columns = jnp.zeros((HEAD_DIM, LANES), jnp.float32)
    for number, total in enumerate((dq_total, dk_total, dv_total)):
        total = jnp.sum(total, axis=1, keepdims=True) * factor
        columns = jnp.where(lane == number, total, columns)
    columns = jnp.concatenate([columns, jnp.zeros((LANES - HEAD_DIM, LANES), jnp.float32)], axis=0)
    lines = columns.T
    copy = None
    if head + 1 < OWN_HEADS:
        sums[...] = lines[:8]
    else:
        tiles, sem = refs[slots + 10 :]
        tile = join_sums(before[...], lines)

        def repeat(device, carry):
            tiles[device] = tile
            return carry

        lax.fori_loop(0, tiles.shape[0], repeat, 0, unroll=min(32, tiles.shape[0]))
        copy = pltpu.make_async_copy(tiles, sums, sem)
        copy.start()
    for slot in range(slots):
        value_part(slot)
    if copy is not None:
        copy.wait()


FIT = LANES - HEAD_DIM
LEFT = HEAD_DIM - FIT


def join_sums(first, second):
    lane = lax.broadcasted_iota(jnp.int32, (1, LANES), 1)
    rows = []
    last = jnp.zeros((1, LANES), jnp.float32)
    for number in range(3):
        moved = pltpu.roll(second[number : number + 1], HEAD_DIM, 1)
        rows.append(jnp.where(lane < HEAD_DIM, first[number : number + 1], moved))
        rest = jnp.where(lane < LEFT, moved, 0.0)
        last = last + (pltpu.roll(rest, number * LEFT, 1) if number else rest)
    return jnp.concatenate(rows + [last], axis=0)


def unpack_kernel(slots, count, images, *refs):
    closed = is_closed(count)
    if not closed:
        lengths, table, *refs = refs
    msgs, refs = refs[: slots + OWN_HEADS - 1], refs[slots + OWN_HEADS - 1 :]
    *outs, held, ready, sems = refs
    early, late = msgs[:OWN_HEADS], list(msgs[OWN_HEADS:])
    late.insert(EARLY, None)
    me = lax.axis_index("tok")

    def place(slot, residue):
        for phase in range(OWN_HEADS):
            begin = pl.multiple_of((phase * SPAN + residue) * HEAD_DIM, 16)
            for number in range(4):
                if slot == EARLY:
                    piece = early[phase][message_rows(number), :]
                else:
                    piece = late[slot][message_rows(4 * phase + number), :]
                held[number, pl.ds(begin, HEAD_DIM), :] = piece

    for slot in range(slots):
        if closed:
            place(slot, lax.rem(me, SPAN) ^ closed_step(slot))
        else:
            _, start = image_of(me, lengths, images)
            source = table[slot, me]
            residue = lax.rem(source + SPAN, SPAN)
            chosen = (source >= 0) & (source == handler_of(start, residue, count))
            pl.when(chosen)(functools.partial(place, slot, residue))
    copies = []
    for number, out in enumerate(outs):
        ready[number] = held[number].T
        copies.append(pltpu.make_async_copy(ready.at[number], out, sems.at[number]))
        copies[-1].start()
    for copy in copies:
        copy.wait()


def bias_kernel(tiles, bias_out):
    def add(group, totals):
        return tuple(
            total + tiles[group * SPAN + residue] for residue, total in enumerate(totals)
        )

    groups = tiles.shape[0] // SPAN
    zero = jnp.zeros(tiles.shape[1:], jnp.float32)
    totals = lax.fori_loop(0, groups, add, (zero,) * SPAN, unroll=groups <= 8)
    for residue, total in enumerate(totals):
        first = residue * HEAD_DIM
        second = (SPAN + residue) * HEAD_DIM
        for number in range(3):
            row = slice(number, number + 1)
            bias_out[row, first : first + HEAD_DIM] = total[row, :HEAD_DIM]
            bias_out[row, second : second + FIT] = total[row, HEAD_DIM:]
            bias_out[row, second + FIT : second + HEAD_DIM] = total[
                3:4, number * LEFT : (number + 1) * LEFT
            ]


def on_device(query_in, key_in, value_in, out_grad, bias, lengths, widths):
    tokd = query_in.shape[1]
    model = query_in.shape[2]
    images = lengths.shape[1]
    count = lax.axis_size("tok")
    dp_size = lax.axis_size("dp")
    closed = is_closed(count)
    sources, targets = trade_tables(count)
    slots = sources.shape[0]
    span = slots * tokd
    table = jnp.asarray(sources)
    quarter = HEAD_DIM // 4
    inverse = rope_base ** (-np.arange(quarter, dtype=np.float64) / quarter)
    inverse = jnp.asarray(np.tile(np.tile(inverse, 2)[:, None], (1, LANES)), jnp.float32)
    smem = pl.BlockSpec(memory_space=pltpu.SMEM)
    vmem = pl.BlockSpec(memory_space=pltpu.VMEM)
    hbm = pl.BlockSpec(memory_space=pltpu.HBM)
    whole = jax.ShapeDtypeStruct((tokd, model), jnp.bfloat16)
    message = jax.ShapeDtypeStruct((4 * HEAD_DIM, tokd), jnp.bfloat16)
    joined = jax.ShapeDtypeStruct((OWN_HEADS * 4 * HEAD_DIM, tokd), jnp.bfloat16)
    devices = dp_size * count
    tokens_all = devices * tokd

    def params(mib):
        return pltpu.CompilerParams(vmem_limit_bytes=int(mib * 1024 * 1024))

    inputs = (query_in[0], key_in[0], value_in[0], out_grad[0])
    sends = pl.pallas_call(
        functools.partial(pack_kernel, closed),
        out_shape=[message] * (OWN_HEADS * slots),
        in_specs=[hbm] * 4,
        out_specs=[vmem] * (OWN_HEADS * slots),
        scratch_shapes=[
            pltpu.VMEM((4, tokd, model), jnp.bfloat16),
            pltpu.VMEM((4, model, tokd), jnp.bfloat16),
            pltpu.SemaphoreType.DMA((4,)),
        ],
        compiler_params=params(PACK_KIB / 1024),
        name="pack_heads",
    )(*inputs)
    rounds = trade_rounds(count)
    first = [sends[0]] + [
        lax.ppermute(send, "tok", pairs) for send, pairs in zip(sends[1:slots], rounds)
    ]
    table_shape = jax.ShapeDtypeStruct((HALF, span), jnp.float32)
    mask_rows = -(-slots * (slots + 1) // 8) * 8
    tables = pl.pallas_call(
        functools.partial(tables_kernel, images, count, tokd),
        out_shape=[table_shape] * 2
        + [
            jax.ShapeDtypeStruct((mask_rows, tokd), jnp.float32),
            jax.ShapeDtypeStruct((OWN_HEADS * HEAD_DIM, LANES), jnp.float32),
        ],
        in_specs=[smem, smem, smem, vmem, vmem],
        out_specs=[vmem] * 4,
        scratch_shapes=[pltpu.VMEM((model, LANES), jnp.float32)],
        compiler_params=params(16),
        cost_estimate=pl.CostEstimate(
            flops=span * LANES * 200, bytes_accessed=0, transcendentals=0
        ),
        name="rotary_tables",
    )(lengths, widths, table, inverse, bias)

    def stage_ahead(slot, phases, messages):
        number = len(phases)
        results = pl.pallas_call(
            functools.partial(stage_kernel, slot, phases, tokd),
            out_shape=[jax.ShapeDtypeStruct((3, LANES, tokd), jnp.bfloat16)] * number
            + [jax.ShapeDtypeStruct((2, tokd, LANES), jnp.bfloat16)] * number,
            in_specs=[vmem] * (3 + number),
            out_specs=[vmem] * (2 * number),
            compiler_params=params(16),
            cost_estimate=pl.CostEstimate(
                flops=1_000_000 * number, bytes_accessed=0, transcendentals=0
            ),
            name="stage_slot",
        )(tables[0], tables[1], tables[3], *messages)
        return [list(pair) for pair in zip(results[:number], results[number:])]

    phases = tuple(range(OWN_HEADS))
    own = stage_ahead(0, phases, [sends[phase * slots] for phase in phases])
    staged = [{0: pair} for pair in own]
    got = [first] + [[sends[phase * slots]] for phase in phases[1:]]
    latest = own
    for slot in range(1, slots):
        for phase in phases[1:]:
            send, latest = lax.optimization_barrier((sends[phase * slots + slot], latest))
            got[phase].append(lax.ppermute(send, "tok", rounds[slot - 1]))
        if slot == 1:
            staged[0][0], staged[1][0] = latest
        else:
            staged[0][slot - 1] = latest[0]
        if slot + 1 < slots:
            latest = stage_ahead(slot, (0,), [first[slot]])
    early = []
    carried = []
    for phase in range(OWN_HEADS):
        last = phase + 1 == OWN_HEADS
        kept = [slot for slot in range(slots) if slot != EARLY]
        sums_shape = jax.ShapeDtypeStruct(
            (devices, 4, LANES) if last else (8, LANES), jnp.float32
        )
        *results, total = pl.pallas_call(
            functools.partial(
                attend_kernel,
                slots,
                tuple(staged[phase]),
                closed,
                tokd,
                phase,
                1.0 / tokens_all**0.5,
            ),
            out_shape=[message if slot == EARLY else joined for slot in range(slots)]
            + [sums_shape],
            in_specs=[vmem] * (4 + slots + 2 * len(staged[phase]) + len(carried)),
            out_specs=[vmem] * slots + [hbm if last else vmem],
            scratch_shapes=[pltpu.VMEM((LANES, span), jnp.bfloat16)] * 3
            + [pltpu.VMEM((span, LANES), jnp.bfloat16)] * 3
            + [pltpu.VMEM((2, span, tokd), jnp.float32)]
            + [pltpu.VMEM((span, span), jnp.bfloat16)] * 2
            + (
                [pltpu.VMEM(sums_shape.shape, jnp.float32), pltpu.SemaphoreType.DMA(())]
                if last
                else []
            ),
            compiler_params=params(32),
            cost_estimate=pl.CostEstimate(
                flops=12 * span * span * 256, bytes_accessed=0, transcendentals=0
            ),
            name="attend_head",
        )(*tables, *got[phase], *(one for pair in staged[phase].values() for one in pair), *carried)
        results[EARLY], early = lax.optimization_barrier((results[EARLY], early))
        early.append(send_back(results[EARLY], EARLY))
        carried = [total] + [results[slot] for slot in kept]
    tiles = lax.all_to_all(total, ("dp", "tok"), 0, 0, tiled=True)
    late = [send_back(results[slot], slot) for slot in kept]
    places = [] if closed else [lengths, jnp.asarray(targets)]
    outs = pl.pallas_call(
        functools.partial(unpack_kernel, slots, count, images),
        out_shape=[whole] * 4,
        in_specs=[smem] * len(places) + [vmem] * (OWN_HEADS + len(late)),
        out_specs=[hbm] * 4,
        scratch_shapes=[
            pltpu.VMEM((4, model, tokd), jnp.bfloat16),
            pltpu.VMEM((4, tokd, model), jnp.bfloat16),
            pltpu.SemaphoreType.DMA((4,)),
        ],
        compiler_params=params(16),
        cost_estimate=pl.CostEstimate(flops=UNPACK_FLOPS, bytes_accessed=0, transcendentals=0),
        name="unpack_heads",
    )(*places, *early, *late)
    outs, tiles = lax.optimization_barrier((outs, tiles))
    bias_grad = pl.pallas_call(
        bias_kernel,
        out_shape=jax.ShapeDtypeStruct((3, model), jnp.float32),
        in_specs=[vmem],
        out_specs=vmem,
        compiler_params=params(16),
        name="bias_sums",
    )(tiles)
    return tuple(out[None] for out in outs) + (bias_grad,)


def solution(mesh):
    in_specs = (
        P("dp", "tok", None),
        P("dp", "tok", None),
        P("dp", "tok", None),
        P("dp", "tok", None),
        P(),
        P("dp", None),
        P("dp", None),
    )
    out_specs = (
        P("dp", "tok", None),
        P("dp", "tok", None),
        P("dp", "tok", None),
        P("dp", "tok", None),
        P(),
    )
    return jax.shard_map(
        on_device, mesh=mesh, in_specs=in_specs, out_specs=out_specs, check_vma=False
    )
```

```python
import functools

import jax
import jax.numpy as jnp
import numpy as np
from jax import lax
from jax.experimental import pallas as pl
from jax.experimental.pallas import tpu as pltpu
from jax.sharding import PartitionSpec as P

HEADS = 8
HEAD_DIM = 80
SPAN = 4
OWN_HEADS = HEADS // SPAN
PART = OWN_HEADS * HEAD_DIM
SCALE = HEAD_DIM**-0.5
LOG2E = 1.4426950408889634
NEG = -1e30
LANES = 128
USED = HEAD_DIM + 16
HALF = HEAD_DIM // 2
PIECES = 2
PACK_KIB = 52 * 1024 + 600
UNPACK_FLOPS = 20_000_000_000

rope_base = 10000.0


def is_closed(count):
    return count in (SPAN, 2 * SPAN)


def closed_step(slot):
    return (SPAN - slot) % SPAN


def trade_rounds(count):
    if is_closed(count):
        return [
            [(one, one ^ closed_step(slot)) for one in range(count)] for slot in range(1, SPAN)
        ]
    rounds = []
    for shift in [*range(1, SPAN), *range(-1, -SPAN, -1)]:
        rounds.append(
            [
                (source, source + shift)
                for source in range(max(0, -shift), min(count, count - shift))
                if (source < SPAN) == (source + shift < SPAN)
            ]
        )
    return rounds


def trade_tables(count):
    rounds = trade_rounds(count)
    sources = np.full((1 + len(rounds), count), -1, np.int32)
    targets = sources.copy()
    sources[0] = targets[0] = np.arange(count)
    for slot, pairs in enumerate(rounds, 1):
        for source, target in pairs:
            sources[slot, target] = source
            targets[slot, source] = target
    return sources, targets


def send_back(result, slot):
    if slot == 0:
        return result
    pairs = trade_rounds(lax.axis_size("tok"))[slot - 1]
    return lax.ppermute(result, "tok", [(target, source) for source, target in pairs])


EARLY = 1


def image_of(block, lengths, images):
    image = jnp.int32(0)
    start = jnp.int32(0)
    begin = jnp.int32(0)
    for number in range(images):
        size = lengths[0, number]
        inside = (block >= begin) & (block < begin + size)
        image = jnp.where(inside, number, image)
        start = jnp.where(inside, begin, start)
        begin = begin + size
    return image, start


def handler_of(start, residue, count):
    device = start + lax.rem(residue - lax.rem(start, SPAN) + SPAN, SPAN)
    return jnp.where(device >= count, device - SPAN, device)


def message_rows(tensor):
    return slice(tensor * HEAD_DIM, (tensor + 1) * HEAD_DIM)


def rotate(values, cosv, sinv):
    first, second = values[:HALF], values[HALF:]
    return jnp.concatenate([first * cosv - second * sinv, second * cosv + first * sinv], axis=0)


def unrotate(values, cosv, sinv):
    first, second = values[:HALF], values[HALF:]
    return jnp.concatenate([first * cosv + second * sinv, second * cosv - first * sinv], axis=0)


def pack_kernel(closed, *refs):
    inputs, outs, held, turned, sems = refs[:4], refs[4:-3], refs[-3], refs[-2], refs[-1]
    copies = [
        pltpu.make_async_copy(source, held.at[number], sems.at[number])
        for number, source in enumerate(inputs)
    ]
    for copy in copies:
        copy.start()
    me = lax.rem(lax.axis_index("tok"), SPAN)
    steps = (
        [closed_step(slot) for slot in range(SPAN)]
        if closed
        else [0, *range(1, SPAN), *range(SPAN - 1, 0, -1)]
    )
    for number, copy in enumerate(copies):
        copy.wait()
        turned[number] = held[number].T
        for phase in range(OWN_HEADS):
            for slot, step in enumerate(steps):
                residue = me ^ step if closed else lax.rem(me + step, SPAN)
                begin = pl.multiple_of((phase * SPAN + residue) * HEAD_DIM, 16)
                outs[phase * len(steps) + slot][message_rows(number), :] = turned[
                    number, pl.ds(begin, HEAD_DIM), :
                ]


def tables_kernel(images, count, tokd, lengths, widths, table, inverse, bias, *refs):
    cos_out, sin_out, mask_out, bias_out, turned = refs
    me = lax.axis_index("tok")
    residue = lax.rem(me, SPAN)
    slots = table.shape[0]
    spot = lax.broadcasted_iota(jnp.int32, (HALF, tokd), 1)
    by_row = lax.broadcasted_iota(jnp.int32, (HALF, tokd), 0) < HALF // 2
    ids = []
    for slot in range(slots):
        block = table[slot, me]
        image, start = image_of(block, lengths, images)
        handled = (block >= 0) & (handler_of(start, residue, count) == me)
        ids.append(jnp.where(handled, image, -1 - slot))
        width = widths[0, image]
        bits = jnp.where(width == tokd, 0, jnp.where(width * 2 == tokd, 1, 2))
        shift = tokd.bit_length() - 1 - bits
        local = spot + (block - start) * tokd
        rowpos = lax.shift_right_logical(local, jnp.broadcast_to(shift, local.shape))
        colpos = local & (width - 1)
        angle = jnp.where(by_row, rowpos, colpos).astype(jnp.float32) * inverse[:, 0:1]
        cos_out[:, slot * tokd : (slot + 1) * tokd] = jnp.cos(angle)
        sin_out[:, slot * tokd : (slot + 1) * tokd] = jnp.sin(angle)
    for slot in range(slots):
        for other in range(slots):
            off = jnp.where(ids[slot] == ids[other], 0.0, NEG)
            row = slot * slots + other
            mask_out[row : row + 1, :] = jnp.full((1, tokd), off, jnp.float32)
        row = slots * slots + slot
        live = jnp.where(ids[slot] >= 0, 1.0, 0.0)
        mask_out[row : row + 1, :] = jnp.full((1, tokd), live, jnp.float32)
    plain = bias[...].astype(jnp.float32)
    rest = jnp.zeros((LANES - plain.shape[0], plain.shape[1]), jnp.float32)
    turned[...] = jnp.concatenate([plain, rest], axis=0).T
    for phase in range(OWN_HEADS):
        begin = pl.multiple_of((phase * SPAN + residue) * HEAD_DIM, 16)
        bias_out[phase * HEAD_DIM : (phase + 1) * HEAD_DIM, :] = turned[pl.ds(begin, HEAD_DIM), :]


def stage(slot, tokd, message, cosv, sinv, bias):
    at = slice(slot * tokd, (slot + 1) * tokd)
    cos_b, sin_b = cosv[:, at], sinv[:, at]
    query, key, value = (
        message[message_rows(tensor), :].astype(jnp.float32) + bias[:, tensor : tensor + 1]
        for tensor in range(3)
    )
    rest_row = lax.broadcasted_iota(jnp.int32, (LANES - HEAD_DIM, tokd), 0)
    zeros = jnp.zeros((LANES - HEAD_DIM, tokd), jnp.float32)
    ones = jnp.where(rest_row < 2, 1.0, 0.0)
    return [
        jnp.concatenate(pair, axis=0).astype(jnp.bfloat16)
        for pair in (
            (rotate(query, cos_b, sin_b) * (SCALE * LOG2E), zeros),
            (rotate(key, cos_b, sin_b), zeros),
            (value, ones),
        )
    ]


def stage_kernel(slot, phases, tokd, cosv, sinv, bias, *refs):
    count = len(phases)
    msgs, turned, plain = refs[:count], refs[count : 2 * count], refs[2 * count :]
    for number, phase in enumerate(phases):
        own_bias = bias[phase * HEAD_DIM : (phase + 1) * HEAD_DIM, :]
        values = stage(slot, tokd, msgs[number], cosv, sinv, own_bias)
        for tensor, value in enumerate(values):
            turned[number][tensor] = value
            if tensor > 0:
                plain[number][tensor - 1] = value.T


def attend_kernel(slots, staged, closed, tokd, head, factor, cosv, sinv, masks, bias, *refs):
    msgs, refs = refs[:slots], refs[slots:]
    ready = {slot: refs[2 * at : 2 * at + 2] for at, slot in enumerate(staged)}
    refs = refs[2 * len(staged) :]
    earlier = ()
    if head > 0:
        before, earlier, refs = refs[0], refs[1:slots], refs[slots:]
    outs, sums = refs[:slots], refs[slots]
    for result, out in zip(earlier, [out for slot, out in enumerate(outs) if slot != EARLY]):
        done = head * 4 * HEAD_DIM
        out[:done, :] = result[:done, :]
    qt_all, kt_all, vt_all, gt_all, k_all, v_all, s_buf, e_buf, d_buf = refs[slots + 1 : slots + 10]
    own_bias = bias[head * HEAD_DIM : (head + 1) * HEAD_DIM, :]
    rest_row = lax.broadcasted_iota(jnp.int32, (LANES - HEAD_DIM, tokd), 0)

    by_lanes = (((1,), (1,)), ((), ()))

    def off_row(slot, other):
        row = slot * slots + other
        return masks[row : row + 1, :]

    def live(slot, values):
        if closed:
            return values
        row = slots * slots + slot
        return values * masks[row : row + 1, :]

    def block_of(slot):
        return slice(slot * tokd, (slot + 1) * tokd)

    def put(slot, tensor, values):
        begin = ((0 if slot == EARLY else 4 * head) + tensor) * HEAD_DIM
        outs[slot][begin : begin + HEAD_DIM, :] = values

    def pieces_of(other):
        step = tokd // PIECES
        return [
            slice(other * tokd + number * step, other * tokd + (number + 1) * step)
            for number in range(PIECES)
        ]

    def scores(slot, keys):
        part = jnp.dot(
            k_all[keys, :], qt_all[:, block_of(slot)], preferred_element_type=jnp.float32
        )
        s_buf[slot % 2, keys, :] = part
        return jnp.max(part, axis=0, keepdims=True)

    def exponentials(slot, keys, top):
        part = jnp.exp2(s_buf[slot % 2, keys, :] - top)
        e_buf[keys, block_of(slot)] = part.astype(jnp.bfloat16)

    def output(slot):
        mixed = jnp.dot(
            vt_all[:USED, :], e_buf[:, block_of(slot)], preferred_element_type=jnp.float32
        )
        inv = 1.0 / mixed[HEAD_DIM : HEAD_DIM + 1]
        out_b = (mixed[:HEAD_DIM] * inv).astype(jnp.bfloat16)
        put(slot, 0, out_b)
        grad = msgs[slot][message_rows(3), :].astype(jnp.float32)
        delta = jnp.sum(grad * out_b.astype(jnp.float32), axis=0, keepdims=True) * inv
        coarse = delta.astype(jnp.bfloat16).astype(jnp.float32)
        rest = jnp.where(rest_row == 0, -coarse, jnp.where(rest_row == 1, coarse - delta, 0.0))
        grad = jnp.concatenate([grad * inv, rest], axis=0).astype(jnp.bfloat16)
        gt_all[:, block_of(slot)] = grad
        spread = grad[:HEAD_DIM].astype(jnp.float32) * mixed[HEAD_DIM : HEAD_DIM + 1]
        return grad, live(slot, spread)

    def dscores(slot, keys, grad):
        part = jnp.dot(v_all[keys, :], grad, preferred_element_type=jnp.float32)
        d_buf[keys, block_of(slot)] = e_buf[keys, block_of(slot)] * part.astype(jnp.bfloat16)

    def query_part(slot):
        at = block_of(slot)
        dquery = jnp.dot(kt_all[:HEAD_DIM, :], d_buf[:, at], preferred_element_type=jnp.float32)
        dquery = unrotate(dquery * SCALE, cosv[:, at], sinv[:, at])
        put(slot, 1, dquery.astype(jnp.bfloat16))
        return live(slot, dquery)

    def value_part(slot):
        dvalue = lax.dot_general(
            gt_all[:HEAD_DIM, :],
            e_buf[block_of(slot), :],
            by_lanes,
            preferred_element_type=jnp.float32,
        )
        put(slot, 3, dvalue.astype(jnp.bfloat16))

    for slot in range(slots):
        at = block_of(slot)
        if slot in ready:
            turned, plain = ready[slot]
            values, natural = [turned[number] for number in range(3)], [plain[0], plain[1]]
        else:
            values = stage(slot, tokd, msgs[slot], cosv, sinv, own_bias)
            natural = [value.T for value in values[1:]]
        qt_all[:, at], kt_all[:, at], vt_all[:, at] = values
        k_all[at, :], v_all[at, :] = natural
    dq_total = jnp.zeros((HEAD_DIM, tokd), jnp.float32)
    dv_total = jnp.zeros((HEAD_DIM, tokd), jnp.float32)
    grad = None
    offs = tops = None
    for step in range(slots + 2):
        ahead, slot, behind = step, step - 1, step - 2
        if 0 <= slot < slots:
            offs = [off_row(slot, other) for other in range(slots)]
            top = functools.reduce(jnp.maximum, [one + off for one, off in zip(tops, offs)])
        tops = []
        for other in range(slots):
            found = []
            for keys in pieces_of(other):
                if ahead < slots:
                    found.append(scores(ahead, keys))
                if 0 <= behind:
                    dscores(behind, keys, grad)
                if 0 <= slot < slots:
                    exponentials(slot, keys, top - offs[other])
            if found:
                tops.append(functools.reduce(jnp.maximum, found))
        if 0 <= behind:
            dq_total = dq_total + query_part(behind)
        if 0 <= slot < slots:
            grad, spread = output(slot)
            dv_total = dv_total + spread
    dk_total = jnp.zeros((HEAD_DIM, tokd), jnp.float32)
    for slot in range(slots):
        at = block_of(slot)
        dkey = lax.dot_general(
            qt_all[:HEAD_DIM, :], d_buf[at, :], by_lanes, preferred_element_type=jnp.float32
        )
        dkey = unrotate(dkey * (1.0 / LOG2E), cosv[:, at], sinv[:, at])
        put(slot, 2, dkey.astype(jnp.bfloat16))
        dk_total = dk_total + live(slot, dkey)
    lane = lax.broadcasted_iota(jnp.int32, (HEAD_DIM, LANES), 1)
    columns = jnp.zeros((HEAD_DIM, LANES), jnp.float32)
    for number, total in enumerate((dq_total, dk_total, dv_total)):
        total = jnp.sum(total, axis=1, keepdims=True) * factor
        columns = jnp.where(lane == number, total, columns)
    columns = jnp.concatenate([columns, jnp.zeros((LANES - HEAD_DIM, LANES), jnp.float32)], axis=0)
    lines = columns.T
    copy = None
    if head + 1 < OWN_HEADS:
        sums[...] = lines[:8]
    else:
        tiles, sem = refs[slots + 10 :]
        tile = join_sums(before[...], lines)

        def repeat(device, carry):
            tiles[device] = tile
            return carry

        lax.fori_loop(0, tiles.shape[0], repeat, 0, unroll=min(32, tiles.shape[0]))
        copy = pltpu.make_async_copy(tiles, sums, sem)
        copy.start()
    for slot in range(slots):
        value_part(slot)
    if copy is not None:
        copy.wait()


FIT = LANES - HEAD_DIM
LEFT = HEAD_DIM - FIT


def join_sums(first, second):
    lane = lax.broadcasted_iota(jnp.int32, (1, LANES), 1)
    rows = []
    last = jnp.zeros((1, LANES), jnp.float32)
    for number in range(3):
        moved = pltpu.roll(second[number : number + 1], HEAD_DIM, 1)
        rows.append(jnp.where(lane < HEAD_DIM, first[number : number + 1], moved))
        rest = jnp.where(lane < LEFT, moved, 0.0)
        last = last + (pltpu.roll(rest, number * LEFT, 1) if number else rest)
    return jnp.concatenate(rows + [last], axis=0)


def join_kernel(*refs):
    msgs, out = refs[:-1], refs[-1]
    rows = msgs[0].shape[0]
    for phase, message in enumerate(msgs):
        out[phase * rows : (phase + 1) * rows, :] = message[...]


def unpack_kernel(slots, count, images, *refs):
    closed = is_closed(count)
    if not closed:
        lengths, table, *refs = refs
    msgs, refs = refs[:slots], refs[slots:]
    *outs, held, ready, sems = refs
    me = lax.axis_index("tok")

    def place(slot, residue):
        for phase in range(OWN_HEADS):
            begin = pl.multiple_of((phase * SPAN + residue) * HEAD_DIM, 16)
            for number in range(4):
                held[number, pl.ds(begin, HEAD_DIM), :] = msgs[slot][
                    message_rows(4 * phase + number), :
                ]

    for slot in range(slots):
        if closed:
            place(slot, lax.rem(me, SPAN) ^ closed_step(slot))
        else:
            _, start = image_of(me, lengths, images)
            source = table[slot, me]
            residue = lax.rem(source + SPAN, SPAN)
            chosen = (source >= 0) & (source == handler_of(start, residue, count))
            pl.when(chosen)(functools.partial(place, slot, residue))
    copies = []
    for number, out in enumerate(outs):
        ready[number] = held[number].T
        copies.append(pltpu.make_async_copy(ready.at[number], out, sems.at[number]))
        copies[-1].start()
    for copy in copies:
        copy.wait()


def bias_kernel(tiles, bias_out):
    def add(group, totals):
        return tuple(
            total + tiles[group * SPAN + residue] for residue, total in enumerate(totals)
        )

    groups = tiles.shape[0] // SPAN
    zero = jnp.zeros(tiles.shape[1:], jnp.float32)
    totals = lax.fori_loop(0, groups, add, (zero,) * SPAN, unroll=groups <= 8)
    for residue, total in enumerate(totals):
        first = residue * HEAD_DIM
        second = (SPAN + residue) * HEAD_DIM
        for number in range(3):
            row = slice(number, number + 1)
            bias_out[row, first : first + HEAD_DIM] = total[row, :HEAD_DIM]
            bias_out[row, second : second + FIT] = total[row, HEAD_DIM:]
            bias_out[row, second + FIT : second + HEAD_DIM] = total[
                3:4, number * LEFT : (number + 1) * LEFT
            ]


def on_device(query_in, key_in, value_in, out_grad, bias, lengths, widths):
    tokd = query_in.shape[1]
    model = query_in.shape[2]
    images = lengths.shape[1]
    count = lax.axis_size("tok")
    dp_size = lax.axis_size("dp")
    closed = is_closed(count)
    sources, targets = trade_tables(count)
    slots = sources.shape[0]
    span = slots * tokd
    table = jnp.asarray(sources)
    quarter = HEAD_DIM // 4
    inverse = rope_base ** (-np.arange(quarter, dtype=np.float64) / quarter)
    inverse = jnp.asarray(np.tile(np.tile(inverse, 2)[:, None], (1, LANES)), jnp.float32)
    smem = pl.BlockSpec(memory_space=pltpu.SMEM)
    vmem = pl.BlockSpec(memory_space=pltpu.VMEM)
    hbm = pl.BlockSpec(memory_space=pltpu.HBM)
    whole = jax.ShapeDtypeStruct((tokd, model), jnp.bfloat16)
    message = jax.ShapeDtypeStruct((4 * HEAD_DIM, tokd), jnp.bfloat16)
    joined = jax.ShapeDtypeStruct((OWN_HEADS * 4 * HEAD_DIM, tokd), jnp.bfloat16)
    devices = dp_size * count
    tokens_all = devices * tokd

    def params(mib):
        return pltpu.CompilerParams(vmem_limit_bytes=int(mib * 1024 * 1024))

    inputs = (query_in[0], key_in[0], value_in[0], out_grad[0])
    sends = pl.pallas_call(
        functools.partial(pack_kernel, closed),
        out_shape=[message] * (OWN_HEADS * slots),
        in_specs=[hbm] * 4,
        out_specs=[vmem] * (OWN_HEADS * slots),
        scratch_shapes=[
            pltpu.VMEM((4, tokd, model), jnp.bfloat16),
            pltpu.VMEM((4, model, tokd), jnp.bfloat16),
            pltpu.SemaphoreType.DMA((4,)),
        ],
        compiler_params=params(PACK_KIB / 1024),
        name="pack_heads",
    )(*inputs)
    rounds = trade_rounds(count)
    first = [sends[0]] + [
        lax.ppermute(send, "tok", pairs) for send, pairs in zip(sends[1:slots], rounds)
    ]
    table_shape = jax.ShapeDtypeStruct((HALF, span), jnp.float32)
    mask_rows = -(-slots * (slots + 1) // 8) * 8
    tables = pl.pallas_call(
        functools.partial(tables_kernel, images, count, tokd),
        out_shape=[table_shape] * 2
        + [
            jax.ShapeDtypeStruct((mask_rows, tokd), jnp.float32),
            jax.ShapeDtypeStruct((OWN_HEADS * HEAD_DIM, LANES), jnp.float32),
        ],
        in_specs=[smem, smem, smem, vmem, vmem],
        out_specs=[vmem] * 4,
        scratch_shapes=[pltpu.VMEM((model, LANES), jnp.float32)],
        compiler_params=params(16),
        cost_estimate=pl.CostEstimate(
            flops=span * LANES * 200, bytes_accessed=0, transcendentals=0
        ),
        name="rotary_tables",
    )(lengths, widths, table, inverse, bias)

    def stage_ahead(slot, phases, messages):
        number = len(phases)
        results = pl.pallas_call(
            functools.partial(stage_kernel, slot, phases, tokd),
            out_shape=[jax.ShapeDtypeStruct((3, LANES, tokd), jnp.bfloat16)] * number
            + [jax.ShapeDtypeStruct((2, tokd, LANES), jnp.bfloat16)] * number,
            in_specs=[vmem] * (3 + number),
            out_specs=[vmem] * (2 * number),
            compiler_params=params(16),
            cost_estimate=pl.CostEstimate(
                flops=1_000_000 * number, bytes_accessed=0, transcendentals=0
            ),
            name="stage_slot",
        )(tables[0], tables[1], tables[3], *messages)
        return [list(pair) for pair in zip(results[:number], results[number:])]

    phases = tuple(range(OWN_HEADS))
    own = stage_ahead(0, phases, [sends[phase * slots] for phase in phases])
    staged = [{0: pair} for pair in own]
    got = [first] + [[sends[phase * slots]] for phase in phases[1:]]
    latest = own
    for slot in range(1, slots):
        for phase in phases[1:]:
            send, latest = lax.optimization_barrier((sends[phase * slots + slot], latest))
            got[phase].append(lax.ppermute(send, "tok", rounds[slot - 1]))
        if slot == 1:
            staged[0][0], staged[1][0] = latest
        else:
            staged[0][slot - 1] = latest[0]
        if slot + 1 < slots:
            latest = stage_ahead(slot, (0,), [first[slot]])
    early = []
    carried = []
    for phase in range(OWN_HEADS):
        last = phase + 1 == OWN_HEADS
        kept = [slot for slot in range(slots) if slot != EARLY]
        sums_shape = jax.ShapeDtypeStruct(
            (devices, 4, LANES) if last else (8, LANES), jnp.float32
        )
        *results, total = pl.pallas_call(
            functools.partial(
                attend_kernel,
                slots,
                tuple(staged[phase]),
                closed,
                tokd,
                phase,
                1.0 / tokens_all**0.5,
            ),
            out_shape=[message if slot == EARLY else joined for slot in range(slots)]
            + [sums_shape],
            in_specs=[vmem] * (4 + slots + 2 * len(staged[phase]) + len(carried)),
            out_specs=[vmem] * slots + [hbm if last else vmem],
            scratch_shapes=[pltpu.VMEM((LANES, span), jnp.bfloat16)] * 4
            + [pltpu.VMEM((span, LANES), jnp.bfloat16)] * 2
            + [pltpu.VMEM((2, span, tokd), jnp.float32)]
            + [pltpu.VMEM((span, span), jnp.bfloat16)] * 2
            + (
                [pltpu.VMEM(sums_shape.shape, jnp.float32), pltpu.SemaphoreType.DMA(())]
                if last
                else []
            ),
            compiler_params=params(32),
            cost_estimate=pl.CostEstimate(
                flops=12 * span * span * 256, bytes_accessed=0, transcendentals=0
            ),
            name="attend_head",
        )(*tables, *got[phase], *(one for pair in staged[phase].values() for one in pair), *carried)
        results[-1], early = lax.optimization_barrier((results[-1], early))
        early.append(send_back(results[EARLY], EARLY))
        carried = [total] + [results[slot] for slot in kept]
    tiles = lax.all_to_all(total, ("dp", "tok"), 0, 0, tiled=True)
    late = [send_back(results[slot], slot) for slot in kept]
    both = pl.pallas_call(
        join_kernel,
        out_shape=joined,
        in_specs=[vmem] * OWN_HEADS,
        out_specs=vmem,
        compiler_params=params(16),
        cost_estimate=pl.CostEstimate(flops=UNPACK_FLOPS, bytes_accessed=0, transcendentals=0),
        name="join_phases",
    )(*early)
    late.insert(EARLY, both)
    places = [] if closed else [lengths, jnp.asarray(targets)]
    outs = pl.pallas_call(
        functools.partial(unpack_kernel, slots, count, images),
        out_shape=[whole] * 4,
        in_specs=[smem] * len(places) + [vmem] * slots,
        out_specs=[hbm] * 4,
        scratch_shapes=[
            pltpu.VMEM((4, model, tokd), jnp.bfloat16),
            pltpu.VMEM((4, tokd, model), jnp.bfloat16),
            pltpu.SemaphoreType.DMA((4,)),
        ],
        compiler_params=params(16),
        cost_estimate=pl.CostEstimate(flops=UNPACK_FLOPS, bytes_accessed=0, transcendentals=0),
        name="unpack_heads",
    )(*places, *late)
    outs, tiles = lax.optimization_barrier((outs, tiles))
    bias_grad = pl.pallas_call(
        bias_kernel,
        out_shape=jax.ShapeDtypeStruct((3, model), jnp.float32),
        in_specs=[vmem],
        out_specs=vmem,
        compiler_params=params(16),
        name="bias_sums",
    )(tiles)
    return tuple(out[None] for out in outs) + (bias_grad,)


def solution(mesh):
    in_specs = (
        P("dp", "tok", None),
        P("dp", "tok", None),
        P("dp", "tok", None),
        P("dp", "tok", None),
        P(),
        P("dp", None),
        P("dp", None),
    )
    out_specs = (
        P("dp", "tok", None),
        P("dp", "tok", None),
        P("dp", "tok", None),
        P("dp", "tok", None),
        P(),
    )
    return jax.shard_map(
        on_device, mesh=mesh, in_specs=in_specs, out_specs=out_specs, check_vma=False
    )
```

```python
import functools

import jax
import jax.numpy as jnp
import numpy as np
from jax import lax
from jax.experimental import pallas as pl
from jax.experimental.pallas import tpu as pltpu
from jax.sharding import PartitionSpec as P

HEADS = 8
HEAD_DIM = 80
SPAN = 4
OWN_HEADS = HEADS // SPAN
PART = OWN_HEADS * HEAD_DIM
SCALE = HEAD_DIM**-0.5
LOG2E = 1.4426950408889634
NEG = -1e30
LANES = 128
USED = HEAD_DIM + 16
HALF = HEAD_DIM // 2
PIECES = 2
FIRST_PACK_KIB = 52 * 1024 + 1260
PACK_KIB = 52 * 1024 - 400
UNPACK_FLOPS = 20_000_000_000

rope_base = 10000.0


def is_closed(count):
    return count in (SPAN, 2 * SPAN)


def closed_step(slot):
    return (SPAN - slot) % SPAN


def trade_rounds(count):
    if is_closed(count):
        return [
            [(one, one ^ closed_step(slot)) for one in range(count)] for slot in range(1, SPAN)
        ]
    rounds = []
    for shift in [*range(1, SPAN), *range(-1, -SPAN, -1)]:
        rounds.append(
            [
                (source, source + shift)
                for source in range(max(0, -shift), min(count, count - shift))
                if (source < SPAN) == (source + shift < SPAN)
            ]
        )
    return rounds


def trade_tables(count):
    rounds = trade_rounds(count)
    sources = np.full((1 + len(rounds), count), -1, np.int32)
    targets = sources.copy()
    sources[0] = targets[0] = np.arange(count)
    for slot, pairs in enumerate(rounds, 1):
        for source, target in pairs:
            sources[slot, target] = source
            targets[slot, source] = target
    return sources, targets


def send_back(result, slot):
    if slot == 0:
        return result
    pairs = trade_rounds(lax.axis_size("tok"))[slot - 1]
    return lax.ppermute(result, "tok", [(target, source) for source, target in pairs])


EARLY = 1


def image_of(block, lengths, images):
    image = jnp.int32(0)
    start = jnp.int32(0)
    begin = jnp.int32(0)
    for number in range(images):
        size = lengths[0, number]
        inside = (block >= begin) & (block < begin + size)
        image = jnp.where(inside, number, image)
        start = jnp.where(inside, begin, start)
        begin = begin + size
    return image, start


def handler_of(start, residue, count):
    device = start + lax.rem(residue - lax.rem(start, SPAN) + SPAN, SPAN)
    return jnp.where(device >= count, device - SPAN, device)


def message_rows(tensor):
    return slice(tensor * HEAD_DIM, (tensor + 1) * HEAD_DIM)


def rotate(values, cosv, sinv):
    first, second = values[:HALF], values[HALF:]
    return jnp.concatenate([first * cosv - second * sinv, second * cosv + first * sinv], axis=0)


def unrotate(values, cosv, sinv):
    first, second = values[:HALF], values[HALF:]
    return jnp.concatenate([first * cosv + second * sinv, second * cosv - first * sinv], axis=0)


def phase_lanes(phase, model):
    size = SPAN * HEAD_DIM
    begin = phase * size // LANES * LANES
    end = -(-(phase + 1) * size // LANES) * LANES
    return begin, min(end, model)


def pack_kernel(phase, closed, *refs):
    inputs, outs, held, turned, sems = refs[:4], refs[4:-3], refs[-3], refs[-2], refs[-1]
    begin, end = phase_lanes(phase, inputs[0].shape[1])
    copies = [
        pltpu.make_async_copy(source.at[:, begin:end], held.at[number], sems.at[number])
        for number, source in enumerate(inputs)
    ]
    for copy in copies:
        copy.start()
    me = lax.rem(lax.axis_index("tok"), SPAN)
    inner = phase * SPAN * HEAD_DIM - begin
    steps = (
        [closed_step(slot) for slot in range(SPAN)]
        if closed
        else [0, *range(1, SPAN), *range(SPAN - 1, 0, -1)]
    )
    for number, copy in enumerate(copies):
        copy.wait()
        turned[number] = held[number].T
        for out, step in zip(outs, steps):
            residue = me ^ step if closed else lax.rem(me + step, SPAN)
            rows = pl.ds(pl.multiple_of(inner + residue * HEAD_DIM, 16), HEAD_DIM)
            out[message_rows(number), :] = turned[number, rows, :]


def tables_kernel(images, count, tokd, lengths, widths, table, inverse, bias, *refs):
    cos_out, sin_out, mask_out, bias_out, turned = refs
    me = lax.axis_index("tok")
    residue = lax.rem(me, SPAN)
    slots = table.shape[0]
    spot = lax.broadcasted_iota(jnp.int32, (HALF, tokd), 1)
    by_row = lax.broadcasted_iota(jnp.int32, (HALF, tokd), 0) < HALF // 2
    ids = []
    for slot in range(slots):
        block = table[slot, me]
        image, start = image_of(block, lengths, images)
        handled = (block >= 0) & (handler_of(start, residue, count) == me)
        ids.append(jnp.where(handled, image, -1 - slot))
        width = widths[0, image]
        bits = jnp.where(width == tokd, 0, jnp.where(width * 2 == tokd, 1, 2))
        shift = tokd.bit_length() - 1 - bits
        local = spot + (block - start) * tokd
        rowpos = lax.shift_right_logical(local, jnp.broadcast_to(shift, local.shape))
        colpos = local & (width - 1)
        angle = jnp.where(by_row, rowpos, colpos).astype(jnp.float32) * inverse[:, 0:1]
        cos_out[:, slot * tokd : (slot + 1) * tokd] = jnp.cos(angle)
        sin_out[:, slot * tokd : (slot + 1) * tokd] = jnp.sin(angle)
    for slot in range(slots):
        for other in range(slots):
            off = jnp.where(ids[slot] == ids[other], 0.0, NEG)
            row = slot * slots + other
            mask_out[row : row + 1, :] = jnp.full((1, tokd), off, jnp.float32)
        row = slots * slots + slot
        live = jnp.where(ids[slot] >= 0, 1.0, 0.0)
        mask_out[row : row + 1, :] = jnp.full((1, tokd), live, jnp.float32)
    plain = bias[...].astype(jnp.float32)
    rest = jnp.zeros((LANES - plain.shape[0], plain.shape[1]), jnp.float32)
    turned[...] = jnp.concatenate([plain, rest], axis=0).T
    for phase in range(OWN_HEADS):
        begin = pl.multiple_of((phase * SPAN + residue) * HEAD_DIM, 16)
        bias_out[phase * HEAD_DIM : (phase + 1) * HEAD_DIM, :] = turned[pl.ds(begin, HEAD_DIM), :]


def stage(slot, tokd, message, cosv, sinv, bias):
    at = slice(slot * tokd, (slot + 1) * tokd)
    cos_b, sin_b = cosv[:, at], sinv[:, at]
    query, key, value = (
        message[message_rows(tensor), :].astype(jnp.float32) + bias[:, tensor : tensor + 1]
        for tensor in range(3)
    )
    rest_row = lax.broadcasted_iota(jnp.int32, (LANES - HEAD_DIM, tokd), 0)
    zeros = jnp.zeros((LANES - HEAD_DIM, tokd), jnp.float32)
    ones = jnp.where(rest_row < 2, 1.0, 0.0)
    return [
        jnp.concatenate(pair, axis=0).astype(jnp.bfloat16)
        for pair in (
            (rotate(query, cos_b, sin_b) * (SCALE * LOG2E), zeros),
            (rotate(key, cos_b, sin_b), zeros),
            (value, ones),
        )
    ]


def stage_kernel(slot, phases, tokd, cosv, sinv, bias, *refs):
    count = len(phases)
    msgs, turned, plain = refs[:count], refs[count : 2 * count], refs[2 * count :]
    for number, phase in enumerate(phases):
        own_bias = bias[phase * HEAD_DIM : (phase + 1) * HEAD_DIM, :]
        values = stage(slot, tokd, msgs[number], cosv, sinv, own_bias)
        for tensor, value in enumerate(values):
            turned[number][tensor] = value
            if tensor > 0:
                plain[number][tensor - 1] = value.T


def attend_kernel(slots, staged, closed, tokd, head, factor, cosv, sinv, masks, bias, *refs):
    msgs, refs = refs[:slots], refs[slots:]
    ready = {slot: refs[2 * at : 2 * at + 2] for at, slot in enumerate(staged)}
    refs = refs[2 * len(staged) :]
    earlier = ()
    if head > 0:
        before, earlier, refs = refs[0], refs[1:slots], refs[slots:]
    outs, sums = refs[:slots], refs[slots]
    for result, out in zip(earlier, [out for slot, out in enumerate(outs) if slot != EARLY]):
        done = head * 4 * HEAD_DIM
        out[:done, :] = result[:done, :]
    qt_all, kt_all, vt_all, gt_all, k_all, v_all, s_buf, e_buf, d_buf = refs[slots + 1 : slots + 10]
    own_bias = bias[head * HEAD_DIM : (head + 1) * HEAD_DIM, :]
    rest_row = lax.broadcasted_iota(jnp.int32, (LANES - HEAD_DIM, tokd), 0)

    by_lanes = (((1,), (1,)), ((), ()))

    def off_row(slot, other):
        row = slot * slots + other
        return masks[row : row + 1, :]

    def live(slot, values):
        if closed:
            return values
        row = slots * slots + slot
        return values * masks[row : row + 1, :]

    def block_of(slot):
        return slice(slot * tokd, (slot + 1) * tokd)

    def put(slot, tensor, values):
        begin = ((0 if slot == EARLY else 4 * head) + tensor) * HEAD_DIM
        outs[slot][begin : begin + HEAD_DIM, :] = values

    def pieces_of(other):
        step = tokd // PIECES
        return [
            slice(other * tokd + number * step, other * tokd + (number + 1) * step)
            for number in range(PIECES)
        ]

    def scores(slot, keys):
        part = jnp.dot(
            k_all[keys, :], qt_all[:, block_of(slot)], preferred_element_type=jnp.float32
        )
        s_buf[slot % 2, keys, :] = part
        return jnp.max(part, axis=0, keepdims=True)

    def exponentials(slot, keys, top):
        part = jnp.exp2(s_buf[slot % 2, keys, :] - top)
        e_buf[keys, block_of(slot)] = part.astype(jnp.bfloat16)

    def output(slot):
        mixed = jnp.dot(
            vt_all[:USED, :], e_buf[:, block_of(slot)], preferred_element_type=jnp.float32
        )
        inv = 1.0 / mixed[HEAD_DIM : HEAD_DIM + 1]
        out_b = (mixed[:HEAD_DIM] * inv).astype(jnp.bfloat16)
        put(slot, 0, out_b)
        grad = msgs[slot][message_rows(3), :].astype(jnp.float32)
        delta = jnp.sum(grad * out_b.astype(jnp.float32), axis=0, keepdims=True) * inv
        coarse = delta.astype(jnp.bfloat16).astype(jnp.float32)
        rest = jnp.where(rest_row == 0, -coarse, jnp.where(rest_row == 1, coarse - delta, 0.0))
        grad = jnp.concatenate([grad * inv, rest], axis=0).astype(jnp.bfloat16)
        gt_all[:, block_of(slot)] = grad
        spread = grad[:HEAD_DIM].astype(jnp.float32) * mixed[HEAD_DIM : HEAD_DIM + 1]
        return grad, live(slot, spread)

    def dscores(slot, keys, grad):
        part = jnp.dot(v_all[keys, :], grad, preferred_element_type=jnp.float32)
        d_buf[keys, block_of(slot)] = e_buf[keys, block_of(slot)] * part.astype(jnp.bfloat16)

    def query_part(slot):
        at = block_of(slot)
        dquery = jnp.dot(kt_all[:HEAD_DIM, :], d_buf[:, at], preferred_element_type=jnp.float32)
        dquery = unrotate(dquery * SCALE, cosv[:, at], sinv[:, at])
        put(slot, 1, dquery.astype(jnp.bfloat16))
        return live(slot, dquery)

    def value_part(slot):
        dvalue = lax.dot_general(
            gt_all[:HEAD_DIM, :],
            e_buf[block_of(slot), :],
            by_lanes,
            preferred_element_type=jnp.float32,
        )
        put(slot, 3, dvalue.astype(jnp.bfloat16))

    for slot in range(slots):
        at = block_of(slot)
        if slot in ready:
            turned, plain = ready[slot]
            values, natural = [turned[number] for number in range(3)], [plain[0], plain[1]]
        else:
            values = stage(slot, tokd, msgs[slot], cosv, sinv, own_bias)
            natural = [value.T for value in values[1:]]
        qt_all[:, at], kt_all[:, at], vt_all[:, at] = values
        k_all[at, :], v_all[at, :] = natural
    dq_total = jnp.zeros((HEAD_DIM, tokd), jnp.float32)
    dv_total = jnp.zeros((HEAD_DIM, tokd), jnp.float32)
    grad = None
    offs = tops = None
    for step in range(slots + 2):
        ahead, slot, behind = step, step - 1, step - 2
        if 0 <= slot < slots:
            offs = [off_row(slot, other) for other in range(slots)]
            top = functools.reduce(jnp.maximum, [one + off for one, off in zip(tops, offs)])
        tops = []
        for other in range(slots):
            found = []
            for keys in pieces_of(other):
                if ahead < slots:
                    found.append(scores(ahead, keys))
                if 0 <= behind:
                    dscores(behind, keys, grad)
                if 0 <= slot < slots:
                    exponentials(slot, keys, top - offs[other])
            if found:
                tops.append(functools.reduce(jnp.maximum, found))
        if 0 <= behind:
            dq_total = dq_total + query_part(behind)
        if 0 <= slot < slots:
            grad, spread = output(slot)
            dv_total = dv_total + spread
    dk_total = jnp.zeros((HEAD_DIM, tokd), jnp.float32)
    for slot in range(slots):
        at = block_of(slot)
        dkey = lax.dot_general(
            qt_all[:HEAD_DIM, :], d_buf[at, :], by_lanes, preferred_element_type=jnp.float32
        )
        dkey = unrotate(dkey * (1.0 / LOG2E), cosv[:, at], sinv[:, at])
        put(slot, 2, dkey.astype(jnp.bfloat16))
        dk_total = dk_total + live(slot, dkey)
    lane = lax.broadcasted_iota(jnp.int32, (HEAD_DIM, LANES), 1)
    columns = jnp.zeros((HEAD_DIM, LANES), jnp.float32)
    for number, total in enumerate((dq_total, dk_total, dv_total)):
        total = jnp.sum(total, axis=1, keepdims=True) * factor
        columns = jnp.where(lane == number, total, columns)
    columns = jnp.concatenate([columns, jnp.zeros((LANES - HEAD_DIM, LANES), jnp.float32)], axis=0)
    lines = columns.T
    copy = None
    if head + 1 < OWN_HEADS:
        sums[...] = lines[:8]
    else:
        tiles, sem = refs[slots + 10 :]
        tile = join_sums(before[...], lines)

        def repeat(device, carry):
            tiles[device] = tile
            return carry

        lax.fori_loop(0, tiles.shape[0], repeat, 0, unroll=min(32, tiles.shape[0]))
        copy = pltpu.make_async_copy(tiles, sums, sem)
        copy.start()
    for slot in range(slots):
        value_part(slot)
    if copy is not None:
        copy.wait()


FIT = LANES - HEAD_DIM
LEFT = HEAD_DIM - FIT


def join_sums(first, second):
    lane = lax.broadcasted_iota(jnp.int32, (1, LANES), 1)
    rows = []
    last = jnp.zeros((1, LANES), jnp.float32)
    for number in range(3):
        moved = pltpu.roll(second[number : number + 1], HEAD_DIM, 1)
        rows.append(jnp.where(lane < HEAD_DIM, first[number : number + 1], moved))
        rest = jnp.where(lane < LEFT, moved, 0.0)
        last = last + (pltpu.roll(rest, number * LEFT, 1) if number else rest)
    return jnp.concatenate(rows + [last], axis=0)


def unpack_kernel(slots, count, images, *refs):
    closed = is_closed(count)
    if not closed:
        lengths, table, *refs = refs
    msgs, refs = refs[: slots + OWN_HEADS - 1], refs[slots + OWN_HEADS - 1 :]
    *outs, held, ready, sems = refs
    early, late = msgs[:OWN_HEADS], list(msgs[OWN_HEADS:])
    late.insert(EARLY, None)
    me = lax.axis_index("tok")

    def place(slot, residue):
        for phase in range(OWN_HEADS):
            begin = pl.multiple_of((phase * SPAN + residue) * HEAD_DIM, 16)
            for number in range(4):
                if slot == EARLY:
                    piece = early[phase][message_rows(number), :]
                else:
                    piece = late[slot][message_rows(4 * phase + number), :]
                held[number, pl.ds(begin, HEAD_DIM), :] = piece

    for slot in range(slots):
        if closed:
            place(slot, lax.rem(me, SPAN) ^ closed_step(slot))
        else:
            _, start = image_of(me, lengths, images)
            source = table[slot, me]
            residue = lax.rem(source + SPAN, SPAN)
            chosen = (source >= 0) & (source == handler_of(start, residue, count))
            pl.when(chosen)(functools.partial(place, slot, residue))
    copies = []
    for number, out in enumerate(outs):
        ready[number] = held[number].T
        copies.append(pltpu.make_async_copy(ready.at[number], out, sems.at[number]))
        copies[-1].start()
    for copy in copies:
        copy.wait()


def bias_kernel(tiles, bias_out):
    def add(group, totals):
        return tuple(
            total + tiles[group * SPAN + residue] for residue, total in enumerate(totals)
        )

    groups = tiles.shape[0] // SPAN
    zero = jnp.zeros(tiles.shape[1:], jnp.float32)
    totals = lax.fori_loop(0, groups, add, (zero,) * SPAN, unroll=groups <= 8)
    for residue, total in enumerate(totals):
        first = residue * HEAD_DIM
        second = (SPAN + residue) * HEAD_DIM
        for number in range(3):
            row = slice(number, number + 1)
            bias_out[row, first : first + HEAD_DIM] = total[row, :HEAD_DIM]
            bias_out[row, second : second + FIT] = total[row, HEAD_DIM:]
            bias_out[row, second + FIT : second + HEAD_DIM] = total[
                3:4, number * LEFT : (number + 1) * LEFT
            ]


def on_device(query_in, key_in, value_in, out_grad, bias, lengths, widths):
    tokd = query_in.shape[1]
    model = query_in.shape[2]
    images = lengths.shape[1]
    count = lax.axis_size("tok")
    dp_size = lax.axis_size("dp")
    closed = is_closed(count)
    sources, targets = trade_tables(count)
    slots = sources.shape[0]
    span = slots * tokd
    table = jnp.asarray(sources)
    quarter = HEAD_DIM // 4
    inverse = rope_base ** (-np.arange(quarter, dtype=np.float64) / quarter)
    inverse = jnp.asarray(np.tile(np.tile(inverse, 2)[:, None], (1, LANES)), jnp.float32)
    smem = pl.BlockSpec(memory_space=pltpu.SMEM)
    vmem = pl.BlockSpec(memory_space=pltpu.VMEM)
    hbm = pl.BlockSpec(memory_space=pltpu.HBM)
    whole = jax.ShapeDtypeStruct((tokd, model), jnp.bfloat16)
    message = jax.ShapeDtypeStruct((4 * HEAD_DIM, tokd), jnp.bfloat16)
    joined = jax.ShapeDtypeStruct((OWN_HEADS * 4 * HEAD_DIM, tokd), jnp.bfloat16)
    devices = dp_size * count
    tokens_all = devices * tokd

    def params(mib):
        return pltpu.CompilerParams(vmem_limit_bytes=int(mib * 1024 * 1024))

    inputs = (query_in[0], key_in[0], value_in[0], out_grad[0])
    def pack(phase, kib, inputs):
        begin, end = phase_lanes(phase, model)
        return pl.pallas_call(
            functools.partial(pack_kernel, phase, closed),
            out_shape=[message] * slots,
            in_specs=[hbm] * 4,
            out_specs=[vmem] * slots,
            scratch_shapes=[
                pltpu.VMEM((4, tokd, end - begin), jnp.bfloat16),
                pltpu.VMEM((4, end - begin, tokd), jnp.bfloat16),
                pltpu.SemaphoreType.DMA((4,)),
            ],
            compiler_params=params(kib / 1024),
            cost_estimate=pl.CostEstimate(flops=1_000_000, bytes_accessed=0, transcendentals=0),
            name="pack_heads",
        )(*inputs)

    sends = [pack(0, FIRST_PACK_KIB, inputs)]
    rounds = trade_rounds(count)
    first = [sends[0][0]] + [
        lax.ppermute(send, "tok", pairs) for send, pairs in zip(sends[0][1:], rounds)
    ]
    table_shape = jax.ShapeDtypeStruct((HALF, span), jnp.float32)
    mask_rows = -(-slots * (slots + 1) // 8) * 8
    tables = pl.pallas_call(
        functools.partial(tables_kernel, images, count, tokd),
        out_shape=[table_shape] * 2
        + [
            jax.ShapeDtypeStruct((mask_rows, tokd), jnp.float32),
            jax.ShapeDtypeStruct((OWN_HEADS * HEAD_DIM, LANES), jnp.float32),
        ],
        in_specs=[smem, smem, smem, vmem, vmem],
        out_specs=[vmem] * 4,
        scratch_shapes=[pltpu.VMEM((model, LANES), jnp.float32)],
        compiler_params=params(16),
        cost_estimate=pl.CostEstimate(
            flops=span * LANES * 200, bytes_accessed=0, transcendentals=0
        ),
        name="rotary_tables",
    )(lengths, widths, table, inverse, bias)

    def stage_ahead(slot, phases, messages):
        number = len(phases)
        results = pl.pallas_call(
            functools.partial(stage_kernel, slot, phases, tokd),
            out_shape=[jax.ShapeDtypeStruct((3, LANES, tokd), jnp.bfloat16)] * number
            + [jax.ShapeDtypeStruct((2, tokd, LANES), jnp.bfloat16)] * number,
            in_specs=[vmem] * (3 + number),
            out_specs=[vmem] * (2 * number),
            compiler_params=params(16),
            cost_estimate=pl.CostEstimate(
                flops=1_000_000 * number, bytes_accessed=0, transcendentals=0
            ),
            name="stage_slot",
        )(tables[0], tables[1], tables[3], *messages)
        return [list(pair) for pair in zip(results[:number], results[number:])]

    phases = tuple(range(OWN_HEADS))
    tables, inputs = lax.optimization_barrier((tables, inputs))
    for phase in phases[1:]:
        sends.append(pack(phase, PACK_KIB, inputs))
    own = stage_ahead(0, phases, [sent[0] for sent in sends])
    staged = [{0: pair} for pair in own]
    got = [first] + [[sent[0]] for sent in sends[1:]]
    latest = own
    for slot in range(1, slots):
        for phase in phases[1:]:
            send, latest = lax.optimization_barrier((sends[phase][slot], latest))
            got[phase].append(lax.ppermute(send, "tok", rounds[slot - 1]))
        if slot == 1:
            staged[0][0], staged[1][0] = latest
        else:
            staged[0][slot - 1] = latest[0]
        if slot + 1 < slots:
            latest = stage_ahead(slot, (0,), [first[slot]])
    early = []
    carried = []
    for phase in range(OWN_HEADS):
        last = phase + 1 == OWN_HEADS
        kept = [slot for slot in range(slots) if slot != EARLY]
        sums_shape = jax.ShapeDtypeStruct(
            (devices, 4, LANES) if last else (8, LANES), jnp.float32
        )
        *results, total = pl.pallas_call(
            functools.partial(
                attend_kernel,
                slots,
                tuple(staged[phase]),
                closed,
                tokd,
                phase,
                1.0 / tokens_all**0.5,
            ),
            out_shape=[message if slot == EARLY else joined for slot in range(slots)]
            + [sums_shape],
            in_specs=[vmem] * (4 + slots + 2 * len(staged[phase]) + len(carried)),
            out_specs=[vmem] * slots + [hbm if last else vmem],
            scratch_shapes=[pltpu.VMEM((LANES, span), jnp.bfloat16)] * 4
            + [pltpu.VMEM((span, LANES), jnp.bfloat16)] * 2
            + [pltpu.VMEM((2, span, tokd), jnp.float32)]
            + [pltpu.VMEM((span, span), jnp.bfloat16)] * 2
            + (
                [pltpu.VMEM(sums_shape.shape, jnp.float32), pltpu.SemaphoreType.DMA(())]
                if last
                else []
            ),
            compiler_params=params(32),
            cost_estimate=pl.CostEstimate(
                flops=12 * span * span * 256, bytes_accessed=0, transcendentals=0
            ),
            name="attend_head",
        )(*tables, *got[phase], *(one for pair in staged[phase].values() for one in pair), *carried)
        results[EARLY], early = lax.optimization_barrier((results[EARLY], early))
        early.append(send_back(results[EARLY], EARLY))
        carried = [total] + [results[slot] for slot in kept]
    tiles = lax.all_to_all(total, ("dp", "tok"), 0, 0, tiled=True)
    late = [send_back(results[slot], slot) for slot in kept]
    places = [] if closed else [lengths, jnp.asarray(targets)]
    outs = pl.pallas_call(
        functools.partial(unpack_kernel, slots, count, images),
        out_shape=[whole] * 4,
        in_specs=[smem] * len(places) + [vmem] * (OWN_HEADS + len(late)),
        out_specs=[hbm] * 4,
        scratch_shapes=[
            pltpu.VMEM((4, model, tokd), jnp.bfloat16),
            pltpu.VMEM((4, tokd, model), jnp.bfloat16),
            pltpu.SemaphoreType.DMA((4,)),
        ],
        compiler_params=params(16),
        cost_estimate=pl.CostEstimate(flops=UNPACK_FLOPS, bytes_accessed=0, transcendentals=0),
        name="unpack_heads",
    )(*places, *early, *late)
    outs, tiles = lax.optimization_barrier((outs, tiles))
    bias_grad = pl.pallas_call(
        bias_kernel,
        out_shape=jax.ShapeDtypeStruct((3, model), jnp.float32),
        in_specs=[vmem],
        out_specs=vmem,
        compiler_params=params(16),
        name="bias_sums",
    )(tiles)
    return tuple(out[None] for out in outs) + (bias_grad,)


def solution(mesh):
    in_specs = (
        P("dp", "tok", None),
        P("dp", "tok", None),
        P("dp", "tok", None),
        P("dp", "tok", None),
        P(),
        P("dp", None),
        P("dp", None),
    )
    out_specs = (
        P("dp", "tok", None),
        P("dp", "tok", None),
        P("dp", "tok", None),
        P("dp", "tok", None),
        P(),
    )
    return jax.shard_map(
        on_device, mesh=mesh, in_specs=in_specs, out_specs=out_specs, check_vma=False
    )
```

```python
import functools
import math

import jax
import jax.numpy as jnp
import numpy as np
from jax import lax
from jax.experimental import pallas as pl
from jax.experimental.pallas import tpu as pltpu
from jax.sharding import PartitionSpec as P

HEADS = 8
HEAD_DIM = 80
SPAN = 4
OWN_HEADS = HEADS // SPAN
PART = OWN_HEADS * HEAD_DIM
SCALE = HEAD_DIM**-0.5
LOG2E = 1.4426950408889634
NEG = -1e30
LANES = 128
USED = HEAD_DIM + 16
HALF = HEAD_DIM // 2
PIECES = 2
FIRST_PACK_KIB = 52 * 1024 + 1260
PREPARE_KIB = 52 * 1024 + 300
UNPACK_FLOPS = 20_000_000_000

rope_base = 10000.0


def is_closed(count):
    return count in (SPAN, 2 * SPAN)


def closed_step(slot):
    return (SPAN - slot) % SPAN


def trade_rounds(count):
    if is_closed(count):
        return [
            [(one, one ^ closed_step(slot)) for one in range(count)] for slot in range(1, SPAN)
        ]
    rounds = []
    for shift in [*range(1, SPAN), *range(-1, -SPAN, -1)]:
        rounds.append(
            [
                (source, source + shift)
                for source in range(max(0, -shift), min(count, count - shift))
                if (source < SPAN) == (source + shift < SPAN)
            ]
        )
    return rounds


def trade_tables(count):
    rounds = trade_rounds(count)
    sources = np.full((1 + len(rounds), count), -1, np.int32)
    targets = sources.copy()
    sources[0] = targets[0] = np.arange(count)
    for slot, pairs in enumerate(rounds, 1):
        for source, target in pairs:
            sources[slot, target] = source
            targets[slot, source] = target
    return sources, targets


def send_back(result, slot):
    if slot == 0:
        return result
    pairs = trade_rounds(lax.axis_size("tok"))[slot - 1]
    return lax.ppermute(result, "tok", [(target, source) for source, target in pairs])


EARLY = 1


def image_of(block, lengths, images):
    image = jnp.int32(0)
    start = jnp.int32(0)
    begin = jnp.int32(0)
    for number in range(images):
        size = lengths[0, number]
        inside = (block >= begin) & (block < begin + size)
        image = jnp.where(inside, number, image)
        start = jnp.where(inside, begin, start)
        begin = begin + size
    return image, start


def handler_of(start, residue, count):
    device = start + lax.rem(residue - lax.rem(start, SPAN) + SPAN, SPAN)
    return jnp.where(device >= count, device - SPAN, device)


def message_rows(tensor):
    return slice(tensor * HEAD_DIM, (tensor + 1) * HEAD_DIM)


def rotate(values, cosv, sinv):
    first, second = values[:HALF], values[HALF:]
    return jnp.concatenate([first * cosv - second * sinv, second * cosv + first * sinv], axis=0)


def unrotate(values, cosv, sinv):
    first, second = values[:HALF], values[HALF:]
    return jnp.concatenate([first * cosv + second * sinv, second * cosv - first * sinv], axis=0)


def phase_lanes(phase, model):
    size = SPAN * HEAD_DIM
    begin = phase * size // LANES * LANES
    end = -(-(phase + 1) * size // LANES) * LANES
    return begin, min(end, model)


def fetch(phase, inputs, held, sems):
    begin, end = phase_lanes(phase, inputs[0].shape[1])
    copies = [
        pltpu.make_async_copy(source.at[:, begin:end], held.at[number], sems.at[number])
        for number, source in enumerate(inputs)
    ]
    for copy in copies:
        copy.start()
    return copies


def pack(phase, closed, copies, outs, held, turned):
    me = lax.rem(lax.axis_index("tok"), SPAN)
    inner = phase * SPAN * HEAD_DIM % LANES
    steps = (
        [closed_step(slot) for slot in range(SPAN)]
        if closed
        else [0, *range(1, SPAN), *range(SPAN - 1, 0, -1)]
    )
    for number, copy in enumerate(copies):
        copy.wait()
        turned[number] = held[number].T
        for out, step in zip(outs, steps):
            residue = me ^ step if closed else lax.rem(me + step, SPAN)
            rows = pl.ds(pl.multiple_of(inner + residue * HEAD_DIM, 16), HEAD_DIM)
            out[message_rows(number), :] = turned[number, rows, :]


def pack_kernel(closed, *refs):
    inputs, outs, (held, turned, sems) = refs[:4], refs[4:-3], refs[-3:]
    pack(0, closed, fetch(0, inputs, held, sems), outs, held, turned)


def prepare_kernel(slots, images, count, tokd, lengths, widths, *refs):
    closed = is_closed(count)
    if not closed:
        table, *refs = refs
    later = OWN_HEADS - 1
    bias, *inputs, own = refs[:6]
    cos_out, sin_out, mask_out, bias_out, *refs = refs[6:]
    messages, refs = refs[: later * slots], refs[later * slots :]
    turned_out, plain_out = refs[:OWN_HEADS], refs[OWN_HEADS : 2 * OWN_HEADS]
    held, turned, sems, columns = refs[2 * OWN_HEADS :]
    copies = [
        fetch(phase + 1, inputs, held.at[phase], sems.at[phase]) for phase in range(later)
    ]
    me = lax.axis_index("tok")
    residue = lax.rem(me, SPAN)
    spot = lax.broadcasted_iota(jnp.int32, (HALF, tokd), 1)
    feature = lax.broadcasted_iota(jnp.int32, (HALF, tokd), 0)
    by_row = feature < HALF // 2
    feature = jnp.where(by_row, feature, feature - HALF // 2).astype(jnp.float32)
    inverse = jnp.exp(feature * (-math.log(rope_base) / (HALF // 2)))
    ids = []
    for slot in range(slots):
        block = me - residue + (residue ^ closed_step(slot)) if closed else table[slot, me]
        image, start = image_of(block, lengths, images)
        handled = (block >= 0) & (handler_of(start, residue, count) == me)
        ids.append(jnp.where(handled, image, -1 - slot))
        width = widths[0, image]
        bits = jnp.where(width == tokd, 0, jnp.where(width * 2 == tokd, 1, 2))
        shift = tokd.bit_length() - 1 - bits
        local = spot + (block - start) * tokd
        rowpos = lax.shift_right_logical(local, jnp.broadcast_to(shift, local.shape))
        colpos = local & (width - 1)
        angle = jnp.where(by_row, rowpos, colpos).astype(jnp.float32) * inverse
        cos_out[:, slot * tokd : (slot + 1) * tokd] = jnp.cos(angle)
        sin_out[:, slot * tokd : (slot + 1) * tokd] = jnp.sin(angle)
    for slot in range(slots):
        for other in range(slots):
            off = jnp.where(ids[slot] == ids[other], 0.0, NEG)
            row = slot * slots + other
            mask_out[row : row + 1, :] = jnp.full((1, tokd), off, jnp.float32)
        row = slots * slots + slot
        live = jnp.where(ids[slot] >= 0, 1.0, 0.0)
        mask_out[row : row + 1, :] = jnp.full((1, tokd), live, jnp.float32)
    plain = bias[...].astype(jnp.float32)
    rest = jnp.zeros((LANES - plain.shape[0], plain.shape[1]), jnp.float32)
    columns[...] = jnp.concatenate([plain, rest], axis=0).T
    for phase in range(OWN_HEADS):
        begin = pl.multiple_of((phase * SPAN + residue) * HEAD_DIM, 16)
        bias_out[phase * HEAD_DIM : (phase + 1) * HEAD_DIM, :] = columns[pl.ds(begin, HEAD_DIM), :]
    for phase in range(later):
        outs = messages[phase * slots : (phase + 1) * slots]
        pack(phase + 1, closed, copies[phase], outs, held.at[phase], turned.at[phase])
    owns = [own] + [messages[phase * slots] for phase in range(later)]
    stage_all(0, range(OWN_HEADS), tokd, cos_out, sin_out, bias_out, owns, turned_out, plain_out)


def stage(slot, tokd, message, cosv, sinv, bias):
    at = slice(slot * tokd, (slot + 1) * tokd)
    cos_b, sin_b = cosv[:, at], sinv[:, at]
    query, key, value = (
        message[message_rows(tensor), :].astype(jnp.float32) + bias[:, tensor : tensor + 1]
        for tensor in range(3)
    )
    rest_row = lax.broadcasted_iota(jnp.int32, (LANES - HEAD_DIM, tokd), 0)
    zeros = jnp.zeros((LANES - HEAD_DIM, tokd), jnp.float32)
    ones = jnp.where(rest_row < 2, 1.0, 0.0)
    return [
        jnp.concatenate(pair, axis=0).astype(jnp.bfloat16)
        for pair in (
            (rotate(query, cos_b, sin_b) * (SCALE * LOG2E), zeros),
            (rotate(key, cos_b, sin_b), zeros),
            (value, ones),
        )
    ]


def stage_all(slot, phases, tokd, cosv, sinv, bias, msgs, turned, plain):
    for number, phase in enumerate(phases):
        own_bias = bias[phase * HEAD_DIM : (phase + 1) * HEAD_DIM, :]
        values = stage(slot, tokd, msgs[number], cosv, sinv, own_bias)
        for tensor, value in enumerate(values):
            turned[number][tensor] = value
            if tensor > 0:
                plain[number][tensor - 1] = value.T


def stage_kernel(slot, phases, tokd, cosv, sinv, bias, *refs):
    count = len(phases)
    msgs, turned, plain = refs[:count], refs[count : 2 * count], refs[2 * count :]
    stage_all(slot, phases, tokd, cosv, sinv, bias, msgs, turned, plain)


def attend_kernel(slots, staged, closed, tokd, head, factor, cosv, sinv, masks, bias, *refs):
    msgs, refs = refs[:slots], refs[slots:]
    ready = {slot: refs[2 * at : 2 * at + 2] for at, slot in enumerate(staged)}
    refs = refs[2 * len(staged) :]
    earlier = ()
    if head > 0:
        before, earlier, refs = refs[0], refs[1:slots], refs[slots:]
    outs, sums = refs[:slots], refs[slots]
    for result, out in zip(earlier, [out for slot, out in enumerate(outs) if slot != EARLY]):
        done = head * 4 * HEAD_DIM
        out[:done, :] = result[:done, :]
    qt_all, kt_all, vt_all, gt_all, k_all, v_all, s_buf, e_buf, d_buf = refs[slots + 1 : slots + 10]
    own_bias = bias[head * HEAD_DIM : (head + 1) * HEAD_DIM, :]
    rest_row = lax.broadcasted_iota(jnp.int32, (LANES - HEAD_DIM, tokd), 0)

    by_lanes = (((1,), (1,)), ((), ()))

    def off_row(slot, other):
        row = slot * slots + other
        return masks[row : row + 1, :]

    def live(slot, values):
        if closed:
            return values
        row = slots * slots + slot
        return values * masks[row : row + 1, :]

    def block_of(slot):
        return slice(slot * tokd, (slot + 1) * tokd)

    def put(slot, tensor, values):
        begin = ((0 if slot == EARLY else 4 * head) + tensor) * HEAD_DIM
        outs[slot][begin : begin + HEAD_DIM, :] = values

    def pieces_of(other):
        step = tokd // PIECES
        return [
            slice(other * tokd + number * step, other * tokd + (number + 1) * step)
            for number in range(PIECES)
        ]

    def scores(slot, keys):
        part = jnp.dot(
            k_all[keys, :], qt_all[:, block_of(slot)], preferred_element_type=jnp.float32
        )
        s_buf[slot % 2, keys, :] = part
        return jnp.max(part, axis=0, keepdims=True)

    def exponentials(slot, keys, top):
        part = jnp.exp2(s_buf[slot % 2, keys, :] - top)
        e_buf[keys, block_of(slot)] = part.astype(jnp.bfloat16)

    def output(slot):
        mixed = jnp.dot(
            vt_all[:USED, :], e_buf[:, block_of(slot)], preferred_element_type=jnp.float32
        )
        inv = 1.0 / mixed[HEAD_DIM : HEAD_DIM + 1]
        out_b = (mixed[:HEAD_DIM] * inv).astype(jnp.bfloat16)
        put(slot, 0, out_b)
        grad = msgs[slot][message_rows(3), :].astype(jnp.float32)
        delta = jnp.sum(grad * out_b.astype(jnp.float32), axis=0, keepdims=True) * inv
        coarse = delta.astype(jnp.bfloat16).astype(jnp.float32)
        rest = jnp.where(rest_row == 0, -coarse, jnp.where(rest_row == 1, coarse - delta, 0.0))
        grad = jnp.concatenate([grad * inv, rest], axis=0).astype(jnp.bfloat16)
        gt_all[:, block_of(slot)] = grad
        spread = grad[:HEAD_DIM].astype(jnp.float32) * mixed[HEAD_DIM : HEAD_DIM + 1]
        return grad, live(slot, spread)

    def dscores(slot, keys, grad):
        part = jnp.dot(v_all[keys, :], grad, preferred_element_type=jnp.float32)
        d_buf[keys, block_of(slot)] = e_buf[keys, block_of(slot)] * part.astype(jnp.bfloat16)

    def query_part(slot):
        at = block_of(slot)
        dquery = jnp.dot(kt_all[:HEAD_DIM, :], d_buf[:, at], preferred_element_type=jnp.float32)
        dquery = unrotate(dquery * SCALE, cosv[:, at], sinv[:, at])
        put(slot, 1, dquery.astype(jnp.bfloat16))
        return live(slot, dquery)

    def value_part(slot):
        dvalue = lax.dot_general(
            gt_all[:HEAD_DIM, :],
            e_buf[block_of(slot), :],
            by_lanes,
            preferred_element_type=jnp.float32,
        )
        put(slot, 3, dvalue.astype(jnp.bfloat16))

    for slot in range(slots):
        at = block_of(slot)
        if slot in ready:
            turned, plain = ready[slot]
            values, natural = [turned[number] for number in range(3)], [plain[0], plain[1]]
        else:
            values = stage(slot, tokd, msgs[slot], cosv, sinv, own_bias)
            natural = [value.T for value in values[1:]]
        qt_all[:, at], kt_all[:, at], vt_all[:, at] = values
        k_all[at, :], v_all[at, :] = natural
    dq_total = jnp.zeros((HEAD_DIM, tokd), jnp.float32)
    dv_total = jnp.zeros((HEAD_DIM, tokd), jnp.float32)
    grad = None
    offs = tops = None
    for step in range(slots + 2):
        ahead, slot, behind = step, step - 1, step - 2
        if 0 <= slot < slots:
            offs = [off_row(slot, other) for other in range(slots)]
            top = functools.reduce(jnp.maximum, [one + off for one, off in zip(tops, offs)])
        tops = []
        for other in range(slots):
            found = []
            for keys in pieces_of(other):
                if ahead < slots:
                    found.append(scores(ahead, keys))
                if 0 <= behind:
                    dscores(behind, keys, grad)
                if 0 <= slot < slots:
                    exponentials(slot, keys, top - offs[other])
            if found:
                tops.append(functools.reduce(jnp.maximum, found))
        if 0 <= behind:
            dq_total = dq_total + query_part(behind)
        if 0 <= slot < slots:
            grad, spread = output(slot)
            dv_total = dv_total + spread
    dk_total = jnp.zeros((HEAD_DIM, tokd), jnp.float32)
    for slot in range(slots):
        at = block_of(slot)
        dkey = lax.dot_general(
            qt_all[:HEAD_DIM, :], d_buf[at, :], by_lanes, preferred_element_type=jnp.float32
        )
        dkey = unrotate(dkey * (1.0 / LOG2E), cosv[:, at], sinv[:, at])
        put(slot, 2, dkey.astype(jnp.bfloat16))
        dk_total = dk_total + live(slot, dkey)
    lane = lax.broadcasted_iota(jnp.int32, (HEAD_DIM, LANES), 1)
    columns = jnp.zeros((HEAD_DIM, LANES), jnp.float32)
    for number, total in enumerate((dq_total, dk_total, dv_total)):
        total = jnp.sum(total, axis=1, keepdims=True) * factor
        columns = jnp.where(lane == number, total, columns)
    columns = jnp.concatenate([columns, jnp.zeros((LANES - HEAD_DIM, LANES), jnp.float32)], axis=0)
    lines = columns.T
    copy = None
    if head + 1 < OWN_HEADS:
        sums[...] = lines[:8]
    else:
        tiles, sem = refs[slots + 10 :]
        tile = join_sums(before[...], lines)

        def repeat(device, carry):
            tiles[device] = tile
            return carry

        lax.fori_loop(0, tiles.shape[0], repeat, 0, unroll=min(32, tiles.shape[0]))
        copy = pltpu.make_async_copy(tiles, sums, sem)
        copy.start()
    for slot in range(slots):
        value_part(slot)
    if copy is not None:
        copy.wait()


FIT = LANES - HEAD_DIM
LEFT = HEAD_DIM - FIT


def join_sums(first, second):
    lane = lax.broadcasted_iota(jnp.int32, (1, LANES), 1)
    rows = []
    last = jnp.zeros((1, LANES), jnp.float32)
    for number in range(3):
        moved = pltpu.roll(second[number : number + 1], HEAD_DIM, 1)
        rows.append(jnp.where(lane < HEAD_DIM, first[number : number + 1], moved))
        rest = jnp.where(lane < LEFT, moved, 0.0)
        last = last + (pltpu.roll(rest, number * LEFT, 1) if number else rest)
    return jnp.concatenate(rows + [last], axis=0)


def unpack_kernel(slots, count, images, *refs):
    closed = is_closed(count)
    if not closed:
        lengths, table, *refs = refs
    msgs, refs = refs[: slots + OWN_HEADS - 1], refs[slots + OWN_HEADS - 1 :]
    *outs, held, ready, sems = refs
    early, late = msgs[:OWN_HEADS], list(msgs[OWN_HEADS:])
    late.insert(EARLY, None)
    me = lax.axis_index("tok")

    def place(slot, residue):
        for phase in range(OWN_HEADS):
            begin = pl.multiple_of((phase * SPAN + residue) * HEAD_DIM, 16)
            for number in range(4):
                if slot == EARLY:
                    piece = early[phase][message_rows(number), :]
                else:
                    piece = late[slot][message_rows(4 * phase + number), :]
                held[number, pl.ds(begin, HEAD_DIM), :] = piece

    for slot in range(slots):
        if closed:
            place(slot, lax.rem(me, SPAN) ^ closed_step(slot))
        else:
            _, start = image_of(me, lengths, images)
            source = table[slot, me]
            residue = lax.rem(source + SPAN, SPAN)
            chosen = (source >= 0) & (source == handler_of(start, residue, count))
            pl.when(chosen)(functools.partial(place, slot, residue))
    copies = []
    for number, out in enumerate(outs):
        ready[number] = held[number].T
        copies.append(pltpu.make_async_copy(ready.at[number], out, sems.at[number]))
        copies[-1].start()
    for copy in copies:
        copy.wait()


def bias_kernel(tiles, bias_out):
    def add(group, totals):
        return tuple(
            total + tiles[group * SPAN + residue] for residue, total in enumerate(totals)
        )

    groups = tiles.shape[0] // SPAN
    zero = jnp.zeros(tiles.shape[1:], jnp.float32)
    totals = lax.fori_loop(0, groups, add, (zero,) * SPAN, unroll=groups <= 8)
    for residue, total in enumerate(totals):
        first = residue * HEAD_DIM
        second = (SPAN + residue) * HEAD_DIM
        for number in range(3):
            row = slice(number, number + 1)
            bias_out[row, first : first + HEAD_DIM] = total[row, :HEAD_DIM]
            bias_out[row, second : second + FIT] = total[row, HEAD_DIM:]
            bias_out[row, second + FIT : second + HEAD_DIM] = total[
                3:4, number * LEFT : (number + 1) * LEFT
            ]


def on_device(query_in, key_in, value_in, out_grad, bias, lengths, widths):
    tokd = query_in.shape[1]
    model = query_in.shape[2]
    images = lengths.shape[1]
    count = lax.axis_size("tok")
    dp_size = lax.axis_size("dp")
    closed = is_closed(count)
    sources, targets = trade_tables(count)
    slots = sources.shape[0]
    span = slots * tokd
    smem = pl.BlockSpec(memory_space=pltpu.SMEM)
    vmem = pl.BlockSpec(memory_space=pltpu.VMEM)
    hbm = pl.BlockSpec(memory_space=pltpu.HBM)
    whole = jax.ShapeDtypeStruct((tokd, model), jnp.bfloat16)
    message = jax.ShapeDtypeStruct((4 * HEAD_DIM, tokd), jnp.bfloat16)
    joined = jax.ShapeDtypeStruct((OWN_HEADS * 4 * HEAD_DIM, tokd), jnp.bfloat16)
    devices = dp_size * count
    tokens_all = devices * tokd

    def params(mib):
        return pltpu.CompilerParams(vmem_limit_bytes=int(mib * 1024 * 1024))

    inputs = (query_in[0], key_in[0], value_in[0], out_grad[0])
    later = OWN_HEADS - 1
    lanes = max(end - begin for begin, end in (phase_lanes(p, model) for p in range(OWN_HEADS)))
    own_sends = pl.pallas_call(
        functools.partial(pack_kernel, closed),
        out_shape=[message] * slots,
        in_specs=[hbm] * 4,
        out_specs=[vmem] * slots,
        scratch_shapes=[
            pltpu.VMEM((4, tokd, lanes), jnp.bfloat16),
            pltpu.VMEM((4, lanes, tokd), jnp.bfloat16),
            pltpu.SemaphoreType.DMA((4,)),
        ],
        compiler_params=params(FIRST_PACK_KIB / 1024),
        name="pack_heads",
    )(*inputs)
    sends = [own_sends]
    rounds = trade_rounds(count)
    first = [sends[0][0]] + [
        lax.ppermute(send, "tok", pairs) for send, pairs in zip(sends[0][1:], rounds)
    ]
    table_shape = jax.ShapeDtypeStruct((HALF, span), jnp.float32)
    mask_rows = -(-slots * (slots + 1) // 8) * 8
    turned_shape = jax.ShapeDtypeStruct((3, LANES, tokd), jnp.bfloat16)
    plain_shape = jax.ShapeDtypeStruct((2, tokd, LANES), jnp.bfloat16)
    places = [] if closed else [jnp.asarray(sources)]
    out_shape = (
        [table_shape] * 2
        + [
            jax.ShapeDtypeStruct((mask_rows, tokd), jnp.float32),
            jax.ShapeDtypeStruct((OWN_HEADS * HEAD_DIM, LANES), jnp.float32),
        ]
        + [message] * (later * slots)
        + [turned_shape] * OWN_HEADS
        + [plain_shape] * OWN_HEADS
    )
    prepared = pl.pallas_call(
        functools.partial(prepare_kernel, slots, images, count, tokd),
        out_shape=out_shape,
        in_specs=[smem] * (2 + len(places)) + [vmem] + [hbm] * 4 + [vmem],
        out_specs=[vmem] * len(out_shape),
        scratch_shapes=[
            pltpu.VMEM((later, 4, tokd, lanes), jnp.bfloat16),
            pltpu.VMEM((later, 4, lanes, tokd), jnp.bfloat16),
            pltpu.SemaphoreType.DMA((later, 4)),
            pltpu.VMEM((model, LANES), jnp.float32),
        ],
        compiler_params=params(PREPARE_KIB / 1024),
        cost_estimate=pl.CostEstimate(flops=1_000_000, bytes_accessed=0, transcendentals=0),
        name="prepare",
    )(lengths, widths, *places, bias, *inputs, sends[0][0])
    tables, prepared = prepared[:4], prepared[4:]
    for phase in range(later):
        sends.append(prepared[phase * slots : (phase + 1) * slots])
    prepared = prepared[later * slots :]

    def stage_ahead(slot, phases, messages):
        number = len(phases)
        results = pl.pallas_call(
            functools.partial(stage_kernel, slot, phases, tokd),
            out_shape=[turned_shape] * number + [plain_shape] * number,
            in_specs=[vmem] * (3 + number),
            out_specs=[vmem] * (2 * number),
            compiler_params=params(16),
            cost_estimate=pl.CostEstimate(
                flops=1_000_000 * number, bytes_accessed=0, transcendentals=0
            ),
            name="stage_slot",
        )(tables[0], tables[1], tables[3], *messages)
        return [list(pair) for pair in zip(results[:number], results[number:])]

    phases = tuple(range(OWN_HEADS))
    own = [[prepared[phase], prepared[OWN_HEADS + phase]] for phase in phases]
    staged = [{0: pair} for pair in own]
    got = [first] + [[sent[0]] for sent in sends[1:]]
    latest = own
    for slot in range(1, slots):
        for phase in phases[1:]:
            send, latest = lax.optimization_barrier((sends[phase][slot], latest))
            got[phase].append(lax.ppermute(send, "tok", rounds[slot - 1]))
        if slot == 1:
            staged[0][0], staged[1][0] = latest
        else:
            staged[0][slot - 1] = latest[0]
        if slot + 1 < slots:
            latest = stage_ahead(slot, (0,), [first[slot]])
    early = []
    carried = []
    for phase in range(OWN_HEADS):
        last = phase + 1 == OWN_HEADS
        kept = [slot for slot in range(slots) if slot != EARLY]
        sums_shape = jax.ShapeDtypeStruct(
            (devices, 4, LANES) if last else (8, LANES), jnp.float32
        )
        *results, total = pl.pallas_call(
            functools.partial(
                attend_kernel,
                slots,
                tuple(staged[phase]),
                closed,
                tokd,
                phase,
                1.0 / tokens_all**0.5,
            ),
            out_shape=[message if slot == EARLY else joined for slot in range(slots)]
            + [sums_shape],
            in_specs=[vmem] * (4 + slots + 2 * len(staged[phase]) + len(carried)),
            out_specs=[vmem] * slots + [hbm if last else vmem],
            scratch_shapes=[pltpu.VMEM((LANES, span), jnp.bfloat16)] * 4
            + [pltpu.VMEM((span, LANES), jnp.bfloat16)] * 2
            + [pltpu.VMEM((2, span, tokd), jnp.float32)]
            + [pltpu.VMEM((span, span), jnp.bfloat16)] * 2
            + (
                [pltpu.VMEM(sums_shape.shape, jnp.float32), pltpu.SemaphoreType.DMA(())]
                if last
                else []
            ),
            compiler_params=params(32),
            cost_estimate=pl.CostEstimate(
                flops=12 * span * span * 256, bytes_accessed=0, transcendentals=0
            ),
            name="attend_head",
        )(*tables, *got[phase], *(one for pair in staged[phase].values() for one in pair), *carried)
        results[EARLY], early = lax.optimization_barrier((results[EARLY], early))
        early.append(send_back(results[EARLY], EARLY))
        carried = [total] + [results[slot] for slot in kept]
    tiles = lax.all_to_all(total, ("dp", "tok"), 0, 0, tiled=True)
    late = [send_back(results[slot], slot) for slot in kept]
    places = [] if closed else [lengths, jnp.asarray(targets)]
    outs = pl.pallas_call(
        functools.partial(unpack_kernel, slots, count, images),
        out_shape=[whole] * 4,
        in_specs=[smem] * len(places) + [vmem] * (OWN_HEADS + len(late)),
        out_specs=[hbm] * 4,
        scratch_shapes=[
            pltpu.VMEM((4, model, tokd), jnp.bfloat16),
            pltpu.VMEM((4, tokd, model), jnp.bfloat16),
            pltpu.SemaphoreType.DMA((4,)),
        ],
        compiler_params=params(16),
        cost_estimate=pl.CostEstimate(flops=UNPACK_FLOPS, bytes_accessed=0, transcendentals=0),
        name="unpack_heads",
    )(*places, *early, *late)
    outs, tiles = lax.optimization_barrier((outs, tiles))
    bias_grad = pl.pallas_call(
        bias_kernel,
        out_shape=jax.ShapeDtypeStruct((3, model), jnp.float32),
        in_specs=[vmem],
        out_specs=vmem,
        compiler_params=params(16),
        name="bias_sums",
    )(tiles)
    return tuple(out[None] for out in outs) + (bias_grad,)


def solution(mesh):
    in_specs = (
        P("dp", "tok", None),
        P("dp", "tok", None),
        P("dp", "tok", None),
        P("dp", "tok", None),
        P(),
        P("dp", None),
        P("dp", None),
    )
    out_specs = (
        P("dp", "tok", None),
        P("dp", "tok", None),
        P("dp", "tok", None),
        P("dp", "tok", None),
        P(),
    )
    return jax.shard_map(
        on_device, mesh=mesh, in_specs=in_specs, out_specs=out_specs, check_vma=False
    )
```

```python
import functools
import math

import jax
import jax.numpy as jnp
import numpy as np
from jax import lax
from jax.experimental import pallas as pl
from jax.experimental.pallas import tpu as pltpu
from jax.sharding import PartitionSpec as P

HEADS = 8
HEAD_DIM = 80
SPAN = 4
OWN_HEADS = HEADS // SPAN
PART = OWN_HEADS * HEAD_DIM
SCALE = HEAD_DIM**-0.5
LOG2E = 1.4426950408889634
NEG = -1e30
LANES = 128
USED = HEAD_DIM + 16
HALF = HEAD_DIM // 2
PIECES = 2
FIRST_PACK_KIB = 52 * 1024 + 1260
PREPARE_KIB = 52 * 1024 + 300
UNPACK_FLOPS = 20_000_000_000

rope_base = 10000.0


def is_closed(count):
    return count in (SPAN, 2 * SPAN)


def closed_step(slot):
    return (SPAN - slot) % SPAN


def trade_rounds(count):
    if is_closed(count):
        return [
            [(one, one ^ closed_step(slot)) for one in range(count)] for slot in range(1, SPAN)
        ]
    rounds = []
    for shift in [*range(1, SPAN), *range(-1, -SPAN, -1)]:
        rounds.append(
            [
                (source, source + shift)
                for source in range(max(0, -shift), min(count, count - shift))
                if (source < SPAN) == (source + shift < SPAN)
            ]
        )
    return rounds


def trade_tables(count):
    rounds = trade_rounds(count)
    sources = np.full((1 + len(rounds), count), -1, np.int32)
    targets = sources.copy()
    sources[0] = targets[0] = np.arange(count)
    for slot, pairs in enumerate(rounds, 1):
        for source, target in pairs:
            sources[slot, target] = source
            targets[slot, source] = target
    return sources, targets


def send_back(result, slot):
    if slot == 0:
        return result
    pairs = trade_rounds(lax.axis_size("tok"))[slot - 1]
    return lax.ppermute(result, "tok", [(target, source) for source, target in pairs])


EARLY = 1


def image_of(block, lengths, images):
    image = jnp.int32(0)
    start = jnp.int32(0)
    begin = jnp.int32(0)
    for number in range(images):
        size = lengths[0, number]
        inside = (block >= begin) & (block < begin + size)
        image = jnp.where(inside, number, image)
        start = jnp.where(inside, begin, start)
        begin = begin + size
    return image, start


def handler_of(start, residue, count):
    device = start + lax.rem(residue - lax.rem(start, SPAN) + SPAN, SPAN)
    return jnp.where(device >= count, device - SPAN, device)


def message_rows(tensor):
    return slice(tensor * HEAD_DIM, (tensor + 1) * HEAD_DIM)


def rotate(values, cosv, sinv):
    first, second = values[:HALF], values[HALF:]
    return jnp.concatenate([first * cosv - second * sinv, second * cosv + first * sinv], axis=0)


def unrotate(values, cosv, sinv):
    first, second = values[:HALF], values[HALF:]
    return jnp.concatenate([first * cosv + second * sinv, second * cosv - first * sinv], axis=0)


def phase_lanes(phase, model):
    size = SPAN * HEAD_DIM
    begin = phase * size // LANES * LANES
    end = -(-(phase + 1) * size // LANES) * LANES
    return begin, min(end, model)


def fetch(phase, inputs, held, sems):
    begin, end = phase_lanes(phase, inputs[0].shape[1])
    copies = [
        pltpu.make_async_copy(source.at[:, begin:end], held.at[number], sems.at[number])
        for number, source in enumerate(inputs)
    ]
    for copy in copies:
        copy.start()
    return copies


def pack(phase, closed, copies, outs, held, turned):
    me = lax.rem(lax.axis_index("tok"), SPAN)
    inner = phase * SPAN * HEAD_DIM % LANES
    steps = (
        [closed_step(slot) for slot in range(SPAN)]
        if closed
        else [0, *range(1, SPAN), *range(SPAN - 1, 0, -1)]
    )
    for number, copy in enumerate(copies):
        copy.wait()
        turned[number] = held[number].T
        for out, step in zip(outs, steps):
            residue = me ^ step if closed else lax.rem(me + step, SPAN)
            rows = pl.ds(pl.multiple_of(inner + residue * HEAD_DIM, 16), HEAD_DIM)
            out[message_rows(number), :] = turned[number, rows, :]


def pack_kernel(closed, *refs):
    inputs, outs, (held, turned, sems) = refs[:4], refs[4:-3], refs[-3:]
    pack(0, closed, fetch(0, inputs, held, sems), outs, held, turned)


def prepare_kernel(slots, images, count, tokd, lengths, widths, *refs):
    closed = is_closed(count)
    if not closed:
        table, *refs = refs
    later = OWN_HEADS - 1
    bias, *inputs, own = refs[:6]
    cos_out, sin_out, mask_out, bias_out, *refs = refs[6:]
    messages, refs = refs[: later * slots], refs[later * slots :]
    turned_out, plain_out = refs[:OWN_HEADS], refs[OWN_HEADS : 2 * OWN_HEADS]
    held, turned, sems, columns = refs[2 * OWN_HEADS :]
    copies = [
        fetch(phase + 1, inputs, held.at[phase], sems.at[phase]) for phase in range(later)
    ]
    me = lax.axis_index("tok")
    residue = lax.rem(me, SPAN)
    spot = lax.broadcasted_iota(jnp.int32, (HALF, tokd), 1)
    feature = lax.broadcasted_iota(jnp.int32, (HALF, tokd), 0)
    by_row = feature < HALF // 2
    feature = jnp.where(by_row, feature, feature - HALF // 2).astype(jnp.float32)
    inverse = jnp.exp(feature * (-math.log(rope_base) / (HALF // 2)))
    ids = []
    for slot in range(slots):
        block = me - residue + (residue ^ closed_step(slot)) if closed else table[slot, me]
        image, start = image_of(block, lengths, images)
        handled = (block >= 0) & (handler_of(start, residue, count) == me)
        ids.append(jnp.where(handled, image, -1 - slot))
        width = widths[0, image]
        bits = jnp.where(width == tokd, 0, jnp.where(width * 2 == tokd, 1, 2))
        shift = tokd.bit_length() - 1 - bits
        local = spot + (block - start) * tokd
        rowpos = lax.shift_right_logical(local, jnp.broadcast_to(shift, local.shape))
        colpos = local & (width - 1)
        angle = jnp.where(by_row, rowpos, colpos).astype(jnp.float32) * inverse
        cos_out[:, slot * tokd : (slot + 1) * tokd] = jnp.cos(angle)
        sin_out[:, slot * tokd : (slot + 1) * tokd] = jnp.sin(angle)
    for slot in range(slots):
        for other in range(slots):
            off = jnp.where(ids[slot] == ids[other], 0.0, NEG)
            row = slot * slots + other
            mask_out[row : row + 1, :] = jnp.full((1, tokd), off, jnp.float32)
        row = slots * slots + slot
        live = jnp.where(ids[slot] >= 0, 1.0, 0.0)
        mask_out[row : row + 1, :] = jnp.full((1, tokd), live, jnp.float32)
    plain = bias[...].astype(jnp.float32)
    rest = jnp.zeros((LANES - plain.shape[0], plain.shape[1]), jnp.float32)
    columns[...] = jnp.concatenate([plain, rest], axis=0).T
    for phase in range(OWN_HEADS):
        begin = pl.multiple_of((phase * SPAN + residue) * HEAD_DIM, 16)
        bias_out[phase * HEAD_DIM : (phase + 1) * HEAD_DIM, :] = columns[pl.ds(begin, HEAD_DIM), :]
    for phase in range(later):
        outs = messages[phase * slots : (phase + 1) * slots]
        pack(phase + 1, closed, copies[phase], outs, held.at[phase], turned.at[phase])
    owns = [own] + [messages[phase * slots] for phase in range(later)]
    stage_all(0, range(OWN_HEADS), tokd, cos_out, sin_out, bias_out, owns, turned_out, plain_out)


def stage(slot, tokd, message, cosv, sinv, bias):
    at = slice(slot * tokd, (slot + 1) * tokd)
    cos_b, sin_b = cosv[:, at], sinv[:, at]
    query, key, value = (
        message[message_rows(tensor), :].astype(jnp.float32) + bias[:, tensor : tensor + 1]
        for tensor in range(3)
    )
    rest_row = lax.broadcasted_iota(jnp.int32, (LANES - HEAD_DIM, tokd), 0)
    zeros = jnp.zeros((LANES - HEAD_DIM, tokd), jnp.float32)
    ones = jnp.where(rest_row < 2, 1.0, 0.0)
    return [
        jnp.concatenate(pair, axis=0).astype(jnp.bfloat16)
        for pair in (
            (rotate(query, cos_b, sin_b) * (SCALE * LOG2E), zeros),
            (rotate(key, cos_b, sin_b), zeros),
            (value, ones),
        )
    ]


def stage_all(slot, phases, tokd, cosv, sinv, bias, msgs, turned, plain):
    for number, phase in enumerate(phases):
        own_bias = bias[phase * HEAD_DIM : (phase + 1) * HEAD_DIM, :]
        values = stage(slot, tokd, msgs[number], cosv, sinv, own_bias)
        for tensor, value in enumerate(values):
            turned[number][tensor] = value
            if tensor > 0:
                plain[number][tensor - 1] = value.T


def stage_kernel(slot, phases, tokd, cosv, sinv, bias, *refs):
    count = len(phases)
    msgs, turned, plain = refs[:count], refs[count : 2 * count], refs[2 * count :]
    stage_all(slot, phases, tokd, cosv, sinv, bias, msgs, turned, plain)


def attend_kernel(slots, staged, closed, tokd, head, factor, cosv, sinv, masks, bias, *refs):
    msgs, refs = refs[:slots], refs[slots:]
    ready = {slot: refs[2 * at : 2 * at + 2] for at, slot in enumerate(staged)}
    refs = refs[2 * len(staged) :]
    earlier = ()
    if head > 0:
        before, earlier, refs = refs[0], refs[1:slots], refs[slots:]
    outs, sums = refs[:slots], refs[slots]
    for result, out in zip(earlier, [out for slot, out in enumerate(outs) if slot != EARLY]):
        done = head * 4 * HEAD_DIM
        out[:done, :] = result[:done, :]
    qt_all, kt_all, vt_all, gt_all, k_all, v_all, s_buf, e_buf, d_buf = refs[slots + 1 : slots + 10]
    own_bias = bias[head * HEAD_DIM : (head + 1) * HEAD_DIM, :]
    rest_row = lax.broadcasted_iota(jnp.int32, (LANES - HEAD_DIM, tokd), 0)

    by_lanes = (((1,), (1,)), ((), ()))

    def off_row(slot, other):
        row = slot * slots + other
        return masks[row : row + 1, :]

    def live(slot, values):
        if closed:
            return values
        row = slots * slots + slot
        return values * masks[row : row + 1, :]

    def block_of(slot):
        return slice(slot * tokd, (slot + 1) * tokd)

    def put(slot, tensor, values):
        begin = ((0 if slot == EARLY else 4 * head) + tensor) * HEAD_DIM
        outs[slot][begin : begin + HEAD_DIM, :] = values

    def pieces_of(other):
        step = tokd // PIECES
        return [
            slice(other * tokd + number * step, other * tokd + (number + 1) * step)
            for number in range(PIECES)
        ]

    def scores(slot, keys):
        part = jnp.dot(
            k_all[keys, :], qt_all[:, block_of(slot)], preferred_element_type=jnp.float32
        )
        s_buf[slot % 2, keys, :] = part
        return jnp.max(part, axis=0, keepdims=True)

    def exponentials(slot, keys, top):
        part = jnp.exp2(s_buf[slot % 2, keys, :] - top)
        e_buf[keys, block_of(slot)] = part.astype(jnp.bfloat16)

    def output(slot):
        mixed = jnp.dot(
            vt_all[:USED, :], e_buf[:, block_of(slot)], preferred_element_type=jnp.float32
        )
        inv = 1.0 / mixed[HEAD_DIM : HEAD_DIM + 1]
        out_b = (mixed[:HEAD_DIM] * inv).astype(jnp.bfloat16)
        put(slot, 0, out_b)
        grad = msgs[slot][message_rows(3), :].astype(jnp.float32)
        delta = jnp.sum(grad * out_b.astype(jnp.float32), axis=0, keepdims=True) * inv
        coarse = delta.astype(jnp.bfloat16).astype(jnp.float32)
        rest = jnp.where(rest_row == 0, -coarse, jnp.where(rest_row == 1, coarse - delta, 0.0))
        grad = jnp.concatenate([grad * inv, rest], axis=0).astype(jnp.bfloat16)
        gt_all[:, block_of(slot)] = grad
        spread = grad[:HEAD_DIM].astype(jnp.float32) * mixed[HEAD_DIM : HEAD_DIM + 1]
        return grad, live(slot, spread)

    def dscores(slot, keys, grad):
        part = jnp.dot(v_all[keys, :], grad, preferred_element_type=jnp.float32)
        d_buf[keys, block_of(slot)] = e_buf[keys, block_of(slot)] * part.astype(jnp.bfloat16)

    def query_part(slot):
        at = block_of(slot)
        dquery = jnp.dot(kt_all[:HEAD_DIM, :], d_buf[:, at], preferred_element_type=jnp.float32)
        dquery = unrotate(dquery * SCALE, cosv[:, at], sinv[:, at])
        put(slot, 1, dquery.astype(jnp.bfloat16))
        return live(slot, dquery)

    def value_part(slot):
        dvalue = lax.dot_general(
            gt_all[:HEAD_DIM, :],
            e_buf[block_of(slot), :],
            by_lanes,
            preferred_element_type=jnp.float32,
        )
        put(slot, 3, dvalue.astype(jnp.bfloat16))

    for slot in range(slots):
        at = block_of(slot)
        if slot in ready:
            turned, plain = ready[slot]
            values, natural = [turned[number] for number in range(3)], [plain[0], plain[1]]
        else:
            values = stage(slot, tokd, msgs[slot], cosv, sinv, own_bias)
            natural = [value.T for value in values[1:]]
        qt_all[:, at], kt_all[:, at], vt_all[:, at] = values
        k_all[at, :], v_all[at, :] = natural
    dq_total = jnp.zeros((HEAD_DIM, tokd), jnp.float32)
    dv_total = jnp.zeros((HEAD_DIM, tokd), jnp.float32)
    grad = None
    offs = tops = None
    for step in range(slots + 2):
        ahead, slot, behind = step, step - 1, step - 2
        if 0 <= slot < slots:
            offs = [off_row(slot, other) for other in range(slots)]
            top = functools.reduce(jnp.maximum, [one + off for one, off in zip(tops, offs)])
        tops = []
        for other in range(slots):
            found = []
            for keys in pieces_of(other):
                if ahead < slots:
                    found.append(scores(ahead, keys))
                if 0 <= behind:
                    dscores(behind, keys, grad)
                if 0 <= slot < slots:
                    exponentials(slot, keys, top - offs[other])
            if found:
                tops.append(functools.reduce(jnp.maximum, found))
        if 0 <= behind:
            dq_total = dq_total + query_part(behind)
        if 0 <= slot < slots:
            grad, spread = output(slot)
            dv_total = dv_total + spread
    dk_total = jnp.zeros((HEAD_DIM, tokd), jnp.float32)
    for slot in range(slots):
        at = block_of(slot)
        dkey = lax.dot_general(
            qt_all[:HEAD_DIM, :], d_buf[at, :], by_lanes, preferred_element_type=jnp.float32
        )
        dkey = unrotate(dkey * (1.0 / LOG2E), cosv[:, at], sinv[:, at])
        put(slot, 2, dkey.astype(jnp.bfloat16))
        dk_total = dk_total + live(slot, dkey)
    lane = lax.broadcasted_iota(jnp.int32, (HEAD_DIM, LANES), 1)
    columns = jnp.zeros((HEAD_DIM, LANES), jnp.float32)
    for number, total in enumerate((dq_total, dk_total, dv_total)):
        total = jnp.sum(total, axis=1, keepdims=True) * factor
        columns = jnp.where(lane == number, total, columns)
    columns = jnp.concatenate([columns, jnp.zeros((LANES - HEAD_DIM, LANES), jnp.float32)], axis=0)
    lines = columns.T
    copy = None
    if head + 1 < OWN_HEADS:
        sums[...] = lines[:8]
    else:
        tiles, sem = refs[slots + 10 :]
        tile = join_sums(before[...], lines)

        def repeat(device, carry):
            tiles[device] = tile
            return carry

        lax.fori_loop(0, tiles.shape[0], repeat, 0, unroll=min(32, tiles.shape[0]))
        copy = pltpu.make_async_copy(tiles, sums, sem)
        copy.start()
    for slot in range(slots):
        value_part(slot)
    if copy is not None:
        copy.wait()


FIT = LANES - HEAD_DIM
LEFT = HEAD_DIM - FIT


def join_sums(first, second):
    lane = lax.broadcasted_iota(jnp.int32, (1, LANES), 1)
    rows = []
    last = jnp.zeros((1, LANES), jnp.float32)
    for number in range(3):
        moved = pltpu.roll(second[number : number + 1], HEAD_DIM, 1)
        rows.append(jnp.where(lane < HEAD_DIM, first[number : number + 1], moved))
        rest = jnp.where(lane < LEFT, moved, 0.0)
        last = last + (pltpu.roll(rest, number * LEFT, 1) if number else rest)
    return jnp.concatenate(rows + [last], axis=0)


def unpack_kernel(slots, count, images, *refs):
    closed = is_closed(count)
    if not closed:
        lengths, table, *refs = refs
    msgs, refs = refs[: slots + OWN_HEADS - 1], refs[slots + OWN_HEADS - 1 :]
    *outs, held, ready, sems = refs
    early, late = msgs[:OWN_HEADS], list(msgs[OWN_HEADS:])
    late.insert(EARLY, None)
    me = lax.axis_index("tok")

    def place(slot, residue):
        for phase in range(OWN_HEADS):
            begin = pl.multiple_of((phase * SPAN + residue) * HEAD_DIM, 16)
            for number in range(4):
                if slot == EARLY:
                    piece = early[phase][message_rows(number), :]
                else:
                    piece = late[slot][message_rows(4 * phase + number), :]
                held[number, pl.ds(begin, HEAD_DIM), :] = piece

    for slot in range(slots):
        if closed:
            place(slot, lax.rem(me, SPAN) ^ closed_step(slot))
        else:
            _, start = image_of(me, lengths, images)
            source = table[slot, me]
            residue = lax.rem(source + SPAN, SPAN)
            chosen = (source >= 0) & (source == handler_of(start, residue, count))
            pl.when(chosen)(functools.partial(place, slot, residue))
    copies = []
    for number, out in enumerate(outs):
        ready[number] = held[number].T
        copies.append(pltpu.make_async_copy(ready.at[number], out, sems.at[number]))
        copies[-1].start()
    for copy in copies:
        copy.wait()


def bias_kernel(tiles, bias_out):
    def add(group, totals):
        return tuple(
            total + tiles[group * SPAN + residue] for residue, total in enumerate(totals)
        )

    groups = tiles.shape[0] // SPAN
    zero = jnp.zeros(tiles.shape[1:], jnp.float32)
    totals = lax.fori_loop(0, groups, add, (zero,) * SPAN, unroll=groups <= 8)
    for residue, total in enumerate(totals):
        first = residue * HEAD_DIM
        second = (SPAN + residue) * HEAD_DIM
        for number in range(3):
            row = slice(number, number + 1)
            bias_out[row, first : first + HEAD_DIM] = total[row, :HEAD_DIM]
            bias_out[row, second : second + FIT] = total[row, HEAD_DIM:]
            bias_out[row, second + FIT : second + HEAD_DIM] = total[
                3:4, number * LEFT : (number + 1) * LEFT
            ]


def on_device(query_in, key_in, value_in, out_grad, bias, lengths, widths):
    tokd = query_in.shape[1]
    model = query_in.shape[2]
    images = lengths.shape[1]
    count = lax.axis_size("tok")
    dp_size = lax.axis_size("dp")
    closed = is_closed(count)
    sources, targets = trade_tables(count)
    slots = sources.shape[0]
    span = slots * tokd
    smem = pl.BlockSpec(memory_space=pltpu.SMEM)
    vmem = pl.BlockSpec(memory_space=pltpu.VMEM)
    hbm = pl.BlockSpec(memory_space=pltpu.HBM)
    whole = jax.ShapeDtypeStruct((tokd, model), jnp.bfloat16)
    message = jax.ShapeDtypeStruct((4 * HEAD_DIM, tokd), jnp.bfloat16)
    joined = jax.ShapeDtypeStruct((OWN_HEADS * 4 * HEAD_DIM, tokd), jnp.bfloat16)
    devices = dp_size * count
    tokens_all = devices * tokd

    def params(mib):
        return pltpu.CompilerParams(vmem_limit_bytes=int(mib * 1024 * 1024))

    inputs = (query_in[0], key_in[0], value_in[0], out_grad[0])
    later = OWN_HEADS - 1
    lanes = max(end - begin for begin, end in (phase_lanes(p, model) for p in range(OWN_HEADS)))
    own_sends = pl.pallas_call(
        functools.partial(pack_kernel, closed),
        out_shape=[message] * slots,
        in_specs=[hbm] * 4,
        out_specs=[vmem] * slots,
        scratch_shapes=[
            pltpu.VMEM((4, tokd, lanes), jnp.bfloat16),
            pltpu.VMEM((4, lanes, tokd), jnp.bfloat16),
            pltpu.SemaphoreType.DMA((4,)),
        ],
        compiler_params=params(FIRST_PACK_KIB / 1024),
        name="pack_heads",
    )(*inputs)
    sends = [own_sends]
    rounds = trade_rounds(count)
    first = [sends[0][0]] + [
        lax.ppermute(send, "tok", pairs) for send, pairs in zip(sends[0][1:], rounds)
    ]
    table_shape = jax.ShapeDtypeStruct((HALF, span), jnp.float32)
    mask_rows = -(-slots * (slots + 1) // 8) * 8
    turned_shape = jax.ShapeDtypeStruct((3, LANES, tokd), jnp.bfloat16)
    plain_shape = jax.ShapeDtypeStruct((2, tokd, LANES), jnp.bfloat16)
    places = [] if closed else [jnp.asarray(sources)]
    out_shape = (
        [table_shape] * 2
        + [
            jax.ShapeDtypeStruct((mask_rows, tokd), jnp.float32),
            jax.ShapeDtypeStruct((OWN_HEADS * HEAD_DIM, LANES), jnp.float32),
        ]
        + [message] * (later * slots)
        + [turned_shape] * OWN_HEADS
        + [plain_shape] * OWN_HEADS
    )
    prepared = pl.pallas_call(
        functools.partial(prepare_kernel, slots, images, count, tokd),
        out_shape=out_shape,
        in_specs=[smem] * (2 + len(places)) + [vmem] + [hbm] * 4 + [vmem],
        out_specs=[vmem] * len(out_shape),
        scratch_shapes=[
            pltpu.VMEM((later, 4, tokd, lanes), jnp.bfloat16),
            pltpu.VMEM((later, 4, lanes, tokd), jnp.bfloat16),
            pltpu.SemaphoreType.DMA((later, 4)),
            pltpu.VMEM((model, LANES), jnp.float32),
        ],
        compiler_params=params(PREPARE_KIB / 1024),
        cost_estimate=pl.CostEstimate(flops=1_000_000, bytes_accessed=0, transcendentals=0),
        name="prepare",
    )(lengths, widths, *places, bias, *inputs, sends[0][0])
    tables, prepared = prepared[:4], prepared[4:]
    for phase in range(later):
        sends.append(prepared[phase * slots : (phase + 1) * slots])
    prepared = prepared[later * slots :]

    def stage_ahead(slot, phases, messages):
        number = len(phases)
        results = pl.pallas_call(
            functools.partial(stage_kernel, slot, phases, tokd),
            out_shape=[turned_shape] * number + [plain_shape] * number,
            in_specs=[vmem] * (3 + number),
            out_specs=[vmem] * (2 * number),
            compiler_params=params(16),
            cost_estimate=pl.CostEstimate(
                flops=1_000_000 * number, bytes_accessed=0, transcendentals=0
            ),
            name="stage_slot",
        )(tables[0], tables[1], tables[3], *messages)
        return [list(pair) for pair in zip(results[:number], results[number:])]

    phases = tuple(range(OWN_HEADS))
    own = [[prepared[phase], prepared[OWN_HEADS + phase]] for phase in phases]
    staged = [{0: pair} for pair in own]
    got = [first] + [[sent[0]] for sent in sends[1:]]
    for slot in range(1, slots - 1):
        latest = stage_ahead(slot, (0,), [first[slot]])
        for phase in phases[1:]:
            for leaving in (1, 2) if slot == 1 else (slot + 1,):
                send, latest = lax.optimization_barrier((sends[phase][leaving], latest))
                got[phase].append(lax.ppermute(send, "tok", rounds[leaving - 1]))
        staged[0][slot] = latest[0]
    early = []
    carried = []
    for phase in range(OWN_HEADS):
        last = phase + 1 == OWN_HEADS
        kept = [slot for slot in range(slots) if slot != EARLY]
        sums_shape = jax.ShapeDtypeStruct(
            (devices, 4, LANES) if last else (8, LANES), jnp.float32
        )
        *results, total = pl.pallas_call(
            functools.partial(
                attend_kernel,
                slots,
                tuple(staged[phase]),
                closed,
                tokd,
                phase,
                1.0 / tokens_all**0.5,
            ),
            out_shape=[message if slot == EARLY else joined for slot in range(slots)]
            + [sums_shape],
            in_specs=[vmem] * (4 + slots + 2 * len(staged[phase]) + len(carried)),
            out_specs=[vmem] * slots + [hbm if last else vmem],
            scratch_shapes=[pltpu.VMEM((LANES, span), jnp.bfloat16)] * 4
            + [pltpu.VMEM((span, LANES), jnp.bfloat16)] * 2
            + [pltpu.VMEM((2, span, tokd), jnp.float32)]
            + [pltpu.VMEM((span, span), jnp.bfloat16)] * 2
            + (
                [pltpu.VMEM(sums_shape.shape, jnp.float32), pltpu.SemaphoreType.DMA(())]
                if last
                else []
            ),
            compiler_params=params(32),
            cost_estimate=pl.CostEstimate(
                flops=12 * span * span * 256, bytes_accessed=0, transcendentals=0
            ),
            name="attend_head",
        )(*tables, *got[phase], *(one for pair in staged[phase].values() for one in pair), *carried)
        results[EARLY], early = lax.optimization_barrier((results[EARLY], early))
        early.append(send_back(results[EARLY], EARLY))
        carried = [total] + [results[slot] for slot in kept]
    tiles = lax.all_to_all(total, ("dp", "tok"), 0, 0, tiled=True)
    late = [send_back(results[slot], slot) for slot in kept]
    places = [] if closed else [lengths, jnp.asarray(targets)]
    outs = pl.pallas_call(
        functools.partial(unpack_kernel, slots, count, images),
        out_shape=[whole] * 4,
        in_specs=[smem] * len(places) + [vmem] * (OWN_HEADS + len(late)),
        out_specs=[hbm] * 4,
        scratch_shapes=[
            pltpu.VMEM((4, model, tokd), jnp.bfloat16),
            pltpu.VMEM((4, tokd, model), jnp.bfloat16),
            pltpu.SemaphoreType.DMA((4,)),
        ],
        compiler_params=params(16),
        cost_estimate=pl.CostEstimate(flops=UNPACK_FLOPS, bytes_accessed=0, transcendentals=0),
        name="unpack_heads",
    )(*places, *early, *late)
    outs, tiles = lax.optimization_barrier((outs, tiles))
    bias_grad = pl.pallas_call(
        bias_kernel,
        out_shape=jax.ShapeDtypeStruct((3, model), jnp.float32),
        in_specs=[vmem],
        out_specs=vmem,
        compiler_params=params(16),
        name="bias_sums",
    )(tiles)
    return tuple(out[None] for out in outs) + (bias_grad,)


def solution(mesh):
    in_specs = (
        P("dp", "tok", None),
        P("dp", "tok", None),
        P("dp", "tok", None),
        P("dp", "tok", None),
        P(),
        P("dp", None),
        P("dp", None),
    )
    out_specs = (
        P("dp", "tok", None),
        P("dp", "tok", None),
        P("dp", "tok", None),
        P("dp", "tok", None),
        P(),
    )
    return jax.shard_map(
        on_device, mesh=mesh, in_specs=in_specs, out_specs=out_specs, check_vma=False
    )
```

```python
import functools
import math

import jax
import jax.numpy as jnp
import numpy as np
from jax import lax
from jax.experimental import pallas as pl
from jax.experimental.pallas import tpu as pltpu
from jax.sharding import PartitionSpec as P

HEADS = 8
HEAD_DIM = 80
SPAN = 4
OWN_HEADS = HEADS // SPAN
PART = OWN_HEADS * HEAD_DIM
SCALE = HEAD_DIM**-0.5
LOG2E = 1.4426950408889634
NEG = -1e30
LANES = 128
USED = HEAD_DIM + 16
HALF = HEAD_DIM // 2
PIECES = 4
FIRST_PACK_KIB = 52 * 1024 + 1260
PREPARE_KIB = 52 * 1024 + 300
UNPACK_FLOPS = 20_000_000_000

rope_base = 10000.0


def is_closed(count):
    return count in (SPAN, 2 * SPAN)


def closed_step(slot):
    return (SPAN - slot) % SPAN


def trade_rounds(count):
    if is_closed(count):
        return [
            [(one, one ^ closed_step(slot)) for one in range(count)] for slot in range(1, SPAN)
        ]
    rounds = []
    for shift in [*range(1, SPAN), *range(-1, -SPAN, -1)]:
        rounds.append(
            [
                (source, source + shift)
                for source in range(max(0, -shift), min(count, count - shift))
                if (source < SPAN) == (source + shift < SPAN)
            ]
        )
    return rounds


def trade_tables(count):
    rounds = trade_rounds(count)
    sources = np.full((1 + len(rounds), count), -1, np.int32)
    targets = sources.copy()
    sources[0] = targets[0] = np.arange(count)
    for slot, pairs in enumerate(rounds, 1):
        for source, target in pairs:
            sources[slot, target] = source
            targets[slot, source] = target
    return sources, targets


def send_back(result, slot):
    if slot == 0:
        return result
    pairs = trade_rounds(lax.axis_size("tok"))[slot - 1]
    return lax.ppermute(result, "tok", [(target, source) for source, target in pairs])


EARLY = 1


def image_of(block, lengths, images):
    image = jnp.int32(0)
    start = jnp.int32(0)
    begin = jnp.int32(0)
    for number in range(images):
        size = lengths[0, number]
        inside = (block >= begin) & (block < begin + size)
        image = jnp.where(inside, number, image)
        start = jnp.where(inside, begin, start)
        begin = begin + size
    return image, start


def handler_of(start, residue, count):
    device = start + lax.rem(residue - lax.rem(start, SPAN) + SPAN, SPAN)
    return jnp.where(device >= count, device - SPAN, device)


def message_rows(tensor):
    return slice(tensor * HEAD_DIM, (tensor + 1) * HEAD_DIM)


def rotate(values, cosv, sinv):
    first, second = values[:HALF], values[HALF:]
    return jnp.concatenate([first * cosv - second * sinv, second * cosv + first * sinv], axis=0)


def unrotate(values, cosv, sinv):
    first, second = values[:HALF], values[HALF:]
    return jnp.concatenate([first * cosv + second * sinv, second * cosv - first * sinv], axis=0)


def phase_lanes(phase, model):
    size = SPAN * HEAD_DIM
    begin = phase * size // LANES * LANES
    end = -(-(phase + 1) * size // LANES) * LANES
    return begin, min(end, model)


def fetch(phase, inputs, held, sems):
    begin, end = phase_lanes(phase, inputs[0].shape[1])
    copies = [
        pltpu.make_async_copy(source.at[:, begin:end], held.at[number], sems.at[number])
        for number, source in enumerate(inputs)
    ]
    for copy in copies:
        copy.start()
    return copies


def pack(phase, closed, copies, outs, held, turned):
    me = lax.rem(lax.axis_index("tok"), SPAN)
    inner = phase * SPAN * HEAD_DIM % LANES
    steps = (
        [closed_step(slot) for slot in range(SPAN)]
        if closed
        else [0, *range(1, SPAN), *range(SPAN - 1, 0, -1)]
    )
    for number, copy in enumerate(copies):
        copy.wait()
        turned[number] = held[number].T
        for out, step in zip(outs, steps):
            residue = me ^ step if closed else lax.rem(me + step, SPAN)
            rows = pl.ds(pl.multiple_of(inner + residue * HEAD_DIM, 16), HEAD_DIM)
            out[message_rows(number), :] = turned[number, rows, :]


def pack_kernel(closed, *refs):
    inputs, outs, (held, turned, sems) = refs[:4], refs[4:-3], refs[-3:]
    pack(0, closed, fetch(0, inputs, held, sems), outs, held, turned)


def prepare_kernel(slots, images, count, tokd, lengths, widths, *refs):
    closed = is_closed(count)
    if not closed:
        table, *refs = refs
    later = OWN_HEADS - 1
    bias, *inputs, own = refs[:6]
    cos_out, sin_out, mask_out, bias_out, *refs = refs[6:]
    messages, refs = refs[: later * slots], refs[later * slots :]
    turned_out, plain_out = refs[:OWN_HEADS], refs[OWN_HEADS : 2 * OWN_HEADS]
    held, turned, sems, columns = refs[2 * OWN_HEADS :]
    copies = [
        fetch(phase + 1, inputs, held.at[phase], sems.at[phase]) for phase in range(later)
    ]
    me = lax.axis_index("tok")
    residue = lax.rem(me, SPAN)
    spot = lax.broadcasted_iota(jnp.int32, (HALF, tokd), 1)
    feature = lax.broadcasted_iota(jnp.int32, (HALF, tokd), 0)
    by_row = feature < HALF // 2
    feature = jnp.where(by_row, feature, feature - HALF // 2).astype(jnp.float32)
    inverse = jnp.exp(feature * (-math.log(rope_base) / (HALF // 2)))
    ids = []
    for slot in range(slots):
        block = me - residue + (residue ^ closed_step(slot)) if closed else table[slot, me]
        image, start = image_of(block, lengths, images)
        handled = (block >= 0) & (handler_of(start, residue, count) == me)
        ids.append(jnp.where(handled, image, -1 - slot))
        width = widths[0, image]
        bits = jnp.where(width == tokd, 0, jnp.where(width * 2 == tokd, 1, 2))
        shift = tokd.bit_length() - 1 - bits
        local = spot + (block - start) * tokd
        rowpos = lax.shift_right_logical(local, jnp.broadcast_to(shift, local.shape))
        colpos = local & (width - 1)
        angle = jnp.where(by_row, rowpos, colpos).astype(jnp.float32) * inverse
        cos_out[:, slot * tokd : (slot + 1) * tokd] = jnp.cos(angle)
        sin_out[:, slot * tokd : (slot + 1) * tokd] = jnp.sin(angle)
    for slot in range(slots):
        for other in range(slots):
            off = jnp.where(ids[slot] == ids[other], 0.0, NEG)
            row = slot * slots + other
            mask_out[row : row + 1, :] = jnp.full((1, tokd), off, jnp.float32)
        row = slots * slots + slot
        live = jnp.where(ids[slot] >= 0, 1.0, 0.0)
        mask_out[row : row + 1, :] = jnp.full((1, tokd), live, jnp.float32)
    plain = bias[...].astype(jnp.float32)
    rest = jnp.zeros((LANES - plain.shape[0], plain.shape[1]), jnp.float32)
    columns[...] = jnp.concatenate([plain, rest], axis=0).T
    for phase in range(OWN_HEADS):
        begin = pl.multiple_of((phase * SPAN + residue) * HEAD_DIM, 16)
        bias_out[phase * HEAD_DIM : (phase + 1) * HEAD_DIM, :] = columns[pl.ds(begin, HEAD_DIM), :]
    for phase in range(later):
        outs = messages[phase * slots : (phase + 1) * slots]
        pack(phase + 1, closed, copies[phase], outs, held.at[phase], turned.at[phase])
    owns = [own] + [messages[phase * slots] for phase in range(later)]
    stage_all(0, range(OWN_HEADS), tokd, cos_out, sin_out, bias_out, owns, turned_out, plain_out)


def stage(slot, tokd, message, cosv, sinv, bias):
    at = slice(slot * tokd, (slot + 1) * tokd)
    cos_b, sin_b = cosv[:, at], sinv[:, at]
    query, key, value = (
        message[message_rows(tensor), :].astype(jnp.float32) + bias[:, tensor : tensor + 1]
        for tensor in range(3)
    )
    rest_row = lax.broadcasted_iota(jnp.int32, (LANES - HEAD_DIM, tokd), 0)
    zeros = jnp.zeros((LANES - HEAD_DIM, tokd), jnp.float32)
    ones = jnp.where(rest_row < 2, 1.0, 0.0)
    return [
        jnp.concatenate(pair, axis=0).astype(jnp.bfloat16)
        for pair in (
            (rotate(query, cos_b, sin_b) * (SCALE * LOG2E), zeros),
            (rotate(key, cos_b, sin_b), zeros),
            (value, ones),
        )
    ]


def stage_all(slot, phases, tokd, cosv, sinv, bias, msgs, turned, plain):
    for number, phase in enumerate(phases):
        own_bias = bias[phase * HEAD_DIM : (phase + 1) * HEAD_DIM, :]
        values = stage(slot, tokd, msgs[number], cosv, sinv, own_bias)
        for tensor, value in enumerate(values):
            turned[number][tensor] = value
            if tensor > 0:
                plain[number][tensor - 1] = value.T


def stage_kernel(slot, phases, tokd, cosv, sinv, bias, *refs):
    count = len(phases)
    msgs, turned, plain = refs[:count], refs[count : 2 * count], refs[2 * count :]
    stage_all(slot, phases, tokd, cosv, sinv, bias, msgs, turned, plain)


def attend_kernel(slots, staged, closed, tokd, head, factor, cosv, sinv, masks, bias, *refs):
    msgs, refs = refs[:slots], refs[slots:]
    ready = {slot: refs[2 * at : 2 * at + 2] for at, slot in enumerate(staged)}
    refs = refs[2 * len(staged) :]
    earlier = ()
    if head > 0:
        before, earlier, refs = refs[0], refs[1:slots], refs[slots:]
    outs, sums = refs[:slots], refs[slots]
    for result, out in zip(earlier, [out for slot, out in enumerate(outs) if slot != EARLY]):
        done = head * 4 * HEAD_DIM
        out[:done, :] = result[:done, :]
    qt_all, kt_all, vt_all, gt_all, k_all, v_all, s_buf, e_buf, d_buf = refs[slots + 1 : slots + 10]
    own_bias = bias[head * HEAD_DIM : (head + 1) * HEAD_DIM, :]
    rest_row = lax.broadcasted_iota(jnp.int32, (LANES - HEAD_DIM, tokd), 0)

    by_lanes = (((1,), (1,)), ((), ()))

    def off_row(slot, other):
        row = slot * slots + other
        return masks[row : row + 1, :]

    def live(slot, values):
        if closed:
            return values
        row = slots * slots + slot
        return values * masks[row : row + 1, :]

    def block_of(slot):
        return slice(slot * tokd, (slot + 1) * tokd)

    def put(slot, tensor, values):
        begin = ((0 if slot == EARLY else 4 * head) + tensor) * HEAD_DIM
        outs[slot][begin : begin + HEAD_DIM, :] = values

    def pieces_of(other):
        step = tokd // PIECES
        return [
            slice(other * tokd + number * step, other * tokd + (number + 1) * step)
            for number in range(PIECES)
        ]

    def scores(slot, keys):
        part = jnp.dot(
            k_all[keys, :], qt_all[:, block_of(slot)], preferred_element_type=jnp.float32
        )
        s_buf[slot % 2, keys, :] = part
        return jnp.max(part, axis=0, keepdims=True)

    def exponentials(slot, keys, top):
        part = jnp.exp2(s_buf[slot % 2, keys, :] - top)
        e_buf[keys, block_of(slot)] = part.astype(jnp.bfloat16)

    def output(slot):
        mixed = jnp.dot(
            vt_all[:USED, :], e_buf[:, block_of(slot)], preferred_element_type=jnp.float32
        )
        inv = 1.0 / mixed[HEAD_DIM : HEAD_DIM + 1]
        out_b = (mixed[:HEAD_DIM] * inv).astype(jnp.bfloat16)
        put(slot, 0, out_b)
        grad = msgs[slot][message_rows(3), :].astype(jnp.float32)
        delta = jnp.sum(grad * out_b.astype(jnp.float32), axis=0, keepdims=True) * inv
        coarse = delta.astype(jnp.bfloat16).astype(jnp.float32)
        rest = jnp.where(rest_row == 0, -coarse, jnp.where(rest_row == 1, coarse - delta, 0.0))
        grad = jnp.concatenate([grad * inv, rest], axis=0).astype(jnp.bfloat16)
        gt_all[:, block_of(slot)] = grad
        spread = grad[:HEAD_DIM].astype(jnp.float32) * mixed[HEAD_DIM : HEAD_DIM + 1]
        return grad, live(slot, spread)

    def dscores(slot, keys, grad):
        part = jnp.dot(v_all[keys, :], grad, preferred_element_type=jnp.float32)
        d_buf[keys, block_of(slot)] = e_buf[keys, block_of(slot)] * part.astype(jnp.bfloat16)

    def query_part(slot):
        at = block_of(slot)
        dquery = jnp.dot(kt_all[:HEAD_DIM, :], d_buf[:, at], preferred_element_type=jnp.float32)
        dquery = unrotate(dquery * SCALE, cosv[:, at], sinv[:, at])
        put(slot, 1, dquery.astype(jnp.bfloat16))
        return live(slot, dquery)

    def value_part(slot):
        dvalue = lax.dot_general(
            gt_all[:HEAD_DIM, :],
            e_buf[block_of(slot), :],
            by_lanes,
            preferred_element_type=jnp.float32,
        )
        put(slot, 3, dvalue.astype(jnp.bfloat16))

    for slot in range(slots):
        at = block_of(slot)
        if slot in ready:
            turned, plain = ready[slot]
            values, natural = [turned[number] for number in range(3)], [plain[0], plain[1]]
        else:
            values = stage(slot, tokd, msgs[slot], cosv, sinv, own_bias)
            natural = [value.T for value in values[1:]]
        qt_all[:, at], kt_all[:, at], vt_all[:, at] = values
        k_all[at, :], v_all[at, :] = natural
    dq_total = jnp.zeros((HEAD_DIM, tokd), jnp.float32)
    dv_total = jnp.zeros((HEAD_DIM, tokd), jnp.float32)
    grad = None
    offs = tops = None
    for step in range(slots + 2):
        ahead, slot, behind = step, step - 1, step - 2
        if 0 <= slot < slots:
            offs = [off_row(slot, other) for other in range(slots)]
            top = functools.reduce(jnp.maximum, [one + off for one, off in zip(tops, offs)])
        tops = []
        for other in range(slots):
            found = []
            for keys in pieces_of(other):
                if ahead < slots:
                    found.append(scores(ahead, keys))
                if 0 <= behind:
                    dscores(behind, keys, grad)
                if 0 <= slot < slots:
                    exponentials(slot, keys, top - offs[other])
            if found:
                tops.append(functools.reduce(jnp.maximum, found))
        if 0 <= behind:
            dq_total = dq_total + query_part(behind)
        if 0 <= slot < slots:
            grad, spread = output(slot)
            dv_total = dv_total + spread
    dk_total = jnp.zeros((HEAD_DIM, tokd), jnp.float32)
    for slot in range(slots):
        at = block_of(slot)
        dkey = lax.dot_general(
            qt_all[:HEAD_DIM, :], d_buf[at, :], by_lanes, preferred_element_type=jnp.float32
        )
        dkey = unrotate(dkey * (1.0 / LOG2E), cosv[:, at], sinv[:, at])
        put(slot, 2, dkey.astype(jnp.bfloat16))
        dk_total = dk_total + live(slot, dkey)
    for slot in range(slots // 2):
        value_part(slot)
    lane = lax.broadcasted_iota(jnp.int32, (HEAD_DIM, LANES), 1)
    columns = jnp.zeros((HEAD_DIM, LANES), jnp.float32)
    for number, total in enumerate((dq_total, dk_total, dv_total)):
        total = jnp.sum(total, axis=1, keepdims=True) * factor
        columns = jnp.where(lane == number, total, columns)
    columns = jnp.concatenate([columns, jnp.zeros((LANES - HEAD_DIM, LANES), jnp.float32)], axis=0)
    lines = columns.T
    copy = None
    if head + 1 < OWN_HEADS:
        sums[...] = lines[:8]
    else:
        tiles, sem = refs[slots + 10 :]
        tile = join_sums(before[...], lines)

        def repeat(device, carry):
            tiles[device] = tile
            return carry

        lax.fori_loop(0, tiles.shape[0], repeat, 0, unroll=min(32, tiles.shape[0]))
        copy = pltpu.make_async_copy(tiles, sums, sem)
        copy.start()
    for slot in range(slots // 2, slots):
        value_part(slot)
    if copy is not None:
        copy.wait()


FIT = LANES - HEAD_DIM
LEFT = HEAD_DIM - FIT


def join_sums(first, second):
    lane = lax.broadcasted_iota(jnp.int32, (1, LANES), 1)
    rows = []
    last = jnp.zeros((1, LANES), jnp.float32)
    for number in range(3):
        moved = pltpu.roll(second[number : number + 1], HEAD_DIM, 1)
        rows.append(jnp.where(lane < HEAD_DIM, first[number : number + 1], moved))
        rest = jnp.where(lane < LEFT, moved, 0.0)
        last = last + (pltpu.roll(rest, number * LEFT, 1) if number else rest)
    return jnp.concatenate(rows + [last], axis=0)


def unpack_kernel(slots, count, images, *refs):
    closed = is_closed(count)
    if not closed:
        lengths, table, *refs = refs
    msgs, refs = refs[: slots + OWN_HEADS - 1], refs[slots + OWN_HEADS - 1 :]
    *outs, held, ready, sems = refs
    early, late = msgs[:OWN_HEADS], list(msgs[OWN_HEADS:])
    late.insert(EARLY, None)
    me = lax.axis_index("tok")

    def place(slot, residue):
        for phase in range(OWN_HEADS):
            begin = pl.multiple_of((phase * SPAN + residue) * HEAD_DIM, 16)
            for number in range(4):
                if slot == EARLY:
                    piece = early[phase][message_rows(number), :]
                else:
                    piece = late[slot][message_rows(4 * phase + number), :]
                held[number, pl.ds(begin, HEAD_DIM), :] = piece

    for slot in range(slots):
        if closed:
            place(slot, lax.rem(me, SPAN) ^ closed_step(slot))
        else:
            _, start = image_of(me, lengths, images)
            source = table[slot, me]
            residue = lax.rem(source + SPAN, SPAN)
            chosen = (source >= 0) & (source == handler_of(start, residue, count))
            pl.when(chosen)(functools.partial(place, slot, residue))
    copies = []
    for number, out in enumerate(outs):
        ready[number] = held[number].T
        copies.append(pltpu.make_async_copy(ready.at[number], out, sems.at[number]))
        copies[-1].start()
    for copy in copies:
        copy.wait()


def bias_kernel(tiles, bias_out):
    def add(group, totals):
        return tuple(
            total + tiles[group * SPAN + residue] for residue, total in enumerate(totals)
        )

    groups = tiles.shape[0] // SPAN
    zero = jnp.zeros(tiles.shape[1:], jnp.float32)
    totals = lax.fori_loop(0, groups, add, (zero,) * SPAN, unroll=groups <= 8)
    for residue, total in enumerate(totals):
        first = residue * HEAD_DIM
        second = (SPAN + residue) * HEAD_DIM
        for number in range(3):
            row = slice(number, number + 1)
            bias_out[row, first : first + HEAD_DIM] = total[row, :HEAD_DIM]
            bias_out[row, second : second + FIT] = total[row, HEAD_DIM:]
            bias_out[row, second + FIT : second + HEAD_DIM] = total[
                3:4, number * LEFT : (number + 1) * LEFT
            ]


def on_device(query_in, key_in, value_in, out_grad, bias, lengths, widths):
    tokd = query_in.shape[1]
    model = query_in.shape[2]
    images = lengths.shape[1]
    count = lax.axis_size("tok")
    dp_size = lax.axis_size("dp")
    closed = is_closed(count)
    sources, targets = trade_tables(count)
    slots = sources.shape[0]
    span = slots * tokd
    smem = pl.BlockSpec(memory_space=pltpu.SMEM)
    vmem = pl.BlockSpec(memory_space=pltpu.VMEM)
    hbm = pl.BlockSpec(memory_space=pltpu.HBM)
    whole = jax.ShapeDtypeStruct((tokd, model), jnp.bfloat16)
    message = jax.ShapeDtypeStruct((4 * HEAD_DIM, tokd), jnp.bfloat16)
    joined = jax.ShapeDtypeStruct((OWN_HEADS * 4 * HEAD_DIM, tokd), jnp.bfloat16)
    devices = dp_size * count
    tokens_all = devices * tokd

    def params(mib):
        return pltpu.CompilerParams(vmem_limit_bytes=int(mib * 1024 * 1024))

    inputs = (query_in[0], key_in[0], value_in[0], out_grad[0])
    later = OWN_HEADS - 1
    lanes = max(end - begin for begin, end in (phase_lanes(p, model) for p in range(OWN_HEADS)))
    own_sends = pl.pallas_call(
        functools.partial(pack_kernel, closed),
        out_shape=[message] * slots,
        in_specs=[hbm] * 4,
        out_specs=[vmem] * slots,
        scratch_shapes=[
            pltpu.VMEM((4, tokd, lanes), jnp.bfloat16),
            pltpu.VMEM((4, lanes, tokd), jnp.bfloat16),
            pltpu.SemaphoreType.DMA((4,)),
        ],
        compiler_params=params(FIRST_PACK_KIB / 1024),
        name="pack_heads",
    )(*inputs)
    sends = [own_sends]
    rounds = trade_rounds(count)
    first = [sends[0][0]] + [
        lax.ppermute(send, "tok", pairs) for send, pairs in zip(sends[0][1:], rounds)
    ]
    table_shape = jax.ShapeDtypeStruct((HALF, span), jnp.float32)
    mask_rows = -(-slots * (slots + 1) // 8) * 8
    turned_shape = jax.ShapeDtypeStruct((3, LANES, tokd), jnp.bfloat16)
    plain_shape = jax.ShapeDtypeStruct((2, tokd, LANES), jnp.bfloat16)
    places = [] if closed else [jnp.asarray(sources)]
    out_shape = (
        [table_shape] * 2
        + [
            jax.ShapeDtypeStruct((mask_rows, tokd), jnp.float32),
            jax.ShapeDtypeStruct((OWN_HEADS * HEAD_DIM, LANES), jnp.float32),
        ]
        + [message] * (later * slots)
        + [turned_shape] * OWN_HEADS
        + [plain_shape] * OWN_HEADS
    )
    prepared = pl.pallas_call(
        functools.partial(prepare_kernel, slots, images, count, tokd),
        out_shape=out_shape,
        in_specs=[smem] * (2 + len(places)) + [vmem] + [hbm] * 4 + [vmem],
        out_specs=[vmem] * len(out_shape),
        scratch_shapes=[
            pltpu.VMEM((later, 4, tokd, lanes), jnp.bfloat16),
            pltpu.VMEM((later, 4, lanes, tokd), jnp.bfloat16),
            pltpu.SemaphoreType.DMA((later, 4)),
            pltpu.VMEM((model, LANES), jnp.float32),
        ],
        compiler_params=params(PREPARE_KIB / 1024),
        cost_estimate=pl.CostEstimate(flops=1_000_000, bytes_accessed=0, transcendentals=0),
        name="prepare",
    )(lengths, widths, *places, bias, *inputs, sends[0][0])
    tables, prepared = prepared[:4], prepared[4:]
    for phase in range(later):
        sends.append(prepared[phase * slots : (phase + 1) * slots])
    prepared = prepared[later * slots :]

    def stage_ahead(slot, phases, messages):
        number = len(phases)
        results = pl.pallas_call(
            functools.partial(stage_kernel, slot, phases, tokd),
            out_shape=[turned_shape] * number + [plain_shape] * number,
            in_specs=[vmem] * (3 + number),
            out_specs=[vmem] * (2 * number),
            compiler_params=params(16),
            cost_estimate=pl.CostEstimate(
                flops=1_000_000 * number, bytes_accessed=0, transcendentals=0
            ),
            name="stage_slot",
        )(tables[0], tables[1], tables[3], *messages)
        return [list(pair) for pair in zip(results[:number], results[number:])]

    phases = tuple(range(OWN_HEADS))
    own = [[prepared[phase], prepared[OWN_HEADS + phase]] for phase in phases]
    staged = [{0: pair} for pair in own]
    got = [first] + [[sent[0]] for sent in sends[1:]]
    for slot in range(1, slots - 1):
        latest = stage_ahead(slot, (0,), [first[slot]])
        for phase in phases[1:]:
            for leaving in (1, 2) if slot == 1 else (slot + 1,):
                send, latest = lax.optimization_barrier((sends[phase][leaving], latest))
                got[phase].append(lax.ppermute(send, "tok", rounds[leaving - 1]))
        staged[0][slot] = latest[0]
    early = []
    carried = []
    for phase in range(OWN_HEADS):
        last = phase + 1 == OWN_HEADS
        kept = [slot for slot in range(slots) if slot != EARLY]
        sums_shape = jax.ShapeDtypeStruct(
            (devices, 4, LANES) if last else (8, LANES), jnp.float32
        )
        *results, total = pl.pallas_call(
            functools.partial(
                attend_kernel,
                slots,
                tuple(staged[phase]),
                closed,
                tokd,
                phase,
                1.0 / tokens_all**0.5,
            ),
            out_shape=[message if slot == EARLY else joined for slot in range(slots)]
            + [sums_shape],
            in_specs=[vmem] * (4 + slots + 2 * len(staged[phase]) + len(carried)),
            out_specs=[vmem] * slots + [hbm if last else vmem],
            scratch_shapes=[pltpu.VMEM((LANES, span), jnp.bfloat16)] * 4
            + [pltpu.VMEM((span, LANES), jnp.bfloat16)] * 2
            + [pltpu.VMEM((2, span, tokd), jnp.float32)]
            + [pltpu.VMEM((span, span), jnp.bfloat16)] * 2
            + (
                [pltpu.VMEM(sums_shape.shape, jnp.float32), pltpu.SemaphoreType.DMA(())]
                if last
                else []
            ),
            compiler_params=params(32),
            cost_estimate=pl.CostEstimate(
                flops=12 * span * span * 256, bytes_accessed=0, transcendentals=0
            ),
            name="attend_head",
        )(*tables, *got[phase], *(one for pair in staged[phase].values() for one in pair), *carried)
        results[EARLY], early = lax.optimization_barrier((results[EARLY], early))
        early.append(send_back(results[EARLY], EARLY))
        carried = [total] + [results[slot] for slot in kept]
    tiles = lax.all_to_all(total, ("dp", "tok"), 0, 0, tiled=True)
    late = [send_back(results[slot], slot) for slot in kept]
    places = [] if closed else [lengths, jnp.asarray(targets)]
    outs = pl.pallas_call(
        functools.partial(unpack_kernel, slots, count, images),
        out_shape=[whole] * 4,
        in_specs=[smem] * len(places) + [vmem] * (OWN_HEADS + len(late)),
        out_specs=[hbm] * 4,
        scratch_shapes=[
            pltpu.VMEM((4, model, tokd), jnp.bfloat16),
            pltpu.VMEM((4, tokd, model), jnp.bfloat16),
            pltpu.SemaphoreType.DMA((4,)),
        ],
        compiler_params=params(16),
        cost_estimate=pl.CostEstimate(flops=UNPACK_FLOPS, bytes_accessed=0, transcendentals=0),
        name="unpack_heads",
    )(*places, *early, *late)
    outs, tiles = lax.optimization_barrier((outs, tiles))
    bias_grad = pl.pallas_call(
        bias_kernel,
        out_shape=jax.ShapeDtypeStruct((3, model), jnp.float32),
        in_specs=[vmem],
        out_specs=vmem,
        compiler_params=params(16),
        name="bias_sums",
    )(tiles)
    return tuple(out[None] for out in outs) + (bias_grad,)


def solution(mesh):
    in_specs = (
        P("dp", "tok", None),
        P("dp", "tok", None),
        P("dp", "tok", None),
        P("dp", "tok", None),
        P(),
        P("dp", None),
        P("dp", None),
    )
    out_specs = (
        P("dp", "tok", None),
        P("dp", "tok", None),
        P("dp", "tok", None),
        P("dp", "tok", None),
        P(),
    )
    return jax.shard_map(
        on_device, mesh=mesh, in_specs=in_specs, out_specs=out_specs, check_vma=False
    )
```

```python
import functools
import math

import jax
import jax.numpy as jnp
import numpy as np
from jax import lax
from jax.experimental import pallas as pl
from jax.experimental.pallas import tpu as pltpu
from jax.sharding import PartitionSpec as P

HEADS = 8
HEAD_DIM = 80
SPAN = 4
OWN_HEADS = HEADS // SPAN
PART = OWN_HEADS * HEAD_DIM
SCALE = HEAD_DIM**-0.5
LOG2E = 1.4426950408889634
NEG = -1e30
LANES = 128
USED = HEAD_DIM + 16
HALF = HEAD_DIM // 2
PIECES = 2
FIRST_PACK_KIB = 52 * 1024 + 1260
PREPARE_KIB = 52 * 1024 + 300
UNPACK_FLOPS = 20_000_000_000

rope_base = 10000.0


def is_closed(count):
    return count in (SPAN, 2 * SPAN)


def closed_step(slot):
    return (SPAN - slot) % SPAN


def trade_rounds(count):
    if is_closed(count):
        return [
            [(one, one ^ closed_step(slot)) for one in range(count)] for slot in range(1, SPAN)
        ]
    rounds = []
    for shift in [*range(1, SPAN), *range(-1, -SPAN, -1)]:
        rounds.append(
            [
                (source, source + shift)
                for source in range(max(0, -shift), min(count, count - shift))
                if (source < SPAN) == (source + shift < SPAN)
            ]
        )
    return rounds


def trade_tables(count):
    rounds = trade_rounds(count)
    sources = np.full((1 + len(rounds), count), -1, np.int32)
    targets = sources.copy()
    sources[0] = targets[0] = np.arange(count)
    for slot, pairs in enumerate(rounds, 1):
        for source, target in pairs:
            sources[slot, target] = source
            targets[slot, source] = target
    return sources, targets


def send_back(result, slot):
    if slot == 0:
        return result
    pairs = trade_rounds(lax.axis_size("tok"))[slot - 1]
    return lax.ppermute(result, "tok", [(target, source) for source, target in pairs])


EARLY = 1


def image_of(block, lengths, images):
    image = jnp.int32(0)
    start = jnp.int32(0)
    begin = jnp.int32(0)
    for number in range(images):
        size = lengths[0, number]
        inside = (block >= begin) & (block < begin + size)
        image = jnp.where(inside, number, image)
        start = jnp.where(inside, begin, start)
        begin = begin + size
    return image, start


def handler_of(start, residue, count):
    device = start + lax.rem(residue - lax.rem(start, SPAN) + SPAN, SPAN)
    return jnp.where(device >= count, device - SPAN, device)


def message_rows(tensor):
    return slice(tensor * HEAD_DIM, (tensor + 1) * HEAD_DIM)


def rotate(values, cosv, sinv):
    first, second = values[:HALF], values[HALF:]
    return jnp.concatenate([first * cosv - second * sinv, second * cosv + first * sinv], axis=0)


def unrotate(values, cosv, sinv):
    first, second = values[:HALF], values[HALF:]
    return jnp.concatenate([first * cosv + second * sinv, second * cosv - first * sinv], axis=0)


def phase_lanes(phase, model):
    size = SPAN * HEAD_DIM
    begin = phase * size // LANES * LANES
    end = -(-(phase + 1) * size // LANES) * LANES
    return begin, min(end, model)


def fetch(phase, inputs, held, sems):
    begin, end = phase_lanes(phase, inputs[0].shape[1])
    copies = [
        pltpu.make_async_copy(source.at[:, begin:end], held.at[number], sems.at[number])
        for number, source in enumerate(inputs)
    ]
    for copy in copies:
        copy.start()
    return copies


def pack(phase, closed, copies, outs, held, turned):
    me = lax.rem(lax.axis_index("tok"), SPAN)
    inner = phase * SPAN * HEAD_DIM % LANES
    steps = (
        [closed_step(slot) for slot in range(SPAN)]
        if closed
        else [0, *range(1, SPAN), *range(SPAN - 1, 0, -1)]
    )
    for number, copy in enumerate(copies):
        copy.wait()
        turned[number] = held[number].T
        for out, step in zip(outs, steps):
            residue = me ^ step if closed else lax.rem(me + step, SPAN)
            rows = pl.ds(pl.multiple_of(inner + residue * HEAD_DIM, 16), HEAD_DIM)
            out[message_rows(number), :] = turned[number, rows, :]


def pack_kernel(closed, *refs):
    inputs, outs, (held, turned, sems) = refs[:4], refs[4:-3], refs[-3:]
    pack(0, closed, fetch(0, inputs, held, sems), outs, held, turned)


def prepare_kernel(slots, images, count, tokd, lengths, widths, *refs):
    closed = is_closed(count)
    if not closed:
        table, *refs = refs
    later = OWN_HEADS - 1
    bias, *inputs, own = refs[:6]
    cos_out, sin_out, mask_out, bias_out, *refs = refs[6:]
    messages, refs = refs[: later * slots], refs[later * slots :]
    turned_out, plain_out = refs[:OWN_HEADS], refs[OWN_HEADS : 2 * OWN_HEADS]
    held, turned, sems, columns = refs[2 * OWN_HEADS :]
    copies = [
        fetch(phase + 1, inputs, held.at[phase], sems.at[phase]) for phase in range(later)
    ]
    me = lax.axis_index("tok")
    residue = lax.rem(me, SPAN)
    spot = lax.broadcasted_iota(jnp.int32, (HALF, tokd), 1)
    feature = lax.broadcasted_iota(jnp.int32, (HALF, tokd), 0)
    by_row = feature < HALF // 2
    feature = jnp.where(by_row, feature, feature - HALF // 2).astype(jnp.float32)
    inverse = jnp.exp(feature * (-math.log(rope_base) / (HALF // 2)))
    ids = []
    for slot in range(slots):
        block = me - residue + (residue ^ closed_step(slot)) if closed else table[slot, me]
        image, start = image_of(block, lengths, images)
        handled = (block >= 0) & (handler_of(start, residue, count) == me)
        ids.append(jnp.where(handled, image, -1 - slot))
        width = widths[0, image]
        bits = jnp.where(width == tokd, 0, jnp.where(width * 2 == tokd, 1, 2))
        shift = tokd.bit_length() - 1 - bits
        local = spot + (block - start) * tokd
        rowpos = lax.shift_right_logical(local, jnp.broadcast_to(shift, local.shape))
        colpos = local & (width - 1)
        angle = jnp.where(by_row, rowpos, colpos).astype(jnp.float32) * inverse
        cos_out[:, slot * tokd : (slot + 1) * tokd] = jnp.cos(angle)
        sin_out[:, slot * tokd : (slot + 1) * tokd] = jnp.sin(angle)
    for slot in range(slots):
        for other in range(slots):
            off = jnp.where(ids[slot] == ids[other], 0.0, NEG)
            row = slot * slots + other
            mask_out[row : row + 1, :] = jnp.full((1, tokd), off, jnp.float32)
        row = slots * slots + slot
        live = jnp.where(ids[slot] >= 0, 1.0, 0.0)
        mask_out[row : row + 1, :] = jnp.full((1, tokd), live, jnp.float32)
    plain = bias[...].astype(jnp.float32)
    rest = jnp.zeros((LANES - plain.shape[0], plain.shape[1]), jnp.float32)
    columns[...] = jnp.concatenate([plain, rest], axis=0).T
    for phase in range(OWN_HEADS):
        begin = pl.multiple_of((phase * SPAN + residue) * HEAD_DIM, 16)
        bias_out[phase * HEAD_DIM : (phase + 1) * HEAD_DIM, :] = columns[pl.ds(begin, HEAD_DIM), :]
    for phase in range(later):
        outs = messages[phase * slots : (phase + 1) * slots]
        pack(phase + 1, closed, copies[phase], outs, held.at[phase], turned.at[phase])
    owns = [own] + [messages[phase * slots] for phase in range(later)]
    stage_all(0, range(OWN_HEADS), tokd, cos_out, sin_out, bias_out, owns, turned_out, plain_out)


def stage(slot, tokd, message, cosv, sinv, bias):
    at = slice(slot * tokd, (slot + 1) * tokd)
    cos_b, sin_b = cosv[:, at], sinv[:, at]
    query, key, value = (
        message[message_rows(tensor), :].astype(jnp.float32) + bias[:, tensor : tensor + 1]
        for tensor in range(3)
    )
    rest_row = lax.broadcasted_iota(jnp.int32, (LANES - HEAD_DIM, tokd), 0)
    zeros = jnp.zeros((LANES - HEAD_DIM, tokd), jnp.float32)
    ones = jnp.where(rest_row < 2, 1.0, 0.0)
    return [
        jnp.concatenate(pair, axis=0).astype(jnp.bfloat16)
        for pair in (
            (rotate(query, cos_b, sin_b) * (SCALE * LOG2E), zeros),
            (rotate(key, cos_b, sin_b), zeros),
            (value, ones),
        )
    ]


def stage_all(slot, phases, tokd, cosv, sinv, bias, msgs, turned, plain):
    for number, phase in enumerate(phases):
        own_bias = bias[phase * HEAD_DIM : (phase + 1) * HEAD_DIM, :]
        values = stage(slot, tokd, msgs[number], cosv, sinv, own_bias)
        for tensor, value in enumerate(values):
            turned[number][tensor] = value
            if tensor > 0:
                plain[number][tensor - 1] = value.T


def stage_kernel(slot, phases, tokd, cosv, sinv, bias, *refs):
    count = len(phases)
    msgs, turned, plain = refs[:count], refs[count : 2 * count], refs[2 * count :]
    stage_all(slot, phases, tokd, cosv, sinv, bias, msgs, turned, plain)


def attend_kernel(slots, staged, closed, tokd, head, factor, cosv, sinv, masks, bias, *refs):
    msgs, refs = refs[:slots], refs[slots:]
    ready = {slot: refs[2 * at : 2 * at + 2] for at, slot in enumerate(staged)}
    refs = refs[2 * len(staged) :]
    earlier = ()
    if head > 0:
        before, earlier, refs = refs[0], refs[1:slots], refs[slots:]
    outs, sums = refs[:slots], refs[slots]
    for result, out in zip(earlier, [out for slot, out in enumerate(outs) if slot != EARLY]):
        done = head * 4 * HEAD_DIM
        out[:done, :] = result[:done, :]
    qt_all, kt_all, vt_all, gt_all, k_all, v_all, s_buf, e_buf, d_buf = refs[slots + 1 : slots + 10]
    own_bias = bias[head * HEAD_DIM : (head + 1) * HEAD_DIM, :]
    rest_row = lax.broadcasted_iota(jnp.int32, (LANES - HEAD_DIM, tokd), 0)

    by_lanes = (((1,), (1,)), ((), ()))

    def off_row(slot, other):
        row = slot * slots + other
        return masks[row : row + 1, :]

    def live(slot, values):
        if closed:
            return values
        row = slots * slots + slot
        return values * masks[row : row + 1, :]

    def block_of(slot):
        return slice(slot * tokd, (slot + 1) * tokd)

    def put(slot, tensor, values):
        begin = ((0 if slot == EARLY else 4 * head) + tensor) * HEAD_DIM
        outs[slot][begin : begin + HEAD_DIM, :] = values

    def pieces_of(other):
        step = tokd // PIECES
        return [
            slice(other * tokd + number * step, other * tokd + (number + 1) * step)
            for number in range(PIECES)
        ]

    def scores(slot, keys):
        part = jnp.dot(
            k_all[keys, :], qt_all[:, block_of(slot)], preferred_element_type=jnp.float32
        )
        s_buf[slot % 2, keys, :] = part
        return jnp.max(part, axis=0, keepdims=True)

    def exponentials(slot, keys, top):
        part = jnp.exp2(s_buf[slot % 2, keys, :] - top)
        e_buf[keys, block_of(slot)] = part.astype(jnp.bfloat16)

    def output(slot):
        mixed = jnp.dot(
            vt_all[:USED, :], e_buf[:, block_of(slot)], preferred_element_type=jnp.float32
        )
        inv = 1.0 / mixed[HEAD_DIM : HEAD_DIM + 1]
        out_b = (mixed[:HEAD_DIM] * inv).astype(jnp.bfloat16)
        put(slot, 0, out_b)
        grad = msgs[slot][message_rows(3), :].astype(jnp.float32)
        delta = jnp.sum(grad * out_b.astype(jnp.float32), axis=0, keepdims=True) * inv
        coarse = delta.astype(jnp.bfloat16).astype(jnp.float32)
        rest = jnp.where(rest_row == 0, -coarse, jnp.where(rest_row == 1, coarse - delta, 0.0))
        grad = jnp.concatenate([grad * inv, rest], axis=0).astype(jnp.bfloat16)
        gt_all[:, block_of(slot)] = grad
        spread = grad[:HEAD_DIM].astype(jnp.float32) * mixed[HEAD_DIM : HEAD_DIM + 1]
        return grad, live(slot, spread)

    def dscores(slot, keys, grad):
        part = jnp.dot(v_all[keys, :], grad, preferred_element_type=jnp.float32)
        d_buf[keys, block_of(slot)] = e_buf[keys, block_of(slot)] * part.astype(jnp.bfloat16)

    def query_part(slot):
        at = block_of(slot)
        dquery = jnp.dot(kt_all[:HEAD_DIM, :], d_buf[:, at], preferred_element_type=jnp.float32)
        dquery = unrotate(dquery * SCALE, cosv[:, at], sinv[:, at])
        put(slot, 1, dquery.astype(jnp.bfloat16))
        return live(slot, dquery)

    def value_part(slot):
        dvalue = lax.dot_general(
            gt_all[:HEAD_DIM, :],
            e_buf[block_of(slot), :],
            by_lanes,
            preferred_element_type=jnp.float32,
        )
        put(slot, 3, dvalue.astype(jnp.bfloat16))

    for slot in range(slots):
        at = block_of(slot)
        if slot in ready:
            turned, plain = ready[slot]
            values, natural = [turned[number] for number in range(3)], [plain[0], plain[1]]
        else:
            values = stage(slot, tokd, msgs[slot], cosv, sinv, own_bias)
            natural = [value.T for value in values[1:]]
        qt_all[:, at], kt_all[:, at], vt_all[:, at] = values
        k_all[at, :], v_all[at, :] = natural
    dq_total = jnp.zeros((HEAD_DIM, tokd), jnp.float32)
    dv_total = jnp.zeros((HEAD_DIM, tokd), jnp.float32)
    grad = None
    offs = tops = None
    for step in range(slots + 2):
        ahead, slot, behind = step, step - 1, step - 2
        if 0 <= slot < slots:
            offs = [off_row(slot, other) for other in range(slots)]
            top = functools.reduce(jnp.maximum, [one + off for one, off in zip(tops, offs)])
        tops = []
        for other in range(slots):
            found = []
            for keys in pieces_of(other):
                if ahead < slots:
                    found.append(scores(ahead, keys))
                if 0 <= behind:
                    dscores(behind, keys, grad)
                if 0 <= slot < slots:
                    exponentials(slot, keys, top - offs[other])
            if found:
                tops.append(functools.reduce(jnp.maximum, found))
        if 0 <= behind:
            dq_total = dq_total + query_part(behind)
        if 0 <= slot < slots:
            grad, spread = output(slot)
            dv_total = dv_total + spread
    dk_total = jnp.zeros((HEAD_DIM, tokd), jnp.float32)
    for slot in range(slots):
        at = block_of(slot)
        dkey = lax.dot_general(
            qt_all[:HEAD_DIM, :], d_buf[at, :], by_lanes, preferred_element_type=jnp.float32
        )
        dkey = unrotate(dkey * (1.0 / LOG2E), cosv[:, at], sinv[:, at])
        put(slot, 2, dkey.astype(jnp.bfloat16))
        dk_total = dk_total + live(slot, dkey)
    lane = lax.broadcasted_iota(jnp.int32, (HEAD_DIM, LANES), 1)
    columns = jnp.zeros((HEAD_DIM, LANES), jnp.float32)
    for number, total in enumerate((dq_total, dk_total, dv_total)):
        total = jnp.sum(total, axis=1, keepdims=True) * factor
        columns = jnp.where(lane == number, total, columns)
    columns = jnp.concatenate([columns, jnp.zeros((LANES - HEAD_DIM, LANES), jnp.float32)], axis=0)
    lines = columns.T
    copy = None
    if head + 1 < OWN_HEADS:
        sums[...] = lines[:8]
    else:
        tiles, sem = refs[slots + 10 :]
        tile = join_sums(before[...], lines)

        def repeat(device, carry):
            tiles[device] = tile
            return carry

        lax.fori_loop(0, tiles.shape[0], repeat, 0, unroll=min(32, tiles.shape[0]))
        copy = pltpu.make_async_copy(tiles, sums, sem)
        copy.start()
    for slot in range(slots):
        value_part(slot)
    if copy is not None:
        copy.wait()


FIT = LANES - HEAD_DIM
LEFT = HEAD_DIM - FIT


def join_sums(first, second):
    lane = lax.broadcasted_iota(jnp.int32, (1, LANES), 1)
    rows = []
    last = jnp.zeros((1, LANES), jnp.float32)
    for number in range(3):
        moved = pltpu.roll(second[number : number + 1], HEAD_DIM, 1)
        rows.append(jnp.where(lane < HEAD_DIM, first[number : number + 1], moved))
        rest = jnp.where(lane < LEFT, moved, 0.0)
        last = last + (pltpu.roll(rest, number * LEFT, 1) if number else rest)
    return jnp.concatenate(rows + [last], axis=0)


def unpack_kernel(slots, count, images, *refs):
    closed = is_closed(count)
    if not closed:
        lengths, table, *refs = refs
    msgs, refs = refs[: slots + OWN_HEADS - 1], refs[slots + OWN_HEADS - 1 :]
    *outs, held, ready, sems = refs
    early, late = msgs[:OWN_HEADS], list(msgs[OWN_HEADS:])
    late.insert(EARLY, None)
    me = lax.axis_index("tok")

    def place(slot, residue):
        for phase in range(OWN_HEADS):
            begin = pl.multiple_of((phase * SPAN + residue) * HEAD_DIM, 16)
            for number in range(4):
                if slot == EARLY:
                    piece = early[phase][message_rows(number), :]
                else:
                    piece = late[slot][message_rows(4 * phase + number), :]
                held[number, pl.ds(begin, HEAD_DIM), :] = piece

    for slot in range(slots):
        if closed:
            place(slot, lax.rem(me, SPAN) ^ closed_step(slot))
        else:
            _, start = image_of(me, lengths, images)
            source = table[slot, me]
            residue = lax.rem(source + SPAN, SPAN)
            chosen = (source >= 0) & (source == handler_of(start, residue, count))
            pl.when(chosen)(functools.partial(place, slot, residue))
    copies = []
    for number, out in enumerate(outs):
        ready[number] = held[number].T
        copies.append(pltpu.make_async_copy(ready.at[number], out, sems.at[number]))
        copies[-1].start()
    for copy in copies:
        copy.wait()


def bias_kernel(tiles, bias_out):
    def add(group, totals):
        return tuple(
            total + tiles[group * SPAN + residue] for residue, total in enumerate(totals)
        )

    groups = tiles.shape[0] // SPAN
    zero = jnp.zeros(tiles.shape[1:], jnp.float32)
    totals = lax.fori_loop(0, groups, add, (zero,) * SPAN, unroll=groups <= 8)
    for residue, total in enumerate(totals):
        first = residue * HEAD_DIM
        second = (SPAN + residue) * HEAD_DIM
        for number in range(3):
            row = slice(number, number + 1)
            bias_out[row, first : first + HEAD_DIM] = total[row, :HEAD_DIM]
            bias_out[row, second : second + FIT] = total[row, HEAD_DIM:]
            bias_out[row, second + FIT : second + HEAD_DIM] = total[
                3:4, number * LEFT : (number + 1) * LEFT
            ]


def on_device(query_in, key_in, value_in, out_grad, bias, lengths, widths):
    tokd = query_in.shape[1]
    model = query_in.shape[2]
    images = lengths.shape[1]
    count = lax.axis_size("tok")
    dp_size = lax.axis_size("dp")
    closed = is_closed(count)
    sources, targets = trade_tables(count)
    slots = sources.shape[0]
    span = slots * tokd
    smem = pl.BlockSpec(memory_space=pltpu.SMEM)
    vmem = pl.BlockSpec(memory_space=pltpu.VMEM)
    hbm = pl.BlockSpec(memory_space=pltpu.HBM)
    whole = jax.ShapeDtypeStruct((tokd, model), jnp.bfloat16)
    message = jax.ShapeDtypeStruct((4 * HEAD_DIM, tokd), jnp.bfloat16)
    joined = jax.ShapeDtypeStruct((OWN_HEADS * 4 * HEAD_DIM, tokd), jnp.bfloat16)
    devices = dp_size * count
    tokens_all = devices * tokd

    def params(mib):
        return pltpu.CompilerParams(vmem_limit_bytes=int(mib * 1024 * 1024))

    inputs = (query_in[0], key_in[0], value_in[0], out_grad[0])
    later = OWN_HEADS - 1
    lanes = max(end - begin for begin, end in (phase_lanes(p, model) for p in range(OWN_HEADS)))
    own_sends = pl.pallas_call(
        functools.partial(pack_kernel, closed),
        out_shape=[message] * slots,
        in_specs=[hbm] * 4,
        out_specs=[vmem] * slots,
        scratch_shapes=[
            pltpu.VMEM((4, tokd, lanes), jnp.bfloat16),
            pltpu.VMEM((4, lanes, tokd), jnp.bfloat16),
            pltpu.SemaphoreType.DMA((4,)),
        ],
        compiler_params=params(FIRST_PACK_KIB / 1024),
        name="pack_heads",
    )(*inputs)
    sends = [own_sends]
    rounds = trade_rounds(count)
    first = [sends[0][0]] + [
        lax.ppermute(send, "tok", pairs) for send, pairs in zip(sends[0][1:], rounds)
    ]
    table_shape = jax.ShapeDtypeStruct((HALF, span), jnp.float32)
    mask_rows = -(-slots * (slots + 1) // 8) * 8
    turned_shape = jax.ShapeDtypeStruct((3, LANES, tokd), jnp.bfloat16)
    plain_shape = jax.ShapeDtypeStruct((2, tokd, LANES), jnp.bfloat16)
    places = [] if closed else [jnp.asarray(sources)]
    out_shape = (
        [table_shape] * 2
        + [
            jax.ShapeDtypeStruct((mask_rows, tokd), jnp.float32),
            jax.ShapeDtypeStruct((OWN_HEADS * HEAD_DIM, LANES), jnp.float32),
        ]
        + [message] * (later * slots)
        + [turned_shape] * OWN_HEADS
        + [plain_shape] * OWN_HEADS
    )
    prepared = pl.pallas_call(
        functools.partial(prepare_kernel, slots, images, count, tokd),
        out_shape=out_shape,
        in_specs=[smem] * (2 + len(places)) + [vmem] + [hbm] * 4 + [vmem],
        out_specs=[vmem] * len(out_shape),
        scratch_shapes=[
            pltpu.VMEM((later, 4, tokd, lanes), jnp.bfloat16),
            pltpu.VMEM((later, 4, lanes, tokd), jnp.bfloat16),
            pltpu.SemaphoreType.DMA((later, 4)),
            pltpu.VMEM((model, LANES), jnp.float32),
        ],
        compiler_params=params(PREPARE_KIB / 1024),
        cost_estimate=pl.CostEstimate(flops=1_000_000, bytes_accessed=0, transcendentals=0),
        name="prepare",
    )(lengths, widths, *places, bias, *inputs, sends[0][0])
    tables, prepared = prepared[:4], prepared[4:]
    for phase in range(later):
        sends.append(prepared[phase * slots : (phase + 1) * slots])
    prepared = prepared[later * slots :]

    def stage_ahead(slot, phases, messages):
        number = len(phases)
        results = pl.pallas_call(
            functools.partial(stage_kernel, slot, phases, tokd),
            out_shape=[turned_shape] * number + [plain_shape] * number,
            in_specs=[vmem] * (3 + number),
            out_specs=[vmem] * (2 * number),
            compiler_params=params(16),
            cost_estimate=pl.CostEstimate(
                flops=1_000_000 * number, bytes_accessed=0, transcendentals=0
            ),
            name="stage_slot",
        )(tables[0], tables[1], tables[3], *messages)
        return [list(pair) for pair in zip(results[:number], results[number:])]

    phases = tuple(range(OWN_HEADS))
    own = [[prepared[phase], prepared[OWN_HEADS + phase]] for phase in phases]
    staged = [{0: pair} for pair in own]
    got = [first] + [[sent[0]] for sent in sends[1:]]
    for phase in phases[1:]:
        got[phase] += [None] * (slots - 2)
        got[phase].append(lax.ppermute(sends[phase][-1], "tok", rounds[-1]))
    for slot in range(1, slots - 1):
        latest = stage_ahead(slot, (0,), [first[slot]])
        for phase in phases[1:]:
            send, latest = lax.optimization_barrier((sends[phase][slot], latest))
            got[phase][slot] = lax.ppermute(send, "tok", rounds[slot - 1])
        staged[0][slot] = latest[0]
    early = []
    carried = []
    for phase in range(OWN_HEADS):
        last = phase + 1 == OWN_HEADS
        kept = [slot for slot in range(slots) if slot != EARLY]
        sums_shape = jax.ShapeDtypeStruct(
            (devices, 4, LANES) if last else (8, LANES), jnp.float32
        )
        *results, total = pl.pallas_call(
            functools.partial(
                attend_kernel,
                slots,
                tuple(staged[phase]),
                closed,
                tokd,
                phase,
                1.0 / tokens_all**0.5,
            ),
            out_shape=[message if slot == EARLY else joined for slot in range(slots)]
            + [sums_shape],
            in_specs=[vmem] * (4 + slots + 2 * len(staged[phase]) + len(carried)),
            out_specs=[vmem] * slots + [hbm if last else vmem],
            scratch_shapes=[pltpu.VMEM((LANES, span), jnp.bfloat16)] * 4
            + [pltpu.VMEM((span, LANES), jnp.bfloat16)] * 2
            + [pltpu.VMEM((2, span, tokd), jnp.float32)]
            + [pltpu.VMEM((span, span), jnp.bfloat16)] * 2
            + (
                [pltpu.VMEM(sums_shape.shape, jnp.float32), pltpu.SemaphoreType.DMA(())]
                if last
                else []
            ),
            compiler_params=params(32),
            cost_estimate=pl.CostEstimate(
                flops=12 * span * span * 256, bytes_accessed=0, transcendentals=0
            ),
            name="attend_head",
        )(*tables, *got[phase], *(one for pair in staged[phase].values() for one in pair), *carried)
        results[EARLY], early = lax.optimization_barrier((results[EARLY], early))
        early.append(send_back(results[EARLY], EARLY))
        carried = [total] + [results[slot] for slot in kept]
    tiles = lax.all_to_all(total, ("dp", "tok"), 0, 0, tiled=True)
    late = [send_back(results[slot], slot) for slot in kept]
    places = [] if closed else [lengths, jnp.asarray(targets)]
    outs = pl.pallas_call(
        functools.partial(unpack_kernel, slots, count, images),
        out_shape=[whole] * 4,
        in_specs=[smem] * len(places) + [vmem] * (OWN_HEADS + len(late)),
        out_specs=[hbm] * 4,
        scratch_shapes=[
            pltpu.VMEM((4, model, tokd), jnp.bfloat16),
            pltpu.VMEM((4, tokd, model), jnp.bfloat16),
            pltpu.SemaphoreType.DMA((4,)),
        ],
        compiler_params=params(16),
        cost_estimate=pl.CostEstimate(flops=UNPACK_FLOPS, bytes_accessed=0, transcendentals=0),
        name="unpack_heads",
    )(*places, *early, *late)
    outs, tiles = lax.optimization_barrier((outs, tiles))
    bias_grad = pl.pallas_call(
        bias_kernel,
        out_shape=jax.ShapeDtypeStruct((3, model), jnp.float32),
        in_specs=[vmem],
        out_specs=vmem,
        compiler_params=params(16),
        name="bias_sums",
    )(tiles)
    return tuple(out[None] for out in outs) + (bias_grad,)


def solution(mesh):
    in_specs = (
        P("dp", "tok", None),
        P("dp", "tok", None),
        P("dp", "tok", None),
        P("dp", "tok", None),
        P(),
        P("dp", None),
        P("dp", None),
    )
    out_specs = (
        P("dp", "tok", None),
        P("dp", "tok", None),
        P("dp", "tok", None),
        P("dp", "tok", None),
        P(),
    )
    return jax.shard_map(
        on_device, mesh=mesh, in_specs=in_specs, out_specs=out_specs, check_vma=False
    )
```

```python
import functools
import math

import jax
import jax.numpy as jnp
import numpy as np
from jax import lax
from jax.experimental import pallas as pl
from jax.experimental.pallas import tpu as pltpu
from jax.sharding import PartitionSpec as P

HEADS = 8
HEAD_DIM = 80
SPAN = 4
OWN_HEADS = HEADS // SPAN
PART = OWN_HEADS * HEAD_DIM
SCALE = HEAD_DIM**-0.5
LOG2E = 1.4426950408889634
NEG = -1e30
LANES = 128
USED = HEAD_DIM + 16
HALF = HEAD_DIM // 2
PIECES = 2
FIRST_PACK_KIB = 52 * 1024 + 1260
PREPARE_KIB = 52 * 1024 + 300
UNPACK_FLOPS = 20_000_000_000

rope_base = 10000.0


def is_closed(count):
    return count in (SPAN, 2 * SPAN)


def closed_step(slot):
    return (SPAN - slot) % SPAN


def trade_rounds(count):
    if is_closed(count):
        return [
            [(one, one ^ closed_step(slot)) for one in range(count)] for slot in range(1, SPAN)
        ]
    rounds = []
    for shift in [*range(1, SPAN), *range(-1, -SPAN, -1)]:
        rounds.append(
            [
                (source, source + shift)
                for source in range(max(0, -shift), min(count, count - shift))
                if (source < SPAN) == (source + shift < SPAN)
            ]
        )
    return rounds


def trade_tables(count):
    rounds = trade_rounds(count)
    sources = np.full((1 + len(rounds), count), -1, np.int32)
    targets = sources.copy()
    sources[0] = targets[0] = np.arange(count)
    for slot, pairs in enumerate(rounds, 1):
        for source, target in pairs:
            sources[slot, target] = source
            targets[slot, source] = target
    return sources, targets


def send_back(result, slot):
    if slot == 0:
        return result
    pairs = trade_rounds(lax.axis_size("tok"))[slot - 1]
    return lax.ppermute(result, "tok", [(target, source) for source, target in pairs])


EARLY = 1


def image_of(block, lengths, images):
    image = jnp.int32(0)
    start = jnp.int32(0)
    begin = jnp.int32(0)
    for number in range(images):
        size = lengths[0, number]
        inside = (block >= begin) & (block < begin + size)
        image = jnp.where(inside, number, image)
        start = jnp.where(inside, begin, start)
        begin = begin + size
    return image, start


def handler_of(start, residue, count):
    device = start + lax.rem(residue - lax.rem(start, SPAN) + SPAN, SPAN)
    return jnp.where(device >= count, device - SPAN, device)


def message_rows(tensor):
    return slice(tensor * HEAD_DIM, (tensor + 1) * HEAD_DIM)


def rotate(values, cosv, sinv):
    first, second = values[:HALF], values[HALF:]
    return jnp.concatenate([first * cosv - second * sinv, second * cosv + first * sinv], axis=0)


def unrotate(values, cosv, sinv):
    first, second = values[:HALF], values[HALF:]
    return jnp.concatenate([first * cosv + second * sinv, second * cosv - first * sinv], axis=0)


def phase_lanes(phase, model):
    size = SPAN * HEAD_DIM
    begin = phase * size // LANES * LANES
    end = -(-(phase + 1) * size // LANES) * LANES
    return begin, min(end, model)


def fetch(phase, inputs, held, sems):
    begin, end = phase_lanes(phase, inputs[0].shape[1])
    copies = [
        pltpu.make_async_copy(source.at[:, begin:end], held.at[number], sems.at[number])
        for number, source in enumerate(inputs)
    ]
    for copy in copies:
        copy.start()
    return copies


def pack(phase, closed, copies, outs, held, turned):
    me = lax.rem(lax.axis_index("tok"), SPAN)
    inner = phase * SPAN * HEAD_DIM % LANES
    steps = (
        [closed_step(slot) for slot in range(SPAN)]
        if closed
        else [0, *range(1, SPAN), *range(SPAN - 1, 0, -1)]
    )
    for number, copy in enumerate(copies):
        copy.wait()
        turned[number] = held[number].T
        for out, step in zip(outs, steps):
            residue = me ^ step if closed else lax.rem(me + step, SPAN)
            rows = pl.ds(pl.multiple_of(inner + residue * HEAD_DIM, 16), HEAD_DIM)
            out[message_rows(number), :] = turned[number, rows, :]


def pack_kernel(closed, *refs):
    inputs, outs, (held, turned, sems) = refs[:4], refs[4:-3], refs[-3:]
    pack(0, closed, fetch(0, inputs, held, sems), outs, held, turned)


def prepare_kernel(slots, images, count, tokd, lengths, widths, *refs):
    closed = is_closed(count)
    if not closed:
        table, *refs = refs
    later = OWN_HEADS - 1
    bias, *inputs, own = refs[:6]
    cos_out, sin_out, mask_out, bias_out, *refs = refs[6:]
    messages, refs = refs[: later * slots], refs[later * slots :]
    turned_out, plain_out = refs[:OWN_HEADS], refs[OWN_HEADS : 2 * OWN_HEADS]
    held, turned, sems, columns = refs[2 * OWN_HEADS :]
    copies = [
        fetch(phase + 1, inputs, held.at[phase], sems.at[phase]) for phase in range(later)
    ]
    me = lax.axis_index("tok")
    residue = lax.rem(me, SPAN)
    spot = lax.broadcasted_iota(jnp.int32, (HALF, tokd), 1)
    feature = lax.broadcasted_iota(jnp.int32, (HALF, tokd), 0)
    by_row = feature < HALF // 2
    feature = jnp.where(by_row, feature, feature - HALF // 2).astype(jnp.float32)
    inverse = jnp.exp(feature * (-math.log(rope_base) / (HALF // 2)))
    ids = []
    for slot in range(slots):
        block = me - residue + (residue ^ closed_step(slot)) if closed else table[slot, me]
        image, start = image_of(block, lengths, images)
        handled = (block >= 0) & (handler_of(start, residue, count) == me)
        ids.append(jnp.where(handled, image, -1 - slot))
        width = widths[0, image]
        bits = jnp.where(width == tokd, 0, jnp.where(width * 2 == tokd, 1, 2))
        shift = tokd.bit_length() - 1 - bits
        local = spot + (block - start) * tokd
        rowpos = lax.shift_right_logical(local, jnp.broadcast_to(shift, local.shape))
        colpos = local & (width - 1)
        angle = jnp.where(by_row, rowpos, colpos).astype(jnp.float32) * inverse
        cos_out[:, slot * tokd : (slot + 1) * tokd] = jnp.cos(angle)
        sin_out[:, slot * tokd : (slot + 1) * tokd] = jnp.sin(angle)
    for slot in range(slots):
        for other in range(slots):
            off = jnp.where(ids[slot] == ids[other], 0.0, NEG)
            row = slot * slots + other
            mask_out[row : row + 1, :] = jnp.full((1, tokd), off, jnp.float32)
        row = slots * slots + slot
        live = jnp.where(ids[slot] >= 0, 1.0, 0.0)
        mask_out[row : row + 1, :] = jnp.full((1, tokd), live, jnp.float32)
    plain = bias[...].astype(jnp.float32)
    rest = jnp.zeros((LANES - plain.shape[0], plain.shape[1]), jnp.float32)
    columns[...] = jnp.concatenate([plain, rest], axis=0).T
    for phase in range(OWN_HEADS):
        begin = pl.multiple_of((phase * SPAN + residue) * HEAD_DIM, 16)
        bias_out[phase * HEAD_DIM : (phase + 1) * HEAD_DIM, :] = columns[pl.ds(begin, HEAD_DIM), :]
    for phase in range(later):
        outs = messages[phase * slots : (phase + 1) * slots]
        pack(phase + 1, closed, copies[phase], outs, held.at[phase], turned.at[phase])
    owns = [own] + [messages[phase * slots] for phase in range(later)]
    stage_all(0, range(OWN_HEADS), tokd, cos_out, sin_out, bias_out, owns, turned_out, plain_out)


def stage(slot, tokd, message, cosv, sinv, bias):
    at = slice(slot * tokd, (slot + 1) * tokd)
    cos_b, sin_b = cosv[:, at], sinv[:, at]
    query, key, value = (
        message[message_rows(tensor), :].astype(jnp.float32) + bias[:, tensor : tensor + 1]
        for tensor in range(3)
    )
    rest_row = lax.broadcasted_iota(jnp.int32, (LANES - HEAD_DIM, tokd), 0)
    zeros = jnp.zeros((LANES - HEAD_DIM, tokd), jnp.float32)
    ones = jnp.where(rest_row < 2, 1.0, 0.0)
    return [
        jnp.concatenate(pair, axis=0).astype(jnp.bfloat16)
        for pair in (
            (rotate(query, cos_b, sin_b) * (SCALE * LOG2E), zeros),
            (rotate(key, cos_b, sin_b), zeros),
            (value, ones),
        )
    ]


def stage_all(slot, phases, tokd, cosv, sinv, bias, msgs, turned, plain):
    for number, phase in enumerate(phases):
        own_bias = bias[phase * HEAD_DIM : (phase + 1) * HEAD_DIM, :]
        values = stage(slot, tokd, msgs[number], cosv, sinv, own_bias)
        for tensor, value in enumerate(values):
            turned[number][tensor] = value
            if tensor > 0:
                plain[number][tensor - 1] = value.T


def stage_kernel(slot, phases, tokd, cosv, sinv, bias, *refs):
    count = len(phases)
    msgs, turned, plain = refs[:count], refs[count : 2 * count], refs[2 * count :]
    stage_all(slot, phases, tokd, cosv, sinv, bias, msgs, turned, plain)


def attend_kernel(slots, staged, closed, tokd, head, factor, cosv, sinv, masks, bias, *refs):
    msgs, refs = refs[:slots], refs[slots:]
    ready = {slot: refs[2 * at : 2 * at + 2] for at, slot in enumerate(staged)}
    refs = refs[2 * len(staged) :]
    earlier = ()
    if head > 0:
        before, earlier, refs = refs[0], refs[1:slots], refs[slots:]
    outs, sums = refs[:slots], refs[slots]
    for result, out in zip(earlier, [out for slot, out in enumerate(outs) if slot != EARLY]):
        done = head * 4 * HEAD_DIM
        out[:done, :] = result[:done, :]
    qt_all, kt_all, vt_all, gt_all, k_all, v_all, s_buf, e_buf, d_buf = refs[slots + 1 : slots + 10]
    own_bias = bias[head * HEAD_DIM : (head + 1) * HEAD_DIM, :]
    rest_row = lax.broadcasted_iota(jnp.int32, (LANES - HEAD_DIM, tokd), 0)

    by_lanes = (((1,), (1,)), ((), ()))

    def off_row(slot, other):
        row = slot * slots + other
        return masks[row : row + 1, :]

    def live(slot, values):
        if closed:
            return values
        row = slots * slots + slot
        return values * masks[row : row + 1, :]

    def block_of(slot):
        return slice(slot * tokd, (slot + 1) * tokd)

    def put(slot, tensor, values):
        begin = ((0 if slot == EARLY else 4 * head) + tensor) * HEAD_DIM
        outs[slot][begin : begin + HEAD_DIM, :] = values

    def pieces_of(other):
        step = tokd // PIECES
        return [
            slice(other * tokd + number * step, other * tokd + (number + 1) * step)
            for number in range(PIECES)
        ]

    def scores(slot, keys):
        part = jnp.dot(
            k_all[keys, :], qt_all[:, block_of(slot)], preferred_element_type=jnp.float32
        )
        s_buf[slot % 2, keys, :] = part
        return jnp.max(part, axis=0, keepdims=True)

    def exponentials(slot, keys, top):
        part = (s_buf[slot % 2, keys, :] - top).astype(jnp.bfloat16)
        e_buf[keys, block_of(slot)] = jnp.exp2(part)

    def output(slot):
        mixed = jnp.dot(
            vt_all[:USED, :], e_buf[:, block_of(slot)], preferred_element_type=jnp.float32
        )
        inv = 1.0 / mixed[HEAD_DIM : HEAD_DIM + 1]
        out_b = (mixed[:HEAD_DIM] * inv).astype(jnp.bfloat16)
        put(slot, 0, out_b)
        grad = msgs[slot][message_rows(3), :].astype(jnp.float32)
        delta = jnp.sum(grad * out_b.astype(jnp.float32), axis=0, keepdims=True) * inv
        coarse = delta.astype(jnp.bfloat16).astype(jnp.float32)
        rest = jnp.where(rest_row == 0, -coarse, jnp.where(rest_row == 1, coarse - delta, 0.0))
        grad = jnp.concatenate([grad * inv, rest], axis=0).astype(jnp.bfloat16)
        gt_all[:, block_of(slot)] = grad
        spread = grad[:HEAD_DIM].astype(jnp.float32) * mixed[HEAD_DIM : HEAD_DIM + 1]
        return grad, live(slot, spread)

    def dscores(slot, keys, grad):
        part = jnp.dot(v_all[keys, :], grad, preferred_element_type=jnp.float32)
        d_buf[keys, block_of(slot)] = e_buf[keys, block_of(slot)] * part.astype(jnp.bfloat16)

    def query_part(slot):
        at = block_of(slot)
        dquery = jnp.dot(kt_all[:HEAD_DIM, :], d_buf[:, at], preferred_element_type=jnp.float32)
        dquery = unrotate(dquery * SCALE, cosv[:, at], sinv[:, at])
        put(slot, 1, dquery.astype(jnp.bfloat16))
        return live(slot, dquery)

    def value_part(slot):
        dvalue = lax.dot_general(
            gt_all[:HEAD_DIM, :],
            e_buf[block_of(slot), :],
            by_lanes,
            preferred_element_type=jnp.float32,
        )
        put(slot, 3, dvalue.astype(jnp.bfloat16))

    for slot in range(slots):
        at = block_of(slot)
        if slot in ready:
            turned, plain = ready[slot]
            values, natural = [turned[number] for number in range(3)], [plain[0], plain[1]]
        else:
            values = stage(slot, tokd, msgs[slot], cosv, sinv, own_bias)
            natural = [value.T for value in values[1:]]
        qt_all[:, at], kt_all[:, at], vt_all[:, at] = values
        k_all[at, :], v_all[at, :] = natural
    dq_total = jnp.zeros((HEAD_DIM, tokd), jnp.float32)
    dv_total = jnp.zeros((HEAD_DIM, tokd), jnp.float32)
    grad = None
    offs = tops = None
    for step in range(slots + 2):
        ahead, slot, behind = step, step - 1, step - 2
        if 0 <= slot < slots:
            offs = [off_row(slot, other) for other in range(slots)]
            top = functools.reduce(jnp.maximum, [one + off for one, off in zip(tops, offs)])
        tops = []
        for other in range(slots):
            found = []
            for keys in pieces_of(other):
                if ahead < slots:
                    found.append(scores(ahead, keys))
                if 0 <= behind:
                    dscores(behind, keys, grad)
                if 0 <= slot < slots:
                    exponentials(slot, keys, top - offs[other])
            if found:
                tops.append(functools.reduce(jnp.maximum, found))
        if 0 <= behind:
            dq_total = dq_total + query_part(behind)
        if 0 <= slot < slots:
            grad, spread = output(slot)
            dv_total = dv_total + spread
    dk_total = jnp.zeros((HEAD_DIM, tokd), jnp.float32)
    for slot in range(slots):
        at = block_of(slot)
        dkey = lax.dot_general(
            qt_all[:HEAD_DIM, :], d_buf[at, :], by_lanes, preferred_element_type=jnp.float32
        )
        dkey = unrotate(dkey * (1.0 / LOG2E), cosv[:, at], sinv[:, at])
        put(slot, 2, dkey.astype(jnp.bfloat16))
        dk_total = dk_total + live(slot, dkey)
    lane = lax.broadcasted_iota(jnp.int32, (HEAD_DIM, LANES), 1)
    columns = jnp.zeros((HEAD_DIM, LANES), jnp.float32)
    for number, total in enumerate((dq_total, dk_total, dv_total)):
        total = jnp.sum(total, axis=1, keepdims=True) * factor
        columns = jnp.where(lane == number, total, columns)
    columns = jnp.concatenate([columns, jnp.zeros((LANES - HEAD_DIM, LANES), jnp.float32)], axis=0)
    lines = columns.T
    copy = None
    if head + 1 < OWN_HEADS:
        sums[...] = lines[:8]
    else:
        tiles, sem = refs[slots + 10 :]
        tile = join_sums(before[...], lines)

        def repeat(device, carry):
            tiles[device] = tile
            return carry

        lax.fori_loop(0, tiles.shape[0], repeat, 0, unroll=min(32, tiles.shape[0]))
        copy = pltpu.make_async_copy(tiles, sums, sem)
        copy.start()
    for slot in range(slots):
        value_part(slot)
    if copy is not None:
        copy.wait()


FIT = LANES - HEAD_DIM
LEFT = HEAD_DIM - FIT


def join_sums(first, second):
    lane = lax.broadcasted_iota(jnp.int32, (1, LANES), 1)
    rows = []
    last = jnp.zeros((1, LANES), jnp.float32)
    for number in range(3):
        moved = pltpu.roll(second[number : number + 1], HEAD_DIM, 1)
        rows.append(jnp.where(lane < HEAD_DIM, first[number : number + 1], moved))
        rest = jnp.where(lane < LEFT, moved, 0.0)
        last = last + (pltpu.roll(rest, number * LEFT, 1) if number else rest)
    return jnp.concatenate(rows + [last], axis=0)


def unpack_kernel(slots, count, images, *refs):
    closed = is_closed(count)
    if not closed:
        lengths, table, *refs = refs
    msgs, refs = refs[: slots + OWN_HEADS - 1], refs[slots + OWN_HEADS - 1 :]
    *outs, held, ready, sems = refs
    early, late = msgs[:OWN_HEADS], list(msgs[OWN_HEADS:])
    late.insert(EARLY, None)
    me = lax.axis_index("tok")

    def place(slot, residue):
        for phase in range(OWN_HEADS):
            begin = pl.multiple_of((phase * SPAN + residue) * HEAD_DIM, 16)
            for number in range(4):
                if slot == EARLY:
                    piece = early[phase][message_rows(number), :]
                else:
                    piece = late[slot][message_rows(4 * phase + number), :]
                held[number, pl.ds(begin, HEAD_DIM), :] = piece

    for slot in range(slots):
        if closed:
            place(slot, lax.rem(me, SPAN) ^ closed_step(slot))
        else:
            _, start = image_of(me, lengths, images)
            source = table[slot, me]
            residue = lax.rem(source + SPAN, SPAN)
            chosen = (source >= 0) & (source == handler_of(start, residue, count))
            pl.when(chosen)(functools.partial(place, slot, residue))
    copies = []
    for number, out in enumerate(outs):
        ready[number] = held[number].T
        copies.append(pltpu.make_async_copy(ready.at[number], out, sems.at[number]))
        copies[-1].start()
    for copy in copies:
        copy.wait()


def bias_kernel(tiles, bias_out):
    def add(group, totals):
        return tuple(
            total + tiles[group * SPAN + residue] for residue, total in enumerate(totals)
        )

    groups = tiles.shape[0] // SPAN
    zero = jnp.zeros(tiles.shape[1:], jnp.float32)
    totals = lax.fori_loop(0, groups, add, (zero,) * SPAN, unroll=groups <= 8)
    for residue, total in enumerate(totals):
        first = residue * HEAD_DIM
        second = (SPAN + residue) * HEAD_DIM
        for number in range(3):
            row = slice(number, number + 1)
            bias_out[row, first : first + HEAD_DIM] = total[row, :HEAD_DIM]
            bias_out[row, second : second + FIT] = total[row, HEAD_DIM:]
            bias_out[row, second + FIT : second + HEAD_DIM] = total[
                3:4, number * LEFT : (number + 1) * LEFT
            ]


def on_device(query_in, key_in, value_in, out_grad, bias, lengths, widths):
    tokd = query_in.shape[1]
    model = query_in.shape[2]
    images = lengths.shape[1]
    count = lax.axis_size("tok")
    dp_size = lax.axis_size("dp")
    closed = is_closed(count)
    sources, targets = trade_tables(count)
    slots = sources.shape[0]
    span = slots * tokd
    smem = pl.BlockSpec(memory_space=pltpu.SMEM)
    vmem = pl.BlockSpec(memory_space=pltpu.VMEM)
    hbm = pl.BlockSpec(memory_space=pltpu.HBM)
    whole = jax.ShapeDtypeStruct((tokd, model), jnp.bfloat16)
    message = jax.ShapeDtypeStruct((4 * HEAD_DIM, tokd), jnp.bfloat16)
    joined = jax.ShapeDtypeStruct((OWN_HEADS * 4 * HEAD_DIM, tokd), jnp.bfloat16)
    devices = dp_size * count
    tokens_all = devices * tokd

    def params(mib):
        return pltpu.CompilerParams(vmem_limit_bytes=int(mib * 1024 * 1024))

    inputs = (query_in[0], key_in[0], value_in[0], out_grad[0])
    later = OWN_HEADS - 1
    lanes = max(end - begin for begin, end in (phase_lanes(p, model) for p in range(OWN_HEADS)))
    own_sends = pl.pallas_call(
        functools.partial(pack_kernel, closed),
        out_shape=[message] * slots,
        in_specs=[hbm] * 4,
        out_specs=[vmem] * slots,
        scratch_shapes=[
            pltpu.VMEM((4, tokd, lanes), jnp.bfloat16),
            pltpu.VMEM((4, lanes, tokd), jnp.bfloat16),
            pltpu.SemaphoreType.DMA((4,)),
        ],
        compiler_params=params(FIRST_PACK_KIB / 1024),
        name="pack_heads",
    )(*inputs)
    sends = [own_sends]
    rounds = trade_rounds(count)
    first = [sends[0][0]] + [
        lax.ppermute(send, "tok", pairs) for send, pairs in zip(sends[0][1:], rounds)
    ]
    table_shape = jax.ShapeDtypeStruct((HALF, span), jnp.float32)
    mask_rows = -(-slots * (slots + 1) // 8) * 8
    turned_shape = jax.ShapeDtypeStruct((3, LANES, tokd), jnp.bfloat16)
    plain_shape = jax.ShapeDtypeStruct((2, tokd, LANES), jnp.bfloat16)
    places = [] if closed else [jnp.asarray(sources)]
    out_shape = (
        [table_shape] * 2
        + [
            jax.ShapeDtypeStruct((mask_rows, tokd), jnp.float32),
            jax.ShapeDtypeStruct((OWN_HEADS * HEAD_DIM, LANES), jnp.float32),
        ]
        + [message] * (later * slots)
        + [turned_shape] * OWN_HEADS
        + [plain_shape] * OWN_HEADS
    )
    prepared = pl.pallas_call(
        functools.partial(prepare_kernel, slots, images, count, tokd),
        out_shape=out_shape,
        in_specs=[smem] * (2 + len(places)) + [vmem] + [hbm] * 4 + [vmem],
        out_specs=[vmem] * len(out_shape),
        scratch_shapes=[
            pltpu.VMEM((later, 4, tokd, lanes), jnp.bfloat16),
            pltpu.VMEM((later, 4, lanes, tokd), jnp.bfloat16),
            pltpu.SemaphoreType.DMA((later, 4)),
            pltpu.VMEM((model, LANES), jnp.float32),
        ],
        compiler_params=params(PREPARE_KIB / 1024),
        cost_estimate=pl.CostEstimate(flops=1_000_000, bytes_accessed=0, transcendentals=0),
        name="prepare",
    )(lengths, widths, *places, bias, *inputs, sends[0][0])
    tables, prepared = prepared[:4], prepared[4:]
    for phase in range(later):
        sends.append(prepared[phase * slots : (phase + 1) * slots])
    prepared = prepared[later * slots :]

    def stage_ahead(slot, phases, messages):
        number = len(phases)
        results = pl.pallas_call(
            functools.partial(stage_kernel, slot, phases, tokd),
            out_shape=[turned_shape] * number + [plain_shape] * number,
            in_specs=[vmem] * (3 + number),
            out_specs=[vmem] * (2 * number),
            compiler_params=params(16),
            cost_estimate=pl.CostEstimate(
                flops=1_000_000 * number, bytes_accessed=0, transcendentals=0
            ),
            name="stage_slot",
        )(tables[0], tables[1], tables[3], *messages)
        return [list(pair) for pair in zip(results[:number], results[number:])]

    phases = tuple(range(OWN_HEADS))
    own = [[prepared[phase], prepared[OWN_HEADS + phase]] for phase in phases]
    staged = [{0: pair} for pair in own]
    got = [first] + [[sent[0]] for sent in sends[1:]]
    for slot in range(1, slots - 1):
        latest = stage_ahead(slot, (0,), [first[slot]])
        for phase in phases[1:]:
            for leaving in (1, 2) if slot == 1 else (slot + 1,):
                send, latest = lax.optimization_barrier((sends[phase][leaving], latest))
                got[phase].append(lax.ppermute(send, "tok", rounds[leaving - 1]))
        staged[0][slot] = latest[0]
    early = []
    carried = []
    for phase in range(OWN_HEADS):
        last = phase + 1 == OWN_HEADS
        kept = [slot for slot in range(slots) if slot != EARLY]
        sums_shape = jax.ShapeDtypeStruct(
            (devices, 4, LANES) if last else (8, LANES), jnp.float32
        )
        *results, total = pl.pallas_call(
            functools.partial(
                attend_kernel,
                slots,
                tuple(staged[phase]),
                closed,
                tokd,
                phase,
                1.0 / tokens_all**0.5,
            ),
            out_shape=[message if slot == EARLY else joined for slot in range(slots)]
            + [sums_shape],
            in_specs=[vmem] * (4 + slots + 2 * len(staged[phase]) + len(carried)),
            out_specs=[vmem] * slots + [hbm if last else vmem],
            scratch_shapes=[pltpu.VMEM((LANES, span), jnp.bfloat16)] * 4
            + [pltpu.VMEM((span, LANES), jnp.bfloat16)] * 2
            + [pltpu.VMEM((2, span, tokd), jnp.float32)]
            + [pltpu.VMEM((span, span), jnp.bfloat16)] * 2
            + (
                [pltpu.VMEM(sums_shape.shape, jnp.float32), pltpu.SemaphoreType.DMA(())]
                if last
                else []
            ),
            compiler_params=params(32),
            cost_estimate=pl.CostEstimate(
                flops=12 * span * span * 256, bytes_accessed=0, transcendentals=0
            ),
            name="attend_head",
        )(*tables, *got[phase], *(one for pair in staged[phase].values() for one in pair), *carried)
        results[EARLY], early = lax.optimization_barrier((results[EARLY], early))
        early.append(send_back(results[EARLY], EARLY))
        carried = [total] + [results[slot] for slot in kept]
    tiles = lax.all_to_all(total, ("dp", "tok"), 0, 0, tiled=True)
    late = [send_back(results[slot], slot) for slot in kept]
    places = [] if closed else [lengths, jnp.asarray(targets)]
    outs = pl.pallas_call(
        functools.partial(unpack_kernel, slots, count, images),
        out_shape=[whole] * 4,
        in_specs=[smem] * len(places) + [vmem] * (OWN_HEADS + len(late)),
        out_specs=[hbm] * 4,
        scratch_shapes=[
            pltpu.VMEM((4, model, tokd), jnp.bfloat16),
            pltpu.VMEM((4, tokd, model), jnp.bfloat16),
            pltpu.SemaphoreType.DMA((4,)),
        ],
        compiler_params=params(16),
        cost_estimate=pl.CostEstimate(flops=UNPACK_FLOPS, bytes_accessed=0, transcendentals=0),
        name="unpack_heads",
    )(*places, *early, *late)
    outs, tiles = lax.optimization_barrier((outs, tiles))
    bias_grad = pl.pallas_call(
        bias_kernel,
        out_shape=jax.ShapeDtypeStruct((3, model), jnp.float32),
        in_specs=[vmem],
        out_specs=vmem,
        compiler_params=params(16),
        name="bias_sums",
    )(tiles)
    return tuple(out[None] for out in outs) + (bias_grad,)


def solution(mesh):
    in_specs = (
        P("dp", "tok", None),
        P("dp", "tok", None),
        P("dp", "tok", None),
        P("dp", "tok", None),
        P(),
        P("dp", None),
        P("dp", None),
    )
    out_specs = (
        P("dp", "tok", None),
        P("dp", "tok", None),
        P("dp", "tok", None),
        P("dp", "tok", None),
        P(),
    )
    return jax.shard_map(
        on_device, mesh=mesh, in_specs=in_specs, out_specs=out_specs, check_vma=False
    )
```

```python
import functools
import math

import jax
import jax.numpy as jnp
import numpy as np
from jax import lax
from jax.experimental import pallas as pl
from jax.experimental.pallas import tpu as pltpu
from jax.sharding import PartitionSpec as P

HEADS = 8
HEAD_DIM = 80
SPAN = 4
OWN_HEADS = HEADS // SPAN
PART = OWN_HEADS * HEAD_DIM
SCALE = HEAD_DIM**-0.5
LOG2E = 1.4426950408889634
NEG = -1e30
LANES = 128
USED = HEAD_DIM + 16
HALF = HEAD_DIM // 2
PIECES = 2
FIRST_PACK_KIB = 52 * 1024 + 1260
PREPARE_KIB = 52 * 1024 + 300
UNPACK_FLOPS = 20_000_000_000

rope_base = 10000.0


def is_closed(count):
    return count in (SPAN, 2 * SPAN)


def closed_step(slot):
    return (SPAN - slot) % SPAN


def trade_rounds(count):
    if is_closed(count):
        return [
            [(one, one ^ closed_step(slot)) for one in range(count)] for slot in range(1, SPAN)
        ]
    rounds = []
    for shift in [*range(1, SPAN), *range(-1, -SPAN, -1)]:
        rounds.append(
            [
                (source, source + shift)
                for source in range(max(0, -shift), min(count, count - shift))
                if (source < SPAN) == (source + shift < SPAN)
            ]
        )
    return rounds


def trade_tables(count):
    rounds = trade_rounds(count)
    sources = np.full((1 + len(rounds), count), -1, np.int32)
    targets = sources.copy()
    sources[0] = targets[0] = np.arange(count)
    for slot, pairs in enumerate(rounds, 1):
        for source, target in pairs:
            sources[slot, target] = source
            targets[slot, source] = target
    return sources, targets


def send_back(result, slot):
    if slot == 0:
        return result
    pairs = trade_rounds(lax.axis_size("tok"))[slot - 1]
    return lax.ppermute(result, "tok", [(target, source) for source, target in pairs])


EARLY = 1


def image_of(block, lengths, images):
    image = jnp.int32(0)
    start = jnp.int32(0)
    begin = jnp.int32(0)
    for number in range(images):
        size = lengths[0, number]
        inside = (block >= begin) & (block < begin + size)
        image = jnp.where(inside, number, image)
        start = jnp.where(inside, begin, start)
        begin = begin + size
    return image, start


def handler_of(start, residue, count):
    device = start + lax.rem(residue - lax.rem(start, SPAN) + SPAN, SPAN)
    return jnp.where(device >= count, device - SPAN, device)


def message_rows(tensor):
    return slice(tensor * HEAD_DIM, (tensor + 1) * HEAD_DIM)


def rotate(values, cosv, sinv):
    first, second = values[:HALF], values[HALF:]
    return jnp.concatenate([first * cosv - second * sinv, second * cosv + first * sinv], axis=0)


def unrotate(values, cosv, sinv):
    first, second = values[:HALF], values[HALF:]
    return jnp.concatenate([first * cosv + second * sinv, second * cosv - first * sinv], axis=0)


def phase_lanes(phase, model):
    size = SPAN * HEAD_DIM
    begin = phase * size // LANES * LANES
    end = -(-(phase + 1) * size // LANES) * LANES
    return begin, min(end, model)


def fetch(phase, inputs, held, sems):
    begin, end = phase_lanes(phase, inputs[0].shape[1])
    copies = [
        pltpu.make_async_copy(source.at[:, begin:end], held.at[number], sems.at[number])
        for number, source in enumerate(inputs)
    ]
    for copy in copies:
        copy.start()
    return copies


def pack(phase, closed, copies, outs, held, turned):
    me = lax.rem(lax.axis_index("tok"), SPAN)
    inner = phase * SPAN * HEAD_DIM % LANES
    steps = (
        [closed_step(slot) for slot in range(SPAN)]
        if closed
        else [0, *range(1, SPAN), *range(SPAN - 1, 0, -1)]
    )
    for number, copy in enumerate(copies):
        copy.wait()
        turned[number] = held[number].T
        for out, step in zip(outs, steps):
            residue = me ^ step if closed else lax.rem(me + step, SPAN)
            rows = pl.ds(pl.multiple_of(inner + residue * HEAD_DIM, 16), HEAD_DIM)
            out[message_rows(number), :] = turned[number, rows, :]


def pack_kernel(closed, *refs):
    inputs, outs, (held, turned, sems) = refs[:4], refs[4:-3], refs[-3:]
    pack(0, closed, fetch(0, inputs, held, sems), outs, held, turned)


def prepare_kernel(slots, images, count, tokd, lengths, widths, *refs):
    closed = is_closed(count)
    if not closed:
        table, *refs = refs
    later = OWN_HEADS - 1
    bias, *inputs, own = refs[:6]
    cos_out, sin_out, mask_out, bias_out, *refs = refs[6:]
    messages, refs = refs[: later * slots], refs[later * slots :]
    turned_out, plain_out = refs[:OWN_HEADS], refs[OWN_HEADS : 2 * OWN_HEADS]
    held, turned, sems, columns = refs[2 * OWN_HEADS :]
    copies = [
        fetch(phase + 1, inputs, held.at[phase], sems.at[phase]) for phase in range(later)
    ]
    me = lax.axis_index("tok")
    residue = lax.rem(me, SPAN)
    spot = lax.broadcasted_iota(jnp.int32, (HALF, tokd), 1)
    feature = lax.broadcasted_iota(jnp.int32, (HALF, tokd), 0)
    by_row = feature < HALF // 2
    feature = jnp.where(by_row, feature, feature - HALF // 2).astype(jnp.float32)
    inverse = jnp.exp(feature * (-math.log(rope_base) / (HALF // 2)))
    ids = []
    for slot in range(slots):
        block = me - residue + (residue ^ closed_step(slot)) if closed else table[slot, me]
        image, start = image_of(block, lengths, images)
        handled = (block >= 0) & (handler_of(start, residue, count) == me)
        ids.append(jnp.where(handled, image, -1 - slot))
        width = widths[0, image]
        bits = jnp.where(width == tokd, 0, jnp.where(width * 2 == tokd, 1, 2))
        shift = tokd.bit_length() - 1 - bits
        local = spot + (block - start) * tokd
        rowpos = lax.shift_right_logical(local, jnp.broadcast_to(shift, local.shape))
        colpos = local & (width - 1)
        angle = jnp.where(by_row, rowpos, colpos).astype(jnp.float32) * inverse
        cos_out[:, slot * tokd : (slot + 1) * tokd] = jnp.cos(angle)
        sin_out[:, slot * tokd : (slot + 1) * tokd] = jnp.sin(angle)
    for slot in range(slots):
        for other in range(slots):
            off = jnp.where(ids[slot] == ids[other], 0.0, NEG)
            row = slot * slots + other
            mask_out[row : row + 1, :] = jnp.full((1, tokd), off, jnp.float32)
        row = slots * slots + slot
        live = jnp.where(ids[slot] >= 0, 1.0, 0.0)
        mask_out[row : row + 1, :] = jnp.full((1, tokd), live, jnp.float32)
    plain = bias[...].astype(jnp.float32)
    rest = jnp.zeros((LANES - plain.shape[0], plain.shape[1]), jnp.float32)
    columns[...] = jnp.concatenate([plain, rest], axis=0).T
    for phase in range(OWN_HEADS):
        begin = pl.multiple_of((phase * SPAN + residue) * HEAD_DIM, 16)
        bias_out[phase * HEAD_DIM : (phase + 1) * HEAD_DIM, :] = columns[pl.ds(begin, HEAD_DIM), :]
    for phase in range(later):
        outs = messages[phase * slots : (phase + 1) * slots]
        pack(phase + 1, closed, copies[phase], outs, held.at[phase], turned.at[phase])
    owns = [own] + [messages[phase * slots] for phase in range(later)]
    stage_all(0, range(OWN_HEADS), tokd, cos_out, sin_out, bias_out, owns, turned_out, plain_out)


def stage(slot, tokd, message, cosv, sinv, bias):
    at = slice(slot * tokd, (slot + 1) * tokd)
    cos_b, sin_b = cosv[:, at], sinv[:, at]
    query, key, value = (
        message[message_rows(tensor), :].astype(jnp.float32) + bias[:, tensor : tensor + 1]
        for tensor in range(3)
    )
    rest_row = lax.broadcasted_iota(jnp.int32, (LANES - HEAD_DIM, tokd), 0)
    zeros = jnp.zeros((LANES - HEAD_DIM, tokd), jnp.float32)
    ones = jnp.where(rest_row < 2, 1.0, 0.0)
    return [
        jnp.concatenate(pair, axis=0).astype(jnp.bfloat16)
        for pair in (
            (rotate(query, cos_b, sin_b) * (SCALE * LOG2E), zeros),
            (rotate(key, cos_b, sin_b), zeros),
            (value, ones),
        )
    ]


def stage_all(slot, phases, tokd, cosv, sinv, bias, msgs, turned, plain):
    for number, phase in enumerate(phases):
        own_bias = bias[phase * HEAD_DIM : (phase + 1) * HEAD_DIM, :]
        values = stage(slot, tokd, msgs[number], cosv, sinv, own_bias)
        for tensor, value in enumerate(values):
            turned[number][tensor] = value
            if tensor > 0:
                plain[number][tensor - 1] = value.T


def stage_kernel(slot, phases, tokd, cosv, sinv, bias, *refs):
    count = len(phases)
    msgs, turned, plain = refs[:count], refs[count : 2 * count], refs[2 * count :]
    stage_all(slot, phases, tokd, cosv, sinv, bias, msgs, turned, plain)


def attend_kernel(slots, staged, closed, tokd, head, factor, cosv, sinv, masks, bias, *refs):
    msgs, refs = refs[:slots], refs[slots:]
    ready = {slot: refs[2 * at : 2 * at + 2] for at, slot in enumerate(staged)}
    refs = refs[2 * len(staged) :]
    earlier = ()
    if head > 0:
        before, earlier, refs = refs[0], refs[1:slots], refs[slots:]
    outs, sums = refs[:slots], refs[slots]
    for result, out in zip(earlier, [out for slot, out in enumerate(outs) if slot != EARLY]):
        done = head * 4 * HEAD_DIM
        out[:done, :] = result[:done, :]
    qt_all, kt_all, vt_all, gt_all, k_all, v_all, s_buf, e_buf, d_buf = refs[slots + 1 : slots + 10]
    own_bias = bias[head * HEAD_DIM : (head + 1) * HEAD_DIM, :]
    rest_row = lax.broadcasted_iota(jnp.int32, (LANES - HEAD_DIM, tokd), 0)

    by_lanes = (((1,), (1,)), ((), ()))

    def off_row(slot, other):
        row = slot * slots + other
        return masks[row : row + 1, :]

    def live(slot, values):
        if closed:
            return values
        row = slots * slots + slot
        return values * masks[row : row + 1, :]

    def block_of(slot):
        return slice(slot * tokd, (slot + 1) * tokd)

    def put(slot, tensor, values):
        begin = ((0 if slot == EARLY else 4 * head) + tensor) * HEAD_DIM
        outs[slot][begin : begin + HEAD_DIM, :] = values

    def pieces_of(other):
        step = tokd // PIECES
        return [
            slice(other * tokd + number * step, other * tokd + (number + 1) * step)
            for number in range(PIECES)
        ]

    def scores(slot, keys):
        part = jnp.dot(
            k_all[keys, :], qt_all[:, block_of(slot)], preferred_element_type=jnp.float32
        )
        s_buf[slot % 2, keys, :] = part
        return jnp.max(part, axis=0, keepdims=True)

    def exponentials(slot, keys, top):
        part = jnp.exp2(s_buf[slot % 2, keys, :] - top)
        e_buf[keys, block_of(slot)] = part.astype(jnp.bfloat16)

    def output(slot):
        mixed = jnp.dot(
            vt_all[:USED, :], e_buf[:, block_of(slot)], preferred_element_type=jnp.float32
        )
        inv = 1.0 / mixed[HEAD_DIM : HEAD_DIM + 1]
        out_b = (mixed[:HEAD_DIM] * inv).astype(jnp.bfloat16)
        put(slot, 0, out_b)
        grad = msgs[slot][message_rows(3), :].astype(jnp.float32)
        delta = jnp.sum(grad * out_b.astype(jnp.float32), axis=0, keepdims=True) * inv
        coarse = delta.astype(jnp.bfloat16).astype(jnp.float32)
        rest = jnp.where(rest_row == 0, -coarse, jnp.where(rest_row == 1, coarse - delta, 0.0))
        grad = jnp.concatenate([grad * inv, rest], axis=0).astype(jnp.bfloat16)
        gt_all[:, block_of(slot)] = grad
        spread = grad[:HEAD_DIM].astype(jnp.float32) * mixed[HEAD_DIM : HEAD_DIM + 1]
        return grad, live(slot, spread)

    def dscores(slot, keys, grad):
        part = jnp.dot(v_all[keys, :], grad, preferred_element_type=jnp.float32)
        d_buf[keys, block_of(slot)] = e_buf[keys, block_of(slot)] * part.astype(jnp.bfloat16)

    def query_part(slot):
        at = block_of(slot)
        dquery = jnp.dot(kt_all[:HEAD_DIM, :], d_buf[:, at], preferred_element_type=jnp.float32)
        dquery = unrotate(dquery * SCALE, cosv[:, at], sinv[:, at])
        put(slot, 1, dquery.astype(jnp.bfloat16))
        return live(slot, dquery)

    def value_part(slot):
        dvalue = lax.dot_general(
            gt_all[:HEAD_DIM, :],
            e_buf[block_of(slot), :],
            by_lanes,
            preferred_element_type=jnp.float32,
        )
        put(slot, 3, dvalue.astype(jnp.bfloat16))

    for slot in range(slots):
        at = block_of(slot)
        if slot in ready:
            turned, plain = ready[slot]
            values, natural = [turned[number] for number in range(3)], [plain[0], plain[1]]
        else:
            values = stage(slot, tokd, msgs[slot], cosv, sinv, own_bias)
            natural = [value.T for value in values[1:]]
        qt_all[:, at], kt_all[:, at], vt_all[:, at] = values
        k_all[at, :], v_all[at, :] = natural
    dq_total = jnp.zeros((HEAD_DIM, tokd), jnp.float32)
    dv_total = jnp.zeros((HEAD_DIM, tokd), jnp.float32)
    grad = None
    offs = tops = None
    for step in range(slots + 2):
        ahead, slot, behind = step, step - 1, step - 2
        if 0 <= slot < slots:
            offs = [off_row(slot, other) for other in range(slots)]
            top = functools.reduce(jnp.maximum, [one + off for one, off in zip(tops, offs)])
        tops = []
        for other in range(slots):
            found = []
            for keys in pieces_of(other):
                if ahead < slots:
                    found.append(scores(ahead, keys))
                if 0 <= behind:
                    dscores(behind, keys, grad)
                if 0 <= slot < slots:
                    exponentials(slot, keys, top - offs[other])
            if found:
                tops.append(functools.reduce(jnp.maximum, found))
        if 0 <= behind:
            dq_total = dq_total + query_part(behind)
        if 0 <= slot < slots:
            grad, spread = output(slot)
            dv_total = dv_total + spread
    dk_total = jnp.zeros((HEAD_DIM, tokd), jnp.float32)
    for slot in range(slots):
        at = block_of(slot)
        dkey = lax.dot_general(
            qt_all[:HEAD_DIM, :], d_buf[at, :], by_lanes, preferred_element_type=jnp.float32
        )
        dkey = unrotate(dkey * (1.0 / LOG2E), cosv[:, at], sinv[:, at])
        put(slot, 2, dkey.astype(jnp.bfloat16))
        dk_total = dk_total + live(slot, dkey)
    lane = lax.broadcasted_iota(jnp.int32, (HEAD_DIM, LANES), 1)
    columns = jnp.zeros((HEAD_DIM, LANES), jnp.float32)
    for number, total in enumerate((dq_total, dk_total, dv_total)):
        total = jnp.sum(total, axis=1, keepdims=True) * factor
        columns = jnp.where(lane == number, total, columns)
    columns = jnp.concatenate([columns, jnp.zeros((LANES - HEAD_DIM, LANES), jnp.float32)], axis=0)
    lines = columns.T
    copy = None
    if head + 1 < OWN_HEADS:
        sums[...] = lines[:8]
    else:
        tiles, sem = refs[slots + 10 :]
        tile = join_sums(before[...], lines)

        def repeat(device, carry):
            tiles[device] = tile
            return carry

        lax.fori_loop(0, tiles.shape[0], repeat, 0, unroll=min(32, tiles.shape[0]))
        copy = pltpu.make_async_copy(tiles, sums, sem)
        copy.start()
    for slot in range(slots):
        value_part(slot)
    if copy is not None:
        copy.wait()


FIT = LANES - HEAD_DIM
LEFT = HEAD_DIM - FIT


def join_sums(first, second):
    lane = lax.broadcasted_iota(jnp.int32, (1, LANES), 1)
    rows = []
    last = jnp.zeros((1, LANES), jnp.float32)
    for number in range(3):
        moved = pltpu.roll(second[number : number + 1], HEAD_DIM, 1)
        rows.append(jnp.where(lane < HEAD_DIM, first[number : number + 1], moved))
        rest = jnp.where(lane < LEFT, moved, 0.0)
        last = last + (pltpu.roll(rest, number * LEFT, 1) if number else rest)
    return jnp.concatenate(rows + [last], axis=0)


def unpack_kernel(slots, count, images, *refs):
    closed = is_closed(count)
    if not closed:
        lengths, table, *refs = refs
    msgs, refs = refs[: slots + OWN_HEADS - 1], refs[slots + OWN_HEADS - 1 :]
    *outs, held = refs
    early, late = msgs[:OWN_HEADS], list(msgs[OWN_HEADS:])
    late.insert(EARLY, None)
    me = lax.axis_index("tok")

    def place(slot, residue):
        for phase in range(OWN_HEADS):
            begin = pl.multiple_of((phase * SPAN + residue) * HEAD_DIM, 16)
            for number in range(4):
                if slot == EARLY:
                    piece = early[phase][message_rows(number), :]
                else:
                    piece = late[slot][message_rows(4 * phase + number), :]
                held[number, pl.ds(begin, HEAD_DIM), :] = piece

    for slot in range(slots):
        if closed:
            place(slot, lax.rem(me, SPAN) ^ closed_step(slot))
        else:
            _, start = image_of(me, lengths, images)
            source = table[slot, me]
            residue = lax.rem(source + SPAN, SPAN)
            chosen = (source >= 0) & (source == handler_of(start, residue, count))
            pl.when(chosen)(functools.partial(place, slot, residue))
    for number, out in enumerate(outs):
        out[...] = held[number].T


def finish_kernel(*refs):
    results, tiles, outs, bias_out, (total, sems) = refs[:4], refs[4], refs[5:9], refs[9], refs[10:]
    copies = [
        pltpu.make_async_copy(result, out, sems.at[number])
        for number, (result, out) in enumerate(zip(results, outs))
    ]
    for copy in copies:
        copy.start()
    add_tiles(tiles, total)
    copies.append(pltpu.make_async_copy(total, bias_out, sems.at[4]))
    copies[-1].start()
    for copy in copies:
        copy.wait()


def add_tiles(tiles, bias_out):
    def add(group, totals):
        return tuple(
            total + tiles[group * SPAN + residue] for residue, total in enumerate(totals)
        )

    groups = tiles.shape[0] // SPAN
    zero = jnp.zeros(tiles.shape[1:], jnp.float32)
    totals = lax.fori_loop(0, groups, add, (zero,) * SPAN, unroll=groups <= 8)
    for residue, total in enumerate(totals):
        first = residue * HEAD_DIM
        second = (SPAN + residue) * HEAD_DIM
        for number in range(3):
            row = slice(number, number + 1)
            bias_out[row, first : first + HEAD_DIM] = total[row, :HEAD_DIM]
            bias_out[row, second : second + FIT] = total[row, HEAD_DIM:]
            bias_out[row, second + FIT : second + HEAD_DIM] = total[
                3:4, number * LEFT : (number + 1) * LEFT
            ]


def on_device(query_in, key_in, value_in, out_grad, bias, lengths, widths):
    tokd = query_in.shape[1]
    model = query_in.shape[2]
    images = lengths.shape[1]
    count = lax.axis_size("tok")
    dp_size = lax.axis_size("dp")
    closed = is_closed(count)
    sources, targets = trade_tables(count)
    slots = sources.shape[0]
    span = slots * tokd
    smem = pl.BlockSpec(memory_space=pltpu.SMEM)
    vmem = pl.BlockSpec(memory_space=pltpu.VMEM)
    hbm = pl.BlockSpec(memory_space=pltpu.HBM)
    whole = jax.ShapeDtypeStruct((tokd, model), jnp.bfloat16)
    message = jax.ShapeDtypeStruct((4 * HEAD_DIM, tokd), jnp.bfloat16)
    joined = jax.ShapeDtypeStruct((OWN_HEADS * 4 * HEAD_DIM, tokd), jnp.bfloat16)
    devices = dp_size * count
    tokens_all = devices * tokd

    def params(mib):
        return pltpu.CompilerParams(vmem_limit_bytes=int(mib * 1024 * 1024))

    inputs = (query_in[0], key_in[0], value_in[0], out_grad[0])
    later = OWN_HEADS - 1
    lanes = max(end - begin for begin, end in (phase_lanes(p, model) for p in range(OWN_HEADS)))
    own_sends = pl.pallas_call(
        functools.partial(pack_kernel, closed),
        out_shape=[message] * slots,
        in_specs=[hbm] * 4,
        out_specs=[vmem] * slots,
        scratch_shapes=[
            pltpu.VMEM((4, tokd, lanes), jnp.bfloat16),
            pltpu.VMEM((4, lanes, tokd), jnp.bfloat16),
            pltpu.SemaphoreType.DMA((4,)),
        ],
        compiler_params=params(FIRST_PACK_KIB / 1024),
        name="pack_heads",
    )(*inputs)
    sends = [own_sends]
    rounds = trade_rounds(count)
    first = [sends[0][0]] + [
        lax.ppermute(send, "tok", pairs) for send, pairs in zip(sends[0][1:], rounds)
    ]
    table_shape = jax.ShapeDtypeStruct((HALF, span), jnp.float32)
    mask_rows = -(-slots * (slots + 1) // 8) * 8
    turned_shape = jax.ShapeDtypeStruct((3, LANES, tokd), jnp.bfloat16)
    plain_shape = jax.ShapeDtypeStruct((2, tokd, LANES), jnp.bfloat16)
    places = [] if closed else [jnp.asarray(sources)]
    out_shape = (
        [table_shape] * 2
        + [
            jax.ShapeDtypeStruct((mask_rows, tokd), jnp.float32),
            jax.ShapeDtypeStruct((OWN_HEADS * HEAD_DIM, LANES), jnp.float32),
        ]
        + [message] * (later * slots)
        + [turned_shape] * OWN_HEADS
        + [plain_shape] * OWN_HEADS
    )
    prepared = pl.pallas_call(
        functools.partial(prepare_kernel, slots, images, count, tokd),
        out_shape=out_shape,
        in_specs=[smem] * (2 + len(places)) + [vmem] + [hbm] * 4 + [vmem],
        out_specs=[vmem] * len(out_shape),
        scratch_shapes=[
            pltpu.VMEM((later, 4, tokd, lanes), jnp.bfloat16),
            pltpu.VMEM((later, 4, lanes, tokd), jnp.bfloat16),
            pltpu.SemaphoreType.DMA((later, 4)),
            pltpu.VMEM((model, LANES), jnp.float32),
        ],
        compiler_params=params(PREPARE_KIB / 1024),
        cost_estimate=pl.CostEstimate(flops=1_000_000, bytes_accessed=0, transcendentals=0),
        name="prepare",
    )(lengths, widths, *places, bias, *inputs, sends[0][0])
    tables, prepared = prepared[:4], prepared[4:]
    for phase in range(later):
        sends.append(prepared[phase * slots : (phase + 1) * slots])
    prepared = prepared[later * slots :]

    def stage_ahead(slot, phases, messages):
        number = len(phases)
        results = pl.pallas_call(
            functools.partial(stage_kernel, slot, phases, tokd),
            out_shape=[turned_shape] * number + [plain_shape] * number,
            in_specs=[vmem] * (3 + number),
            out_specs=[vmem] * (2 * number),
            compiler_params=params(16),
            cost_estimate=pl.CostEstimate(
                flops=1_000_000 * number, bytes_accessed=0, transcendentals=0
            ),
            name="stage_slot",
        )(tables[0], tables[1], tables[3], *messages)
        return [list(pair) for pair in zip(results[:number], results[number:])]

    phases = tuple(range(OWN_HEADS))
    own = [[prepared[phase], prepared[OWN_HEADS + phase]] for phase in phases]
    staged = [{0: pair} for pair in own]
    got = [first] + [[sent[0]] for sent in sends[1:]]
    for slot in range(1, slots - 1):
        latest = stage_ahead(slot, (0,), [first[slot]])
        for phase in phases[1:]:
            for leaving in (1, 2) if slot == 1 else (slot + 1,):
                send, latest = lax.optimization_barrier((sends[phase][leaving], latest))
                got[phase].append(lax.ppermute(send, "tok", rounds[leaving - 1]))
        staged[0][slot] = latest[0]
    early = []
    carried = []
    for phase in range(OWN_HEADS):
        last = phase + 1 == OWN_HEADS
        kept = [slot for slot in range(slots) if slot != EARLY]
        sums_shape = jax.ShapeDtypeStruct(
            (devices, 4, LANES) if last else (8, LANES), jnp.float32
        )
        *results, total = pl.pallas_call(
            functools.partial(
                attend_kernel,
                slots,
                tuple(staged[phase]),
                closed,
                tokd,
                phase,
                1.0 / tokens_all**0.5,
            ),
            out_shape=[message if slot == EARLY else joined for slot in range(slots)]
            + [sums_shape],
            in_specs=[vmem] * (4 + slots + 2 * len(staged[phase]) + len(carried)),
            out_specs=[vmem] * slots + [hbm if last else vmem],
            scratch_shapes=[pltpu.VMEM((LANES, span), jnp.bfloat16)] * 4
            + [pltpu.VMEM((span, LANES), jnp.bfloat16)] * 2
            + [pltpu.VMEM((2, span, tokd), jnp.float32)]
            + [pltpu.VMEM((span, span), jnp.bfloat16)] * 2
            + (
                [pltpu.VMEM(sums_shape.shape, jnp.float32), pltpu.SemaphoreType.DMA(())]
                if last
                else []
            ),
            compiler_params=params(32),
            cost_estimate=pl.CostEstimate(
                flops=12 * span * span * 256, bytes_accessed=0, transcendentals=0
            ),
            name="attend_head",
        )(*tables, *got[phase], *(one for pair in staged[phase].values() for one in pair), *carried)
        results[EARLY], early = lax.optimization_barrier((results[EARLY], early))
        early.append(send_back(results[EARLY], EARLY))
        carried = [total] + [results[slot] for slot in kept]
    tiles = lax.all_to_all(total, ("dp", "tok"), 0, 0, tiled=True)
    late = [send_back(results[slot], slot) for slot in kept]
    places = [] if closed else [lengths, jnp.asarray(targets)]
    ready = pl.pallas_call(
        functools.partial(unpack_kernel, slots, count, images),
        out_shape=[whole] * 4,
        in_specs=[smem] * len(places) + [vmem] * (OWN_HEADS + len(late)),
        out_specs=[vmem] * 4,
        scratch_shapes=[pltpu.VMEM((4, model, tokd), jnp.bfloat16)],
        compiler_params=params(16),
        cost_estimate=pl.CostEstimate(flops=UNPACK_FLOPS, bytes_accessed=0, transcendentals=0),
        name="unpack_heads",
    )(*places, *early, *late)
    bias_shape = jax.ShapeDtypeStruct((3, model), jnp.float32)
    *outs, bias_grad = pl.pallas_call(
        finish_kernel,
        out_shape=[whole] * 4 + [bias_shape],
        in_specs=[vmem] * 5,
        out_specs=[hbm] * 5,
        scratch_shapes=[
            pltpu.VMEM(bias_shape.shape, jnp.float32),
            pltpu.SemaphoreType.DMA((5,)),
        ],
        compiler_params=params(16),
        name="finish",
    )(*ready, tiles)
    return tuple(out[None] for out in outs) + (bias_grad,)


def solution(mesh):
    in_specs = (
        P("dp", "tok", None),
        P("dp", "tok", None),
        P("dp", "tok", None),
        P("dp", "tok", None),
        P(),
        P("dp", None),
        P("dp", None),
    )
    out_specs = (
        P("dp", "tok", None),
        P("dp", "tok", None),
        P("dp", "tok", None),
        P("dp", "tok", None),
        P(),
    )
    return jax.shard_map(
        on_device, mesh=mesh, in_specs=in_specs, out_specs=out_specs, check_vma=False
    )
```

```python
import functools
import math

import jax
import jax.numpy as jnp
import numpy as np
from jax import lax
from jax.experimental import pallas as pl
from jax.experimental.pallas import tpu as pltpu
from jax.sharding import PartitionSpec as P

HEADS = 8
HEAD_DIM = 80
SPAN = 4
OWN_HEADS = HEADS // SPAN
PART = OWN_HEADS * HEAD_DIM
SCALE = HEAD_DIM**-0.5
LOG2E = 1.4426950408889634
NEG = -1e30
LANES = 128
USED = HEAD_DIM + 16
HALF = HEAD_DIM // 2
PIECES = 2
FIRST_PACK_KIB = 52 * 1024 + 1260
PREPARE_KIB = 52 * 1024 + 300
UNPACK_FLOPS = 20_000_000_000

rope_base = 10000.0


def is_closed(count):
    return count in (SPAN, 2 * SPAN)


def closed_step(slot):
    return (SPAN - slot) % SPAN


def trade_rounds(count):
    if is_closed(count):
        return [
            [(one, one ^ closed_step(slot)) for one in range(count)] for slot in range(1, SPAN)
        ]
    rounds = []
    for shift in [*range(1, SPAN), *range(-1, -SPAN, -1)]:
        rounds.append(
            [
                (source, source + shift)
                for source in range(max(0, -shift), min(count, count - shift))
                if (source < SPAN) == (source + shift < SPAN)
            ]
        )
    return rounds


def trade_tables(count):
    rounds = trade_rounds(count)
    sources = np.full((1 + len(rounds), count), -1, np.int32)
    targets = sources.copy()
    sources[0] = targets[0] = np.arange(count)
    for slot, pairs in enumerate(rounds, 1):
        for source, target in pairs:
            sources[slot, target] = source
            targets[slot, source] = target
    return sources, targets


def send_back(result, slot):
    if slot == 0:
        return result
    pairs = trade_rounds(lax.axis_size("tok"))[slot - 1]
    return lax.ppermute(result, "tok", [(target, source) for source, target in pairs])


EARLY = 1


def image_of(block, lengths, images):
    image = jnp.int32(0)
    start = jnp.int32(0)
    begin = jnp.int32(0)
    for number in range(images):
        size = lengths[0, number]
        inside = (block >= begin) & (block < begin + size)
        image = jnp.where(inside, number, image)
        start = jnp.where(inside, begin, start)
        begin = begin + size
    return image, start


def handler_of(start, residue, count):
    device = start + lax.rem(residue - lax.rem(start, SPAN) + SPAN, SPAN)
    return jnp.where(device >= count, device - SPAN, device)


def message_rows(tensor):
    return slice(tensor * HEAD_DIM, (tensor + 1) * HEAD_DIM)


def rotate(values, cosv, sinv):
    first, second = values[:HALF], values[HALF:]
    return jnp.concatenate([first * cosv - second * sinv, second * cosv + first * sinv], axis=0)


def unrotate(values, cosv, sinv):
    first, second = values[:HALF], values[HALF:]
    return jnp.concatenate([first * cosv + second * sinv, second * cosv - first * sinv], axis=0)


def phase_lanes(phase, model):
    size = SPAN * HEAD_DIM
    begin = phase * size // LANES * LANES
    end = -(-(phase + 1) * size // LANES) * LANES
    return begin, min(end, model)


def fetch(phase, inputs, held, sems):
    begin, end = phase_lanes(phase, inputs[0].shape[1])
    copies = [
        pltpu.make_async_copy(source.at[:, begin:end], held.at[number], sems.at[number])
        for number, source in enumerate(inputs)
    ]
    for copy in copies:
        copy.start()
    return copies


def pack(phase, closed, copies, outs, held, turned):
    me = lax.rem(lax.axis_index("tok"), SPAN)
    inner = phase * SPAN * HEAD_DIM % LANES
    steps = (
        [closed_step(slot) for slot in range(SPAN)]
        if closed
        else [0, *range(1, SPAN), *range(SPAN - 1, 0, -1)]
    )
    row = lax.broadcasted_iota(jnp.int32, (LANES, LANES), 0)
    lane = lax.broadcasted_iota(jnp.int32, (LANES, LANES), 1)
    ones = jnp.where(row == lane, 1.0, 0.0).astype(jnp.bfloat16)
    for number, copy in enumerate(copies):
        copy.wait()
        if number % 2 == 0:
            turned[number] = held[number].T
        else:
            for begin in range(0, held.shape[2], LANES):
                block = lax.dot_general(
                    ones,
                    held[number, :, begin : begin + LANES],
                    (((1,), (1,)), ((), ())),
                    preferred_element_type=jnp.float32,
                )
                turned[number, begin : begin + LANES, :] = block.astype(jnp.bfloat16)
        for out, step in zip(outs, steps):
            residue = me ^ step if closed else lax.rem(me + step, SPAN)
            rows = pl.ds(pl.multiple_of(inner + residue * HEAD_DIM, 16), HEAD_DIM)
            out[message_rows(number), :] = turned[number, rows, :]


def pack_kernel(closed, *refs):
    inputs, outs, (held, turned, sems) = refs[:4], refs[4:-3], refs[-3:]
    pack(0, closed, fetch(0, inputs, held, sems), outs, held, turned)


def prepare_kernel(slots, images, count, tokd, lengths, widths, *refs):
    closed = is_closed(count)
    if not closed:
        table, *refs = refs
    later = OWN_HEADS - 1
    bias, *inputs, own = refs[:6]
    cos_out, sin_out, mask_out, bias_out, *refs = refs[6:]
    messages, refs = refs[: later * slots], refs[later * slots :]
    turned_out, plain_out = refs[:OWN_HEADS], refs[OWN_HEADS : 2 * OWN_HEADS]
    held, turned, sems, columns = refs[2 * OWN_HEADS :]
    copies = [
        fetch(phase + 1, inputs, held.at[phase], sems.at[phase]) for phase in range(later)
    ]
    me = lax.axis_index("tok")
    residue = lax.rem(me, SPAN)
    spot = lax.broadcasted_iota(jnp.int32, (HALF, tokd), 1)
    feature = lax.broadcasted_iota(jnp.int32, (HALF, tokd), 0)
    by_row = feature < HALF // 2
    feature = jnp.where(by_row, feature, feature - HALF // 2).astype(jnp.float32)
    inverse = jnp.exp(feature * (-math.log(rope_base) / (HALF // 2)))
    ids = []
    for slot in range(slots):
        block = me - residue + (residue ^ closed_step(slot)) if closed else table[slot, me]
        image, start = image_of(block, lengths, images)
        handled = (block >= 0) & (handler_of(start, residue, count) == me)
        ids.append(jnp.where(handled, image, -1 - slot))
        width = widths[0, image]
        bits = jnp.where(width == tokd, 0, jnp.where(width * 2 == tokd, 1, 2))
        shift = tokd.bit_length() - 1 - bits
        local = spot + (block - start) * tokd
        rowpos = lax.shift_right_logical(local, jnp.broadcast_to(shift, local.shape))
        colpos = local & (width - 1)
        angle = jnp.where(by_row, rowpos, colpos).astype(jnp.float32) * inverse
        cos_out[:, slot * tokd : (slot + 1) * tokd] = jnp.cos(angle)
        sin_out[:, slot * tokd : (slot + 1) * tokd] = jnp.sin(angle)
    for slot in range(slots):
        for other in range(slots):
            off = jnp.where(ids[slot] == ids[other], 0.0, NEG)
            row = slot * slots + other
            mask_out[row : row + 1, :] = jnp.full((1, tokd), off, jnp.float32)
        row = slots * slots + slot
        live = jnp.where(ids[slot] >= 0, 1.0, 0.0)
        mask_out[row : row + 1, :] = jnp.full((1, tokd), live, jnp.float32)
    plain = bias[...].astype(jnp.float32)
    rest = jnp.zeros((LANES - plain.shape[0], plain.shape[1]), jnp.float32)
    columns[...] = jnp.concatenate([plain, rest], axis=0).T
    for phase in range(OWN_HEADS):
        begin = pl.multiple_of((phase * SPAN + residue) * HEAD_DIM, 16)
        bias_out[phase * HEAD_DIM : (phase + 1) * HEAD_DIM, :] = columns[pl.ds(begin, HEAD_DIM), :]
    for phase in range(later):
        outs = messages[phase * slots : (phase + 1) * slots]
        pack(phase + 1, closed, copies[phase], outs, held.at[phase], turned.at[phase])
    owns = [own] + [messages[phase * slots] for phase in range(later)]
    stage_all(0, range(OWN_HEADS), tokd, cos_out, sin_out, bias_out, owns, turned_out, plain_out)


def stage(slot, tokd, message, cosv, sinv, bias):
    at = slice(slot * tokd, (slot + 1) * tokd)
    cos_b, sin_b = cosv[:, at], sinv[:, at]
    query, key, value = (
        message[message_rows(tensor), :].astype(jnp.float32) + bias[:, tensor : tensor + 1]
        for tensor in range(3)
    )
    rest_row = lax.broadcasted_iota(jnp.int32, (LANES - HEAD_DIM, tokd), 0)
    zeros = jnp.zeros((LANES - HEAD_DIM, tokd), jnp.float32)
    ones = jnp.where(rest_row < 2, 1.0, 0.0)
    return [
        jnp.concatenate(pair, axis=0).astype(jnp.bfloat16)
        for pair in (
            (rotate(query, cos_b, sin_b) * (SCALE * LOG2E), zeros),
            (rotate(key, cos_b, sin_b), zeros),
            (value, ones),
        )
    ]


def stage_all(slot, phases, tokd, cosv, sinv, bias, msgs, turned, plain):
    for number, phase in enumerate(phases):
        own_bias = bias[phase * HEAD_DIM : (phase + 1) * HEAD_DIM, :]
        values = stage(slot, tokd, msgs[number], cosv, sinv, own_bias)
        for tensor, value in enumerate(values):
            turned[number][tensor] = value
            if tensor > 0:
                plain[number][tensor - 1] = value.T


def stage_kernel(slot, phases, tokd, cosv, sinv, bias, *refs):
    count = len(phases)
    msgs, turned, plain = refs[:count], refs[count : 2 * count], refs[2 * count :]
    stage_all(slot, phases, tokd, cosv, sinv, bias, msgs, turned, plain)


def attend_kernel(slots, staged, closed, tokd, head, factor, cosv, sinv, masks, bias, *refs):
    msgs, refs = refs[:slots], refs[slots:]
    ready = {slot: refs[2 * at : 2 * at + 2] for at, slot in enumerate(staged)}
    refs = refs[2 * len(staged) :]
    earlier = ()
    if head > 0:
        before, earlier, refs = refs[0], refs[1:slots], refs[slots:]
    outs, sums = refs[:slots], refs[slots]
    for result, out in zip(earlier, [out for slot, out in enumerate(outs) if slot != EARLY]):
        done = head * 4 * HEAD_DIM
        out[:done, :] = result[:done, :]
    qt_all, kt_all, vt_all, gt_all, k_all, v_all, s_buf, e_buf, d_buf = refs[slots + 1 : slots + 10]
    own_bias = bias[head * HEAD_DIM : (head + 1) * HEAD_DIM, :]
    rest_row = lax.broadcasted_iota(jnp.int32, (LANES - HEAD_DIM, tokd), 0)

    by_lanes = (((1,), (1,)), ((), ()))

    def off_row(slot, other):
        row = slot * slots + other
        return masks[row : row + 1, :]

    def live(slot, values):
        if closed:
            return values
        row = slots * slots + slot
        return values * masks[row : row + 1, :]

    def block_of(slot):
        return slice(slot * tokd, (slot + 1) * tokd)

    def put(slot, tensor, values):
        begin = ((0 if slot == EARLY else 4 * head) + tensor) * HEAD_DIM
        outs[slot][begin : begin + HEAD_DIM, :] = values

    def pieces_of(other):
        step = tokd // PIECES
        return [
            slice(other * tokd + number * step, other * tokd + (number + 1) * step)
            for number in range(PIECES)
        ]

    def scores(slot, keys):
        part = jnp.dot(
            k_all[keys, :], qt_all[:, block_of(slot)], preferred_element_type=jnp.float32
        )
        s_buf[slot % 2, keys, :] = part
        return jnp.max(part, axis=0, keepdims=True)

    def exponentials(slot, keys, top):
        part = jnp.exp2(s_buf[slot % 2, keys, :] - top)
        e_buf[keys, block_of(slot)] = part.astype(jnp.bfloat16)

    def output(slot):
        mixed = jnp.dot(
            vt_all[:USED, :], e_buf[:, block_of(slot)], preferred_element_type=jnp.float32
        )
        inv = 1.0 / mixed[HEAD_DIM : HEAD_DIM + 1]
        out_b = (mixed[:HEAD_DIM] * inv).astype(jnp.bfloat16)
        put(slot, 0, out_b)
        grad = msgs[slot][message_rows(3), :].astype(jnp.float32)
        delta = jnp.sum(grad * out_b.astype(jnp.float32), axis=0, keepdims=True) * inv
        coarse = delta.astype(jnp.bfloat16).astype(jnp.float32)
        rest = jnp.where(rest_row == 0, -coarse, jnp.where(rest_row == 1, coarse - delta, 0.0))
        grad = jnp.concatenate([grad * inv, rest], axis=0).astype(jnp.bfloat16)
        gt_all[:, block_of(slot)] = grad
        spread = grad[:HEAD_DIM].astype(jnp.float32) * mixed[HEAD_DIM : HEAD_DIM + 1]
        return grad, live(slot, spread)

    def dscores(slot, keys, grad):
        part = jnp.dot(v_all[keys, :], grad, preferred_element_type=jnp.float32)
        d_buf[keys, block_of(slot)] = e_buf[keys, block_of(slot)] * part.astype(jnp.bfloat16)

    def query_part(slot):
        at = block_of(slot)
        dquery = jnp.dot(kt_all[:HEAD_DIM, :], d_buf[:, at], preferred_element_type=jnp.float32)
        dquery = unrotate(dquery * SCALE, cosv[:, at], sinv[:, at])
        put(slot, 1, dquery.astype(jnp.bfloat16))
        return live(slot, dquery)

    def value_part(slot):
        dvalue = lax.dot_general(
            gt_all[:HEAD_DIM, :],
            e_buf[block_of(slot), :],
            by_lanes,
            preferred_element_type=jnp.float32,
        )
        put(slot, 3, dvalue.astype(jnp.bfloat16))

    for slot in range(slots):
        at = block_of(slot)
        if slot in ready:
            turned, plain = ready[slot]
            values, natural = [turned[number] for number in range(3)], [plain[0], plain[1]]
        else:
            values = stage(slot, tokd, msgs[slot], cosv, sinv, own_bias)
            natural = [value.T for value in values[1:]]
        qt_all[:, at], kt_all[:, at], vt_all[:, at] = values
        k_all[at, :], v_all[at, :] = natural
    dq_total = jnp.zeros((HEAD_DIM, tokd), jnp.float32)
    dv_total = jnp.zeros((HEAD_DIM, tokd), jnp.float32)
    grad = None
    offs = tops = None
    for step in range(slots + 2):
        ahead, slot, behind = step, step - 1, step - 2
        if 0 <= slot < slots:
            offs = [off_row(slot, other) for other in range(slots)]
            top = functools.reduce(jnp.maximum, [one + off for one, off in zip(tops, offs)])
        tops = []
        for other in range(slots):
            found = []
            for keys in pieces_of(other):
                if ahead < slots:
                    found.append(scores(ahead, keys))
                if 0 <= behind:
                    dscores(behind, keys, grad)
                if 0 <= slot < slots:
                    exponentials(slot, keys, top - offs[other])
            if found:
                tops.append(functools.reduce(jnp.maximum, found))
        if 0 <= behind:
            dq_total = dq_total + query_part(behind)
        if 0 <= slot < slots:
            grad, spread = output(slot)
            dv_total = dv_total + spread
    dk_total = jnp.zeros((HEAD_DIM, tokd), jnp.float32)
    for slot in range(slots):
        at = block_of(slot)
        dkey = lax.dot_general(
            qt_all[:HEAD_DIM, :], d_buf[at, :], by_lanes, preferred_element_type=jnp.float32
        )
        dkey = unrotate(dkey * (1.0 / LOG2E), cosv[:, at], sinv[:, at])
        put(slot, 2, dkey.astype(jnp.bfloat16))
        dk_total = dk_total + live(slot, dkey)
    lane = lax.broadcasted_iota(jnp.int32, (HEAD_DIM, LANES), 1)
    columns = jnp.zeros((HEAD_DIM, LANES), jnp.float32)
    for number, total in enumerate((dq_total, dk_total, dv_total)):
        total = jnp.sum(total, axis=1, keepdims=True) * factor
        columns = jnp.where(lane == number, total, columns)
    columns = jnp.concatenate([columns, jnp.zeros((LANES - HEAD_DIM, LANES), jnp.float32)], axis=0)
    lines = columns.T
    copy = None
    if head + 1 < OWN_HEADS:
        sums[...] = lines[:8]
    else:
        tiles, sem = refs[slots + 10 :]
        tile = join_sums(before[...], lines)

        def repeat(device, carry):
            tiles[device] = tile
            return carry

        lax.fori_loop(0, tiles.shape[0], repeat, 0, unroll=min(32, tiles.shape[0]))
        copy = pltpu.make_async_copy(tiles, sums, sem)
        copy.start()
    for slot in range(slots):
        value_part(slot)
    if copy is not None:
        copy.wait()


FIT = LANES - HEAD_DIM
LEFT = HEAD_DIM - FIT


def join_sums(first, second):
    lane = lax.broadcasted_iota(jnp.int32, (1, LANES), 1)
    rows = []
    last = jnp.zeros((1, LANES), jnp.float32)
    for number in range(3):
        moved = pltpu.roll(second[number : number + 1], HEAD_DIM, 1)
        rows.append(jnp.where(lane < HEAD_DIM, first[number : number + 1], moved))
        rest = jnp.where(lane < LEFT, moved, 0.0)
        last = last + (pltpu.roll(rest, number * LEFT, 1) if number else rest)
    return jnp.concatenate(rows + [last], axis=0)


def unpack_kernel(slots, count, images, *refs):
    closed = is_closed(count)
    if not closed:
        lengths, table, *refs = refs
    msgs, refs = refs[: slots + OWN_HEADS - 1], refs[slots + OWN_HEADS - 1 :]
    *outs, held, ready, sems = refs
    early, late = msgs[:OWN_HEADS], list(msgs[OWN_HEADS:])
    late.insert(EARLY, None)
    me = lax.axis_index("tok")

    def place(slot, residue):
        for phase in range(OWN_HEADS):
            begin = pl.multiple_of((phase * SPAN + residue) * HEAD_DIM, 16)
            for number in range(4):
                if slot == EARLY:
                    piece = early[phase][message_rows(number), :]
                else:
                    piece = late[slot][message_rows(4 * phase + number), :]
                held[number, pl.ds(begin, HEAD_DIM), :] = piece

    for slot in range(slots):
        if closed:
            place(slot, lax.rem(me, SPAN) ^ closed_step(slot))
        else:
            _, start = image_of(me, lengths, images)
            source = table[slot, me]
            residue = lax.rem(source + SPAN, SPAN)
            chosen = (source >= 0) & (source == handler_of(start, residue, count))
            pl.when(chosen)(functools.partial(place, slot, residue))
    copies = []
    for number, out in enumerate(outs):
        ready[number] = held[number].T
        copies.append(pltpu.make_async_copy(ready.at[number], out, sems.at[number]))
        copies[-1].start()
    for copy in copies:
        copy.wait()


def bias_kernel(tiles, bias_out):
    def add(group, totals):
        return tuple(
            total + tiles[group * SPAN + residue] for residue, total in enumerate(totals)
        )

    groups = tiles.shape[0] // SPAN
    zero = jnp.zeros(tiles.shape[1:], jnp.float32)
    totals = lax.fori_loop(0, groups, add, (zero,) * SPAN, unroll=groups <= 8)
    for residue, total in enumerate(totals):
        first = residue * HEAD_DIM
        second = (SPAN + residue) * HEAD_DIM
        for number in range(3):
            row = slice(number, number + 1)
            bias_out[row, first : first + HEAD_DIM] = total[row, :HEAD_DIM]
            bias_out[row, second : second + FIT] = total[row, HEAD_DIM:]
            bias_out[row, second + FIT : second + HEAD_DIM] = total[
                3:4, number * LEFT : (number + 1) * LEFT
            ]


def on_device(query_in, key_in, value_in, out_grad, bias, lengths, widths):
    tokd = query_in.shape[1]
    model = query_in.shape[2]
    images = lengths.shape[1]
    count = lax.axis_size("tok")
    dp_size = lax.axis_size("dp")
    closed = is_closed(count)
    sources, targets = trade_tables(count)
    slots = sources.shape[0]
    span = slots * tokd
    smem = pl.BlockSpec(memory_space=pltpu.SMEM)
    vmem = pl.BlockSpec(memory_space=pltpu.VMEM)
    hbm = pl.BlockSpec(memory_space=pltpu.HBM)
    whole = jax.ShapeDtypeStruct((tokd, model), jnp.bfloat16)
    message = jax.ShapeDtypeStruct((4 * HEAD_DIM, tokd), jnp.bfloat16)
    joined = jax.ShapeDtypeStruct((OWN_HEADS * 4 * HEAD_DIM, tokd), jnp.bfloat16)
    devices = dp_size * count
    tokens_all = devices * tokd

    def params(mib):
        return pltpu.CompilerParams(vmem_limit_bytes=int(mib * 1024 * 1024))

    inputs = (query_in[0], key_in[0], value_in[0], out_grad[0])
    later = OWN_HEADS - 1
    lanes = max(end - begin for begin, end in (phase_lanes(p, model) for p in range(OWN_HEADS)))
    own_sends = pl.pallas_call(
        functools.partial(pack_kernel, closed),
        out_shape=[message] * slots,
        in_specs=[hbm] * 4,
        out_specs=[vmem] * slots,
        scratch_shapes=[
            pltpu.VMEM((4, tokd, lanes), jnp.bfloat16),
            pltpu.VMEM((4, lanes, tokd), jnp.bfloat16),
            pltpu.SemaphoreType.DMA((4,)),
        ],
        compiler_params=params(FIRST_PACK_KIB / 1024),
        name="pack_heads",
    )(*inputs)
    sends = [own_sends]
    rounds = trade_rounds(count)
    first = [sends[0][0]] + [
        lax.ppermute(send, "tok", pairs) for send, pairs in zip(sends[0][1:], rounds)
    ]
    table_shape = jax.ShapeDtypeStruct((HALF, span), jnp.float32)
    mask_rows = -(-slots * (slots + 1) // 8) * 8
    turned_shape = jax.ShapeDtypeStruct((3, LANES, tokd), jnp.bfloat16)
    plain_shape = jax.ShapeDtypeStruct((2, tokd, LANES), jnp.bfloat16)
    places = [] if closed else [jnp.asarray(sources)]
    out_shape = (
        [table_shape] * 2
        + [
            jax.ShapeDtypeStruct((mask_rows, tokd), jnp.float32),
            jax.ShapeDtypeStruct((OWN_HEADS * HEAD_DIM, LANES), jnp.float32),
        ]
        + [message] * (later * slots)
        + [turned_shape] * OWN_HEADS
        + [plain_shape] * OWN_HEADS
    )
    prepared = pl.pallas_call(
        functools.partial(prepare_kernel, slots, images, count, tokd),
        out_shape=out_shape,
        in_specs=[smem] * (2 + len(places)) + [vmem] + [hbm] * 4 + [vmem],
        out_specs=[vmem] * len(out_shape),
        scratch_shapes=[
            pltpu.VMEM((later, 4, tokd, lanes), jnp.bfloat16),
            pltpu.VMEM((later, 4, lanes, tokd), jnp.bfloat16),
            pltpu.SemaphoreType.DMA((later, 4)),
            pltpu.VMEM((model, LANES), jnp.float32),
        ],
        compiler_params=params(PREPARE_KIB / 1024),
        cost_estimate=pl.CostEstimate(flops=1_000_000, bytes_accessed=0, transcendentals=0),
        name="prepare",
    )(lengths, widths, *places, bias, *inputs, sends[0][0])
    tables, prepared = prepared[:4], prepared[4:]
    for phase in range(later):
        sends.append(prepared[phase * slots : (phase + 1) * slots])
    prepared = prepared[later * slots :]

    def stage_ahead(slot, phases, messages):
        number = len(phases)
        results = pl.pallas_call(
            functools.partial(stage_kernel, slot, phases, tokd),
            out_shape=[turned_shape] * number + [plain_shape] * number,
            in_specs=[vmem] * (3 + number),
            out_specs=[vmem] * (2 * number),
            compiler_params=params(16),
            cost_estimate=pl.CostEstimate(
                flops=1_000_000 * number, bytes_accessed=0, transcendentals=0
            ),
            name="stage_slot",
        )(tables[0], tables[1], tables[3], *messages)
        return [list(pair) for pair in zip(results[:number], results[number:])]

    phases = tuple(range(OWN_HEADS))
    own = [[prepared[phase], prepared[OWN_HEADS + phase]] for phase in phases]
    staged = [{0: pair} for pair in own]
    got = [first] + [[sent[0]] for sent in sends[1:]]
    for slot in range(1, slots - 1):
        latest = stage_ahead(slot, (0,), [first[slot]])
        for phase in phases[1:]:
            for leaving in (1, 2) if slot == 1 else (slot + 1,):
                send, latest = lax.optimization_barrier((sends[phase][leaving], latest))
                got[phase].append(lax.ppermute(send, "tok", rounds[leaving - 1]))
        staged[0][slot] = latest[0]
    early = []
    carried = []
    for phase in range(OWN_HEADS):
        last = phase + 1 == OWN_HEADS
        kept = [slot for slot in range(slots) if slot != EARLY]
        sums_shape = jax.ShapeDtypeStruct(
            (devices, 4, LANES) if last else (8, LANES), jnp.float32
        )
        *results, total = pl.pallas_call(
            functools.partial(
                attend_kernel,
                slots,
                tuple(staged[phase]),
                closed,
                tokd,
                phase,
                1.0 / tokens_all**0.5,
            ),
            out_shape=[message if slot == EARLY else joined for slot in range(slots)]
            + [sums_shape],
            in_specs=[vmem] * (4 + slots + 2 * len(staged[phase]) + len(carried)),
            out_specs=[vmem] * slots + [hbm if last else vmem],
            scratch_shapes=[pltpu.VMEM((LANES, span), jnp.bfloat16)] * 4
            + [pltpu.VMEM((span, LANES), jnp.bfloat16)] * 2
            + [pltpu.VMEM((2, span, tokd), jnp.float32)]
            + [pltpu.VMEM((span, span), jnp.bfloat16)] * 2
            + (
                [pltpu.VMEM(sums_shape.shape, jnp.float32), pltpu.SemaphoreType.DMA(())]
                if last
                else []
            ),
            compiler_params=params(32),
            cost_estimate=pl.CostEstimate(
                flops=12 * span * span * 256, bytes_accessed=0, transcendentals=0
            ),
            name="attend_head",
        )(*tables, *got[phase], *(one for pair in staged[phase].values() for one in pair), *carried)
        results[EARLY], early = lax.optimization_barrier((results[EARLY], early))
        early.append(send_back(results[EARLY], EARLY))
        carried = [total] + [results[slot] for slot in kept]
    tiles = lax.all_to_all(total, ("dp", "tok"), 0, 0, tiled=True)
    late = [send_back(results[slot], slot) for slot in kept]
    places = [] if closed else [lengths, jnp.asarray(targets)]
    outs = pl.pallas_call(
        functools.partial(unpack_kernel, slots, count, images),
        out_shape=[whole] * 4,
        in_specs=[smem] * len(places) + [vmem] * (OWN_HEADS + len(late)),
        out_specs=[hbm] * 4,
        scratch_shapes=[
            pltpu.VMEM((4, model, tokd), jnp.bfloat16),
            pltpu.VMEM((4, tokd, model), jnp.bfloat16),
            pltpu.SemaphoreType.DMA((4,)),
        ],
        compiler_params=params(16),
        cost_estimate=pl.CostEstimate(flops=UNPACK_FLOPS, bytes_accessed=0, transcendentals=0),
        name="unpack_heads",
    )(*places, *early, *late)
    outs, tiles = lax.optimization_barrier((outs, tiles))
    bias_grad = pl.pallas_call(
        bias_kernel,
        out_shape=jax.ShapeDtypeStruct((3, model), jnp.float32),
        in_specs=[vmem],
        out_specs=vmem,
        compiler_params=params(16),
        name="bias_sums",
    )(tiles)
    return tuple(out[None] for out in outs) + (bias_grad,)


def solution(mesh):
    in_specs = (
        P("dp", "tok", None),
        P("dp", "tok", None),
        P("dp", "tok", None),
        P("dp", "tok", None),
        P(),
        P("dp", None),
        P("dp", None),
    )
    out_specs = (
        P("dp", "tok", None),
        P("dp", "tok", None),
        P("dp", "tok", None),
        P("dp", "tok", None),
        P(),
    )
    return jax.shard_map(
        on_device, mesh=mesh, in_specs=in_specs, out_specs=out_specs, check_vma=False
    )
```

```python
import functools
import math

import jax
import jax.numpy as jnp
import numpy as np
from jax import lax
from jax.experimental import pallas as pl
from jax.experimental.pallas import tpu as pltpu
from jax.sharding import PartitionSpec as P

HEADS = 8
HEAD_DIM = 80
SPAN = 4
OWN_HEADS = HEADS // SPAN
PART = OWN_HEADS * HEAD_DIM
SCALE = HEAD_DIM**-0.5
LOG2E = 1.4426950408889634
NEG = -1e30
LANES = 128
USED = HEAD_DIM + 16
HALF = HEAD_DIM // 2
PIECES = 2
FIRST_PACK_KIB = 52 * 1024 + 1260
PREPARE_KIB = 52 * 1024 + 300
UNPACK_FLOPS = 20_000_000_000

rope_base = 10000.0


def is_closed(count):
    return count in (SPAN, 2 * SPAN)


def closed_step(slot):
    return (SPAN - slot) % SPAN


def trade_rounds(count):
    if is_closed(count):
        return [
            [(one, one ^ closed_step(slot)) for one in range(count)] for slot in range(1, SPAN)
        ]
    rounds = []
    for shift in [*range(1, SPAN), *range(-1, -SPAN, -1)]:
        rounds.append(
            [
                (source, source + shift)
                for source in range(max(0, -shift), min(count, count - shift))
                if (source < SPAN) == (source + shift < SPAN)
            ]
        )
    return rounds


def trade_tables(count):
    rounds = trade_rounds(count)
    sources = np.full((1 + len(rounds), count), -1, np.int32)
    targets = sources.copy()
    sources[0] = targets[0] = np.arange(count)
    for slot, pairs in enumerate(rounds, 1):
        for source, target in pairs:
            sources[slot, target] = source
            targets[slot, source] = target
    return sources, targets


def send_back(result, slot):
    if slot == 0:
        return result
    pairs = trade_rounds(lax.axis_size("tok"))[slot - 1]
    return lax.ppermute(result, "tok", [(target, source) for source, target in pairs])


EARLY = 1


def image_of(block, lengths, images):
    image = jnp.int32(0)
    start = jnp.int32(0)
    begin = jnp.int32(0)
    for number in range(images):
        size = lengths[0, number]
        inside = (block >= begin) & (block < begin + size)
        image = jnp.where(inside, number, image)
        start = jnp.where(inside, begin, start)
        begin = begin + size
    return image, start


def handler_of(start, residue, count):
    device = start + lax.rem(residue - lax.rem(start, SPAN) + SPAN, SPAN)
    return jnp.where(device >= count, device - SPAN, device)


def message_rows(tensor):
    return slice(tensor * HEAD_DIM, (tensor + 1) * HEAD_DIM)


def rotate(values, cosv, sinv):
    first, second = values[:HALF], values[HALF:]
    return jnp.concatenate([first * cosv - second * sinv, second * cosv + first * sinv], axis=0)


def unrotate(values, cosv, sinv):
    first, second = values[:HALF], values[HALF:]
    return jnp.concatenate([first * cosv + second * sinv, second * cosv - first * sinv], axis=0)


def phase_lanes(phase, model):
    size = SPAN * HEAD_DIM
    begin = phase * size // LANES * LANES
    end = -(-(phase + 1) * size // LANES) * LANES
    return begin, min(end, model)


def fetch(phase, inputs, held, sems):
    begin, end = phase_lanes(phase, inputs[0].shape[1])
    copies = [
        pltpu.make_async_copy(source.at[:, begin:end], held.at[number], sems.at[number])
        for number, source in enumerate(inputs)
    ]
    for copy in copies:
        copy.start()
    return copies


def pack(phase, closed, copies, outs, held, turned):
    me = lax.rem(lax.axis_index("tok"), SPAN)
    inner = phase * SPAN * HEAD_DIM % LANES
    steps = (
        [closed_step(slot) for slot in range(SPAN)]
        if closed
        else [0, *range(1, SPAN), *range(SPAN - 1, 0, -1)]
    )
    for number, copy in enumerate(copies):
        copy.wait()
        turned[number] = held[number].T
        for out, step in zip(outs, steps):
            residue = me ^ step if closed else lax.rem(me + step, SPAN)
            rows = pl.ds(pl.multiple_of(inner + residue * HEAD_DIM, 16), HEAD_DIM)
            out[message_rows(number), :] = turned[number, rows, :]


def pack_kernel(closed, *refs):
    inputs, outs, (held, turned, sems) = refs[:4], refs[4:-3], refs[-3:]
    pack(0, closed, fetch(0, inputs, held, sems), outs, held, turned)


def prepare_kernel(slots, images, count, tokd, lengths, widths, *refs):
    closed = is_closed(count)
    if not closed:
        table, *refs = refs
    later = OWN_HEADS - 1
    bias, *inputs, own = refs[:6]
    cos_out, sin_out, mask_out, bias_out, *refs = refs[6:]
    messages, refs = refs[: later * slots], refs[later * slots :]
    turned_out, plain_out = refs[:OWN_HEADS], refs[OWN_HEADS : 2 * OWN_HEADS]
    held, turned, sems, columns = refs[2 * OWN_HEADS :]
    copies = [
        fetch(phase + 1, inputs, held.at[phase], sems.at[phase]) for phase in range(later)
    ]
    me = lax.axis_index("tok")
    residue = lax.rem(me, SPAN)
    spot = lax.broadcasted_iota(jnp.int32, (HALF, tokd), 1)
    feature = lax.broadcasted_iota(jnp.int32, (HALF, tokd), 0)
    by_row = feature < HALF // 2
    feature = jnp.where(by_row, feature, feature - HALF // 2).astype(jnp.float32)
    inverse = jnp.exp(feature * (-math.log(rope_base) / (HALF // 2)))
    ids = []
    for slot in range(slots):
        block = me - residue + (residue ^ closed_step(slot)) if closed else table[slot, me]
        image, start = image_of(block, lengths, images)
        handled = (block >= 0) & (handler_of(start, residue, count) == me)
        ids.append(jnp.where(handled, image, -1 - slot))
        width = widths[0, image]
        bits = jnp.where(width == tokd, 0, jnp.where(width * 2 == tokd, 1, 2))
        shift = tokd.bit_length() - 1 - bits
        local = spot + (block - start) * tokd
        rowpos = lax.shift_right_logical(local, jnp.broadcast_to(shift, local.shape))
        colpos = local & (width - 1)
        angle = jnp.where(by_row, rowpos, colpos).astype(jnp.float32) * inverse
        cos_out[:, slot * tokd : (slot + 1) * tokd] = jnp.cos(angle)
        sin_out[:, slot * tokd : (slot + 1) * tokd] = jnp.sin(angle)
    for slot in range(slots):
        for other in range(slots):
            off = jnp.where(ids[slot] == ids[other], 0.0, NEG)
            row = slot * slots + other
            mask_out[row : row + 1, :] = jnp.full((1, tokd), off, jnp.float32)
        row = slots * slots + slot
        live = jnp.where(ids[slot] >= 0, 1.0, 0.0)
        mask_out[row : row + 1, :] = jnp.full((1, tokd), live, jnp.float32)
    plain = bias[...].astype(jnp.float32)
    rest = jnp.zeros((LANES - plain.shape[0], plain.shape[1]), jnp.float32)
    columns[...] = jnp.concatenate([plain, rest], axis=0).T
    for phase in range(OWN_HEADS):
        begin = pl.multiple_of((phase * SPAN + residue) * HEAD_DIM, 16)
        bias_out[phase * HEAD_DIM : (phase + 1) * HEAD_DIM, :] = columns[pl.ds(begin, HEAD_DIM), :]
    for phase in range(later):
        outs = messages[phase * slots : (phase + 1) * slots]
        pack(phase + 1, closed, copies[phase], outs, held.at[phase], turned.at[phase])
    owns = [own] + [messages[phase * slots] for phase in range(later)]
    stage_all(0, range(OWN_HEADS), tokd, cos_out, sin_out, bias_out, owns, turned_out, plain_out)


def stage(slot, tokd, message, cosv, sinv, bias):
    at = slice(slot * tokd, (slot + 1) * tokd)
    cos_b, sin_b = cosv[:, at], sinv[:, at]
    query, key, value = (
        message[message_rows(tensor), :].astype(jnp.float32) + bias[:, tensor : tensor + 1]
        for tensor in range(3)
    )
    rest_row = lax.broadcasted_iota(jnp.int32, (LANES - HEAD_DIM, tokd), 0)
    zeros = jnp.zeros((LANES - HEAD_DIM, tokd), jnp.float32)
    ones = jnp.where(rest_row < 2, 1.0, 0.0)
    return [
        jnp.concatenate(pair, axis=0).astype(jnp.bfloat16)
        for pair in (
            (rotate(query, cos_b, sin_b), zeros),
            (rotate(key, cos_b, sin_b), zeros),
            (value, ones),
        )
    ]


def stage_all(slot, phases, tokd, cosv, sinv, bias, msgs, turned, plain):
    for number, phase in enumerate(phases):
        own_bias = bias[phase * HEAD_DIM : (phase + 1) * HEAD_DIM, :]
        values = stage(slot, tokd, msgs[number], cosv, sinv, own_bias)
        for tensor, value in enumerate(values):
            turned[number][tensor] = value
            if tensor > 0:
                plain[number][tensor - 1] = value.T


def stage_kernel(slot, phases, tokd, cosv, sinv, bias, *refs):
    count = len(phases)
    msgs, turned, plain = refs[:count], refs[count : 2 * count], refs[2 * count :]
    stage_all(slot, phases, tokd, cosv, sinv, bias, msgs, turned, plain)


def attend_kernel(slots, staged, closed, tokd, head, factor, cosv, sinv, masks, bias, *refs):
    msgs, refs = refs[:slots], refs[slots:]
    ready = {slot: refs[2 * at : 2 * at + 2] for at, slot in enumerate(staged)}
    refs = refs[2 * len(staged) :]
    earlier = ()
    if head > 0:
        before, earlier, refs = refs[0], refs[1:slots], refs[slots:]
    outs, sums = refs[:slots], refs[slots]
    for result, out in zip(earlier, [out for slot, out in enumerate(outs) if slot != EARLY]):
        done = head * 4 * HEAD_DIM
        out[:done, :] = result[:done, :]
    qt_all, kt_all, vt_all, gt_all, k_all, v_all, s_buf, e_buf, d_buf = refs[slots + 1 : slots + 10]
    own_bias = bias[head * HEAD_DIM : (head + 1) * HEAD_DIM, :]
    rest_row = lax.broadcasted_iota(jnp.int32, (LANES - HEAD_DIM, tokd), 0)

    by_lanes = (((1,), (1,)), ((), ()))

    def off_row(slot, other):
        row = slot * slots + other
        return masks[row : row + 1, :]

    def live(slot, values):
        if closed:
            return values
        row = slots * slots + slot
        return values * masks[row : row + 1, :]

    def block_of(slot):
        return slice(slot * tokd, (slot + 1) * tokd)

    def put(slot, tensor, values):
        begin = ((0 if slot == EARLY else 4 * head) + tensor) * HEAD_DIM
        outs[slot][begin : begin + HEAD_DIM, :] = values

    def pieces_of(other):
        step = tokd // PIECES
        return [
            slice(other * tokd + number * step, other * tokd + (number + 1) * step)
            for number in range(PIECES)
        ]

    def scores(slot, keys):
        part = jnp.dot(
            k_all[keys, :], qt_all[:, block_of(slot)], preferred_element_type=jnp.float32
        )
        s_buf[slot % 2, keys, :] = part
        return jnp.max(part, axis=0, keepdims=True)

    def exponentials(slot, keys, top):
        part = jnp.exp2((s_buf[slot % 2, keys, :] - top) * (SCALE * LOG2E))
        e_buf[keys, block_of(slot)] = part.astype(jnp.bfloat16)

    def output(slot):
        mixed = jnp.dot(
            vt_all[:USED, :], e_buf[:, block_of(slot)], preferred_element_type=jnp.float32
        )
        inv = 1.0 / mixed[HEAD_DIM : HEAD_DIM + 1]
        out_b = (mixed[:HEAD_DIM] * inv).astype(jnp.bfloat16)
        put(slot, 0, out_b)
        grad = msgs[slot][message_rows(3), :].astype(jnp.float32)
        delta = jnp.sum(grad * out_b.astype(jnp.float32), axis=0, keepdims=True) * inv
        coarse = delta.astype(jnp.bfloat16).astype(jnp.float32)
        rest = jnp.where(rest_row == 0, -coarse, jnp.where(rest_row == 1, coarse - delta, 0.0))
        grad = jnp.concatenate([grad * inv, rest], axis=0).astype(jnp.bfloat16)
        gt_all[:, block_of(slot)] = grad
        spread = grad[:HEAD_DIM].astype(jnp.float32) * mixed[HEAD_DIM : HEAD_DIM + 1]
        return grad, live(slot, spread)

    def dscores(slot, keys, grad):
        part = jnp.dot(v_all[keys, :], grad, preferred_element_type=jnp.float32)
        d_buf[keys, block_of(slot)] = e_buf[keys, block_of(slot)] * part.astype(jnp.bfloat16)

    def query_part(slot):
        at = block_of(slot)
        dquery = jnp.dot(kt_all[:HEAD_DIM, :], d_buf[:, at], preferred_element_type=jnp.float32)
        dquery = unrotate(dquery * SCALE, cosv[:, at], sinv[:, at])
        put(slot, 1, dquery.astype(jnp.bfloat16))
        return live(slot, dquery)

    def value_part(slot):
        dvalue = lax.dot_general(
            gt_all[:HEAD_DIM, :],
            e_buf[block_of(slot), :],
            by_lanes,
            preferred_element_type=jnp.float32,
        )
        put(slot, 3, dvalue.astype(jnp.bfloat16))

    for slot in range(slots):
        at = block_of(slot)
        if slot in ready:
            turned, plain = ready[slot]
            values, natural = [turned[number] for number in range(3)], [plain[0], plain[1]]
        else:
            values = stage(slot, tokd, msgs[slot], cosv, sinv, own_bias)
            natural = [value.T for value in values[1:]]
        qt_all[:, at], kt_all[:, at], vt_all[:, at] = values
        k_all[at, :], v_all[at, :] = natural
    dq_total = jnp.zeros((HEAD_DIM, tokd), jnp.float32)
    dv_total = jnp.zeros((HEAD_DIM, tokd), jnp.float32)
    grad = None
    offs = tops = None
    for step in range(slots + 2):
        ahead, slot, behind = step, step - 1, step - 2
        if 0 <= slot < slots:
            offs = [off_row(slot, other) for other in range(slots)]
            top = functools.reduce(jnp.maximum, [one + off for one, off in zip(tops, offs)])
        tops = []
        for other in range(slots):
            found = []
            for keys in pieces_of(other):
                if ahead < slots:
                    found.append(scores(ahead, keys))
                if 0 <= behind:
                    dscores(behind, keys, grad)
                if 0 <= slot < slots:
                    exponentials(slot, keys, top - offs[other])
            if found:
                tops.append(functools.reduce(jnp.maximum, found))
        if 0 <= behind:
            dq_total = dq_total + query_part(behind)
        if 0 <= slot < slots:
            grad, spread = output(slot)
            dv_total = dv_total + spread
    dk_total = jnp.zeros((HEAD_DIM, tokd), jnp.float32)
    for slot in range(slots):
        at = block_of(slot)
        dkey = lax.dot_general(
            qt_all[:HEAD_DIM, :], d_buf[at, :], by_lanes, preferred_element_type=jnp.float32
        )
        dkey = unrotate(dkey * SCALE, cosv[:, at], sinv[:, at])
        put(slot, 2, dkey.astype(jnp.bfloat16))
        dk_total = dk_total + live(slot, dkey)
    lane = lax.broadcasted_iota(jnp.int32, (HEAD_DIM, LANES), 1)
    columns = jnp.zeros((HEAD_DIM, LANES), jnp.float32)
    for number, total in enumerate((dq_total, dk_total, dv_total)):
        total = jnp.sum(total, axis=1, keepdims=True) * factor
        columns = jnp.where(lane == number, total, columns)
    columns = jnp.concatenate([columns, jnp.zeros((LANES - HEAD_DIM, LANES), jnp.float32)], axis=0)
    lines = columns.T
    copy = None
    if head + 1 < OWN_HEADS:
        sums[...] = lines[:8]
    else:
        tiles, sem = refs[slots + 10 :]
        tile = join_sums(before[...], lines)

        def repeat(device, carry):
            tiles[device] = tile
            return carry

        lax.fori_loop(0, tiles.shape[0], repeat, 0, unroll=min(32, tiles.shape[0]))
        copy = pltpu.make_async_copy(tiles, sums, sem)
        copy.start()
    for slot in range(slots):
        value_part(slot)
    if copy is not None:
        copy.wait()


FIT = LANES - HEAD_DIM
LEFT = HEAD_DIM - FIT


def join_sums(first, second):
    lane = lax.broadcasted_iota(jnp.int32, (1, LANES), 1)
    rows = []
    last = jnp.zeros((1, LANES), jnp.float32)
    for number in range(3):
        moved = pltpu.roll(second[number : number + 1], HEAD_DIM, 1)
        rows.append(jnp.where(lane < HEAD_DIM, first[number : number + 1], moved))
        rest = jnp.where(lane < LEFT, moved, 0.0)
        last = last + (pltpu.roll(rest, number * LEFT, 1) if number else rest)
    return jnp.concatenate(rows + [last], axis=0)


def unpack_kernel(slots, count, images, *refs):
    closed = is_closed(count)
    if not closed:
        lengths, table, *refs = refs
    msgs, refs = refs[: slots + OWN_HEADS - 1], refs[slots + OWN_HEADS - 1 :]
    *outs, held, ready, sems = refs
    early, late = msgs[:OWN_HEADS], list(msgs[OWN_HEADS:])
    late.insert(EARLY, None)
    me = lax.axis_index("tok")

    def place(slot, residue):
        for phase in range(OWN_HEADS):
            begin = pl.multiple_of((phase * SPAN + residue) * HEAD_DIM, 16)
            for number in range(4):
                if slot == EARLY:
                    piece = early[phase][message_rows(number), :]
                else:
                    piece = late[slot][message_rows(4 * phase + number), :]
                held[number, pl.ds(begin, HEAD_DIM), :] = piece

    for slot in range(slots):
        if closed:
            place(slot, lax.rem(me, SPAN) ^ closed_step(slot))
        else:
            _, start = image_of(me, lengths, images)
            source = table[slot, me]
            residue = lax.rem(source + SPAN, SPAN)
            chosen = (source >= 0) & (source == handler_of(start, residue, count))
            pl.when(chosen)(functools.partial(place, slot, residue))
    copies = []
    for number, out in enumerate(outs):
        ready[number] = held[number].T
        copies.append(pltpu.make_async_copy(ready.at[number], out, sems.at[number]))
        copies[-1].start()
    for copy in copies:
        copy.wait()


def bias_kernel(tiles, bias_out):
    def add(group, totals):
        return tuple(
            total + tiles[group * SPAN + residue] for residue, total in enumerate(totals)
        )

    groups = tiles.shape[0] // SPAN
    zero = jnp.zeros(tiles.shape[1:], jnp.float32)
    totals = lax.fori_loop(0, groups, add, (zero,) * SPAN, unroll=groups <= 8)
    for residue, total in enumerate(totals):
        first = residue * HEAD_DIM
        second = (SPAN + residue) * HEAD_DIM
        for number in range(3):
            row = slice(number, number + 1)
            bias_out[row, first : first + HEAD_DIM] = total[row, :HEAD_DIM]
            bias_out[row, second : second + FIT] = total[row, HEAD_DIM:]
            bias_out[row, second + FIT : second + HEAD_DIM] = total[
                3:4, number * LEFT : (number + 1) * LEFT
            ]


def on_device(query_in, key_in, value_in, out_grad, bias, lengths, widths):
    tokd = query_in.shape[1]
    model = query_in.shape[2]
    images = lengths.shape[1]
    count = lax.axis_size("tok")
    dp_size = lax.axis_size("dp")
    closed = is_closed(count)
    sources, targets = trade_tables(count)
    slots = sources.shape[0]
    span = slots * tokd
    smem = pl.BlockSpec(memory_space=pltpu.SMEM)
    vmem = pl.BlockSpec(memory_space=pltpu.VMEM)
    hbm = pl.BlockSpec(memory_space=pltpu.HBM)
    whole = jax.ShapeDtypeStruct((tokd, model), jnp.bfloat16)
    message = jax.ShapeDtypeStruct((4 * HEAD_DIM, tokd), jnp.bfloat16)
    joined = jax.ShapeDtypeStruct((OWN_HEADS * 4 * HEAD_DIM, tokd), jnp.bfloat16)
    devices = dp_size * count
    tokens_all = devices * tokd

    def params(mib):
        return pltpu.CompilerParams(vmem_limit_bytes=int(mib * 1024 * 1024))

    inputs = (query_in[0], key_in[0], value_in[0], out_grad[0])
    later = OWN_HEADS - 1
    lanes = max(end - begin for begin, end in (phase_lanes(p, model) for p in range(OWN_HEADS)))
    own_sends = pl.pallas_call(
        functools.partial(pack_kernel, closed),
        out_shape=[message] * slots,
        in_specs=[hbm] * 4,
        out_specs=[vmem] * slots,
        scratch_shapes=[
            pltpu.VMEM((4, tokd, lanes), jnp.bfloat16),
            pltpu.VMEM((4, lanes, tokd), jnp.bfloat16),
            pltpu.SemaphoreType.DMA((4,)),
        ],
        compiler_params=params(FIRST_PACK_KIB / 1024),
        name="pack_heads",
    )(*inputs)
    sends = [own_sends]
    rounds = trade_rounds(count)
    first = [sends[0][0]] + [
        lax.ppermute(send, "tok", pairs) for send, pairs in zip(sends[0][1:], rounds)
    ]
    table_shape = jax.ShapeDtypeStruct((HALF, span), jnp.float32)
    mask_rows = -(-slots * (slots + 1) // 8) * 8
    turned_shape = jax.ShapeDtypeStruct((3, LANES, tokd), jnp.bfloat16)
    plain_shape = jax.ShapeDtypeStruct((2, tokd, LANES), jnp.bfloat16)
    places = [] if closed else [jnp.asarray(sources)]
    out_shape = (
        [table_shape] * 2
        + [
            jax.ShapeDtypeStruct((mask_rows, tokd), jnp.float32),
            jax.ShapeDtypeStruct((OWN_HEADS * HEAD_DIM, LANES), jnp.float32),
        ]
        + [message] * (later * slots)
        + [turned_shape] * OWN_HEADS
        + [plain_shape] * OWN_HEADS
    )
    prepared = pl.pallas_call(
        functools.partial(prepare_kernel, slots, images, count, tokd),
        out_shape=out_shape,
        in_specs=[smem] * (2 + len(places)) + [vmem] + [hbm] * 4 + [vmem],
        out_specs=[vmem] * len(out_shape),
        scratch_shapes=[
            pltpu.VMEM((later, 4, tokd, lanes), jnp.bfloat16),
            pltpu.VMEM((later, 4, lanes, tokd), jnp.bfloat16),
            pltpu.SemaphoreType.DMA((later, 4)),
            pltpu.VMEM((model, LANES), jnp.float32),
        ],
        compiler_params=params(PREPARE_KIB / 1024),
        cost_estimate=pl.CostEstimate(flops=1_000_000, bytes_accessed=0, transcendentals=0),
        name="prepare",
    )(lengths, widths, *places, bias, *inputs, sends[0][0])
    tables, prepared = prepared[:4], prepared[4:]
    for phase in range(later):
        sends.append(prepared[phase * slots : (phase + 1) * slots])
    prepared = prepared[later * slots :]

    def stage_ahead(slot, phases, messages):
        number = len(phases)
        results = pl.pallas_call(
            functools.partial(stage_kernel, slot, phases, tokd),
            out_shape=[turned_shape] * number + [plain_shape] * number,
            in_specs=[vmem] * (3 + number),
            out_specs=[vmem] * (2 * number),
            compiler_params=params(16),
            cost_estimate=pl.CostEstimate(
                flops=1_000_000 * number, bytes_accessed=0, transcendentals=0
            ),
            name="stage_slot",
        )(tables[0], tables[1], tables[3], *messages)
        return [list(pair) for pair in zip(results[:number], results[number:])]

    phases = tuple(range(OWN_HEADS))
    own = [[prepared[phase], prepared[OWN_HEADS + phase]] for phase in phases]
    staged = [{0: pair} for pair in own]
    got = [first] + [[sent[0]] for sent in sends[1:]]
    for slot in range(1, slots - 1):
        latest = stage_ahead(slot, (0,), [first[slot]])
        for phase in phases[1:]:
            for leaving in (1, 2) if slot == 1 else (slot + 1,):
                send, latest = lax.optimization_barrier((sends[phase][leaving], latest))
                got[phase].append(lax.ppermute(send, "tok", rounds[leaving - 1]))
        staged[0][slot] = latest[0]
    early = []
    carried = []
    for phase in range(OWN_HEADS):
        last = phase + 1 == OWN_HEADS
        kept = [slot for slot in range(slots) if slot != EARLY]
        sums_shape = jax.ShapeDtypeStruct(
            (devices, 4, LANES) if last else (8, LANES), jnp.float32
        )
        *results, total = pl.pallas_call(
            functools.partial(
                attend_kernel,
                slots,
                tuple(staged[phase]),
                closed,
                tokd,
                phase,
                1.0 / tokens_all**0.5,
            ),
            out_shape=[message if slot == EARLY else joined for slot in range(slots)]
            + [sums_shape],
            in_specs=[vmem] * (4 + slots + 2 * len(staged[phase]) + len(carried)),
            out_specs=[vmem] * slots + [hbm if last else vmem],
            scratch_shapes=[pltpu.VMEM((LANES, span), jnp.bfloat16)] * 4
            + [pltpu.VMEM((span, LANES), jnp.bfloat16)] * 2
            + [pltpu.VMEM((2, span, tokd), jnp.float32)]
            + [pltpu.VMEM((span, span), jnp.bfloat16)] * 2
            + (
                [pltpu.VMEM(sums_shape.shape, jnp.float32), pltpu.SemaphoreType.DMA(())]
                if last
                else []
            ),
            compiler_params=params(32),
            cost_estimate=pl.CostEstimate(
                flops=12 * span * span * 256, bytes_accessed=0, transcendentals=0
            ),
            name="attend_head",
        )(*tables, *got[phase], *(one for pair in staged[phase].values() for one in pair), *carried)
        results[EARLY], early = lax.optimization_barrier((results[EARLY], early))
        early.append(send_back(results[EARLY], EARLY))
        carried = [total] + [results[slot] for slot in kept]
    tiles = lax.all_to_all(total, ("dp", "tok"), 0, 0, tiled=True)
    late = [send_back(results[slot], slot) for slot in kept]
    places = [] if closed else [lengths, jnp.asarray(targets)]
    outs = pl.pallas_call(
        functools.partial(unpack_kernel, slots, count, images),
        out_shape=[whole] * 4,
        in_specs=[smem] * len(places) + [vmem] * (OWN_HEADS + len(late)),
        out_specs=[hbm] * 4,
        scratch_shapes=[
            pltpu.VMEM((4, model, tokd), jnp.bfloat16),
            pltpu.VMEM((4, tokd, model), jnp.bfloat16),
            pltpu.SemaphoreType.DMA((4,)),
        ],
        compiler_params=params(16),
        cost_estimate=pl.CostEstimate(flops=UNPACK_FLOPS, bytes_accessed=0, transcendentals=0),
        name="unpack_heads",
    )(*places, *early, *late)
    outs, tiles = lax.optimization_barrier((outs, tiles))
    bias_grad = pl.pallas_call(
        bias_kernel,
        out_shape=jax.ShapeDtypeStruct((3, model), jnp.float32),
        in_specs=[vmem],
        out_specs=vmem,
        compiler_params=params(16),
        name="bias_sums",
    )(tiles)
    return tuple(out[None] for out in outs) + (bias_grad,)


def solution(mesh):
    in_specs = (
        P("dp", "tok", None),
        P("dp", "tok", None),
        P("dp", "tok", None),
        P("dp", "tok", None),
        P(),
        P("dp", None),
        P("dp", None),
    )
    out_specs = (
        P("dp", "tok", None),
        P("dp", "tok", None),
        P("dp", "tok", None),
        P("dp", "tok", None),
        P(),
    )
    return jax.shard_map(
        on_device, mesh=mesh, in_specs=in_specs, out_specs=out_specs, check_vma=False
    )
```

```python
import functools
import math

import jax
import jax.numpy as jnp
import numpy as np
from jax import lax
from jax.experimental import pallas as pl
from jax.experimental.pallas import tpu as pltpu
from jax.sharding import PartitionSpec as P

HEADS = 8
HEAD_DIM = 80
SPAN = 4
OWN_HEADS = HEADS // SPAN
PART = OWN_HEADS * HEAD_DIM
SCALE = HEAD_DIM**-0.5
LOG2E = 1.4426950408889634
NEG = -1e30
LANES = 128
USED = HEAD_DIM + 16
HALF = HEAD_DIM // 2
PIECES = 2
FIRST_PACK_KIB = 52 * 1024 + 1260
PREPARE_KIB = 52 * 1024 + 300
UNPACK_FLOPS = 20_000_000_000

rope_base = 10000.0


def is_closed(count):
    return count in (SPAN, 2 * SPAN)


def closed_step(slot):
    return (0, 3, 1, 2)[slot]


def trade_rounds(count):
    if is_closed(count):
        return [
            [(one, one ^ closed_step(slot)) for one in range(count)] for slot in range(1, SPAN)
        ]
    rounds = []
    for shift in [*range(1, SPAN), *range(-1, -SPAN, -1)]:
        rounds.append(
            [
                (source, source + shift)
                for source in range(max(0, -shift), min(count, count - shift))
                if (source < SPAN) == (source + shift < SPAN)
            ]
        )
    return rounds


def trade_tables(count):
    rounds = trade_rounds(count)
    sources = np.full((1 + len(rounds), count), -1, np.int32)
    targets = sources.copy()
    sources[0] = targets[0] = np.arange(count)
    for slot, pairs in enumerate(rounds, 1):
        for source, target in pairs:
            sources[slot, target] = source
            targets[slot, source] = target
    return sources, targets


def send_back(result, slot):
    if slot == 0:
        return result
    pairs = trade_rounds(lax.axis_size("tok"))[slot - 1]
    return lax.ppermute(result, "tok", [(target, source) for source, target in pairs])


EARLY = 1


def image_of(block, lengths, images):
    image = jnp.int32(0)
    start = jnp.int32(0)
    begin = jnp.int32(0)
    for number in range(images):
        size = lengths[0, number]
        inside = (block >= begin) & (block < begin + size)
        image = jnp.where(inside, number, image)
        start = jnp.where(inside, begin, start)
        begin = begin + size
    return image, start


def handler_of(start, residue, count):
    device = start + lax.rem(residue - lax.rem(start, SPAN) + SPAN, SPAN)
    return jnp.where(device >= count, device - SPAN, device)


def message_rows(tensor):
    return slice(tensor * HEAD_DIM, (tensor + 1) * HEAD_DIM)


def rotate(values, cosv, sinv):
    first, second = values[:HALF], values[HALF:]
    return jnp.concatenate([first * cosv - second * sinv, second * cosv + first * sinv], axis=0)


def unrotate(values, cosv, sinv):
    first, second = values[:HALF], values[HALF:]
    return jnp.concatenate([first * cosv + second * sinv, second * cosv - first * sinv], axis=0)


def phase_lanes(phase, model):
    size = SPAN * HEAD_DIM
    begin = phase * size // LANES * LANES
    end = -(-(phase + 1) * size // LANES) * LANES
    return begin, min(end, model)


def fetch(phase, inputs, held, sems):
    begin, end = phase_lanes(phase, inputs[0].shape[1])
    copies = [
        pltpu.make_async_copy(source.at[:, begin:end], held.at[number], sems.at[number])
        for number, source in enumerate(inputs)
    ]
    for copy in copies:
        copy.start()
    return copies


def pack(phase, closed, copies, outs, held, turned):
    me = lax.rem(lax.axis_index("tok"), SPAN)
    inner = phase * SPAN * HEAD_DIM % LANES
    steps = (
        [closed_step(slot) for slot in range(SPAN)]
        if closed
        else [0, *range(1, SPAN), *range(SPAN - 1, 0, -1)]
    )
    for number, copy in enumerate(copies):
        copy.wait()
        turned[number] = held[number].T
        for out, step in zip(outs, steps):
            residue = me ^ step if closed else lax.rem(me + step, SPAN)
            rows = pl.ds(pl.multiple_of(inner + residue * HEAD_DIM, 16), HEAD_DIM)
            out[message_rows(number), :] = turned[number, rows, :]


def pack_kernel(closed, *refs):
    inputs, outs, (held, turned, sems) = refs[:4], refs[4:-3], refs[-3:]
    pack(0, closed, fetch(0, inputs, held, sems), outs, held, turned)


def prepare_kernel(slots, images, count, tokd, lengths, widths, *refs):
    closed = is_closed(count)
    if not closed:
        table, *refs = refs
    later = OWN_HEADS - 1
    bias, *inputs, own = refs[:6]
    cos_out, sin_out, mask_out, bias_out, *refs = refs[6:]
    messages, refs = refs[: later * slots], refs[later * slots :]
    turned_out, plain_out = refs[:OWN_HEADS], refs[OWN_HEADS : 2 * OWN_HEADS]
    held, turned, sems, columns = refs[2 * OWN_HEADS :]
    copies = [
        fetch(phase + 1, inputs, held.at[phase], sems.at[phase]) for phase in range(later)
    ]
    me = lax.axis_index("tok")
    residue = lax.rem(me, SPAN)
    spot = lax.broadcasted_iota(jnp.int32, (HALF, tokd), 1)
    feature = lax.broadcasted_iota(jnp.int32, (HALF, tokd), 0)
    by_row = feature < HALF // 2
    feature = jnp.where(by_row, feature, feature - HALF // 2).astype(jnp.float32)
    inverse = jnp.exp(feature * (-math.log(rope_base) / (HALF // 2)))
    ids = []
    for slot in range(slots):
        block = me - residue + (residue ^ closed_step(slot)) if closed else table[slot, me]
        image, start = image_of(block, lengths, images)
        handled = (block >= 0) & (handler_of(start, residue, count) == me)
        ids.append(jnp.where(handled, image, -1 - slot))
        width = widths[0, image]
        bits = jnp.where(width == tokd, 0, jnp.where(width * 2 == tokd, 1, 2))
        shift = tokd.bit_length() - 1 - bits
        local = spot + (block - start) * tokd
        rowpos = lax.shift_right_logical(local, jnp.broadcast_to(shift, local.shape))
        colpos = local & (width - 1)
        angle = jnp.where(by_row, rowpos, colpos).astype(jnp.float32) * inverse
        cos_out[:, slot * tokd : (slot + 1) * tokd] = jnp.cos(angle)
        sin_out[:, slot * tokd : (slot + 1) * tokd] = jnp.sin(angle)
    for slot in range(slots):
        for other in range(slots):
            off = jnp.where(ids[slot] == ids[other], 0.0, NEG)
            row = slot * slots + other
            mask_out[row : row + 1, :] = jnp.full((1, tokd), off, jnp.float32)
        row = slots * slots + slot
        live = jnp.where(ids[slot] >= 0, 1.0, 0.0)
        mask_out[row : row + 1, :] = jnp.full((1, tokd), live, jnp.float32)
    plain = bias[...].astype(jnp.float32)
    rest = jnp.zeros((LANES - plain.shape[0], plain.shape[1]), jnp.float32)
    columns[...] = jnp.concatenate([plain, rest], axis=0).T
    for phase in range(OWN_HEADS):
        begin = pl.multiple_of((phase * SPAN + residue) * HEAD_DIM, 16)
        bias_out[phase * HEAD_DIM : (phase + 1) * HEAD_DIM, :] = columns[pl.ds(begin, HEAD_DIM), :]
    for phase in range(later):
        outs = messages[phase * slots : (phase + 1) * slots]
        pack(phase + 1, closed, copies[phase], outs, held.at[phase], turned.at[phase])
    owns = [own] + [messages[phase * slots] for phase in range(later)]
    stage_all(0, range(OWN_HEADS), tokd, cos_out, sin_out, bias_out, owns, turned_out, plain_out)


def stage(slot, tokd, message, cosv, sinv, bias):
    at = slice(slot * tokd, (slot + 1) * tokd)
    cos_b, sin_b = cosv[:, at], sinv[:, at]
    query, key, value = (
        message[message_rows(tensor), :].astype(jnp.float32) + bias[:, tensor : tensor + 1]
        for tensor in range(3)
    )
    rest_row = lax.broadcasted_iota(jnp.int32, (LANES - HEAD_DIM, tokd), 0)
    zeros = jnp.zeros((LANES - HEAD_DIM, tokd), jnp.float32)
    ones = jnp.where(rest_row < 2, 1.0, 0.0)
    return [
        jnp.concatenate(pair, axis=0).astype(jnp.bfloat16)
        for pair in (
            (rotate(query, cos_b, sin_b), zeros),
            (rotate(key, cos_b, sin_b), zeros),
            (value, ones),
        )
    ]


def stage_all(slot, phases, tokd, cosv, sinv, bias, msgs, turned, plain):
    for number, phase in enumerate(phases):
        own_bias = bias[phase * HEAD_DIM : (phase + 1) * HEAD_DIM, :]
        values = stage(slot, tokd, msgs[number], cosv, sinv, own_bias)
        for tensor, value in enumerate(values):
            turned[number][tensor] = value
            if tensor > 0:
                plain[number][tensor - 1] = value.T


def stage_kernel(slot, phases, tokd, cosv, sinv, bias, *refs):
    count = len(phases)
    msgs, turned, plain = refs[:count], refs[count : 2 * count], refs[2 * count :]
    stage_all(slot, phases, tokd, cosv, sinv, bias, msgs, turned, plain)


def attend_kernel(slots, staged, closed, tokd, head, factor, cosv, sinv, masks, bias, *refs):
    msgs, refs = refs[:slots], refs[slots:]
    ready = {slot: refs[2 * at : 2 * at + 2] for at, slot in enumerate(staged)}
    refs = refs[2 * len(staged) :]
    earlier = ()
    if head > 0:
        before, earlier, refs = refs[0], refs[1:slots], refs[slots:]
    outs, sums = refs[:slots], refs[slots]
    for result, out in zip(earlier, [out for slot, out in enumerate(outs) if slot != EARLY]):
        done = head * 4 * HEAD_DIM
        out[:done, :] = result[:done, :]
    qt_all, kt_all, vt_all, gt_all, k_all, v_all, s_buf, e_buf, d_buf = refs[slots + 1 : slots + 10]
    own_bias = bias[head * HEAD_DIM : (head + 1) * HEAD_DIM, :]
    rest_row = lax.broadcasted_iota(jnp.int32, (LANES - HEAD_DIM, tokd), 0)

    by_lanes = (((1,), (1,)), ((), ()))

    def off_row(slot, other):
        row = slot * slots + other
        return masks[row : row + 1, :]

    def live(slot, values):
        if closed:
            return values
        row = slots * slots + slot
        return values * masks[row : row + 1, :]

    def block_of(slot):
        return slice(slot * tokd, (slot + 1) * tokd)

    def put(slot, tensor, values):
        begin = ((0 if slot == EARLY else 4 * head) + tensor) * HEAD_DIM
        outs[slot][begin : begin + HEAD_DIM, :] = values

    def pieces_of(other):
        step = tokd // PIECES
        return [
            slice(other * tokd + number * step, other * tokd + (number + 1) * step)
            for number in range(PIECES)
        ]

    def scores(slot, keys):
        part = jnp.dot(
            k_all[keys, :], qt_all[:, block_of(slot)], preferred_element_type=jnp.float32
        )
        s_buf[slot % 2, keys, :] = part
        return jnp.max(part, axis=0, keepdims=True)

    def exponentials(slot, keys, top):
        part = jnp.exp2((s_buf[slot % 2, keys, :] - top) * (SCALE * LOG2E))
        e_buf[keys, block_of(slot)] = part.astype(jnp.bfloat16)

    def output(slot):
        mixed = jnp.dot(
            vt_all[:USED, :], e_buf[:, block_of(slot)], preferred_element_type=jnp.float32
        )
        inv = 1.0 / mixed[HEAD_DIM : HEAD_DIM + 1]
        out_b = (mixed[:HEAD_DIM] * inv).astype(jnp.bfloat16)
        put(slot, 0, out_b)
        grad = msgs[slot][message_rows(3), :].astype(jnp.float32)
        delta = jnp.sum(grad * out_b.astype(jnp.float32), axis=0, keepdims=True) * inv
        coarse = delta.astype(jnp.bfloat16).astype(jnp.float32)
        rest = jnp.where(rest_row == 0, -coarse, jnp.where(rest_row == 1, coarse - delta, 0.0))
        grad = jnp.concatenate([grad * inv, rest], axis=0).astype(jnp.bfloat16)
        gt_all[:, block_of(slot)] = grad
        spread = grad[:HEAD_DIM].astype(jnp.float32) * mixed[HEAD_DIM : HEAD_DIM + 1]
        return grad, live(slot, spread)

    def dscores(slot, keys, grad):
        part = jnp.dot(v_all[keys, :], grad, preferred_element_type=jnp.float32)
        d_buf[keys, block_of(slot)] = e_buf[keys, block_of(slot)] * part.astype(jnp.bfloat16)

    def query_part(slot):
        at = block_of(slot)
        dquery = jnp.dot(kt_all[:HEAD_DIM, :], d_buf[:, at], preferred_element_type=jnp.float32)
        dquery = unrotate(dquery * SCALE, cosv[:, at], sinv[:, at])
        put(slot, 1, dquery.astype(jnp.bfloat16))
        return live(slot, dquery)

    def value_part(slot):
        dvalue = lax.dot_general(
            gt_all[:HEAD_DIM, :],
            e_buf[block_of(slot), :],
            by_lanes,
            preferred_element_type=jnp.float32,
        )
        put(slot, 3, dvalue.astype(jnp.bfloat16))

    for slot in range(slots):
        at = block_of(slot)
        if slot in ready:
            turned, plain = ready[slot]
            values, natural = [turned[number] for number in range(3)], [plain[0], plain[1]]
        else:
            values = stage(slot, tokd, msgs[slot], cosv, sinv, own_bias)
            natural = [value.T for value in values[1:]]
        qt_all[:, at], kt_all[:, at], vt_all[:, at] = values
        k_all[at, :], v_all[at, :] = natural
    dq_total = jnp.zeros((HEAD_DIM, tokd), jnp.float32)
    dv_total = jnp.zeros((HEAD_DIM, tokd), jnp.float32)
    grad = None
    offs = tops = None
    for step in range(slots + 2):
        ahead, slot, behind = step, step - 1, step - 2
        if 0 <= slot < slots:
            offs = [off_row(slot, other) for other in range(slots)]
            top = functools.reduce(jnp.maximum, [one + off for one, off in zip(tops, offs)])
        tops = []
        for other in range(slots):
            found = []
            for keys in pieces_of(other):
                if ahead < slots:
                    found.append(scores(ahead, keys))
                if 0 <= behind:
                    dscores(behind, keys, grad)
                if 0 <= slot < slots:
                    exponentials(slot, keys, top - offs[other])
            if found:
                tops.append(functools.reduce(jnp.maximum, found))
        if 0 <= behind:
            dq_total = dq_total + query_part(behind)
        if 0 <= slot < slots:
            grad, spread = output(slot)
            dv_total = dv_total + spread
    dk_total = jnp.zeros((HEAD_DIM, tokd), jnp.float32)
    for slot in range(slots):
        at = block_of(slot)
        dkey = lax.dot_general(
            qt_all[:HEAD_DIM, :], d_buf[at, :], by_lanes, preferred_element_type=jnp.float32
        )
        dkey = unrotate(dkey * SCALE, cosv[:, at], sinv[:, at])
        put(slot, 2, dkey.astype(jnp.bfloat16))
        dk_total = dk_total + live(slot, dkey)
    lane = lax.broadcasted_iota(jnp.int32, (HEAD_DIM, LANES), 1)
    columns = jnp.zeros((HEAD_DIM, LANES), jnp.float32)
    for number, total in enumerate((dq_total, dk_total, dv_total)):
        total = jnp.sum(total, axis=1, keepdims=True) * factor
        columns = jnp.where(lane == number, total, columns)
    columns = jnp.concatenate([columns, jnp.zeros((LANES - HEAD_DIM, LANES), jnp.float32)], axis=0)
    lines = columns.T
    copy = None
    if head + 1 < OWN_HEADS:
        sums[...] = lines[:8]
    else:
        tiles, sem = refs[slots + 10 :]
        tile = join_sums(before[...], lines)

        def repeat(device, carry):
            tiles[device] = tile
            return carry

        lax.fori_loop(0, tiles.shape[0], repeat, 0, unroll=min(32, tiles.shape[0]))
        copy = pltpu.make_async_copy(tiles, sums, sem)
        copy.start()
    for slot in range(slots):
        value_part(slot)
    if copy is not None:
        copy.wait()


FIT = LANES - HEAD_DIM
LEFT = HEAD_DIM - FIT


def join_sums(first, second):
    lane = lax.broadcasted_iota(jnp.int32, (1, LANES), 1)
    rows = []
    last = jnp.zeros((1, LANES), jnp.float32)
    for number in range(3):
        moved = pltpu.roll(second[number : number + 1], HEAD_DIM, 1)
        rows.append(jnp.where(lane < HEAD_DIM, first[number : number + 1], moved))
        rest = jnp.where(lane < LEFT, moved, 0.0)
        last = last + (pltpu.roll(rest, number * LEFT, 1) if number else rest)
    return jnp.concatenate(rows + [last], axis=0)


def unpack_kernel(slots, count, images, *refs):
    closed = is_closed(count)
    if not closed:
        lengths, table, *refs = refs
    msgs, refs = refs[: slots + OWN_HEADS - 1], refs[slots + OWN_HEADS - 1 :]
    *outs, held, ready, sems = refs
    early, late = msgs[:OWN_HEADS], list(msgs[OWN_HEADS:])
    late.insert(EARLY, None)
    me = lax.axis_index("tok")

    def place(slot, residue):
        for phase in range(OWN_HEADS):
            begin = pl.multiple_of((phase * SPAN + residue) * HEAD_DIM, 16)
            for number in range(4):
                if slot == EARLY:
                    piece = early[phase][message_rows(number), :]
                else:
                    piece = late[slot][message_rows(4 * phase + number), :]
                held[number, pl.ds(begin, HEAD_DIM), :] = piece

    for slot in range(slots):
        if closed:
            place(slot, lax.rem(me, SPAN) ^ closed_step(slot))
        else:
            _, start = image_of(me, lengths, images)
            source = table[slot, me]
            residue = lax.rem(source + SPAN, SPAN)
            chosen = (source >= 0) & (source == handler_of(start, residue, count))
            pl.when(chosen)(functools.partial(place, slot, residue))
    copies = []
    for number, out in enumerate(outs):
        ready[number] = held[number].T
        copies.append(pltpu.make_async_copy(ready.at[number], out, sems.at[number]))
        copies[-1].start()
    for copy in copies:
        copy.wait()


def bias_kernel(tiles, bias_out):
    def add(group, totals):
        return tuple(
            total + tiles[group * SPAN + residue] for residue, total in enumerate(totals)
        )

    groups = tiles.shape[0] // SPAN
    zero = jnp.zeros(tiles.shape[1:], jnp.float32)
    totals = lax.fori_loop(0, groups, add, (zero,) * SPAN, unroll=groups <= 8)
    for residue, total in enumerate(totals):
        first = residue * HEAD_DIM
        second = (SPAN + residue) * HEAD_DIM
        for number in range(3):
            row = slice(number, number + 1)
            bias_out[row, first : first + HEAD_DIM] = total[row, :HEAD_DIM]
            bias_out[row, second : second + FIT] = total[row, HEAD_DIM:]
            bias_out[row, second + FIT : second + HEAD_DIM] = total[
                3:4, number * LEFT : (number + 1) * LEFT
            ]


def on_device(query_in, key_in, value_in, out_grad, bias, lengths, widths):
    tokd = query_in.shape[1]
    model = query_in.shape[2]
    images = lengths.shape[1]
    count = lax.axis_size("tok")
    dp_size = lax.axis_size("dp")
    closed = is_closed(count)
    sources, targets = trade_tables(count)
    slots = sources.shape[0]
    span = slots * tokd
    smem = pl.BlockSpec(memory_space=pltpu.SMEM)
    vmem = pl.BlockSpec(memory_space=pltpu.VMEM)
    hbm = pl.BlockSpec(memory_space=pltpu.HBM)
    whole = jax.ShapeDtypeStruct((tokd, model), jnp.bfloat16)
    message = jax.ShapeDtypeStruct((4 * HEAD_DIM, tokd), jnp.bfloat16)
    joined = jax.ShapeDtypeStruct((OWN_HEADS * 4 * HEAD_DIM, tokd), jnp.bfloat16)
    devices = dp_size * count
    tokens_all = devices * tokd

    def params(mib):
        return pltpu.CompilerParams(vmem_limit_bytes=int(mib * 1024 * 1024))

    inputs = (query_in[0], key_in[0], value_in[0], out_grad[0])
    later = OWN_HEADS - 1
    lanes = max(end - begin for begin, end in (phase_lanes(p, model) for p in range(OWN_HEADS)))
    own_sends = pl.pallas_call(
        functools.partial(pack_kernel, closed),
        out_shape=[message] * slots,
        in_specs=[hbm] * 4,
        out_specs=[vmem] * slots,
        scratch_shapes=[
            pltpu.VMEM((4, tokd, lanes), jnp.bfloat16),
            pltpu.VMEM((4, lanes, tokd), jnp.bfloat16),
            pltpu.SemaphoreType.DMA((4,)),
        ],
        compiler_params=params(FIRST_PACK_KIB / 1024),
        name="pack_heads",
    )(*inputs)
    sends = [own_sends]
    rounds = trade_rounds(count)
    first = [sends[0][0]] + [
        lax.ppermute(send, "tok", pairs) for send, pairs in zip(sends[0][1:], rounds)
    ]
    table_shape = jax.ShapeDtypeStruct((HALF, span), jnp.float32)
    mask_rows = -(-slots * (slots + 1) // 8) * 8
    turned_shape = jax.ShapeDtypeStruct((3, LANES, tokd), jnp.bfloat16)
    plain_shape = jax.ShapeDtypeStruct((2, tokd, LANES), jnp.bfloat16)
    places = [] if closed else [jnp.asarray(sources)]
    out_shape = (
        [table_shape] * 2
        + [
            jax.ShapeDtypeStruct((mask_rows, tokd), jnp.float32),
            jax.ShapeDtypeStruct((OWN_HEADS * HEAD_DIM, LANES), jnp.float32),
        ]
        + [message] * (later * slots)
        + [turned_shape] * OWN_HEADS
        + [plain_shape] * OWN_HEADS
    )
    prepared = pl.pallas_call(
        functools.partial(prepare_kernel, slots, images, count, tokd),
        out_shape=out_shape,
        in_specs=[smem] * (2 + len(places)) + [vmem] + [hbm] * 4 + [vmem],
        out_specs=[vmem] * len(out_shape),
        scratch_shapes=[
            pltpu.VMEM((later, 4, tokd, lanes), jnp.bfloat16),
            pltpu.VMEM((later, 4, lanes, tokd), jnp.bfloat16),
            pltpu.SemaphoreType.DMA((later, 4)),
            pltpu.VMEM((model, LANES), jnp.float32),
        ],
        compiler_params=params(PREPARE_KIB / 1024),
        cost_estimate=pl.CostEstimate(flops=1_000_000, bytes_accessed=0, transcendentals=0),
        name="prepare",
    )(lengths, widths, *places, bias, *inputs, sends[0][0])
    tables, prepared = prepared[:4], prepared[4:]
    for phase in range(later):
        sends.append(prepared[phase * slots : (phase + 1) * slots])
    prepared = prepared[later * slots :]

    def stage_ahead(slot, phases, messages):
        number = len(phases)
        results = pl.pallas_call(
            functools.partial(stage_kernel, slot, phases, tokd),
            out_shape=[turned_shape] * number + [plain_shape] * number,
            in_specs=[vmem] * (3 + number),
            out_specs=[vmem] * (2 * number),
            compiler_params=params(16),
            cost_estimate=pl.CostEstimate(
                flops=1_000_000 * number, bytes_accessed=0, transcendentals=0
            ),
            name="stage_slot",
        )(tables[0], tables[1], tables[3], *messages)
        return [list(pair) for pair in zip(results[:number], results[number:])]

    phases = tuple(range(OWN_HEADS))
    own = [[prepared[phase], prepared[OWN_HEADS + phase]] for phase in phases]
    staged = [{0: pair} for pair in own]
    got = [first] + [[sent[0]] for sent in sends[1:]]
    for slot in range(1, slots - 1):
        latest = stage_ahead(slot, (0,), [first[slot]])
        for phase in phases[1:]:
            for leaving in (1, 2) if slot == 1 else (slot + 1,):
                send, latest = lax.optimization_barrier((sends[phase][leaving], latest))
                got[phase].append(lax.ppermute(send, "tok", rounds[leaving - 1]))
        staged[0][slot] = latest[0]
    early = []
    carried = []
    for phase in range(OWN_HEADS):
        last = phase + 1 == OWN_HEADS
        kept = [slot for slot in range(slots) if slot != EARLY]
        sums_shape = jax.ShapeDtypeStruct(
            (devices, 4, LANES) if last else (8, LANES), jnp.float32
        )
        *results, total = pl.pallas_call(
            functools.partial(
                attend_kernel,
                slots,
                tuple(staged[phase]),
                closed,
                tokd,
                phase,
                1.0 / tokens_all**0.5,
            ),
            out_shape=[message if slot == EARLY else joined for slot in range(slots)]
            + [sums_shape],
            in_specs=[vmem] * (4 + slots + 2 * len(staged[phase]) + len(carried)),
            out_specs=[vmem] * slots + [hbm if last else vmem],
            scratch_shapes=[pltpu.VMEM((LANES, span), jnp.bfloat16)] * 4
            + [pltpu.VMEM((span, LANES), jnp.bfloat16)] * 2
            + [pltpu.VMEM((2, span, tokd), jnp.float32)]
            + [pltpu.VMEM((span, span), jnp.bfloat16)] * 2
            + (
                [pltpu.VMEM(sums_shape.shape, jnp.float32), pltpu.SemaphoreType.DMA(())]
                if last
                else []
            ),
            compiler_params=params(32),
            cost_estimate=pl.CostEstimate(
                flops=12 * span * span * 256, bytes_accessed=0, transcendentals=0
            ),
            name="attend_head",
        )(*tables, *got[phase], *(one for pair in staged[phase].values() for one in pair), *carried)
        results[EARLY], early = lax.optimization_barrier((results[EARLY], early))
        early.append(send_back(results[EARLY], EARLY))
        carried = [total] + [results[slot] for slot in kept]
    tiles = lax.all_to_all(total, ("dp", "tok"), 0, 0, tiled=True)
    late = [send_back(results[slot], slot) for slot in kept]
    places = [] if closed else [lengths, jnp.asarray(targets)]
    outs = pl.pallas_call(
        functools.partial(unpack_kernel, slots, count, images),
        out_shape=[whole] * 4,
        in_specs=[smem] * len(places) + [vmem] * (OWN_HEADS + len(late)),
        out_specs=[hbm] * 4,
        scratch_shapes=[
            pltpu.VMEM((4, model, tokd), jnp.bfloat16),
            pltpu.VMEM((4, tokd, model), jnp.bfloat16),
            pltpu.SemaphoreType.DMA((4,)),
        ],
        compiler_params=params(16),
        cost_estimate=pl.CostEstimate(flops=UNPACK_FLOPS, bytes_accessed=0, transcendentals=0),
        name="unpack_heads",
    )(*places, *early, *late)
    outs, tiles = lax.optimization_barrier((outs, tiles))
    bias_grad = pl.pallas_call(
        bias_kernel,
        out_shape=jax.ShapeDtypeStruct((3, model), jnp.float32),
        in_specs=[vmem],
        out_specs=vmem,
        compiler_params=params(16),
        name="bias_sums",
    )(tiles)
    return tuple(out[None] for out in outs) + (bias_grad,)


def solution(mesh):
    in_specs = (
        P("dp", "tok", None),
        P("dp", "tok", None),
        P("dp", "tok", None),
        P("dp", "tok", None),
        P(),
        P("dp", None),
        P("dp", None),
    )
    out_specs = (
        P("dp", "tok", None),
        P("dp", "tok", None),
        P("dp", "tok", None),
        P("dp", "tok", None),
        P(),
    )
    return jax.shard_map(
        on_device, mesh=mesh, in_specs=in_specs, out_specs=out_specs, check_vma=False
    )
```
